32 devices in a mesh: seq: 8 (over y, x, core), head: 4 (over z).
Axes of the slice: x: 2, y: 2, z: 4, core: 2. Of those that a mesh axis runs over, the one named last changes fastest.
Arguments:
- queries: bfloat16 [8192, 8192], P('seq', 'head'), may hold values from -6 to 6
- key_rows: bfloat16 [8192, 8192], P('seq', 'head'), may hold values from -6 to 6
- value_rows: bfloat16 [8192, 8192], P('seq', 'head')
- log_decay: float32 [64, 8192], P('head', 'seq')
- doc_start: int32 [8192], P('seq'), may hold values from 0 to 1, as said below
- gate_input: bfloat16 [8192, 8192], P('seq', 'head'), may hold values from -6 to 6
- norm_gain: float32 [8192], P('head'), may hold values from 0.1 to 1.9
- out_grad: bfloat16 [8192, 8192], P('seq', 'head'), may hold values from -6 to 6
Outputs:
- gated: bfloat16 [8192, 8192], P('seq', 'head')
- gate_grad: bfloat16 [8192, 8192], P('seq', 'head')
- query_grad: bfloat16 [8192, 8192], P('seq', 'head')
- key_grad: bfloat16 [8192, 8192], P('seq', 'head')
- value_grad: bfloat16 [8192, 8192], P('seq', 'head')
The draws below stay inside these ranges and needn't reach their ends.
Inputs may be any that keep to these rules, and one draw needn't show every extreme that they name: `doc_start`: only the first 512 and the last 512 tokens of the sequence can begin a document, and each of these two ranges holds at least one start; one document runs over all devices but the first and the last.
All inputs are finite; a program needn't handle non-finite values.
Results may differ from the reference program's by a relative error of at most 0.0062.
Values sent between devices are 32-bit elements; how exact they have to be, the bound alone decides.
No kernel may reach another device: no remote copies, remote signals or barrier semaphores. Data moves between devices by JAX's collectives and lax.ppermute only.
A program may use at most 128 MiB of HBM per device.

```python
import math
import jax
import jax.numpy as jnp
from jax import lax

HEAD_TOTAL = 64
HD = 128
TOK_DEV = 1024
BLOCK = 512
TOKEN_TOTAL = 8192


def draw_value_rows(key, part):
    key = jax.random.fold_in(key, 7)
    random_subkeys = jax.random.split(key, 3)
    column = jnp.arange(HEAD_TOTAL * HD) // HD
    col_scale = 10.0 ** (column.astype(jnp.float32) / max(HEAD_TOTAL - 1, 1))
    sample = jnp.clip(jax.random.normal(random_subkeys[0], (TOKEN_TOTAL, HEAD_TOTAL * HD), jnp.float32), -4.0, 4.0)
    row_scale = jnp.exp(jax.random.uniform(random_subkeys[2], (TOKEN_TOTAL, 1), jnp.float32, 0.0, math.log(3.0)))
    return (sample * col_scale[None, :] * row_scale * 0.25).astype(jnp.bfloat16)


def draw_log_decay(key, part):
    key = jax.random.fold_in(key, 13)
    random_subkeys = jax.random.split(key, 8)
    fast_count = max(1, 3 * HEAD_TOTAL // 8)
    middle_count = max(1, HEAD_TOTAL // 4)
    head_rank = jax.random.permutation(random_subkeys[0], HEAD_TOTAL)[:, None]
    fast = head_rank < fast_count
    middle = (head_rank >= fast_count) & (head_rank < fast_count + middle_count)
    fast_rate = jnp.exp(jax.random.uniform(random_subkeys[1], (HEAD_TOTAL, 1), jnp.float32, math.log(1.0 / 50.0), math.log(1.0 / 30.0)))
    slow_rate = jnp.exp(jax.random.uniform(random_subkeys[2], (HEAD_TOTAL, 1), jnp.float32, math.log(0.05), math.log(0.4))) / TOKEN_TOTAL
    middle_rate = jnp.exp(jax.random.uniform(random_subkeys[7], (HEAD_TOTAL, 1), jnp.float32, math.log(0.8), math.log(2.5))) / TOK_DEV
    decay_rates = jnp.where(fast, fast_rate, jnp.where(middle, middle_rate, slow_rate))
    shards = TOKEN_TOTAL // TOK_DEV
    machine_multiplier = jnp.exp(jax.random.uniform(random_subkeys[3], (HEAD_TOTAL, shards), jnp.float32, -math.log(2.0), math.log(2.0)))
    machine_multiplier = jnp.repeat(machine_multiplier, TOK_DEV, axis=1)
    random_noise = jnp.exp(jax.random.uniform(random_subkeys[4], (HEAD_TOTAL, TOKEN_TOTAL), jnp.float32, -0.35, 0.35))
    spike_amount = jax.random.uniform(random_subkeys[5], (HEAD_TOTAL, TOKEN_TOTAL), jnp.float32) < 2.0 / TOKEN_TOTAL
    layer_depth_level = jnp.log(jax.random.uniform(random_subkeys[6], (HEAD_TOTAL, TOKEN_TOTAL), jnp.float32, 0.5, 0.8))
    return jnp.where(spike_amount, layer_depth_level, -decay_rates * machine_multiplier * random_noise).astype(jnp.float32)


def draw_doc_start(key, part):
    key = jax.random.fold_in(key, 21)
    random_subkeys = jax.random.split(key, 3)
    position = jnp.arange(TOKEN_TOTAL, dtype=jnp.int32)
    half_dev = TOK_DEV // 2
    rolls = jax.random.randint(random_subkeys[0], (TOKEN_TOTAL,), 0, TOK_DEV, dtype=jnp.int32)
    edges = (position < half_dev) | (position >= TOKEN_TOTAL - half_dev)
    scattered = edges & (rolls < 4)
    first_pick = jax.random.randint(random_subkeys[1], (), 0, half_dev, dtype=jnp.int32)
    last_pick = jax.random.randint(random_subkeys[2], (), TOKEN_TOTAL - half_dev, TOKEN_TOTAL, dtype=jnp.int32)
    chosen = scattered | (position == first_pick) | (position == last_pick)
    return chosen.astype(jnp.int32)


def steps_of(key, shape, cuts, smallest, largest):
    factor_of, own = 1.0, jax.random.fold_in(key, 6)
    for dim, parts in cuts:
        draws = jnp.exp(jax.random.uniform(jax.random.fold_in(own, dim), (parts,), jnp.float32, smallest / len(cuts), largest / len(cuts)))
        factor_of = factor_of * jnp.repeat(draws, shape[dim] // parts).reshape([-1 if axis == dim else 1 for axis in range(len(shape))])
    return factor_of


def gaussian(stream_key, dims, deviation, reach, pieces=(), kind=jnp.bfloat16):
    level = steps_of(stream_key, dims, pieces, -0.22, 0.18) if pieces else 1.0
    result = jax.random.normal(stream_key, dims, jnp.float32) * deviation * level
    return jnp.minimum(jnp.maximum(result, -reach), reach).astype(kind)


def setup_inputs(seed: int = 0) -> dict:
    streams_of = jax.random.split(jax.random.key(seed), 9)
    queries = gaussian(streams_of[0], (TOKEN_TOTAL, HEAD_TOTAL * HD), 1.0, 6.0, ((0, 8), (1, 4)))
    key_rows = gaussian(streams_of[1], (TOKEN_TOTAL, HEAD_TOTAL * HD), 1.0, 6.0, ((0, 8), (1, 4)))
    value_rows = draw_value_rows(jax.random.fold_in(streams_of[8], 71), 0)
    log_decay = draw_log_decay(jax.random.fold_in(streams_of[8], 71), 0)
    doc_start = draw_doc_start(jax.random.fold_in(streams_of[8], 71), 0)
    gate_input = gaussian(streams_of[5], (TOKEN_TOTAL, HEAD_TOTAL * HD), 1.0, 6.0, ((0, 8), (1, 4)))
    norm_gain = jnp.clip(1.0 + 0.18 * jax.random.normal(streams_of[6], (HEAD_TOTAL * HD,), jnp.float32), 0.1, 1.9)
    out_grad = gaussian(streams_of[7], (TOKEN_TOTAL, HEAD_TOTAL * HD), 1.0, 6.0, ((0, 8), (1, 4)))
    return dict(queries=queries, key_rows=key_rows, value_rows=value_rows, log_decay=log_decay, doc_start=doc_start, gate_input=gate_input, norm_gain=norm_gain, out_grad=out_grad)


epsilon = 1e-06

def block_terms(log_rates, start_flags):
    cumulative = jnp.cumsum(log_rates, axis=-1)
    doc_count = jnp.cumsum(start_flags, axis=-1, dtype=jnp.int32)
    length = start_flags.shape[-1]
    position = jnp.arange(length, dtype=jnp.int32)
    allowed = (doc_count[:, None] == doc_count[None, :]) & (position[:, None] >= position[None, :])
    difference = jnp.where(allowed[None], cumulative[:, :, None] - cumulative[:, None, :], 0.0)
    weight = jnp.where(allowed[None], jnp.exp(difference), 0.0)
    entering = jnp.where((doc_count == 0)[None], jnp.exp(cumulative), 0.0)
    last_doc = doc_count[-1]
    leaving = jnp.where((doc_count == last_doc)[None], jnp.exp(cumulative[:, -1:] - cumulative), 0.0)
    passing = jnp.where(last_doc == 0, jnp.exp(cumulative[:, -1]), 0.0)
    return (weight, entering, leaving, passing)

def reference(queries, key_rows, value_rows, log_decay, doc_start, gate_input, norm_gain, out_grad):
    block_count = TOKEN_TOTAL // BLOCK
    width = HEAD_TOTAL * HD
    query_all = queries.reshape(block_count, BLOCK, HEAD_TOTAL, HD)
    key_all = key_rows.reshape(block_count, BLOCK, HEAD_TOTAL, HD)
    value_all = value_rows.reshape(block_count, BLOCK, HEAD_TOTAL, HD)
    rate_all = log_decay.reshape(HEAD_TOTAL, block_count, BLOCK).transpose(1, 0, 2)
    start_all = doc_start.reshape(block_count, BLOCK)

    def forward_step(carried, inputs):
        query_block, key_block, value_block, rate_block, start_block = inputs
        weight, entering, leaving, passing = block_terms(rate_block, start_block)
        query_f = query_block.astype(jnp.float32)
        key_f = key_block.astype(jnp.float32)
        value_f = value_block.astype(jnp.float32)
        scores = jnp.einsum('thd,shd->hts', query_f, key_f)
        weights_bf = (scores * weight).astype(jnp.bfloat16)
        held = carried.astype(jnp.bfloat16)
        inside = jnp.einsum('hts,she->the', weights_bf.astype(jnp.float32), value_f)
        outside = jnp.einsum('thd,hde->the', query_f, held.astype(jnp.float32)) * entering.T[:, :, None]
        keyed = (key_f * leaving.T[:, :, None]).astype(jnp.bfloat16)
        local = jnp.einsum('shd,she->hde', keyed.astype(jnp.float32), value_f)
        updated = passing[:, None, None] * carried + local
        return (updated, (inside + outside, held))
    start_state = jnp.zeros((HEAD_TOTAL, HD, HD), jnp.float32)
    _, (attn_blocks, held_all) = lax.scan(forward_step, start_state, (query_all, key_all, value_all, rate_all, start_all))
    attn = attn_blocks.reshape(TOKEN_TOTAL, width)
    inverse = lax.rsqrt(lax.optimization_barrier(jnp.sum(attn * attn, axis=1)) / width + epsilon)
    sig = jax.nn.sigmoid(gate_input.astype(jnp.float32))
    normed = attn * inverse[:, None] * norm_gain[None, :]
    gated = (normed * sig).astype(jnp.bfloat16)
    grad_f = out_grad.astype(jnp.float32)
    gate_grad = (grad_f * normed * sig * (1.0 - sig)).astype(jnp.bfloat16)
    gnorm = grad_f * sig
    inner = lax.optimization_barrier(jnp.sum(gnorm * norm_gain[None, :] * attn, axis=1))
    cube = inverse * inverse * inverse
    attn_grad = (inverse[:, None] * norm_gain[None, :] * gnorm - attn * cube[:, None] * inner[:, None] / width).astype(jnp.bfloat16)
    agrad_all = attn_grad.reshape(block_count, BLOCK, HEAD_TOTAL, HD)

    def backward_step(behind, inputs):
        query_block, key_block, value_block, rate_block, start_block, agrad_block, held = inputs
        weight, entering, leaving, passing = block_terms(rate_block, start_block)
        query_f = query_block.astype(jnp.float32)
        key_f = key_block.astype(jnp.float32)
        value_f = value_block.astype(jnp.float32)
        agrad_f = agrad_block.astype(jnp.float32)
        held_f = held.astype(jnp.float32)
        scores = jnp.einsum('thd,shd->hts', query_f, key_f)
        weights_bf = (scores * weight).astype(jnp.bfloat16).astype(jnp.float32)
        dscore = (jnp.einsum('the,she->hts', agrad_f, value_f) * weight).astype(jnp.bfloat16).astype(jnp.float32)
        behind_f = behind.astype(jnp.bfloat16).astype(jnp.float32)
        qgrad = jnp.einsum('hts,shd->thd', dscore, key_f) + entering.T[:, :, None] * jnp.einsum('the,hde->thd', agrad_f, held_f)
        kgrad = jnp.einsum('hts,thd->shd', dscore, query_f) + leaving.T[:, :, None] * jnp.einsum('she,hde->shd', value_f, behind_f)
        vgrad = jnp.einsum('hts,the->she', weights_bf, agrad_f) + leaving.T[:, :, None] * jnp.einsum('shd,hde->she', key_f, behind_f)
        qkeyed = (query_f * entering.T[:, :, None]).astype(jnp.bfloat16).astype(jnp.float32)
        local = jnp.einsum('thd,the->hde', qkeyed, agrad_f)
        updated = local + passing[:, None, None] * behind
        return (updated, (qgrad.astype(jnp.bfloat16), kgrad.astype(jnp.bfloat16), vgrad.astype(jnp.bfloat16)))
    _, (qgrad_all, kgrad_all, vgrad_all) = lax.scan(backward_step, start_state, (query_all, key_all, value_all, rate_all, start_all, agrad_all, held_all), reverse=True)
    query_grad = qgrad_all.reshape(TOKEN_TOTAL, width)
    key_grad = kgrad_all.reshape(TOKEN_TOTAL, width)
    value_grad = vgrad_all.reshape(TOKEN_TOTAL, width)
    return (gated, gate_grad, query_grad, key_grad, value_grad)
```

```python
import functools

import jax
import jax.numpy as jnp
from jax import lax
from jax.experimental import pallas as pl
from jax.experimental.pallas import tpu as pltpu
from jax.sharding import PartitionSpec as P

HEAD_TOTAL = 64
HD = 128
CHUNK = 256
GROUP = 2
WIDTH = HEAD_TOTAL * HD

epsilon = 1e-06
LOG2E = 1.4426950408889634

F32 = jnp.float32
BF16 = jnp.bfloat16
MIB = 1024 * 1024


def dot(a, b, dims=((1,), (0,))):
    return lax.dot_general(a, b, (dims, ((), ())), preferred_element_type=F32)


NT = ((1,), (1,))


def column(row):
    return jnp.broadcast_to(row, (HD, row.shape[1])).T


def wide(col):
    return jnp.concatenate([col] * (CHUNK // HD), axis=1)


def chunk_cumsum(x):
    lane = lax.broadcasted_iota(jnp.int32, x.shape, 1) % CHUNK
    shift = 1
    while shift < CHUNK:
        x = x + jnp.where(lane >= shift, pltpu.roll(x, shift, 1), 0.0)
        shift *= 2
    return x


def fill_masks(rrow_ref, mask_ref, transposed):
    for n in range(mask_ref.shape[0]):
        r_row = rrow_ref[0:1, n * CHUNK : (n + 1) * CHUNK]
        r_col = wide(column(r_row))
        sub = lax.broadcasted_iota(jnp.int32, (CHUNK, CHUNK), 0)
        lane = lax.broadcasted_iota(jnp.int32, (CHUNK, CHUNK), 1)
        causal = (sub <= lane) if transposed else (lane <= sub)
        mask_ref[n] = jnp.where((r_col == r_row) & causal, 0.0, -jnp.inf)


def state_kernel(
    chunks, piece, lc_ref, doc_ref, k_ref, v_ref,
    crow_ref, enter_ref, leave_ref, rrow_ref, loc_ref, sext_ref,
):
    step = pl.program_id(0)

    @pl.when(step == 0)
    def _():
        c = chunk_cumsum(lc_ref[...] * LOG2E)
        r = chunk_cumsum(jnp.broadcast_to(doc_ref[...].astype(F32), (8, doc_ref.shape[1])))
        crow_ref[...] = c
        rrow_ref[...] = r
        r1 = r[0:1]
        enter_ref[...] = jnp.where(r1 == 0.0, jnp.exp2(c), 0.0)
        for n in range(chunks):
            span = slice(n * CHUNK, (n + 1) * CHUNK)
            cn, rn = c[:, span], r1[:, span]
            leave_ref[:, span] = jnp.where(
                rn == rn[:, -1:], jnp.exp2(cn[:, -1:] - cn), 0.0
            )

    for g in range(GROUP):
        h = step * GROUP + g
        cols = slice(g * HD, (g + 1) * HD)
        state = None
        total = None
        for n in range(chunks):
            span = slice(n * CHUNK, (n + 1) * CHUNK)
            keyed = (k_ref[span, cols].T.astype(F32) * leave_ref[pl.ds(h, 1), span]).astype(BF16)
            local = dot(keyed, v_ref[span, cols])
            loc_ref[g, n] = local
            passing = enter_ref[pl.ds(h, 1), span][:, CHUNK - 1 : CHUNK]
            state = local if state is None else passing * state + local
            total = passing if total is None else passing * total
        for i in range(HD // piece):
            at = g * (HD // piece) + i
            sext_ref[at, 0:piece, :] = state[i * piece : (i + 1) * piece]
            sext_ref[at, piece : piece + 8, :] = jnp.broadcast_to(total, (8, HD))


def inside_kernel(chunks, rrow_ref, crow_ref, q_ref, k_ref, v_ref, out_ref, mask_ref):
    step = pl.program_id(0)

    @pl.when(step == 0)
    def _():
        fill_masks(rrow_ref, mask_ref, False)

    for g in range(GROUP):
        h = step * GROUP + g
        cols = slice(g * HD, (g + 1) * HD)
        for n in range(chunks):
            span = slice(n * CHUNK, (n + 1) * CHUNK)
            c_row = crow_ref[pl.ds(h, 1), span]
            weight = jnp.exp2(wide(column(c_row)) - c_row + mask_ref[n])
            scores = dot(q_ref[span, cols], k_ref[span, cols], NT)
            probs = (scores * weight).astype(BF16)
            out_ref[span, cols] = dot(probs, v_ref[span, cols])


def outside_kernel(
    chunks, enter_ref, gain_ref, q_ref, gate_ref, grad_ref, inside_ref, loc_ref, in_ref,
    attn_ref, held_ref, sums_ref, sq_ref, inner_ref,
):
    step = pl.program_id(0)

    @pl.when(step == 0)
    def _():
        sq_ref[...] = jnp.zeros_like(sq_ref)
        inner_ref[...] = jnp.zeros_like(inner_ref)

    for g in range(GROUP):
        h = step * GROUP + g
        cols = slice(g * HD, (g + 1) * HD)
        gain = gain_ref[0:1, cols]
        carry = in_ref[g]
        for n in range(chunks):
            span = slice(n * CHUNK, (n + 1) * CHUNK)
            enter = enter_ref[pl.ds(h, 1), span]
            held = carry.astype(BF16)
            held_ref[g, n] = held
            attn = inside_ref[span, cols] + column(enter) * dot(q_ref[span, cols], held)
            attn_ref[span, cols] = attn
            sig = jax.nn.sigmoid(gate_ref[span, cols].astype(F32))
            gnorm = grad_ref[span, cols].astype(F32) * sig
            sq_ref[span, :] += attn * attn
            inner_ref[span, :] += gnorm * gain * attn
            if n + 1 < chunks:
                carry = enter[:, CHUNK - 1 : CHUNK] * carry + loc_ref[g, n]

    @pl.when(step == pl.num_programs(0) - 1)
    def _():
        sums_ref[0:1, :] = jnp.sum(sq_ref[...].T, axis=0, keepdims=True)
        sums_ref[1:2, :] = jnp.sum(inner_ref[...].T, axis=0, keepdims=True)


def grad_kernel(
    chunks, piece, parts, enter_ref, gain_ref, *refs,
):
    sums_refs = refs[:parts]
    q_ref, gate_ref, grad_ref, attn_ref = refs[parts : parts + 4]
    gated_ref, ggate_ref, agrad_ref, bloc_ref, dback_ref, alpha_ref, beta_ref = refs[parts + 4 :]
    step = pl.program_id(0)

    @pl.when(step == 0)
    def _():
        sums = sums_refs[0][...]
        for ref in sums_refs[1:]:
            sums = sums + ref[...]
        inverse = lax.rsqrt(sums[0:1] / WIDTH + epsilon)
        alpha_ref[...] = column(inverse)
        beta_ref[...] = column(inverse * inverse * inverse * sums[1:2] / WIDTH)

    for g in range(GROUP):
        h = step * GROUP + g
        cols = slice(g * HD, (g + 1) * HD)
        gain = gain_ref[0:1, cols]
        back = None
        for n in reversed(range(chunks)):
            span = slice(n * CHUNK, (n + 1) * CHUNK)
            enter = enter_ref[pl.ds(h, 1), span]
            attn = attn_ref[span, cols]
            sig = jax.nn.sigmoid(gate_ref[span, cols].astype(F32))
            grad = grad_ref[span, cols].astype(F32)
            scale = alpha_ref[span, :] * gain
            gated = attn * scale * sig
            gated_ref[span, cols] = gated.astype(BF16)
            ggate_ref[span, cols] = (grad * gated * (1.0 - sig)).astype(BF16)
            agrad = (scale * (grad * sig) - attn * beta_ref[span, :]).astype(BF16)
            agrad_ref[span, cols] = agrad
            qkeyed = (q_ref[span, cols].T.astype(F32) * enter).astype(BF16)
            local = dot(qkeyed, agrad)
            bloc_ref[g, n] = local
            back = local if back is None else local + enter[:, CHUNK - 1 : CHUNK] * back
        for i in range(HD // piece):
            dback_ref[g * (HD // piece) + i] = back[i * piece : (i + 1) * piece]


def inner_grad_kernel(
    chunks, rrow_ref, crow_ref, enter_ref, q_ref, k_ref, v_ref, agrad_ref, held_ref,
    dq_ref, dk_ref, dv_ref, mask_ref,
):
    step = pl.program_id(0)

    @pl.when(step == 0)
    def _():
        fill_masks(rrow_ref, mask_ref, True)

    for g in range(GROUP):
        h = step * GROUP + g
        cols = slice(g * HD, (g + 1) * HD)
        for n in range(chunks):
            span = slice(n * CHUNK, (n + 1) * CHUNK)
            c_row = crow_ref[pl.ds(h, 1), span]
            q, k = q_ref[span, cols], k_ref[span, cols]
            v, agrad = v_ref[span, cols], agrad_ref[span, cols]
            weight = jnp.exp2(c_row - wide(column(c_row)) + mask_ref[n])
            probs = (dot(k, q, NT) * weight).astype(BF16)
            dv_ref[span, cols] = dot(probs, agrad).astype(dv_ref.dtype)
            dscore = (dot(v, agrad, NT) * weight).astype(BF16)
            dk_ref[span, cols] = dot(dscore, q).astype(dk_ref.dtype)
            outside = column(enter_ref[pl.ds(h, 1), span]) * dot(agrad, held_ref[g, n], NT)
            dq_ref[span, cols] = (dot(dscore.T, k) + outside).astype(BF16)


def outer_grad_kernel(
    chunks, enter_ref, leave_ref, k_ref, v_ref, dkin_ref, dvin_ref, bloc_ref, out_ref,
    dk_ref, dv_ref,
):
    step = pl.program_id(0)
    for g in range(GROUP):
        h = step * GROUP + g
        cols = slice(g * HD, (g + 1) * HD)
        carry = out_ref[g]
        for n in reversed(range(chunks)):
            span = slice(n * CHUNK, (n + 1) * CHUNK)
            leave = column(leave_ref[pl.ds(h, 1), span])
            back = carry.astype(BF16)
            dk = dkin_ref[span, cols].astype(F32) + leave * dot(v_ref[span, cols], back, NT)
            dv = dvin_ref[span, cols].astype(F32) + leave * dot(k_ref[span, cols], back)
            dk_ref[span, cols] = dk.astype(BF16)
            dv_ref[span, cols] = dv.astype(BF16)
            if n > 0:
                passing = enter_ref[pl.ds(h, 1), span][:, CHUNK - 1 : CHUNK]
                carry = bloc_ref[g, n] + passing * carry


def prefix_kernel(devices, piece, ext_ref, out_ref):
    carry = jnp.zeros((piece, HD), F32)
    for d in range(devices):
        out_ref[d, 0] = carry
        if d + 1 < devices:
            carry = ext_ref[d, 0, piece : piece + 1, :] * carry + ext_ref[d, 0, 0:piece, :]


def suffix_kernel(devices, pass_ref, back_ref, out_ref):
    carry = jnp.zeros(back_ref.shape[2:], F32)
    for d in reversed(range(devices)):
        out_ref[d, 0] = carry
        if d > 0:
            carry = back_ref[d, 0] + pass_ref[d, 0, 0:1, :] * carry


def call(kernel, grid, in_specs, out_specs, out_shape, scratch=(), flops=0, moved=0, exps=0):
    return pl.pallas_call(
        kernel,
        grid=grid,
        in_specs=in_specs,
        out_specs=out_specs,
        out_shape=out_shape,
        scratch_shapes=list(scratch),
        compiler_params=pltpu.CompilerParams(
            dimension_semantics=("arbitrary",) * len(grid), vmem_limit_bytes=40 * MIB
        ),
        cost_estimate=pl.CostEstimate(flops=flops, bytes_accessed=moved, transcendentals=exps),
    )


def shape(dims, dtype):
    return jax.ShapeDtypeStruct(dims, dtype)


def body(queries, key_rows, value_rows, log_decay, doc_start, gate_input, norm_gain, out_grad):
    rows, cols = queries.shape
    heads = cols // HD
    chunks = rows // CHUNK
    devices = lax.axis_size("seq")
    parts = lax.axis_size("head")
    piece = min(HD, heads * HD // devices)
    per = HD // piece
    own = heads * per // devices
    grid = (heads // GROUP,)
    big = rows * cols * 2
    tile = 2 * rows * CHUNK * cols
    small = 2 * rows * HD * cols

    whole = lambda *dims: pl.BlockSpec(dims, lambda i: (0,) * len(dims))
    wide_spec = pl.BlockSpec((rows, GROUP * HD), lambda i: (0, i))
    row_spec = whole(heads, rows)
    rrow_spec = whole(8, rows)
    loc_spec = pl.BlockSpec((GROUP, chunks, HD, HD), lambda i: (i, 0, 0, 0))
    state_spec = pl.BlockSpec((GROUP, HD, HD), lambda i: (i, 0, 0))
    gain_spec = pl.BlockSpec((1, GROUP * HD), lambda i: (0, i))
    mask = pltpu.VMEM((chunks, CHUNK, CHUNK), F32)
    tall = pltpu.VMEM((rows, HD), F32)

    row_shape = shape((heads, rows), F32)
    loc_shape = shape((heads, chunks, HD, HD), F32)
    big_shape = shape((rows, cols), BF16)

    doc_row = doc_start.reshape(1, rows)
    gain_row = norm_gain.reshape(1, cols)

    crow, enter, leave, rrow, loc, sext = call(
        functools.partial(state_kernel, chunks, piece),
        grid,
        [row_spec, whole(1, rows), wide_spec, wide_spec],
        [
            row_spec, row_spec, row_spec, rrow_spec, loc_spec,
            pl.BlockSpec((GROUP * per, piece + 8, HD), lambda i: (i, 0, 0)),
        ],
        [
            row_shape, row_shape, row_shape, shape((8, rows), F32), loc_shape,
            shape((heads * per, piece + 8, HD), F32),
        ],
        flops=small, moved=2 * big + 6 * MIB,
    )(log_decay, doc_row, key_rows, value_rows)

    ext = lax.all_to_all(sext.reshape(devices, own, piece + 8, HD), "seq", 0, 0)

    inside = call(
        functools.partial(inside_kernel, chunks),
        grid,
        [rrow_spec, row_spec, wide_spec, wide_spec, wide_spec],
        wide_spec,
        shape((rows, cols), F32),
        [mask],
        flops=2 * tile, moved=5 * big, exps=rows * CHUNK * heads,
    )(rrow, crow, queries, key_rows, value_rows)

    scan_spec = pl.BlockSpec((devices, 1, piece, HD), lambda i: (0, i, 0, 0))
    before = call(
        functools.partial(prefix_kernel, devices, piece),
        (own,),
        [pl.BlockSpec((devices, 1, piece + 8, HD), lambda i: (0, i, 0, 0))],
        scan_spec,
        shape((devices, own, piece, HD), F32),
        moved=2 * MIB,
    )(ext)
    incoming = lax.all_to_all(before, "seq", 0, 0).reshape(heads, HD, HD)

    attn, held, sums = call(
        functools.partial(outside_kernel, chunks),
        grid,
        [row_spec, gain_spec, wide_spec, wide_spec, wide_spec, wide_spec, loc_spec, state_spec],
        [wide_spec, loc_spec, whole(2, rows)],
        [shape((rows, cols), F32), shape((heads, chunks, HD, HD), BF16), shape((2, rows), F32)],
        [tall, tall],
        flops=small, moved=7 * big + 6 * MIB, exps=rows * cols,
    )(enter, gain_row, queries, gate_input, out_grad, inside, loc, incoming)

    all_sums = [sums]
    for hop in range(1, parts):
        route = [(i, (i + hop) % parts) for i in range(parts)]
        all_sums.append(lax.ppermute(sums, "head", route))

    gated, gate_grad, agrad, bloc, dback = call(
        functools.partial(grad_kernel, chunks, piece, parts),
        grid,
        [row_spec, gain_spec] + [whole(2, rows)] * parts + [wide_spec] * 4,
        [
            wide_spec, wide_spec, wide_spec, loc_spec,
            pl.BlockSpec((GROUP * per, piece, HD), lambda i: (i, 0, 0)),
        ],
        [big_shape, big_shape, big_shape, loc_shape, shape((heads * per, piece, HD), F32)],
        [tall, tall],
        flops=small, moved=8 * big + 5 * MIB, exps=rows * cols,
    )(enter, gain_row, *all_sums, queries, gate_input, out_grad, attn)

    backs = lax.all_to_all(dback.reshape(devices, own, piece, HD), "seq", 0, 0)

    dq, dk_inner, dv_inner = call(
        functools.partial(inner_grad_kernel, chunks),
        grid,
        [rrow_spec, row_spec, row_spec] + [wide_spec] * 4 + [loc_spec],
        [wide_spec] * 3,
        [big_shape] * 3,
        [mask],
        flops=5 * tile + small, moved=7 * big + 2 * MIB, exps=rows * CHUNK * heads,
    )(rrow, crow, enter, queries, key_rows, value_rows, agrad, held)

    after = call(
        functools.partial(suffix_kernel, devices),
        (own,),
        [pl.BlockSpec((devices, 1, 8, HD), lambda i: (0, i, piece // 8, 0)), scan_spec],
        scan_spec,
        shape((devices, own, piece, HD), F32),
        moved=2 * MIB,
    )(ext, backs)
    outgoing = lax.all_to_all(after, "seq", 0, 0).reshape(heads, HD, HD)

    dk, dv = call(
        functools.partial(outer_grad_kernel, chunks),
        grid,
        [row_spec, row_spec] + [wide_spec] * 4 + [loc_spec, state_spec],
        [wide_spec] * 2,
        [big_shape] * 2,
        flops=2 * small, moved=6 * big + 5 * MIB,
    )(enter, leave, key_rows, value_rows, dk_inner, dv_inner, bloc, outgoing)
    return (gated, gate_grad, dq, dk, dv)


def solution(mesh):
    in_specs = (
        P("seq", "head"),
        P("seq", "head"),
        P("seq", "head"),
        P("head", "seq"),
        P("seq"),
        P("seq", "head"),
        P("head"),
        P("seq", "head"),
    )
    out_specs = (P("seq", "head"),) * 5
    return jax.shard_map(body, mesh=mesh, in_specs=in_specs, out_specs=out_specs, check_vma=False)
```

```python
import functools

import jax
import jax.numpy as jnp
from jax import lax
from jax.experimental import pallas as pl
from jax.experimental.pallas import tpu as pltpu
from jax.sharding import PartitionSpec as P

HEAD_TOTAL = 64
HD = 128
CHUNK = 256
GROUP = 2
WINDOWS = 4
WIDTH = HEAD_TOTAL * HD

epsilon = 1e-06
LOG2E = 1.4426950408889634

F32 = jnp.float32
BF16 = jnp.bfloat16
MIB = 1024 * 1024
NT = ((1,), (1,))


def dot(a, b, dims=((1,), (0,))):
    return lax.dot_general(a, b, (dims, ((), ())), preferred_element_type=F32)


def column(row):
    return jnp.broadcast_to(row, (HD, row.shape[1])).T


def spread(cols, lane, width=HD):
    return jnp.broadcast_to(cols[:, lane : lane + 1], (cols.shape[0], width))


def turned(cols_ref, first):
    return pltpu.roll(cols_ref[...], (HD - first) % HD, 1)


def chunk_cumsum(x):
    lane = lax.broadcasted_iota(jnp.int32, x.shape, 1) % CHUNK
    shift = 1
    while shift < CHUNK:
        x = x + jnp.where(lane >= shift, pltpu.roll(x, shift, 1), 0.0)
        shift *= 2
    return x


def fill_masks(rrow_ref, mask_ref, transposed):
    for n in range(mask_ref.shape[0]):
        r_row = rrow_ref[0:1, n * CHUNK : (n + 1) * CHUNK]
        r_col = jnp.concatenate([column(r_row)] * (CHUNK // HD), axis=1)
        sub = lax.broadcasted_iota(jnp.int32, (CHUNK, CHUNK), 0)
        lane = lax.broadcasted_iota(jnp.int32, (CHUNK, CHUNK), 1)
        causal = (sub <= lane) if transposed else (lane <= sub)
        mask_ref[n] = jnp.where((r_col == r_row) & causal, 0.0, -jnp.inf)


def state_kernel(
    chunks, heads, lc_ref, doc_ref, k_ref, v_ref,
    crow_ref, enter_ref, leave_ref, rrow_ref, cols_ref, loc_ref, state_ref,
):
    step = pl.program_id(0)

    @pl.when(step == 0)
    def _():
        c = chunk_cumsum(lc_ref[...] * LOG2E)
        r = chunk_cumsum(jnp.broadcast_to(doc_ref[...].astype(F32), (8, doc_ref.shape[1])))
        crow_ref[...] = c
        rrow_ref[...] = r
        enter = jnp.where(r[0:1] == 0.0, jnp.exp2(c), 0.0)
        enter_ref[...] = enter
        spare = jnp.zeros((HD - 3 * heads, CHUNK), F32)
        for n in range(chunks):
            span = slice(n * CHUNK, (n + 1) * CHUNK)
            cn, rn = c[:, span], r[0:1, span]
            leave = jnp.where(rn == rn[:, -1:], jnp.exp2(cn[:, -1:] - cn), 0.0)
            leave_ref[:, span] = leave
            cols_ref[span, :] = jnp.concatenate([cn, enter[:, span], leave, spare], axis=0).T

    for g in range(GROUP):
        h = step * GROUP + g
        cols = slice(g * HD, (g + 1) * HD)
        state = None
        for n in range(chunks):
            span = slice(n * CHUNK, (n + 1) * CHUNK)
            keyed = (k_ref[span, cols].T.astype(F32) * leave_ref[pl.ds(h, 1), span]).astype(BF16)
            local = dot(keyed, v_ref[span, cols])
            loc_ref[g, n] = local
            passing = enter_ref[pl.ds(h, 1), span][:, CHUNK - 1 : CHUNK]
            state = local if state is None else passing * state + local
        state_ref[g] = state


def inside_kernel(
    chunks, first, rrow_ref, crow_ref, cols_ref, gain_ref, q_ref, k_ref, v_ref, gate_ref,
    grad_ref, *refs,
):
    out_ref, gnorm_ref, mask_ref = refs[-3:]
    step = pl.program_id(0)

    @pl.when(step == 0)
    def _():
        fill_masks(rrow_ref, mask_ref, False)

    cols_now = turned(cols_ref, first + step * GROUP)
    for g in range(GROUP):
        h = first + step * GROUP + g
        cols = slice(g * HD, (g + 1) * HD)
        for n in range(chunks):
            span = slice(n * CHUNK, (n + 1) * CHUNK)
            c_row = crow_ref[pl.ds(h, 1), span]
            c_col = spread(cols_now[span], g, CHUNK)
            weight = jnp.exp2(c_col - c_row + mask_ref[n])
            scores = dot(q_ref[span, cols], k_ref[span, cols], NT)
            probs = (scores * weight).astype(BF16)
            out_ref[span, cols] = dot(probs, v_ref[span, cols])
            sig = jax.nn.sigmoid(gate_ref[span, cols].astype(F32))
            gnorm = grad_ref[span, cols].astype(F32) * sig * gain_ref[0:1, cols]
            gnorm_ref[span, cols] = gnorm.astype(BF16)


def outside_kernel(
    chunks, heads, cols_ref, enter_ref, q_ref, gnorm_ref, inside_ref, loc_ref, in_ref,
    attn_ref, held_ref, sums_ref, sq_ref, inner_ref,
):
    step = pl.program_id(0)

    @pl.when(step == 0)
    def _():
        sq_ref[...] = jnp.zeros_like(sq_ref)
        inner_ref[...] = jnp.zeros_like(inner_ref)

    cols_now = turned(cols_ref, heads + step * GROUP)
    carries = [in_ref[g] for g in range(GROUP)]
    for n in range(chunks):
        span = slice(n * CHUNK, (n + 1) * CHUNK)
        squares = sq_ref[span, :]
        inners = inner_ref[span, :]
        for g in range(GROUP):
            h = step * GROUP + g
            cols = slice(g * HD, (g + 1) * HD)
            held = carries[g].astype(BF16)
            held_ref[g, n] = held
            enter = spread(cols_now[span], g)
            attn = inside_ref[span, cols] + enter * dot(q_ref[span, cols], held)
            attn_ref[span, cols] = attn
            squares = squares + attn * attn
            inners = inners + gnorm_ref[span, cols].astype(F32) * attn
            if n + 1 < chunks:
                passing = enter_ref[pl.ds(h, 1), span][:, CHUNK - 1 : CHUNK]
                carries[g] = passing * carries[g] + loc_ref[g, n]
        sq_ref[span, :] = squares
        inner_ref[span, :] = inners

    @pl.when(step == pl.num_programs(0) - 1)
    def _():
        sums_ref[0:1, :] = jnp.sum(sq_ref[...].T, axis=0, keepdims=True)
        sums_ref[1:2, :] = jnp.sum(inner_ref[...].T, axis=0, keepdims=True)


def token_scales(sums_refs):
    sums = sums_refs[0][...]
    for ref in sums_refs[1:]:
        sums = sums + ref[...]
    inverse = lax.rsqrt(sums[0:1] / WIDTH + epsilon)
    return inverse, inverse * inverse * inverse * sums[1:2] / WIDTH


def grad_kernel(chunks, parts, enter_ref, *refs):
    q_ref, gnorm_ref, attn_ref, agrad_ref, bloc_ref, back_ref, alpha_ref, beta_ref = refs[parts:]
    step = pl.program_id(0)

    @pl.when(step == 0)
    def _():
        inverse, slope = token_scales(refs[:parts])
        alpha_ref[...] = column(inverse)
        beta_ref[...] = column(slope)

    backs = [None] * GROUP
    for n in reversed(range(chunks)):
        span = slice(n * CHUNK, (n + 1) * CHUNK)
        alpha, beta = alpha_ref[span, :], beta_ref[span, :]
        for g in range(GROUP):
            h = step * GROUP + g
            cols = slice(g * HD, (g + 1) * HD)
            enter = enter_ref[pl.ds(h, 1), span]
            gnorm = gnorm_ref[span, cols].astype(F32)
            agrad = (alpha * gnorm - attn_ref[span, cols] * beta).astype(BF16)
            agrad_ref[span, cols] = agrad
            qkeyed = (q_ref[span, cols].T.astype(F32) * enter).astype(BF16)
            local = dot(qkeyed, agrad)
            bloc_ref[g, n] = local
            passing = enter[:, CHUNK - 1 : CHUNK]
            backs[g] = local if backs[g] is None else local + passing * backs[g]
    for g in range(GROUP):
        back_ref[g] = backs[g]


def gate_kernel(chunks, parts, gain_ref, *refs):
    gate_ref, grad_ref, attn_ref, gated_ref, ggate_ref, alpha_ref = refs[parts:]
    step = pl.program_id(0)

    @pl.when(step == 0)
    def _():
        inverse, _ = token_scales(refs[:parts])
        alpha_ref[...] = column(inverse)

    for n in range(chunks):
        span = slice(n * CHUNK, (n + 1) * CHUNK)
        alpha = alpha_ref[span, :]
        for g in range(GROUP):
            cols = slice(g * HD, (g + 1) * HD)
            sig = jax.nn.sigmoid(gate_ref[span, cols].astype(F32))
            gated = attn_ref[span, cols] * alpha * gain_ref[0:1, cols] * sig
            gated_ref[span, cols] = gated.astype(BF16)
            ggate = grad_ref[span, cols].astype(F32) * gated * (1.0 - sig)
            ggate_ref[span, cols] = ggate.astype(BF16)


def inner_grad_kernel(
    chunks, first, rrow_ref, crow_ref, enter_ref, cols_ref, q_ref, k_ref, v_ref, agrad_ref,
    held_ref, *refs,
):
    dq_ref, dk_ref, dv_ref, mask_ref = refs[-4:]
    step = pl.program_id(0)

    @pl.when(step == 0)
    def _():
        fill_masks(rrow_ref, mask_ref, True)

    cols_now = turned(cols_ref, first + step * GROUP)
    for g in range(GROUP):
        h = first + step * GROUP + g
        cols = slice(g * HD, (g + 1) * HD)
        for n in range(chunks):
            span = slice(n * CHUNK, (n + 1) * CHUNK)
            c_row = crow_ref[pl.ds(h, 1), span]
            c_col = spread(cols_now[span], g, CHUNK)
            q, k = q_ref[span, cols], k_ref[span, cols]
            v, agrad = v_ref[span, cols], agrad_ref[span, cols]
            weight = jnp.exp2(c_row - c_col + mask_ref[n])
            probs = (dot(k, q, NT) * weight).astype(BF16)
            dv_ref[span, cols] = dot(probs, agrad).astype(BF16)
            both = dot(jnp.concatenate([v, held_ref[g, n]], axis=0), agrad, NT)
            dscore = (both[:CHUNK] * weight).astype(BF16)
            dk_ref[span, cols] = dot(dscore, q).astype(BF16)
            dq = dot(k.T, dscore) + enter_ref[pl.ds(h, 1), span] * both[CHUNK:]
            dq_ref[span, cols] = dq.astype(BF16).T


def outer_grad_kernel(
    chunks, heads, cols_ref, enter_ref, k_ref, v_ref, dkin_ref, dvin_ref, bloc_ref, out_ref,
    dk_ref, dv_ref,
):
    step = pl.program_id(0)
    cols_now = turned(cols_ref, 2 * heads + step * GROUP)
    for g in range(GROUP):
        h = step * GROUP + g
        cols = slice(g * HD, (g + 1) * HD)
        carry = out_ref[g]
        for n in reversed(range(chunks)):
            span = slice(n * CHUNK, (n + 1) * CHUNK)
            leave = spread(cols_now[span], g)
            back = carry.astype(BF16)
            dk = dkin_ref[span, cols].astype(F32) + leave * dot(v_ref[span, cols], back, NT)
            dv = dvin_ref[span, cols].astype(F32) + leave * dot(k_ref[span, cols], back)
            dk_ref[span, cols] = dk.astype(BF16)
            dv_ref[span, cols] = dv.astype(BF16)
            if n > 0:
                passing = enter_ref[pl.ds(h, 1), span][:, CHUNK - 1 : CHUNK]
                carry = bloc_ref[g, n] + passing * carry


def call(kernel, grid, ins, outs, scratch=(), aliases=None, flops=0, moved=0, exps=0):
    arrays, shapes = [], []
    for x, _ in ins:
        large = x.size * x.dtype.itemsize >= MIB
        arrays.append(pltpu.with_memory_space_constraint(x, pltpu.HBM) if large else x)
    for dims, dtype, _ in outs:
        large = jnp.dtype(dtype).itemsize * functools.reduce(lambda a, b: a * b, dims) >= MIB
        shapes.append(pltpu.HBM(dims, dtype) if large else jax.ShapeDtypeStruct(dims, dtype))
    return pl.pallas_call(
        kernel,
        grid=grid,
        in_specs=[spec for _, spec in ins],
        out_specs=[spec for _, _, spec in outs],
        out_shape=shapes,
        scratch_shapes=list(scratch),
        input_output_aliases=aliases or {},
        compiler_params=pltpu.CompilerParams(
            dimension_semantics=("arbitrary",) * len(grid), vmem_limit_bytes=40 * MIB
        ),
        cost_estimate=pl.CostEstimate(flops=flops, bytes_accessed=moved, transcendentals=exps),
    )(*arrays)


def after(x, *others):
    return lax.optimization_barrier((x, *others))[0]


def swap(x, bit, devices):
    return lax.ppermute(x, "seq", [(i, i ^ (1 << bit)) for i in range(devices)])


def cube_scan(state, passes, index, fill):
    heads = state.shape[0]
    half, quarter = heads // 2, heads // 4
    core, x, y = index % 2, (index // 2) % 2, index // 4
    chip = index // 2
    factor = lambda rows: rows[:, None, None]

    other = swap(state, 0, 8)
    other = after(other, fill(0, state))
    early = jnp.where(core == 0, state, other)
    late = jnp.where(core == 0, other, state)
    even = lax.dynamic_index_in_dim(passes, 2 * chip, 0, False)
    odd = lax.dynamic_index_in_dim(passes, 2 * chip + 1, 0, False)
    mine = lambda a, axis: lax.dynamic_slice_in_dim(a, core * half, half, axis)
    total = factor(mine(odd, 0)) * mine(early, 0) + mine(late, 0)
    chip_pass = mine(passes[0::2] * passes[1::2], 1)
    to_x, to_y = total[:quarter], total[quarter:]
    pass_x, pass_y = chip_pass[:, :quarter], chip_pass[:, quarter:]

    from_x, from_y = swap(to_x, 1, 8), swap(to_y, 2, 8)
    from_x, from_y = lax.optimization_barrier((from_x, from_y, fill(1, total)))[:2]
    left = jnp.where(x == 0, to_x, from_x)
    right = jnp.where(x == 0, from_x, to_x)
    row = factor(jnp.where(y == 0, pass_x[1], pass_x[3])) * left + right
    through = factor(pass_y[2]) * (factor(pass_y[1]) * from_y) + to_y
    sent = jnp.where(y == 0, to_y, jnp.where(x == 0, through, from_y))

    row_in, sent_in = swap(row, 2, 8), swap(sent, 1, 8)
    row_in, sent_in = lax.optimization_barrier((row_in, sent_in, fill(2, sent)))[:2]
    lower = jnp.where(x == 0, row_in, factor(pass_x[2]) * row_in + from_x)
    upper = jnp.where(x == 0, 0.0, from_x)
    in_x = jnp.where(y == 0, upper, lower)
    more = factor(jnp.where(x == 0, pass_y[1], pass_y[2])) * from_y
    in_y = jnp.where(y == 0, jnp.where(x == 0, 0.0, sent_in), more + sent_in)
    ahead = jnp.concatenate([in_x, in_y], axis=0)

    beside = swap(ahead, 0, 8)
    beside = after(beside, fill(3, ahead))
    low = jnp.where(core == 0, ahead, beside)
    high = jnp.where(core == 0, beside, ahead)
    entering = jnp.concatenate([low, high], axis=0)
    return jnp.where(core == 0, entering, factor(even) * entering + early)


def doubling_scan(state, passes, index, fill, reverse):
    devices = passes.shape[0]
    route = lambda hop: [
        (i, i - hop if reverse else i + hop)
        for i in range(devices)
        if 0 <= (i - hop if reverse else i + hop) < devices
    ]
    for window in range(WINDOWS):
        state = after(state, fill(window, state))
    hop = 1
    while hop < devices:
        factor = lax.dynamic_index_in_dim(passes, index, 0, False)
        state = factor[:, None, None] * lax.ppermute(state, "seq", route(hop)) + state
        before = jnp.concatenate([jnp.zeros_like(passes[:hop]), passes[:-hop]], axis=0)
        passes = passes * before
        hop *= 2
    return lax.ppermute(state, "seq", route(1))


def scan_devices(state, passes, fill, reverse):
    devices = passes.shape[0]
    index = lax.axis_index("seq")
    if reverse:
        passes = passes[::-1]
        index = devices - 1 - index
    if devices == 8 and state.shape[0] % 4 == 0:
        return cube_scan(state, passes, index, fill)
    return doubling_scan(state, passes, index, fill, reverse)


def body(queries, key_rows, value_rows, log_decay, doc_start, gate_input, norm_gain, out_grad):
    rows, cols = queries.shape
    heads = cols // HD
    chunks = rows // CHUNK
    parts = lax.axis_size("head")
    grid = (heads // GROUP,)
    share = heads // WINDOWS
    big = rows * cols * 2
    tile = 2 * rows * CHUNK * cols
    small = 2 * rows * HD * cols

    whole = lambda *dims: pl.BlockSpec(dims, lambda i: (0,) * len(dims))

    def wide(base=0):
        return pl.BlockSpec((rows, GROUP * HD), lambda i: (0, i + base // GROUP))

    def loc(base=0):
        return pl.BlockSpec((GROUP, chunks, HD, HD), lambda i: (i + base // GROUP, 0, 0, 0))

    state_spec = pl.BlockSpec((GROUP, HD, HD), lambda i: (i, 0, 0))
    gain_spec = lambda base=0: pl.BlockSpec((1, GROUP * HD), lambda i: (0, i + base // GROUP))
    row_spec = whole(heads, rows)
    rrow_spec = whole(8, rows)
    cols_spec = whole(rows, HD)
    sums_spec = whole(2, rows)
    anywhere = pl.BlockSpec(memory_space=pl.ANY)
    mask = pltpu.VMEM((chunks, CHUNK, CHUNK), F32)
    tall = pltpu.VMEM((rows, HD), F32)

    doc_row = doc_start.reshape(1, rows)
    gain_row = norm_gain.reshape(1, cols)
    dev_pass = jnp.where(jnp.any(doc_start != 0), 0.0, jnp.exp(jnp.sum(log_decay, axis=1)))
    passes = lax.all_gather(dev_pass, "seq")

    loc_out = ((heads, chunks, HD, HD), F32, loc())
    state_out = ((heads, HD, HD), F32, state_spec)
    wide_out = ((rows, cols), BF16, wide())
    row_out = ((heads, rows), F32, row_spec)

    crow, enter, leave, rrow, columns, local, state = call(
        functools.partial(state_kernel, chunks, heads),
        grid,
        [(log_decay, row_spec), (doc_row, whole(1, rows)), (key_rows, wide()), (value_rows, wide())],
        [
            row_out, row_out, row_out, ((8, rows), F32, rrow_spec),
            ((rows, HD), F32, cols_spec), loc_out, state_out,
        ],
        flops=small, moved=2 * big + 6 * MIB,
    )

    made = []

    def fill_forward(window, tie):
        base = window * share
        spec = wide(base)
        ins = [
            (after(rrow, tie), rrow_spec), (crow, row_spec), (columns, cols_spec),
            (gain_row, gain_spec(base)), (queries, spec), (key_rows, spec), (value_rows, spec),
            (gate_input, spec), (out_grad, spec),
        ]
        aliases = {}
        if made:
            aliases = {len(ins): 0, len(ins) + 1: 1}
            ins += [(x, anywhere) for x in made]
        made[:] = call(
            functools.partial(inside_kernel, chunks, base),
            (share // GROUP,),
            ins,
            [((rows, cols), F32, spec), ((rows, cols), BF16, spec)],
            [mask],
            aliases,
            flops=2 * tile // WINDOWS, moved=8 * big // WINDOWS,
            exps=rows * (CHUNK + HD) * heads // WINDOWS,
        )
        return made[1]

    incoming = scan_devices(state, passes, fill_forward, False)
    inside, gnorm = made

    attn, held, sums = call(
        functools.partial(outside_kernel, chunks, heads),
        grid,
        [
            (columns, cols_spec), (enter, row_spec), (queries, wide()), (gnorm, wide()),
            (inside, wide()), (local, loc()), (incoming, state_spec),
        ],
        [
            ((rows, cols), F32, wide()), ((heads, chunks, HD, HD), BF16, loc()),
            ((2, rows), F32, sums_spec),
        ],
        [tall, tall],
        flops=small, moved=6 * big + 7 * MIB,
    )

    all_sums = [(sums, sums_spec)]
    for hop in range(1, parts):
        route = [(i, (i + hop) % parts) for i in range(parts)]
        all_sums.append((lax.ppermute(sums, "head", route), sums_spec))

    agrad, bloc, back = call(
        functools.partial(grad_kernel, chunks, parts),
        grid,
        [(enter, row_spec)] + all_sums + [(queries, wide()), (gnorm, wide()), (attn, wide())],
        [wide_out, loc_out, state_out],
        [tall, tall],
        flops=small, moved=5 * big + 5 * MIB,
    )

    grads = []
    gates = []

    def fill_backward(window, tie):
        base = window * share
        spec = wide(base)
        ins = [
            (after(rrow, tie), rrow_spec), (crow, row_spec), (enter, row_spec),
            (columns, cols_spec), (queries, spec), (key_rows, spec), (value_rows, spec),
            (agrad, spec), (held, loc(base)),
        ]
        aliases = {}
        if grads:
            aliases = {len(ins): 0, len(ins) + 1: 1, len(ins) + 2: 2}
            ins += [(x, anywhere) for x in grads]
        grads[:] = call(
            functools.partial(inner_grad_kernel, chunks, base),
            (share // GROUP,),
            ins,
            [((rows, cols), BF16, spec)] * 3,
            [mask],
            aliases,
            flops=(5 * tile + small) // WINDOWS, moved=8 * big // WINDOWS,
            exps=rows * CHUNK * heads // WINDOWS,
        )
        if window != 1:
            return grads[2]
        gates[:] = call(
            functools.partial(gate_kernel, chunks, parts),
            grid,
            [(after(gain_row, grads[2]), gain_spec())] + all_sums
            + [(gate_input, wide()), (out_grad, wide()), (attn, wide())],
            [wide_out, wide_out],
            [tall],
            flops=20 * rows * cols, moved=6 * big, exps=rows * cols,
        )
        return gates[1]

    outgoing = scan_devices(back, passes, fill_backward, True)
    dq, dk_inner, dv_inner = grads

    dk, dv = call(
        functools.partial(outer_grad_kernel, chunks, heads),
        grid,
        [
            (columns, cols_spec), (enter, row_spec), (key_rows, wide()), (value_rows, wide()),
            (dk_inner, wide()), (dv_inner, wide()), (bloc, loc()), (outgoing, state_spec),
        ],
        [wide_out, wide_out],
        flops=2 * small, moved=6 * big + 5 * MIB,
    )
    return (*gates, dq, dk, dv)


def solution(mesh):
    in_specs = (
        P("seq", "head"),
        P("seq", "head"),
        P("seq", "head"),
        P("head", "seq"),
        P("seq"),
        P("seq", "head"),
        P("head"),
        P("seq", "head"),
    )
    out_specs = (P("seq", "head"),) * 5
    return jax.shard_map(body, mesh=mesh, in_specs=in_specs, out_specs=out_specs, check_vma=False)
```

```python
import functools

import jax
import jax.numpy as jnp
from jax import lax
from jax.experimental import pallas as pl
from jax.experimental.pallas import tpu as pltpu
from jax.sharding import PartitionSpec as P

HEAD_TOTAL = 64
HD = 128
CHUNK = 256
GROUP = 2
WINDOWS = 4
WIDTH = HEAD_TOTAL * HD

epsilon = 1e-06
LOG2E = 1.4426950408889634

F32 = jnp.float32
BF16 = jnp.bfloat16
MIB = 1024 * 1024
NT = ((1,), (1,))


def dot(a, b, dims=((1,), (0,))):
    return lax.dot_general(a, b, (dims, ((), ())), preferred_element_type=F32)


def chunk_cumsum(x):
    lane = lax.broadcasted_iota(jnp.int32, x.shape, 1) % CHUNK
    shift = 1
    while shift < CHUNK:
        x = x + jnp.where(lane >= shift, pltpu.roll(x, shift, 1), 0.0)
        shift *= 2
    return x


def spans(chunks):
    return [slice(n * CHUNK, (n + 1) * CHUNK) for n in range(chunks)]


def state_kernel(
    chunks, heads, lc_ref, doc_ref, k_ref, v_ref,
    crow_ref, enter_ref, leave_ref, rrow_ref, cols_ref, kept_k_ref, kept_v_ref, loc_ref,
    state_ref, pass_ref,
):
    step = pl.program_id(0)

    @pl.when(step == 0)
    def _():
        c = chunk_cumsum(lc_ref[...] * LOG2E)
        r = chunk_cumsum(jnp.broadcast_to(doc_ref[...].astype(F32), (8, doc_ref.shape[1])))
        crow_ref[...] = c
        rrow_ref[...] = r
        enter = jnp.where(r[0:1] == 0.0, jnp.exp2(c), 0.0)
        enter_ref[...] = enter
        spare = jnp.zeros((HD - heads, CHUNK), F32)
        for span in spans(chunks):
            cn, rn = c[:, span], r[0:1, span]
            leave_ref[:, span] = jnp.where(rn == rn[:, -1:], jnp.exp2(cn[:, -1:] - cn), 0.0)
            cols_ref[span, :] = jnp.concatenate([cn, spare], axis=0).T

    here = pl.ds(pl.multiple_of(step * GROUP * HD, GROUP * HD), GROUP * HD)
    kept_k_ref[:, here] = k_ref[...]
    kept_v_ref[:, here] = v_ref[...]
    for g in range(GROUP):
        h = step * GROUP + g
        cols = slice(g * HD, (g + 1) * HD)
        state = None
        total = None
        for n, span in enumerate(spans(chunks)):
            keyed = (k_ref[span, cols].T.astype(F32) * leave_ref[pl.ds(h, 1), span]).astype(BF16)
            local = dot(keyed, v_ref[span, cols])
            loc_ref[h, n] = local
            passing = enter_ref[pl.ds(h, 1), span][:, CHUNK - 1 : CHUNK]
            state = local if state is None else passing * state + local
            total = passing if total is None else passing * total
        state_ref[h] = state
        pass_ref[pl.ds(h, 1), :] = jnp.broadcast_to(total, (1, HD))


def mask_kernel(rrow_ref, mask_ref):
    sub = lax.broadcasted_iota(jnp.int32, (CHUNK, CHUNK), 0)
    lane = lax.broadcasted_iota(jnp.int32, (CHUNK, CHUNK), 1)
    for n, span in enumerate(spans(mask_ref.shape[0])):
        r_row = rrow_ref[0:1, span]
        r_col = jnp.broadcast_to(r_row, (CHUNK, CHUNK)).T
        mask_ref[n] = jnp.where((r_col == r_row) & (sub <= lane), 0.0, -jnp.inf)


def weight_of(crow_ref, cols_now, mask_ref, h, g, n, span):
    c_col = jnp.broadcast_to(cols_now[span, g : g + 1], (CHUNK, CHUNK))
    return jnp.exp2(crow_ref[pl.ds(h, 1), span] - c_col + mask_ref[n])


def head_columns(cols_ref, head):
    return pltpu.roll(cols_ref[...], (HD - head) % HD, 1)


def head_span(head):
    return pl.ds(pl.multiple_of(head * HD, HD), HD)


def inside_kernel(
    chunks, first, crow_ref, cols_ref, mask_ref, k_ref, v_ref, gain_ref, q_ref, gate_ref,
    grad_ref, *refs,
):
    attn_ref, gnorm_ref, kept_q_ref, probs_ref = refs[-4:]
    step = pl.program_id(0)
    cols_now = head_columns(cols_ref, first + step * GROUP)
    for g in range(GROUP):
        h = first + step * GROUP + g
        cols = slice(g * HD, (g + 1) * HD)
        mine = head_span(h)
        for n, span in enumerate(spans(chunks)):
            q = q_ref[span, cols].T
            kept_q_ref[h, :, span] = q
            weight = weight_of(crow_ref, cols_now, mask_ref, h, g, n, span)
            probs = (dot(k_ref[span, mine], q) * weight).astype(BF16)
            probs_ref[g, n] = probs
            attn_ref[h, :, span] = dot(v_ref[span, mine].T, probs)
            sig = jax.nn.sigmoid(gate_ref[span, cols].astype(F32))
            gnorm = grad_ref[span, cols].astype(F32) * sig * gain_ref[0:1, cols]
            gnorm_ref[h, :, span] = gnorm.astype(BF16).T


def folded(x):
    return jnp.sum(x.reshape(x.shape[0] // 8, 8, x.shape[1]), axis=0)


def outside_kernel(
    chunks, enter_ref, q_ref, gnorm_ref, loc_ref, in_ref, inside_ref,
    attn_ref, held_ref, sums_ref, sq_ref, inner_ref,
):
    step = pl.program_id(0)

    @pl.when(step == 0)
    def _():
        sq_ref[...] = jnp.zeros_like(sq_ref)
        inner_ref[...] = jnp.zeros_like(inner_ref)

    heads = [step * GROUP + g for g in range(GROUP)]
    carries = [in_ref[h] for h in heads]
    for n, span in enumerate(spans(chunks)):
        squares = sq_ref[:, span]
        inners = inner_ref[:, span]
        for g, h in enumerate(heads):
            held = carries[g].astype(BF16)
            held_ref[h, n] = held
            enter = enter_ref[pl.ds(h, 1), span]
            attn = inside_ref[h, :, span] + enter * dot(held.T, q_ref[h, :, span])
            attn_ref[h, :, span] = attn
            squares = squares + folded(attn * attn)
            inners = inners + folded(gnorm_ref[h, :, span].astype(F32) * attn)
            if n + 1 < chunks:
                carries[g] = enter[:, CHUNK - 1 : CHUNK] * carries[g] + loc_ref[h, n]
        sq_ref[:, span] = squares
        inner_ref[:, span] = inners

    @pl.when(step == pl.num_programs(0) - 1)
    def _():
        sums_ref[0:1, :] = jnp.sum(sq_ref[...], axis=0, keepdims=True)
        sums_ref[1:2, :] = jnp.sum(inner_ref[...], axis=0, keepdims=True)


def grad_kernel(chunks, parts, enter_ref, *refs):
    q_ref, gnorm_ref, attn_ref, _, agrad_ref, bloc_ref, back_ref, scale_ref = refs[parts:]
    step = pl.program_id(0)

    @pl.when(step == 0)
    def _():
        sums = refs[0][...]
        for ref in refs[1:parts]:
            sums = sums + ref[...]
        inverse = lax.rsqrt(sums[0:1] / WIDTH + epsilon)
        scale_ref[0:1, :] = inverse
        scale_ref[1:2, :] = inverse * inverse * inverse * sums[1:2] / WIDTH

    for g in range(GROUP):
        h = step * GROUP + g
        back = None
        for n, span in reversed(list(enumerate(spans(chunks)))):
            enter = enter_ref[pl.ds(h, 1), span]
            gnorm = gnorm_ref[h, :, span].astype(F32)
            agrad = scale_ref[0:1, span] * gnorm - attn_ref[h, :, span] * scale_ref[1:2, span]
            agrad = agrad.astype(BF16)
            agrad_ref[h, :, span] = agrad
            qkeyed = (q_ref[h, :, span].astype(F32) * enter).astype(BF16)
            local = dot(qkeyed, agrad, NT)
            bloc_ref[h, n] = local
            back = local if back is None else local + enter[:, CHUNK - 1 : CHUNK] * back
        back_ref[h] = back


def inner_grad_kernel(
    chunks, first, crow_ref, enter_ref, scale_ref, cols_ref, mask_ref, k_ref, v_ref, attn_ref,
    held_ref, q_ref, agrad_ref, gain_ref, gate_ref, grad_ref, probs_ref, *refs,
):
    dk_ref, dv_ref, dq_ref, gated_ref, ggate_ref = refs[-5:]
    step = pl.program_id(0)
    cols_now = head_columns(cols_ref, first + step * GROUP)
    for g in range(GROUP):
        h = first + step * GROUP + g
        cols = slice(g * HD, (g + 1) * HD)
        mine = head_span(h)
        for n, span in enumerate(spans(chunks)):
            q, agrad = q_ref[h, :, span], agrad_ref[h, :, span]
            k, v = k_ref[span, mine], v_ref[span, mine]
            weight = weight_of(crow_ref, cols_now, mask_ref, h, g, n, span)
            both = dot(jnp.concatenate([v, held_ref[h, n]], axis=0), agrad)
            dscore = (both[:CHUNK] * weight).astype(BF16)
            dq = dot(k.T, dscore) + enter_ref[pl.ds(h, 1), span] * both[CHUNK:]
            dq_ref[span, cols] = dq.astype(BF16).T
            dv_ref[h, :, span] = dot(agrad, probs_ref[g, n], NT).astype(BF16)
            dk_ref[h, :, span] = dot(q, dscore, NT).astype(BF16)
            normed = (attn_ref[h, :, span] * scale_ref[0:1, span]).T * gain_ref[0:1, cols]
            sig = jax.nn.sigmoid(gate_ref[span, cols].astype(F32))
            gated = normed * sig
            gated_ref[span, cols] = gated.astype(BF16)
            ggate = grad_ref[span, cols].astype(F32) * gated * (1.0 - sig)
            ggate_ref[span, cols] = ggate.astype(BF16)


def outer_grad_kernel(
    chunks, enter_ref, leave_ref, k_ref, v_ref, dkin_ref, dvin_ref, bloc_ref, out_ref,
    dk_ref, dv_ref,
):
    step = pl.program_id(0)
    for g in range(GROUP):
        h = step * GROUP + g
        cols = slice(g * HD, (g + 1) * HD)
        mine = head_span(h)
        carry = out_ref[h]
        for n, span in reversed(list(enumerate(spans(chunks)))):
            leave = leave_ref[pl.ds(h, 1), span]
            back = carry.astype(BF16)
            dk = dkin_ref[h, :, span].astype(F32) + leave * dot(back, v_ref[span, mine], NT)
            dv = dvin_ref[h, :, span].astype(F32) + leave * dot(back.T, k_ref[span, mine], NT)
            dk_ref[span, cols] = dk.astype(BF16).T
            dv_ref[span, cols] = dv.astype(BF16).T
            if n > 0:
                passing = enter_ref[pl.ds(h, 1), span][:, CHUNK - 1 : CHUNK]
                carry = bloc_ref[h, n] + passing * carry


def hbm(x):
    return pltpu.with_memory_space_constraint(x, pltpu.HBM)


def kept(*arrays):
    spec = pl.BlockSpec(memory_space=pltpu.VMEM)
    return [(pltpu.with_memory_space_constraint(x, pltpu.VMEM), spec) for x in arrays]


def keep(dims, dtype):
    return pltpu.VMEM(dims, dtype), pl.BlockSpec(memory_space=pltpu.VMEM)


def call(kernel, grid, ins, outs, scratch=(), aliases=None, room=8, flops=0, moved=0, exps=0):
    return pl.pallas_call(
        kernel,
        grid=grid,
        in_specs=[spec for _, spec in ins],
        out_specs=[spec for _, spec in outs],
        out_shape=[shape for shape, _ in outs],
        scratch_shapes=list(scratch),
        input_output_aliases=aliases or {},
        compiler_params=pltpu.CompilerParams(
            dimension_semantics=("arbitrary",) * len(grid), vmem_limit_bytes=room * MIB
        ),
        cost_estimate=pl.CostEstimate(flops=flops, bytes_accessed=moved, transcendentals=exps),
    )(*[x for x, _ in ins])


def after(x, *others):
    return lax.optimization_barrier((x, *others))[0]


def across(x, flips, devices=8):
    return lax.ppermute(x, "seq", [(i, i ^ flips) for i in range(devices)])


def cube_scan(state, own_pass, passes, index, fill):
    heads = state.shape[0]
    half, quarter = heads // 2, heads // 4
    core, x, y = index % 2, (index // 2) % 2, index // 4
    factor = lambda rows: rows[:, None, :]
    mine = lambda a: lax.dynamic_slice_in_dim(a, core * half, half, 0)

    other = across(state, 1)
    beside_pass = passes[0] if passes else across(own_pass, 1)
    other, beside_pass = lax.optimization_barrier((other, beside_pass, fill(0, state)))[:2]
    early = jnp.where(core == 0, state, other)
    late = jnp.where(core == 0, other, state)
    early_pass = jnp.where(core == 0, own_pass, beside_pass)
    late_pass = jnp.where(core == 0, beside_pass, own_pass)
    total = factor(mine(late_pass)) * mine(early) + mine(late)
    to_x, to_y = total[:quarter], total[quarter:]

    chip_pass = own_pass * beside_pass
    from_x, from_y = across(to_x, 2), across(to_y, 4)
    x_pass, far_pass = passes[1:] if passes else (across(chip_pass, 2), across(chip_pass, 6))
    from_x, from_y, x_pass, far_pass = lax.optimization_barrier(
        (from_x, from_y, x_pass, far_pass, fill(1, total))
    )[:4]
    chip_x, chip_y = mine(chip_pass)[:quarter], mine(chip_pass)[quarter:]
    side_x, side_y = mine(x_pass)[:quarter], mine(x_pass)[quarter:]
    far_y = mine(far_pass)[quarter:]
    left = jnp.where(x == 0, to_x, from_x)
    right = jnp.where(x == 0, from_x, to_x)
    row = factor(jnp.where(x == 0, side_x, chip_x)) * left + right
    through = factor(chip_y) * (factor(far_y) * from_y) + to_y
    sent = jnp.where(y == 0, to_y, jnp.where(x == 0, through, from_y))

    row_in, sent_in = across(row, 4), across(sent, 2)
    row_in, sent_in = lax.optimization_barrier((row_in, sent_in, fill(2, sent)))[:2]
    lower = jnp.where(x == 0, row_in, factor(side_x) * row_in + from_x)
    upper = jnp.where(x == 0, 0.0, from_x)
    in_x = jnp.where(y == 0, upper, lower)
    more = factor(jnp.where(x == 0, far_y, side_y)) * from_y
    in_y = jnp.where(y == 0, jnp.where(x == 0, 0.0, sent_in), more + sent_in)
    ahead = jnp.concatenate([in_x, in_y], axis=0)

    beside = across(ahead, 1)
    beside = after(beside, fill(3, ahead))
    low = jnp.where(core == 0, ahead, beside)
    high = jnp.where(core == 0, beside, ahead)
    entering = jnp.concatenate([low, high], axis=0)
    entering = jnp.where(core == 0, entering, factor(early_pass) * entering + early)
    return entering, (beside_pass, x_pass, far_pass)


def doubling_scan(state, own_pass, fill, reverse):
    devices = lax.axis_size("seq")
    index = lax.axis_index("seq")
    passes = lax.all_gather(own_pass, "seq")
    if reverse:
        passes = passes[::-1]
        index = devices - 1 - index
    route = lambda hop: [
        (i, i - hop if reverse else i + hop)
        for i in range(devices)
        if 0 <= (i - hop if reverse else i + hop) < devices
    ]
    for window in range(WINDOWS):
        state = after(state, fill(window, state))
    hop = 1
    while hop < devices:
        factor = lax.dynamic_index_in_dim(passes, index, 0, False)
        state = factor[:, None, :] * lax.ppermute(state, "seq", route(hop)) + state
        before = jnp.concatenate([jnp.zeros_like(passes[:hop]), passes[:-hop]], axis=0)
        passes = passes * before
        hop *= 2
    return lax.ppermute(state, "seq", route(1))


def scan_devices(state, own_pass, passes, fill, reverse):
    devices = lax.axis_size("seq")
    if devices == 8 and state.shape[0] % 4 == 0:
        index = lax.axis_index("seq")
        index = devices - 1 - index if reverse else index
        return cube_scan(state, own_pass, passes, index, fill)
    return doubling_scan(state, own_pass, fill, reverse), None


def body(queries, key_rows, value_rows, log_decay, doc_start, gate_input, norm_gain, out_grad):
    rows, cols = queries.shape
    heads = cols // HD
    chunks = rows // CHUNK
    parts = lax.axis_size("head")
    grid = (heads // GROUP,)
    share = heads // WINDOWS
    big = rows * cols * 2
    tile = 2 * rows * CHUNK * cols
    small = 2 * rows * HD * cols

    whole = lambda *dims: pl.BlockSpec(dims, lambda i: (0,) * len(dims))
    anywhere = pl.BlockSpec(memory_space=pl.ANY)

    def wide(base=0):
        return pl.BlockSpec((rows, GROUP * HD), lambda i: (0, i + base // GROUP))

    def gain_spec(base=0):
        return pl.BlockSpec((1, GROUP * HD), lambda i: (0, i + base // GROUP))

    probs_spec = pl.BlockSpec((GROUP, chunks, CHUNK, CHUNK), lambda i: (i, 0, 0, 0))
    by_head = (heads, HD, rows)
    local_dims = (heads, chunks, HD, HD)
    wide_shape = pltpu.HBM((rows, cols), BF16)
    queries, key_rows, value_rows, gate_input, out_grad = map(
        hbm, (queries, key_rows, value_rows, gate_input, out_grad)
    )
    doc_row = doc_start.reshape(1, rows)
    gain_row = norm_gain.reshape(1, cols)

    crow, enter, leave, rrow, columns, keys, values, local, state, own_pass = call(
        functools.partial(state_kernel, chunks, heads),
        grid,
        [
            (log_decay, whole(heads, rows)), (doc_row, whole(1, rows)),
            (key_rows, wide()), (value_rows, wide()),
        ],
        [keep((heads, rows), F32)] * 3
        + [
            keep((8, rows), F32), keep((rows, HD), F32), keep((rows, cols), BF16),
            keep((rows, cols), BF16), keep(local_dims, F32), keep((heads, HD, HD), F32),
            keep((heads, HD), F32),
        ],
        flops=small, moved=2 * big,
    )

    mask = []
    made = []
    probs = []

    def fill_forward(window, tie):
        base = window * share
        if not mask:
            mask[:] = call(
                mask_kernel, (), kept(after(rrow, tie)), [keep((chunks, CHUNK, CHUNK), F32)],
                flops=8 * rows * CHUNK,
            )
        ins = kept(after(crow, tie), columns, mask[0], keys, values) + [
            (gain_row, gain_spec(base)), (queries, wide(base)), (gate_input, wide(base)),
            (out_grad, wide(base)),
        ]
        aliases = {len(ins) + i: i for i in range(len(made))}
        ins += kept(*made)
        *made[:], fresh = call(
            functools.partial(inside_kernel, chunks, base),
            (share // GROUP,),
            ins,
            [
                keep(by_head, F32), keep(by_head, BF16), keep(by_head, BF16),
                (pltpu.HBM((share, chunks, CHUNK, CHUNK), BF16), probs_spec),
            ],
            aliases=aliases, room=12,
            flops=2 * tile // WINDOWS, moved=5 * big // WINDOWS,
            exps=rows * (CHUNK + HD) * heads // WINDOWS,
        )
        probs.append(fresh)
        return fresh

    incoming, passes = scan_devices(state, own_pass, None, fill_forward, False)
    inside, gnorm, turned = made

    attn, held, sums = call(
        functools.partial(outside_kernel, chunks),
        grid,
        kept(enter, turned, gnorm, local, incoming, inside),
        [keep(by_head, F32), keep(local_dims, BF16), keep((2, rows), F32)],
        [pltpu.VMEM((8, rows), F32)] * 2,
        {5: 0},
        flops=small, moved=big,
    )

    all_sums = [sums]
    for hop in range(1, parts):
        route = [(i, (i + hop) % parts) for i in range(parts)]
        all_sums.append(lax.ppermute(sums, "head", route))

    agrad, bloc, back, scales = call(
        functools.partial(grad_kernel, chunks, parts),
        grid,
        kept(enter, *all_sums, turned, gnorm, attn, local),
        [
            keep(by_head, BF16), keep(local_dims, F32), keep((heads, HD, HD), F32),
            keep((2, rows), F32),
        ],
        aliases={parts + 4: 1},
        flops=small, moved=big,
    )

    inner = [turned, agrad]
    outs = []

    def fill_backward(window, tie):
        base = window * share
        ins = kept(
            after(crow, tie), enter, scales, columns, mask[0], keys, values, attn, held, *inner
        )
        aliases = {len(ins) - 2: 0, len(ins) - 1: 1}
        ins += [
            (gain_row, gain_spec(base)), (gate_input, wide(base)), (out_grad, wide(base)),
            (hbm(probs[window]), probs_spec),
        ]
        aliases.update({len(ins) + i: 2 + i for i in range(len(outs))})
        ins += [(hbm(x), anywhere) for x in outs]
        inner[0], inner[1], *outs[:] = call(
            functools.partial(inner_grad_kernel, chunks, base),
            (share // GROUP,),
            ins,
            [keep(by_head, BF16)] * 2 + [(wide_shape, wide(base))] * 3,
            aliases=aliases, room=14,
            flops=(4 * tile + small) // WINDOWS, moved=7 * big // WINDOWS,
            exps=rows * (CHUNK + HD) * heads // WINDOWS,
        )
        return outs[0]

    outgoing, _ = scan_devices(back, own_pass, passes, fill_backward, True)
    dq, gated, gate_grad = outs

    dk, dv = call(
        functools.partial(outer_grad_kernel, chunks),
        grid,
        kept(enter, leave, keys, values, *inner, bloc, outgoing),
        [(wide_shape, wide())] * 2,
        flops=2 * small, moved=2 * big,
    )
    return (gated, gate_grad, dq, dk, dv)


def solution(mesh):
    in_specs = (
        P("seq", "head"),
        P("seq", "head"),
        P("seq", "head"),
        P("head", "seq"),
        P("seq"),
        P("seq", "head"),
        P("head"),
        P("seq", "head"),
    )
    out_specs = (P("seq", "head"),) * 5
    return jax.shard_map(body, mesh=mesh, in_specs=in_specs, out_specs=out_specs, check_vma=False)
```

```python
import functools

import jax
import jax.numpy as jnp
from jax import lax
from jax.experimental import pallas as pl
from jax.experimental.pallas import tpu as pltpu
from jax.sharding import PartitionSpec as P

HEAD_TOTAL = 64
HD = 128
CHUNK = 256
GROUP = 2
WINDOWS = 4
WIDTH = HEAD_TOTAL * HD

epsilon = 1e-06
LOG2E = 1.4426950408889634

F32 = jnp.float32
BF16 = jnp.bfloat16
MIB = 1024 * 1024
NT = ((1,), (1,))


def dot(a, b, dims=((1,), (0,))):
    return lax.dot_general(a, b, (dims, ((), ())), preferred_element_type=F32)


def chunk_cumsum(x):
    lane = lax.broadcasted_iota(jnp.int32, x.shape, 1) % CHUNK
    shift = 1
    while shift < CHUNK:
        x = x + jnp.where(lane >= shift, pltpu.roll(x, shift, 1), 0.0)
        shift *= 2
    return x


def spans(chunks):
    return [slice(n * CHUNK, (n + 1) * CHUNK) for n in range(chunks)]


def head_span(head, count=1):
    return pl.ds(pl.multiple_of(head * HD, HD), count * HD)


def sigmoid(x):
    return 0.5 * jnp.tanh(0.5 * x) + 0.5


def spread(cols, lane):
    return jnp.broadcast_to(cols[:, lane : lane + 1], cols.shape)


def turned(cols_ref, lane):
    return pltpu.roll(cols_ref[...], (HD - lane) % HD, 1)


def column(row):
    return jnp.broadcast_to(row, (HD, row.shape[1])).T


def state_kernel(
    chunks, steps, lc_ref, doc_ref, k_hbm, v_hbm,
    crow_ref, enter_ref, leave_ref, rrow_ref, k_ref, v_ref, loc_ref, state_ref, pass_ref, sems,
):
    step = pl.program_id(0)

    def copies(at):
        here = head_span(at * GROUP, GROUP)
        return (
            pltpu.make_async_copy(k_hbm.at[:, here], k_ref.at[:, here], sems.at[0, at]),
            pltpu.make_async_copy(v_hbm.at[:, here], v_ref.at[:, here], sems.at[1, at]),
        )

    @pl.when(step == 0)
    def _():
        for at in range(steps):
            for copy in copies(at):
                copy.start()
        c = chunk_cumsum(lc_ref[...] * LOG2E)
        r = chunk_cumsum(jnp.broadcast_to(doc_ref[...].astype(F32), (8, doc_ref.shape[1])))
        crow_ref[...] = c
        rrow_ref[...] = r
        enter_ref[...] = jnp.where(r[0:1] == 0.0, jnp.exp2(c), 0.0)
        for span in spans(chunks):
            cn, rn = c[:, span], r[0:1, span]
            leave_ref[:, span] = jnp.where(rn == rn[:, -1:], jnp.exp2(cn[:, -1:] - cn), 0.0)

    for copy in copies(step):
        copy.wait()
    for g in range(GROUP):
        h = step * GROUP + g
        mine = head_span(h)
        state = None
        total = None
        for n, span in enumerate(spans(chunks)):
            keyed = (k_ref[span, mine].T.astype(F32) * leave_ref[pl.ds(h, 1), span]).astype(BF16)
            local = dot(keyed, v_ref[span, mine])
            loc_ref[h, n] = local
            passing = enter_ref[pl.ds(h, 1), span][:, CHUNK - 1 : CHUNK]
            state = local if state is None else passing * state + local
            total = passing if total is None else passing * total
        state_ref[h] = state
        pass_ref[pl.ds(h, 1), :] = jnp.broadcast_to(total, (1, HD))


def prepare_kernel(rrow_ref, crow_ref, enter_ref, mask_ref, cols_ref):
    sub = lax.broadcasted_iota(jnp.int32, (CHUNK, CHUNK), 0)
    lane = lax.broadcasted_iota(jnp.int32, (CHUNK, CHUNK), 1)
    spare = jnp.zeros((HD - 2 * crow_ref.shape[0], CHUNK), F32)
    for n, span in enumerate(spans(mask_ref.shape[0])):
        r_row = rrow_ref[0:1, span]
        r_col = jnp.concatenate([column(r_row)] * (CHUNK // HD), axis=1)
        mask_ref[n] = jnp.where((r_col == r_row) & (lane <= sub), 0.0, -jnp.inf)
        cols_ref[span, :] = jnp.concatenate([crow_ref[:, span], enter_ref[:, span], spare], axis=0).T


def decayed(scores, c_col, c_row, mask):
    top, low = slice(0, HD), slice(HD, CHUNK)
    row_blocks = []
    for rows, width in ((top, HD), (low, CHUNK)):
        col = c_col[rows]
        col = col if width == HD else jnp.concatenate([col] * (width // HD), axis=1)
        weight = jnp.exp2(col - c_row[:, :width] + mask[rows, :width])
        row_blocks.append((scores[rows, :width] * weight).astype(BF16))
    row_blocks[0] = jnp.concatenate([row_blocks[0], jnp.zeros((HD, CHUNK - HD), BF16)], axis=1)
    return jnp.concatenate(row_blocks, axis=0)


def inside_kernel(
    chunks, first, steps, crow_ref, cols_ref, mask_ref, k_ref, v_ref, gain_ref, q_hbm, gate_ref,
    grad_ref, *refs,
):
    attn_ref, gnorm_ref, q_ref, turned_q_ref, probs_ref, sems = refs[-6:]
    step = pl.program_id(0)

    def copy(at):
        here = head_span(first + at * GROUP, GROUP)
        return pltpu.make_async_copy(q_hbm.at[:, here], q_ref.at[:, here], sems.at[at])

    @pl.when(step == 0)
    def _():
        for at in range(steps):
            copy(at).start()

    cols_now = turned(cols_ref, first + step * GROUP)
    copy(step).wait()
    for g in range(GROUP):
        h = first + step * GROUP + g
        cols = slice(g * HD, (g + 1) * HD)
        mine = head_span(h)
        for n, span in enumerate(spans(chunks)):
            q = q_ref[span, mine]
            scores = dot(q, k_ref[span, mine], NT)
            c_row = crow_ref[pl.ds(h, 1), span]
            probs = decayed(scores, spread(cols_now[span], g), c_row, mask_ref.at[n])
            probs_ref[g, n] = probs
            attn_ref[span, mine] = dot(probs, v_ref[span, mine])
            turned_q_ref[h, :, span] = q.T
            sig = sigmoid(gate_ref[span, cols].astype(F32))
            gnorm = grad_ref[span, cols].astype(F32) * sig * gain_ref[0:1, cols]
            gnorm_ref[span, mine] = gnorm.astype(BF16)


def outside_kernel(chunks, entering, inputs, cols_ref, enter_ref, q_ref, gnorm_ref, loc_ref, *refs):
    in_refs = refs[:inputs]
    inside_ref, attn_ref, held_ref, sums_ref, sq_ref, inner_ref = refs[inputs:]
    step = pl.program_id(0)

    @pl.when(step == 0)
    def _():
        sq_ref[...] = jnp.zeros_like(sq_ref)
        inner_ref[...] = jnp.zeros_like(inner_ref)

    heads = [step * GROUP + g for g in range(GROUP)]
    cols_now = turned(cols_ref, enter_ref.shape[0] + step * GROUP)
    carries = [entering(in_refs, h) for h in heads]
    for n, span in enumerate(spans(chunks)):
        squares = sq_ref[span, :]
        inners = inner_ref[span, :]
        for g, h in enumerate(heads):
            mine = head_span(h)
            held = carries[g].astype(BF16)
            held_ref[h, n] = held
            enter = spread(cols_now[span], g)
            attn = inside_ref[span, mine] + enter * dot(q_ref[span, mine], held)
            attn_ref[span, mine] = attn
            squares = squares + attn * attn
            inners = inners + gnorm_ref[span, mine].astype(F32) * attn
            if n + 1 < chunks:
                passing = enter_ref[pl.ds(h, 1), span][:, CHUNK - 1 : CHUNK]
                carries[g] = passing * carries[g] + loc_ref[h, n]
        sq_ref[span, :] = squares
        inner_ref[span, :] = inners

    @pl.when(step == pl.num_programs(0) - 1)
    def _():
        sums_ref[0:1, :] = jnp.sum(sq_ref[...].T, axis=0, keepdims=True)
        sums_ref[1:2, :] = jnp.sum(inner_ref[...].T, axis=0, keepdims=True)


def grad_kernel(chunks, parts, enter_ref, *refs):
    turned_q_ref, gnorm_ref, attn_ref, _ = refs[parts : parts + 4]
    agrad_ref, turned_ref, bloc_ref, back_ref, alpha_ref, beta_ref = refs[parts + 4 :]
    step = pl.program_id(0)

    @pl.when(step == 0)
    def _():
        sums = refs[0][...]
        for ref in refs[1:parts]:
            sums = sums + ref[...]
        inverse = lax.rsqrt(sums[0:1] / WIDTH + epsilon)
        alpha_ref[...] = column(inverse)
        beta_ref[...] = column(inverse * inverse * inverse * sums[1:2] / WIDTH)

    for g in range(GROUP):
        h = step * GROUP + g
        mine = head_span(h)
        back = None
        for n, span in reversed(list(enumerate(spans(chunks)))):
            enter = enter_ref[pl.ds(h, 1), span]
            gnorm = gnorm_ref[span, mine].astype(F32)
            agrad = alpha_ref[span, :] * gnorm - attn_ref[span, mine] * beta_ref[span, :]
            agrad = agrad.astype(BF16)
            agrad_ref[span, mine] = agrad
            turned_ref[h, :, span] = agrad.T
            qkeyed = (turned_q_ref[h, :, span].astype(F32) * enter).astype(BF16)
            local = dot(qkeyed, agrad)
            bloc_ref[h, n] = local
            back = local if back is None else local + enter[:, CHUNK - 1 : CHUNK] * back
        back_ref[h] = back


def inner_grad_kernel(
    chunks, first, crow_ref, alpha_ref, cols_ref, mask_ref, k_ref, v_ref, attn_ref, held_ref,
    agrad_ref, turned_q_ref, turned_agrad_ref, gain_ref, gate_ref, grad_ref, probs_ref, *refs,
):
    dk_ref, dv_ref, dq_ref, gated_ref, ggate_ref = refs[-5:]
    step = pl.program_id(0)
    cols_now = turned(cols_ref, first + step * GROUP)
    for g in range(GROUP):
        h = first + step * GROUP + g
        cols = slice(g * HD, (g + 1) * HD)
        mine = head_span(h)
        for n, span in enumerate(spans(chunks)):
            k, v, agrad = k_ref[span, mine], v_ref[span, mine], agrad_ref[span, mine]
            both = dot(agrad, jnp.concatenate([v, held_ref[h, n]], axis=0), NT)
            c_row = crow_ref[pl.ds(h, 1), span]
            dscore = decayed(both[:, :CHUNK], spread(cols_now[span], g), c_row, mask_ref.at[n])
            enter = spread(cols_now[span], crow_ref.shape[0] + g)
            dq_ref[span, cols] = (dot(dscore, k) + enter * both[:, CHUNK:]).astype(BF16)
            dv_ref[h, :, span] = dot(turned_agrad_ref[h, :, span], probs_ref[g, n]).astype(BF16)
            dk_ref[h, :, span] = dot(turned_q_ref[h, :, span], dscore).astype(BF16)
            normed = attn_ref[span, mine] * alpha_ref[span, :] * gain_ref[0:1, cols]
            sig = sigmoid(gate_ref[span, cols].astype(F32))
            gated = normed * sig
            gated_ref[span, cols] = gated.astype(BF16)
            ggate = grad_ref[span, cols].astype(F32) * gated * (1.0 - sig)
            ggate_ref[span, cols] = ggate.astype(BF16)


def outer_grad_kernel(chunks, entering, inputs, enter_ref, leave_ref, k_ref, v_ref, *refs):
    in_refs = refs[:inputs]
    dkin_ref, dvin_ref, bloc_ref, dk_ref, dv_ref = refs[inputs:]
    step = pl.program_id(0)
    for g in range(GROUP):
        h = step * GROUP + g
        cols = slice(g * HD, (g + 1) * HD)
        mine = head_span(h)
        carry = entering(in_refs, h)
        for n, span in reversed(list(enumerate(spans(chunks)))):
            leave = leave_ref[pl.ds(h, 1), span]
            back = carry.astype(BF16)
            dk = dkin_ref[h, :, span].astype(F32) + leave * dot(back, v_ref[span, mine], NT)
            dv = dvin_ref[h, :, span].astype(F32) + leave * dot(back.T, k_ref[span, mine], NT)
            dk_ref[span, cols] = dk.astype(BF16).T
            dv_ref[span, cols] = dv.astype(BF16).T
            if n > 0:
                passing = enter_ref[pl.ds(h, 1), span][:, CHUNK - 1 : CHUNK]
                carry = bloc_ref[h, n] + passing * carry


def hbm(x):
    return pltpu.with_memory_space_constraint(x, pltpu.HBM)


def kept(*arrays):
    spec = pl.BlockSpec(memory_space=pltpu.VMEM)
    return [(pltpu.with_memory_space_constraint(x, pltpu.VMEM), spec) for x in arrays]


def keep(dims, dtype):
    return pltpu.VMEM(dims, dtype), pl.BlockSpec(memory_space=pltpu.VMEM)


def call(kernel, grid, ins, outs, scratch=(), aliases=None, room=8, flops=0, moved=0, exps=0):
    return pl.pallas_call(
        kernel,
        grid=grid,
        in_specs=[spec for _, spec in ins],
        out_specs=[spec for _, spec in outs],
        out_shape=[shape for shape, _ in outs],
        scratch_shapes=list(scratch),
        input_output_aliases=aliases or {},
        compiler_params=pltpu.CompilerParams(
            dimension_semantics=("arbitrary",) * len(grid), vmem_limit_bytes=room * MIB
        ),
        cost_estimate=pl.CostEstimate(flops=flops, bytes_accessed=moved, transcendentals=exps),
    )(*[x for x, _ in ins])


def after(x, *others):
    return lax.optimization_barrier((x, *others))[0]


def across(x, flips, devices=8):
    return lax.ppermute(x, "seq", [(i, i ^ flips) for i in range(devices)])


def place(reverse):
    index = lax.axis_index("seq")
    index = 7 - index if reverse else index
    return lax.rem(index, 2), lax.rem(lax.div(index, 2), 2), lax.div(index, 4)


def pair_kernel(reverse, state_ref, other_ref, pass_ref, beside_ref, x_ref, y_ref, chip_ref):
    core, _, _ = place(reverse)
    quarter = x_ref.shape[0]
    chip_ref[...] = pass_ref[...] * beside_ref[...]
    for i in range(quarter):
        for at, out_ref in ((i, x_ref), (quarter + i, y_ref)):
            h = core * 2 * quarter + at
            mine, other = state_ref[h], other_ref[h]

            @pl.when(core == 0)
            def _():
                out_ref[i] = beside_ref[pl.ds(h, 1), :] * mine + other

            @pl.when(core == 1)
            def _():
                out_ref[i] = pass_ref[pl.ds(h, 1), :] * other + mine


def row_kernel(
    reverse, to_x_ref, to_y_ref, from_x_ref, from_y_ref, chip_ref, side_ref, far_ref,
    row_ref, sent_ref,
):
    core, x, y = place(reverse)
    quarter = row_ref.shape[0]
    for i in range(quarter):
        h = core * 2 * quarter + i
        hy = h + quarter

        @pl.when(x == 0)
        def _():
            row_ref[i] = side_ref[pl.ds(h, 1), :] * to_x_ref[i] + from_x_ref[i]

        @pl.when(x == 1)
        def _():
            row_ref[i] = chip_ref[pl.ds(h, 1), :] * from_x_ref[i] + to_x_ref[i]

        @pl.when(y == 0)
        def _():
            sent_ref[i] = to_y_ref[i]

        @pl.when((y == 1) & (x == 0))
        def _():
            far = far_ref[pl.ds(hy, 1), :] * from_y_ref[i]
            sent_ref[i] = chip_ref[pl.ds(hy, 1), :] * far + to_y_ref[i]

        @pl.when((y == 1) & (x == 1))
        def _():
            sent_ref[i] = from_y_ref[i]


def ahead_kernel(
    reverse, from_x_ref, from_y_ref, row_ref, sent_ref, side_ref, far_ref, out_ref,
):
    core, x, y = place(reverse)
    quarter = row_ref.shape[0]
    for i in range(quarter):
        h = core * 2 * quarter + i
        hy = h + quarter

        @pl.when((y == 0) & (x == 0))
        def _():
            out_ref[i] = jnp.zeros_like(out_ref[i])
            out_ref[quarter + i] = jnp.zeros_like(out_ref[i])

        @pl.when((y == 0) & (x == 1))
        def _():
            out_ref[i] = from_x_ref[i]
            out_ref[quarter + i] = sent_ref[i]

        @pl.when((y == 1) & (x == 0))
        def _():
            out_ref[i] = row_ref[i]
            out_ref[quarter + i] = far_ref[pl.ds(hy, 1), :] * from_y_ref[i] + sent_ref[i]

        @pl.when((y == 1) & (x == 1))
        def _():
            out_ref[i] = side_ref[pl.ds(h, 1), :] * row_ref[i] + from_x_ref[i]
            out_ref[quarter + i] = side_ref[pl.ds(hy, 1), :] * from_y_ref[i] + sent_ref[i]


def cube_entering(reverse, refs, h):
    ahead_ref, beside_ref, other_ref, beside_pass_ref = refs
    core, _, _ = place(reverse)
    half = ahead_ref.shape[0]
    at = lax.rem(h, half)
    chip = jnp.where(lax.div(h, half) == core, ahead_ref[at], beside_ref[at])
    through = beside_pass_ref[pl.ds(h, 1), :] * chip + other_ref[h]
    return jnp.where(core == 0, chip, through)


def plain_entering(refs, h):
    return refs[0][h]


def cube_scan(state, own_pass, passes, fill, reverse):
    heads = state.shape[0]
    quarter = heads // 4
    part = keep((quarter, HD, HD), F32)

    other = across(state, 1)
    beside_pass = passes[0] if passes else across(own_pass, 1)
    other, beside_pass = lax.optimization_barrier((other, beside_pass, fill(0, state)))[:2]
    to_x, to_y, chip_pass = call(
        functools.partial(pair_kernel, reverse), (),
        kept(state, other, own_pass, beside_pass), [part, part, keep((heads, HD), F32)], room=2,
    )

    from_x, from_y = across(to_x, 2), across(to_y, 4)
    x_pass, far_pass = passes[1:] if passes else (across(chip_pass, 2), across(chip_pass, 6))
    from_x, from_y, x_pass, far_pass = lax.optimization_barrier(
        (from_x, from_y, x_pass, far_pass, fill(1, to_y))
    )[:4]
    row, sent = call(
        functools.partial(row_kernel, reverse), (),
        kept(to_x, to_y, from_x, from_y, chip_pass, x_pass, far_pass), [part, part], room=2,
    )

    row_in, sent_in = across(row, 4), across(sent, 2)
    row_in, sent_in = lax.optimization_barrier((row_in, sent_in, fill(2, sent)))[:2]
    (ahead,) = call(
        functools.partial(ahead_kernel, reverse), (),
        kept(from_x, from_y, row_in, sent_in, x_pass, far_pass),
        [keep((2 * quarter, HD, HD), F32)], room=2,
    )

    beside = across(ahead, 1)
    beside = after(beside, fill(3, ahead))
    entering = functools.partial(cube_entering, reverse)
    return entering, (ahead, beside, other, beside_pass), (beside_pass, x_pass, far_pass)


def doubling_scan(state, own_pass, fill, reverse):
    devices = lax.axis_size("seq")
    index = lax.axis_index("seq")
    passes = lax.all_gather(own_pass, "seq")
    if reverse:
        passes = passes[::-1]
        index = devices - 1 - index
    route = lambda hop: [
        (i, i - hop if reverse else i + hop)
        for i in range(devices)
        if 0 <= (i - hop if reverse else i + hop) < devices
    ]
    for window in range(WINDOWS):
        state = after(state, fill(window, state))
    hop = 1
    while hop < devices:
        factor = lax.dynamic_index_in_dim(passes, index, 0, False)
        state = factor[:, None, :] * lax.ppermute(state, "seq", route(hop)) + state
        before = jnp.concatenate([jnp.zeros_like(passes[:hop]), passes[:-hop]], axis=0)
        passes = passes * before
        hop *= 2
    return lax.ppermute(state, "seq", route(1))


def scan_devices(state, own_pass, passes, fill, reverse):
    if lax.axis_size("seq") == 8 and state.shape[0] % 4 == 0:
        return cube_scan(state, own_pass, passes, fill, reverse)
    return plain_entering, (doubling_scan(state, own_pass, fill, reverse),), None


def body(queries, key_rows, value_rows, log_decay, doc_start, gate_input, norm_gain, out_grad):
    rows, cols = queries.shape
    heads = cols // HD
    chunks = rows // CHUNK
    parts = lax.axis_size("head")
    grid = (heads // GROUP,)
    share = heads // WINDOWS
    big = rows * cols * 2
    tile = 2 * rows * CHUNK * cols
    small = 2 * rows * HD * cols

    whole = lambda *dims: pl.BlockSpec(dims, lambda i: (0,) * len(dims))
    anywhere = pl.BlockSpec(memory_space=pl.ANY)

    def wide(base=0):
        return pl.BlockSpec((rows, GROUP * HD), lambda i: (0, i + base // GROUP))

    def gain_spec(base=0):
        return pl.BlockSpec((1, GROUP * HD), lambda i: (0, i + base // GROUP))

    probs_spec = pl.BlockSpec((GROUP, chunks, CHUNK, CHUNK), lambda i: (i, 0, 0, 0))
    by_head = (heads, HD, rows)
    local_dims = (heads, chunks, HD, HD)
    wide_shape = pltpu.HBM((rows, cols), BF16)
    queries, key_rows, value_rows, gate_input, out_grad = map(
        hbm, (queries, key_rows, value_rows, gate_input, out_grad)
    )
    doc_row = doc_start.reshape(1, rows)
    gain_row = norm_gain.reshape(1, cols)

    by_token = (rows, cols)
    steps = heads // GROUP
    crow, enter, leave, rrow, keys, values, local, state, own_pass = call(
        functools.partial(state_kernel, chunks, steps),
        grid,
        [
            (hbm(log_decay), whole(heads, rows)), (hbm(doc_row), whole(1, rows)),
            (key_rows, anywhere), (value_rows, anywhere),
        ],
        [keep((heads, rows), F32)] * 3
        + [
            keep((8, rows), F32), keep(by_token, BF16), keep(by_token, BF16),
            keep(local_dims, F32), keep((heads, HD, HD), F32), keep((heads, HD), F32),
        ],
        [pltpu.SemaphoreType.DMA((2, steps))],
        flops=small, moved=2 * big,
    )

    ready = []
    made = []
    probs = []

    def fill_forward(window, tie):
        base = window * share
        if not ready:
            ready[:] = call(
                prepare_kernel, (), kept(after(rrow, tie), crow, enter),
                [keep((chunks, CHUNK, CHUNK), F32), keep((rows, HD), F32)],
                flops=8 * rows * CHUNK,
            )
        mask, columns = ready
        ins = kept(after(crow, tie), columns, mask, keys, values) + [
            (hbm(gain_row), gain_spec(base)), (queries, anywhere), (gate_input, wide(base)),
            (out_grad, wide(base)),
        ]
        aliases = {len(ins) + i: i for i in range(len(made))}
        ins += kept(*made)
        *made[:], fresh = call(
            functools.partial(inside_kernel, chunks, base, share // GROUP),
            (share // GROUP,),
            ins,
            [
                keep(by_token, F32), keep(by_token, BF16), keep(by_token, BF16),
                keep(by_head, BF16),
                (pltpu.HBM((share, chunks, CHUNK, CHUNK), BF16), probs_spec),
            ],
            [pltpu.SemaphoreType.DMA((share // GROUP,))],
            aliases=aliases, room=10,
            flops=2 * tile // WINDOWS, moved=5 * big // WINDOWS,
            exps=rows * (CHUNK + HD) * heads // WINDOWS,
        )
        probs.append(fresh)
        return fresh

    entering, incoming, passes = scan_devices(state, own_pass, None, fill_forward, False)
    mask, columns = ready
    inside, gnorm, kept_q, turned_q = made
    tall = pltpu.VMEM((rows, HD), F32)

    attn, held, sums = call(
        functools.partial(outside_kernel, chunks, entering, len(incoming)),
        grid,
        kept(columns, enter, kept_q, gnorm, local, *incoming, inside),
        [keep(by_token, F32), keep(local_dims, BF16), keep((2, rows), F32)],
        [tall, tall],
        {5 + len(incoming): 0},
        flops=small, moved=big,
    )

    all_sums = [sums]
    for hop in range(1, parts):
        route = [(i, (i + hop) % parts) for i in range(parts)]
        all_sums.append(lax.ppermute(sums, "head", route))

    agrad, turned_agrad, bloc, back, alpha, _ = call(
        functools.partial(grad_kernel, chunks, parts),
        grid,
        kept(enter, *all_sums, turned_q, gnorm, attn, local),
        [
            keep(by_token, BF16), keep(by_head, BF16), keep(local_dims, F32),
            keep((heads, HD, HD), F32), keep((rows, HD), F32), keep((rows, HD), F32),
        ],
        aliases={parts + 4: 2},
        flops=small, moved=big,
    )

    inner = [turned_q, turned_agrad]
    outs = []

    def fill_backward(window, tie):
        base = window * share
        ins = kept(
            after(crow, tie), alpha, columns, mask, keys, values, attn, held, agrad, *inner
        )
        aliases = {len(ins) - 2: 0, len(ins) - 1: 1}
        ins += [
            (hbm(gain_row), gain_spec(base)), (gate_input, wide(base)), (out_grad, wide(base)),
            (hbm(probs[window]), probs_spec),
        ]
        aliases.update({len(ins) + i: 2 + i for i in range(len(outs))})
        ins += [(hbm(x), anywhere) for x in outs]
        inner[0], inner[1], *outs[:] = call(
            functools.partial(inner_grad_kernel, chunks, base),
            (share // GROUP,),
            ins,
            [keep(by_head, BF16)] * 2 + [(wide_shape, wide(base))] * 3,
            aliases=aliases, room=12,
            flops=(4 * tile + small) // WINDOWS, moved=7 * big // WINDOWS,
            exps=rows * (CHUNK + HD) * heads // WINDOWS,
        )
        return outs[0]

    entering, outgoing, _ = scan_devices(back, own_pass, passes, fill_backward, True)
    dq, gated, gate_grad = outs

    dk, dv = call(
        functools.partial(outer_grad_kernel, chunks, entering, len(outgoing)),
        grid,
        kept(enter, leave, keys, values, *outgoing, *inner, bloc),
        [(wide_shape, wide())] * 2,
        flops=2 * small, moved=2 * big,
    )
    return (gated, gate_grad, dq, dk, dv)


def solution(mesh):
    in_specs = (
        P("seq", "head"),
        P("seq", "head"),
        P("seq", "head"),
        P("head", "seq"),
        P("seq"),
        P("seq", "head"),
        P("head"),
        P("seq", "head"),
    )
    out_specs = (P("seq", "head"),) * 5
    return jax.shard_map(body, mesh=mesh, in_specs=in_specs, out_specs=out_specs, check_vma=False)
```

```python
import functools

import jax
import jax.numpy as jnp
from jax import lax
from jax.experimental import pallas as pl
from jax.experimental.pallas import tpu as pltpu
from jax.sharding import PartitionSpec as P

HEAD_TOTAL = 64
HD = 128
CHUNK = 256
GROUP = 2
WINDOWS = 4
WIDTH = HEAD_TOTAL * HD

epsilon = 1e-06
LOG2E = 1.4426950408889634

F32 = jnp.float32
BF16 = jnp.bfloat16
MIB = 1024 * 1024
NT = ((1,), (1,))


def dot(a, b, dims=((1,), (0,))):
    return lax.dot_general(a, b, (dims, ((), ())), preferred_element_type=F32)


def chunk_cumsum(x):
    lane = lax.broadcasted_iota(jnp.int32, x.shape, 1) % CHUNK
    shift = 1
    while shift < CHUNK:
        x = x + jnp.where(lane >= shift, pltpu.roll(x, shift, 1), 0.0)
        shift *= 2
    return x


def spans(chunks):
    return [slice(n * CHUNK, (n + 1) * CHUNK) for n in range(chunks)]


def head_span(head, count=1):
    return pl.ds(pl.multiple_of(head * HD, HD), count * HD)


def sigmoid(x):
    return 0.5 * jnp.tanh(0.5 * x) + 0.5


def spread(cols, lane):
    return jnp.broadcast_to(cols[:, lane : lane + 1], cols.shape)


def turned(cols_ref, lane):
    return pltpu.roll(cols_ref[...], (HD - lane) % HD, 1)


def column(row):
    return jnp.broadcast_to(row, (HD, row.shape[1])).T


def state_kernel(
    chunks, steps, lc_ref, doc_ref, k_hbm, v_hbm,
    crow_ref, enter_ref, leave_ref, rrow_ref, k_ref, v_ref, loc_ref, state_ref, pass_ref, sems,
):
    step = pl.program_id(0)

    def copies(at):
        here = head_span(at * GROUP, GROUP)
        return (
            pltpu.make_async_copy(k_hbm.at[:, here], k_ref.at[:, here], sems.at[0, at]),
            pltpu.make_async_copy(v_hbm.at[:, here], v_ref.at[:, here], sems.at[1, at]),
        )

    @pl.when(step == 0)
    def _():
        for at in range(steps):
            for copy in copies(at):
                copy.start()
        c = chunk_cumsum(lc_ref[...] * LOG2E)
        r = chunk_cumsum(jnp.broadcast_to(doc_ref[...].astype(F32), (8, doc_ref.shape[1])))
        crow_ref[...] = c
        rrow_ref[...] = r
        enter_ref[...] = jnp.where(r[0:1] == 0.0, jnp.exp2(c), 0.0)
        for span in spans(chunks):
            cn, rn = c[:, span], r[0:1, span]
            leave_ref[:, span] = jnp.where(rn == rn[:, -1:], jnp.exp2(cn[:, -1:] - cn), 0.0)

    for copy in copies(step):
        copy.wait()
    for g in range(GROUP):
        h = step * GROUP + g
        mine = head_span(h)
        state = None
        total = None
        for n, span in enumerate(spans(chunks)):
            keyed = (k_ref[span, mine].T.astype(F32) * leave_ref[pl.ds(h, 1), span]).astype(BF16)
            local = dot(keyed, v_ref[span, mine])
            loc_ref[h, n] = local
            passing = enter_ref[pl.ds(h, 1), span][:, CHUNK - 1 : CHUNK]
            state = local if state is None else passing * state + local
            total = passing if total is None else passing * total
        state_ref[h] = state
        pass_ref[pl.ds(h, 1), :] = jnp.broadcast_to(total, (1, HD))


def prepare_kernel(rrow_ref, crow_ref, enter_ref, mask_ref, cols_ref):
    sub = lax.broadcasted_iota(jnp.int32, (CHUNK, CHUNK), 0)
    lane = lax.broadcasted_iota(jnp.int32, (CHUNK, CHUNK), 1)
    spare = jnp.zeros((HD - 2 * crow_ref.shape[0], CHUNK), F32)
    for n, span in enumerate(spans(mask_ref.shape[0])):
        r_row = rrow_ref[0:1, span]
        r_col = jnp.concatenate([column(r_row)] * (CHUNK // HD), axis=1)
        mask_ref[n] = jnp.where((r_col == r_row) & (lane <= sub), 0.0, -jnp.inf)
        cols_ref[span, :] = jnp.concatenate([crow_ref[:, span], enter_ref[:, span], spare], axis=0).T


def decayed(scores, c_col, c_row, mask):
    top, low = slice(0, HD), slice(HD, CHUNK)
    row_blocks = []
    for rows, width in ((top, HD), (low, CHUNK)):
        col = c_col[rows]
        col = col if width == HD else jnp.concatenate([col] * (width // HD), axis=1)
        weight = jnp.exp2(col - c_row[:, :width] + mask[rows, :width])
        row_blocks.append((scores[rows, :width] * weight).astype(BF16))
    row_blocks[0] = jnp.concatenate([row_blocks[0], jnp.zeros((HD, CHUNK - HD), BF16)], axis=1)
    return jnp.concatenate(row_blocks, axis=0)


def inside_kernel(
    chunks, first, steps, crow_ref, cols_ref, mask_ref, k_ref, v_ref, gain_ref, q_hbm, gate_ref,
    grad_ref, *refs,
):
    attn_ref, gnorm_ref, q_ref, turned_q_ref, probs_ref, sems = refs[-6:]
    step = pl.program_id(0)

    def copy(at):
        here = head_span(first + at)
        return pltpu.make_async_copy(q_hbm.at[:, here], q_ref.at[:, here], sems.at[at])

    @pl.when(step == 0)
    def _():
        for at in range(steps):
            copy(at).start()

    cols_now = turned(cols_ref, first + step)
    copy(step).wait()
    for g in range(1):
        h = first + step
        cols = slice(g * HD, (g + 1) * HD)
        mine = head_span(h)
        for n, span in enumerate(spans(chunks)):
            q = q_ref[span, mine]
            scores = dot(q, k_ref[span, mine], NT)
            c_row = crow_ref[pl.ds(h, 1), span]
            probs = decayed(scores, spread(cols_now[span], g), c_row, mask_ref.at[n])
            probs_ref[g, n] = probs
            attn_ref[span, mine] = dot(probs, v_ref[span, mine])
            turned_q_ref[h, :, span] = q.T
            sig = sigmoid(gate_ref[span, cols].astype(F32))
            gnorm = grad_ref[span, cols].astype(F32) * sig * gain_ref[0:1, cols]
            gnorm_ref[span, mine] = gnorm.astype(BF16)


def outside_kernel(chunks, entering, inputs, cols_ref, enter_ref, q_ref, gnorm_ref, loc_ref, *refs):
    in_refs = refs[:inputs]
    inside_ref, attn_ref, held_ref, sums_ref, sq_ref, inner_ref = refs[inputs:]
    step = pl.program_id(0)

    @pl.when(step == 0)
    def _():
        sq_ref[...] = jnp.zeros_like(sq_ref)
        inner_ref[...] = jnp.zeros_like(inner_ref)

    heads = [step * GROUP + g for g in range(GROUP)]
    cols_now = turned(cols_ref, enter_ref.shape[0] + step * GROUP)
    carries = [entering(in_refs, h) for h in heads]
    for n, span in enumerate(spans(chunks)):
        squares = sq_ref[span, :]
        inners = inner_ref[span, :]
        for g, h in enumerate(heads):
            mine = head_span(h)
            held = carries[g].astype(BF16)
            held_ref[h, n] = held
            enter = spread(cols_now[span], g)
            attn = inside_ref[span, mine] + enter * dot(q_ref[span, mine], held)
            attn_ref[span, mine] = attn
            squares = squares + attn * attn
            inners = inners + gnorm_ref[span, mine].astype(F32) * attn
            if n + 1 < chunks:
                passing = enter_ref[pl.ds(h, 1), span][:, CHUNK - 1 : CHUNK]
                carries[g] = passing * carries[g] + loc_ref[h, n]
        sq_ref[span, :] = squares
        inner_ref[span, :] = inners

    @pl.when(step == pl.num_programs(0) - 1)
    def _():
        sums_ref[0:1, :] = jnp.sum(sq_ref[...].T, axis=0, keepdims=True)
        sums_ref[1:2, :] = jnp.sum(inner_ref[...].T, axis=0, keepdims=True)


def grad_kernel(chunks, parts, enter_ref, *refs):
    turned_q_ref, gnorm_ref, attn_ref = refs[parts : parts + 3]
    agrad_ref, turned_ref, bloc_ref, back_ref, alpha_ref, beta_ref = refs[parts + 3 :]
    step = pl.program_id(0)

    @pl.when(step == 0)
    def _():
        sums = refs[0][...]
        for ref in refs[1:parts]:
            sums = sums + ref[...]
        inverse = lax.rsqrt(sums[0:1] / WIDTH + epsilon)
        alpha_ref[...] = column(inverse)
        beta_ref[...] = column(inverse * inverse * inverse * sums[1:2] / WIDTH)

    for g in range(GROUP):
        h = step * GROUP + g
        mine = head_span(h)
        back = None
        for n, span in reversed(list(enumerate(spans(chunks)))):
            enter = enter_ref[pl.ds(h, 1), span]
            gnorm = gnorm_ref[span, mine].astype(F32)
            agrad = alpha_ref[span, :] * gnorm - attn_ref[span, mine] * beta_ref[span, :]
            agrad = agrad.astype(BF16)
            agrad_ref[span, mine] = agrad
            turned_ref[h, :, span] = agrad.T
            qkeyed = (turned_q_ref[h, :, span].astype(F32) * enter).astype(BF16)
            local = dot(qkeyed, agrad)
            bloc_ref[h, n] = local
            back = local if back is None else local + enter[:, CHUNK - 1 : CHUNK] * back
        back_ref[h] = back


def inner_grad_kernel(
    chunks, first, crow_ref, alpha_ref, cols_ref, mask_ref, k_ref, v_ref, attn_ref, held_ref,
    agrad_ref, turned_q_ref, turned_agrad_ref, gain_ref, gate_ref, grad_ref, probs_ref, *refs,
):
    dk_ref, dv_ref, dq_ref, gated_ref, ggate_ref = refs[-5:]
    step = pl.program_id(0)
    cols_now = turned(cols_ref, first + step)
    for g in range(1):
        h = first + step
        cols = slice(g * HD, (g + 1) * HD)
        mine = head_span(h)
        for n, span in enumerate(spans(chunks)):
            k, v, agrad = k_ref[span, mine], v_ref[span, mine], agrad_ref[span, mine]
            both = dot(agrad, jnp.concatenate([v, held_ref[h, n]], axis=0), NT)
            c_row = crow_ref[pl.ds(h, 1), span]
            dscore = decayed(both[:, :CHUNK], spread(cols_now[span], g), c_row, mask_ref.at[n])
            enter = spread(cols_now[span], crow_ref.shape[0] + g)
            dq_ref[span, cols] = (dot(dscore, k) + enter * both[:, CHUNK:]).astype(BF16)
            dv_ref[h, :, span] = dot(turned_agrad_ref[h, :, span], probs_ref[g, n]).astype(BF16)
            dk_ref[h, :, span] = dot(turned_q_ref[h, :, span], dscore).astype(BF16)
            normed = attn_ref[span, mine] * alpha_ref[span, :] * gain_ref[0:1, cols]
            sig = sigmoid(gate_ref[span, cols].astype(F32))
            gated = normed * sig
            gated_ref[span, cols] = gated.astype(BF16)
            ggate = grad_ref[span, cols].astype(F32) * gated * (1.0 - sig)
            ggate_ref[span, cols] = ggate.astype(BF16)


def outer_grad_kernel(chunks, entering, inputs, enter_ref, leave_ref, k_ref, v_ref, *refs):
    in_refs = refs[:inputs]
    dkin_ref, dvin_ref, bloc_ref, dk_ref, dv_ref = refs[inputs:]
    step = pl.program_id(0)
    for g in range(GROUP):
        h = step * GROUP + g
        cols = slice(g * HD, (g + 1) * HD)
        mine = head_span(h)
        carry = entering(in_refs, h)
        for n, span in reversed(list(enumerate(spans(chunks)))):
            leave = leave_ref[pl.ds(h, 1), span]
            back = carry.astype(BF16)
            dk = dkin_ref[h, :, span].astype(F32) + leave * dot(back, v_ref[span, mine], NT)
            dv = dvin_ref[h, :, span].astype(F32) + leave * dot(back.T, k_ref[span, mine], NT)
            dk_ref[span, cols] = dk.astype(BF16).T
            dv_ref[span, cols] = dv.astype(BF16).T
            if n > 0:
                passing = enter_ref[pl.ds(h, 1), span][:, CHUNK - 1 : CHUNK]
                carry = bloc_ref[h, n] + passing * carry


def hbm(x):
    return pltpu.with_memory_space_constraint(x, pltpu.HBM)


def kept(*arrays):
    spec = pl.BlockSpec(memory_space=pltpu.VMEM)
    return [(pltpu.with_memory_space_constraint(x, pltpu.VMEM), spec) for x in arrays]


def keep(dims, dtype):
    return pltpu.VMEM(dims, dtype), pl.BlockSpec(memory_space=pltpu.VMEM)


def add_kernel(a_ref, b_ref, out_ref):
    out_ref[...] = a_ref[...] + b_ref[...]


def call(kernel, grid, ins, outs, scratch=(), aliases=None, room=8, flops=0, moved=0, exps=0):
    return pl.pallas_call(
        kernel,
        grid=grid,
        in_specs=[spec for _, spec in ins],
        out_specs=[spec for _, spec in outs],
        out_shape=[shape for shape, _ in outs],
        scratch_shapes=list(scratch),
        input_output_aliases=aliases or {},
        compiler_params=pltpu.CompilerParams(
            dimension_semantics=("arbitrary",) * len(grid), vmem_limit_bytes=room * MIB
        ),
        cost_estimate=pl.CostEstimate(flops=flops, bytes_accessed=moved, transcendentals=exps),
    )(*[x for x, _ in ins])


def after(x, *others):
    return lax.optimization_barrier((x, *others))[0]


def across(x, flips, devices=8):
    return lax.ppermute(x, "seq", [(i, i ^ flips) for i in range(devices)])


def place(reverse):
    index = lax.axis_index("seq")
    index = 7 - index if reverse else index
    return lax.rem(index, 2), lax.rem(lax.div(index, 2), 2), lax.div(index, 4)


def pair_kernel(reverse, state_ref, other_ref, pass_ref, beside_ref, x_ref, y_ref, chip_ref):
    core, _, _ = place(reverse)
    quarter = x_ref.shape[0]
    chip_ref[...] = pass_ref[...] * beside_ref[...]
    for i in range(quarter):
        for at, out_ref in ((i, x_ref), (quarter + i, y_ref)):
            h = core * 2 * quarter + at
            mine, other = state_ref[h], other_ref[h]

            @pl.when(core == 0)
            def _():
                out_ref[i] = beside_ref[pl.ds(h, 1), :] * mine + other

            @pl.when(core == 1)
            def _():
                out_ref[i] = pass_ref[pl.ds(h, 1), :] * other + mine


def row_kernel(
    reverse, to_x_ref, to_y_ref, from_x_ref, from_y_ref, chip_ref, side_ref, far_ref,
    row_ref, sent_ref,
):
    core, x, y = place(reverse)
    quarter = row_ref.shape[0]
    for i in range(quarter):
        h = core * 2 * quarter + i
        hy = h + quarter

        @pl.when(x == 0)
        def _():
            row_ref[i] = side_ref[pl.ds(h, 1), :] * to_x_ref[i] + from_x_ref[i]

        @pl.when(x == 1)
        def _():
            row_ref[i] = chip_ref[pl.ds(h, 1), :] * from_x_ref[i] + to_x_ref[i]

        @pl.when(y == 0)
        def _():
            sent_ref[i] = to_y_ref[i]

        @pl.when((y == 1) & (x == 0))
        def _():
            far = far_ref[pl.ds(hy, 1), :] * from_y_ref[i]
            sent_ref[i] = chip_ref[pl.ds(hy, 1), :] * far + to_y_ref[i]

        @pl.when((y == 1) & (x == 1))
        def _():
            sent_ref[i] = from_y_ref[i]


def ahead_kernel(
    reverse, from_x_ref, from_y_ref, row_ref, sent_ref, side_ref, far_ref, out_ref,
):
    core, x, y = place(reverse)
    quarter = row_ref.shape[0]
    for i in range(quarter):
        h = core * 2 * quarter + i
        hy = h + quarter

        @pl.when((y == 0) & (x == 0))
        def _():
            out_ref[i] = jnp.zeros_like(out_ref[i])
            out_ref[quarter + i] = jnp.zeros_like(out_ref[i])

        @pl.when((y == 0) & (x == 1))
        def _():
            out_ref[i] = from_x_ref[i]
            out_ref[quarter + i] = sent_ref[i]

        @pl.when((y == 1) & (x == 0))
        def _():
            out_ref[i] = row_ref[i]
            out_ref[quarter + i] = far_ref[pl.ds(hy, 1), :] * from_y_ref[i] + sent_ref[i]

        @pl.when((y == 1) & (x == 1))
        def _():
            out_ref[i] = side_ref[pl.ds(h, 1), :] * row_ref[i] + from_x_ref[i]
            out_ref[quarter + i] = side_ref[pl.ds(hy, 1), :] * from_y_ref[i] + sent_ref[i]


def cube_entering(reverse, refs, h):
    ahead_ref, beside_ref, other_ref, beside_pass_ref = refs
    core, _, _ = place(reverse)
    half = ahead_ref.shape[0]
    at = lax.rem(h, half)
    chip = jnp.where(lax.div(h, half) == core, ahead_ref[at], beside_ref[at])
    through = beside_pass_ref[pl.ds(h, 1), :] * chip + other_ref[h]
    return jnp.where(core == 0, chip, through)


def plain_entering(refs, h):
    return refs[0][h]


def cube_scan(state, own_pass, passes, fill, reverse):
    heads = state.shape[0]
    quarter = heads // 4
    part = keep((quarter, HD, HD), F32)

    other = across(state, 1)
    beside_pass = passes[0] if passes else across(own_pass, 1)
    other, beside_pass = lax.optimization_barrier((other, beside_pass, fill(0, state)))[:2]
    to_x, to_y, chip_pass = call(
        functools.partial(pair_kernel, reverse), (),
        kept(state, other, own_pass, beside_pass), [part, part, keep((heads, HD), F32)], room=2,
    )

    from_x, from_y = across(to_x, 2), across(to_y, 4)
    x_pass, far_pass = passes[1:] if passes else (across(chip_pass, 2), across(chip_pass, 6))
    from_x, from_y, x_pass, far_pass = lax.optimization_barrier(
        (from_x, from_y, x_pass, far_pass, fill(1, to_y))
    )[:4]
    row, sent = call(
        functools.partial(row_kernel, reverse), (),
        kept(to_x, to_y, from_x, from_y, chip_pass, x_pass, far_pass), [part, part], room=2,
    )

    row_in, sent_in = across(row, 4), across(sent, 2)
    row_in, sent_in = lax.optimization_barrier((row_in, sent_in, fill(2, sent)))[:2]
    (ahead,) = call(
        functools.partial(ahead_kernel, reverse), (),
        kept(from_x, from_y, row_in, sent_in, x_pass, far_pass),
        [keep((2 * quarter, HD, HD), F32)], room=2,
    )

    beside = across(ahead, 1)
    beside = after(beside, fill(3, ahead))
    entering = functools.partial(cube_entering, reverse)
    return entering, (ahead, beside, other, beside_pass), (beside_pass, x_pass, far_pass)


def doubling_scan(state, own_pass, fill, reverse):
    devices = lax.axis_size("seq")
    index = lax.axis_index("seq")
    passes = lax.all_gather(own_pass, "seq")
    if reverse:
        passes = passes[::-1]
        index = devices - 1 - index
    route = lambda hop: [
        (i, i - hop if reverse else i + hop)
        for i in range(devices)
        if 0 <= (i - hop if reverse else i + hop) < devices
    ]
    for window in range(WINDOWS):
        state = after(state, fill(window, state))
    hop = 1
    while hop < devices:
        factor = lax.dynamic_index_in_dim(passes, index, 0, False)
        state = factor[:, None, :] * lax.ppermute(state, "seq", route(hop)) + state
        before = jnp.concatenate([jnp.zeros_like(passes[:hop]), passes[:-hop]], axis=0)
        passes = passes * before
        hop *= 2
    return lax.ppermute(state, "seq", route(1))


def scan_devices(state, own_pass, passes, fill, reverse):
    if lax.axis_size("seq") == 8 and state.shape[0] % 4 == 0:
        return cube_scan(state, own_pass, passes, fill, reverse)
    return plain_entering, (doubling_scan(state, own_pass, fill, reverse),), None


def body(queries, key_rows, value_rows, log_decay, doc_start, gate_input, norm_gain, out_grad):
    rows, cols = queries.shape
    heads = cols // HD
    chunks = rows // CHUNK
    parts = lax.axis_size("head")
    grid = (heads // GROUP,)
    share = heads // WINDOWS
    big = rows * cols * 2
    tile = 2 * rows * CHUNK * cols
    small = 2 * rows * HD * cols

    whole = lambda *dims: pl.BlockSpec(dims, lambda i: (0,) * len(dims))
    anywhere = pl.BlockSpec(memory_space=pl.ANY)

    def wide(base=0, group=1):
        return pl.BlockSpec((rows, group * HD), lambda i: (0, i + base // group))

    def gain_spec(base=0):
        return pl.BlockSpec((1, HD), lambda i: (0, i + base))

    probs_spec = pl.BlockSpec((1, chunks, CHUNK, CHUNK), lambda i: (i, 0, 0, 0))
    by_head = (heads, HD, rows)
    local_dims = (heads, chunks, HD, HD)
    wide_shape = pltpu.HBM((rows, cols), BF16)
    queries, key_rows, value_rows, gate_input, out_grad = map(
        hbm, (queries, key_rows, value_rows, gate_input, out_grad)
    )
    doc_row = doc_start.reshape(1, rows)
    gain_row = norm_gain.reshape(1, cols)

    by_token = (rows, cols)
    steps = heads // GROUP
    crow, enter, leave, rrow, keys, values, local, state, own_pass = call(
        functools.partial(state_kernel, chunks, steps),
        grid,
        [
            (hbm(log_decay), whole(heads, rows)), (hbm(doc_row), whole(1, rows)),
            (key_rows, anywhere), (value_rows, anywhere),
        ],
        [keep((heads, rows), F32)] * 3
        + [
            keep((8, rows), F32), keep(by_token, BF16), keep(by_token, BF16),
            keep(local_dims, F32), keep((heads, HD, HD), F32), keep((heads, HD), F32),
        ],
        [pltpu.SemaphoreType.DMA((2, steps))],
        flops=small, moved=2 * big,
    )

    ready = []
    made = []
    probs = []

    def fill_forward(window, tie):
        base = window * share
        if not ready:
            ready[:] = call(
                prepare_kernel, (), kept(after(rrow, tie), crow, enter),
                [keep((chunks, CHUNK, CHUNK), F32), keep((rows, HD), F32)],
                flops=8 * rows * CHUNK,
            )
        mask, columns = ready
        ins = kept(after(crow, tie), columns, mask, keys, values) + [
            (hbm(gain_row), gain_spec(base)), (queries, anywhere), (gate_input, wide(base)),
            (out_grad, wide(base)),
        ]
        aliases = {len(ins) + i: i for i in range(len(made))}
        ins += kept(*made)
        *made[:], fresh = call(
            functools.partial(inside_kernel, chunks, base, share),
            (share,),
            ins,
            [
                keep(by_token, F32), keep(by_token, BF16), keep(by_token, BF16),
                keep(by_head, BF16),
                (pltpu.HBM((share, chunks, CHUNK, CHUNK), BF16), probs_spec),
            ],
            [pltpu.SemaphoreType.DMA((share,))],
            aliases=aliases, room=6,
            flops=2 * tile // WINDOWS, moved=5 * big // WINDOWS,
            exps=rows * (CHUNK + HD) * heads // WINDOWS,
        )
        probs.append(fresh)
        return fresh

    entering, incoming, passes = scan_devices(state, own_pass, None, fill_forward, False)
    mask, columns = ready
    inside, gnorm, kept_q, turned_q = made
    tall = pltpu.VMEM((rows, HD), F32)

    attn, held, sums = call(
        functools.partial(outside_kernel, chunks, entering, len(incoming)),
        grid,
        kept(columns, enter, kept_q, gnorm, local, *incoming, inside),
        [keep(by_token, F32), keep(local_dims, BF16), keep((2, rows), F32)],
        [tall, tall],
        {5 + len(incoming): 0},
        flops=small, moved=big,
    )

    apart = 1
    while apart < parts // 2:
        other_sums = lax.ppermute(sums, "head", [(i, i ^ apart) for i in range(parts)])
        (sums,) = call(add_kernel, (), kept(sums, other_sums), [keep((2, rows), F32)], room=2)
        apart *= 2
    other_sums = lax.ppermute(sums, "head", [(i, i ^ apart) for i in range(parts)])

    agrad, turned_agrad, bloc, back, alpha, _ = call(
        functools.partial(grad_kernel, chunks, 2),
        grid,
        kept(enter, sums, other_sums, turned_q, gnorm, attn),
        [
            keep(by_token, BF16), keep(by_head, BF16), keep(local_dims, F32),
            keep((heads, HD, HD), F32), keep((rows, HD), F32), keep((rows, HD), F32),
        ],
        flops=small, moved=big,
    )

    inner = [turned_q, turned_agrad]
    outs = []

    def fill_backward(window, tie):
        base = window * share
        ins = kept(
            after(crow, tie), alpha, columns, mask, keys, values, attn, held, agrad, *inner
        )
        aliases = {len(ins) - 2: 0, len(ins) - 1: 1}
        ins += [
            (hbm(gain_row), gain_spec(base)), (gate_input, wide(base)), (out_grad, wide(base)),
            (hbm(probs[window]), probs_spec),
        ]
        aliases.update({len(ins) + i: 2 + i for i in range(len(outs))})
        ins += [(hbm(x), anywhere) for x in outs]
        inner[0], inner[1], *outs[:] = call(
            functools.partial(inner_grad_kernel, chunks, base),
            (share,),
            ins,
            [keep(by_head, BF16)] * 2 + [(wide_shape, wide(base))] * 3,
            aliases=aliases, room=6,
            flops=(4 * tile + small) // WINDOWS, moved=7 * big // WINDOWS,
            exps=rows * (CHUNK + HD) * heads // WINDOWS,
        )
        return outs[0]

    entering, outgoing, _ = scan_devices(back, own_pass, passes, fill_backward, True)
    dq, gated, gate_grad = outs

    dk, dv = call(
        functools.partial(outer_grad_kernel, chunks, entering, len(outgoing)),
        grid,
        kept(enter, leave, keys, values, *outgoing, *inner, bloc),
        [(wide_shape, wide(0, GROUP))] * 2,
        flops=2 * small, moved=2 * big,
    )
    return (gated, gate_grad, dq, dk, dv)


def solution(mesh):
    in_specs = (
        P("seq", "head"),
        P("seq", "head"),
        P("seq", "head"),
        P("head", "seq"),
        P("seq"),
        P("seq", "head"),
        P("head"),
        P("seq", "head"),
    )
    out_specs = (P("seq", "head"),) * 5
    return jax.shard_map(body, mesh=mesh, in_specs=in_specs, out_specs=out_specs, check_vma=False)
```

```python
import functools

import jax
import jax.numpy as jnp
from jax import lax
from jax.experimental import pallas as pl
from jax.experimental.pallas import tpu as pltpu
from jax.sharding import PartitionSpec as P

HEAD_TOTAL = 64
HD = 128
CHUNK = 256
GROUP = 2
WINDOWS = 4
WIDTH = HEAD_TOTAL * HD

epsilon = 1e-06
LOG2E = 1.4426950408889634

F32 = jnp.float32
BF16 = jnp.bfloat16
MIB = 1024 * 1024
NT = ((1,), (1,))


def dot(a, b, dims=((1,), (0,))):
    return lax.dot_general(a, b, (dims, ((), ())), preferred_element_type=F32)


def chunk_cumsum(x):
    lane = lax.broadcasted_iota(jnp.int32, x.shape, 1) % CHUNK
    shift = 1
    while shift < CHUNK:
        x = x + jnp.where(lane >= shift, pltpu.roll(x, shift, 1), 0.0)
        shift *= 2
    return x


def spans(chunks):
    return [slice(n * CHUNK, (n + 1) * CHUNK) for n in range(chunks)]


def head_span(head, count=1):
    return pl.ds(pl.multiple_of(head * HD, HD), count * HD)


def save(stores):
    for ref, index, value in stores:
        ref[index] = value


def sigmoid(x):
    return 0.5 * jnp.tanh(0.5 * x) + 0.5


def spread(cols, lane):
    return jnp.broadcast_to(cols[:, lane : lane + 1], cols.shape)


def turned(cols_ref, lane):
    return pltpu.roll(cols_ref[...], (HD - lane) % HD, 1)


def column(row):
    return jnp.broadcast_to(row, (HD, row.shape[1])).T


def state_kernel(
    chunks, steps, lc_ref, doc_ref, k_hbm, v_hbm,
    crow_ref, enter_ref, leave_ref, rrow_ref, k_ref, v_ref, loc_ref, state_ref, pass_ref, sems,
):
    step = pl.program_id(0)

    def copies(at):
        here = head_span(at * GROUP, GROUP)
        return (
            pltpu.make_async_copy(k_hbm.at[:, here], k_ref.at[:, here], sems.at[0, at]),
            pltpu.make_async_copy(v_hbm.at[:, here], v_ref.at[:, here], sems.at[1, at]),
        )

    @pl.when(step == 0)
    def _():
        for at in range(steps):
            for copy in copies(at):
                copy.start()
        c = chunk_cumsum(lc_ref[...] * LOG2E)
        r = chunk_cumsum(jnp.broadcast_to(doc_ref[...].astype(F32), (8, doc_ref.shape[1])))
        crow_ref[...] = c
        rrow_ref[...] = r
        enter_ref[...] = jnp.where(r[0:1] == 0.0, jnp.exp2(c), 0.0)
        for span in spans(chunks):
            cn, rn = c[:, span], r[0:1, span]
            leave_ref[:, span] = jnp.where(rn == rn[:, -1:], jnp.exp2(cn[:, -1:] - cn), 0.0)

    for copy in copies(step):
        copy.wait()
    late = []
    for g in range(GROUP):
        h = step * GROUP + g
        mine = head_span(h)
        state = None
        total = None
        for n, span in enumerate(spans(chunks)):
            keyed = (k_ref[span, mine].T.astype(F32) * leave_ref[pl.ds(h, 1), span]).astype(BF16)
            local = dot(keyed, v_ref[span, mine])
            passing = enter_ref[pl.ds(h, 1), span][:, CHUNK - 1 : CHUNK]
            state = local if state is None else passing * state + local
            total = passing if total is None else passing * total
            save(late)
            late = [(loc_ref, (h, n), local)]
        late.append((state_ref, h, state))
        late.append((pass_ref, (pl.ds(h, 1), slice(None)), jnp.broadcast_to(total, (1, HD))))
    save(late)


def prepare_kernel(rrow_ref, crow_ref, enter_ref, mask_ref, cols_ref):
    sub = lax.broadcasted_iota(jnp.int32, (CHUNK, CHUNK), 0)
    lane = lax.broadcasted_iota(jnp.int32, (CHUNK, CHUNK), 1)
    spare = jnp.zeros((HD - 2 * crow_ref.shape[0], CHUNK), F32)
    for n, span in enumerate(spans(mask_ref.shape[0])):
        r_row = rrow_ref[0:1, span]
        r_col = jnp.concatenate([column(r_row)] * (CHUNK // HD), axis=1)
        mask_ref[n] = jnp.where((r_col == r_row) & (lane <= sub), 0.0, -jnp.inf)
        cols_ref[span, :] = jnp.concatenate([crow_ref[:, span], enter_ref[:, span], spare], axis=0).T


def decayed(scores, c_col, c_row, mask):
    top, low = slice(0, HD), slice(HD, CHUNK)
    row_blocks = []
    for rows, width in ((top, HD), (low, CHUNK)):
        col = c_col[rows]
        col = col if width == HD else jnp.concatenate([col] * (width // HD), axis=1)
        weight = jnp.exp2(col - c_row[:, :width] + mask[rows, :width])
        row_blocks.append((scores[rows, :width] * weight).astype(BF16))
    row_blocks[0] = jnp.concatenate([row_blocks[0], jnp.zeros((HD, CHUNK - HD), BF16)], axis=1)
    return jnp.concatenate(row_blocks, axis=0)


def inside_kernel(
    chunks, first, steps, crow_ref, cols_ref, mask_ref, k_ref, v_ref, gain_ref, q_hbm, gate_ref,
    grad_ref, *refs,
):
    attn_ref, gnorm_ref, q_ref, turned_q_ref, probs_ref, sems = refs[-6:]
    step = pl.program_id(0)

    def copy(at):
        here = head_span(first + at)
        return pltpu.make_async_copy(q_hbm.at[:, here], q_ref.at[:, here], sems.at[at])

    @pl.when(step == 0)
    def _():
        for at in range(steps):
            copy(at).start()

    cols_now = turned(cols_ref, first + step)
    copy(step).wait()
    late = []
    for g in range(1):
        h = first + step
        cols = slice(g * HD, (g + 1) * HD)
        mine = head_span(h)
        for n, span in enumerate(spans(chunks)):
            q = q_ref[span, mine]
            scores = dot(q, k_ref[span, mine], NT)
            c_row = crow_ref[pl.ds(h, 1), span]
            probs = decayed(scores, spread(cols_now[span], g), c_row, mask_ref.at[n])
            inside = dot(probs, v_ref[span, mine])
            sig = sigmoid(gate_ref[span, cols].astype(F32))
            gnorm = grad_ref[span, cols].astype(F32) * sig * gain_ref[0:1, cols]
            save(late)
            late = [
                (probs_ref, (g, n), probs),
                (attn_ref, (span, mine), inside),
                (turned_q_ref, (h, slice(None), span), q.T),
                (gnorm_ref, (span, mine), gnorm.astype(BF16)),
            ]
    save(late)


def outside_kernel(chunks, entering, inputs, cols_ref, enter_ref, q_ref, gnorm_ref, loc_ref, *refs):
    in_refs = refs[:inputs]
    inside_ref, attn_ref, held_ref, sums_ref, sq_ref, inner_ref = refs[inputs:]
    step = pl.program_id(0)

    @pl.when(step == 0)
    def _():
        sq_ref[...] = jnp.zeros_like(sq_ref)
        inner_ref[...] = jnp.zeros_like(inner_ref)

    heads = [step * GROUP + g for g in range(GROUP)]
    cols_now = turned(cols_ref, enter_ref.shape[0] + step * GROUP)
    carries = [entering(in_refs, h) for h in heads]
    late = []
    for n, span in enumerate(spans(chunks)):
        squares = sq_ref[span, :]
        inners = inner_ref[span, :]
        for g, h in enumerate(heads):
            mine = head_span(h)
            held = carries[g].astype(BF16)
            enter = spread(cols_now[span], g)
            attn = inside_ref[span, mine] + enter * dot(q_ref[span, mine], held)
            squares = squares + attn * attn
            inners = inners + gnorm_ref[span, mine].astype(F32) * attn
            if n + 1 < chunks:
                passing = enter_ref[pl.ds(h, 1), span][:, CHUNK - 1 : CHUNK]
                carries[g] = passing * carries[g] + loc_ref[h, n]
            save(late)
            late = [(held_ref, (h, n), held), (attn_ref, (span, mine), attn)]
        late += [(sq_ref, (span, slice(None)), squares), (inner_ref, (span, slice(None)), inners)]
    save(late)

    @pl.when(step == pl.num_programs(0) - 1)
    def _():
        sums_ref[0:1, :] = jnp.sum(sq_ref[...].T, axis=0, keepdims=True)
        sums_ref[1:2, :] = jnp.sum(inner_ref[...].T, axis=0, keepdims=True)


def grad_kernel(chunks, parts, enter_ref, *refs):
    turned_q_ref, gnorm_ref, attn_ref = refs[parts : parts + 3]
    agrad_ref, turned_ref, bloc_ref, back_ref, alpha_ref, beta_ref = refs[parts + 3 :]
    step = pl.program_id(0)

    @pl.when(step == 0)
    def _():
        sums = refs[0][...]
        for ref in refs[1:parts]:
            sums = sums + ref[...]
        inverse = lax.rsqrt(sums[0:1] / WIDTH + epsilon)
        alpha_ref[...] = column(inverse)
        beta_ref[...] = column(inverse * inverse * inverse * sums[1:2] / WIDTH)

    late = []
    for g in range(GROUP):
        h = step * GROUP + g
        mine = head_span(h)
        back = None
        for n, span in reversed(list(enumerate(spans(chunks)))):
            enter = enter_ref[pl.ds(h, 1), span]
            gnorm = gnorm_ref[span, mine].astype(F32)
            agrad = alpha_ref[span, :] * gnorm - attn_ref[span, mine] * beta_ref[span, :]
            agrad = agrad.astype(BF16)
            qkeyed = (turned_q_ref[h, :, span].astype(F32) * enter).astype(BF16)
            local = dot(qkeyed, agrad)
            back = local if back is None else local + enter[:, CHUNK - 1 : CHUNK] * back
            save(late)
            late = [
                (agrad_ref, (span, mine), agrad),
                (turned_ref, (h, slice(None), span), agrad.T),
                (bloc_ref, (h, n), local),
            ]
        late.append((back_ref, h, back))
    save(late)


def inner_grad_kernel(
    chunks, first, crow_ref, alpha_ref, cols_ref, mask_ref, k_ref, v_ref, attn_ref, held_ref,
    agrad_ref, turned_q_ref, turned_agrad_ref, gain_ref, gate_ref, grad_ref, probs_ref, *refs,
):
    dk_ref, dv_ref, dq_ref, gated_ref, ggate_ref = refs[-5:]
    step = pl.program_id(0)
    cols_now = turned(cols_ref, first + step)
    late = []
    for g in range(1):
        h = first + step
        cols = slice(g * HD, (g + 1) * HD)
        mine = head_span(h)
        for n, span in enumerate(spans(chunks)):
            k, v, agrad = k_ref[span, mine], v_ref[span, mine], agrad_ref[span, mine]
            both = dot(agrad, jnp.concatenate([v, held_ref[h, n]], axis=0), NT)
            c_row = crow_ref[pl.ds(h, 1), span]
            dscore = decayed(both[:, :CHUNK], spread(cols_now[span], g), c_row, mask_ref.at[n])
            enter = spread(cols_now[span], crow_ref.shape[0] + g)
            dq = dot(dscore, k) + enter * both[:, CHUNK:]
            dv = dot(turned_agrad_ref[h, :, span], probs_ref[g, n])
            dk = dot(turned_q_ref[h, :, span], dscore)
            normed = attn_ref[span, mine] * alpha_ref[span, :] * gain_ref[0:1, cols]
            sig = sigmoid(gate_ref[span, cols].astype(F32))
            gated = normed * sig
            ggate = grad_ref[span, cols].astype(F32) * gated * (1.0 - sig)
            save(late)
            late = [
                (dq_ref, (span, cols), dq.astype(BF16)),
                (dv_ref, (h, slice(None), span), dv.astype(BF16)),
                (dk_ref, (h, slice(None), span), dk.astype(BF16)),
                (gated_ref, (span, cols), gated.astype(BF16)),
                (ggate_ref, (span, cols), ggate.astype(BF16)),
            ]
    save(late)


def outer_grad_kernel(chunks, entering, inputs, enter_ref, leave_ref, k_ref, v_ref, *refs):
    in_refs = refs[:inputs]
    dkin_ref, dvin_ref, bloc_ref, dk_ref, dv_ref = refs[inputs:]
    step = pl.program_id(0)
    late = []
    for g in range(GROUP):
        h = step * GROUP + g
        cols = slice(g * HD, (g + 1) * HD)
        mine = head_span(h)
        carry = entering(in_refs, h)
        for n, span in reversed(list(enumerate(spans(chunks)))):
            leave = leave_ref[pl.ds(h, 1), span]
            back = carry.astype(BF16)
            dk = dkin_ref[h, :, span].astype(F32) + leave * dot(back, v_ref[span, mine], NT)
            dv = dvin_ref[h, :, span].astype(F32) + leave * dot(back.T, k_ref[span, mine], NT)
            if n > 0:
                passing = enter_ref[pl.ds(h, 1), span][:, CHUNK - 1 : CHUNK]
                carry = bloc_ref[h, n] + passing * carry
            save(late)
            late = [
                (dk_ref, (span, cols), dk.astype(BF16).T),
                (dv_ref, (span, cols), dv.astype(BF16).T),
            ]
    save(late)


def hbm(x):
    return pltpu.with_memory_space_constraint(x, pltpu.HBM)


def kept(*arrays):
    spec = pl.BlockSpec(memory_space=pltpu.VMEM)
    return [(pltpu.with_memory_space_constraint(x, pltpu.VMEM), spec) for x in arrays]


def keep(dims, dtype):
    return pltpu.VMEM(dims, dtype), pl.BlockSpec(memory_space=pltpu.VMEM)


def add_kernel(a_ref, b_ref, out_ref):
    out_ref[...] = a_ref[...] + b_ref[...]


def call(kernel, grid, ins, outs, scratch=(), aliases=None, room=8, flops=0, moved=0, exps=0):
    return pl.pallas_call(
        kernel,
        grid=grid,
        in_specs=[spec for _, spec in ins],
        out_specs=[spec for _, spec in outs],
        out_shape=[shape for shape, _ in outs],
        scratch_shapes=list(scratch),
        input_output_aliases=aliases or {},
        compiler_params=pltpu.CompilerParams(
            dimension_semantics=("arbitrary",) * len(grid), vmem_limit_bytes=room * MIB
        ),
        cost_estimate=pl.CostEstimate(flops=flops, bytes_accessed=moved, transcendentals=exps),
    )(*[x for x, _ in ins])


def after(x, *others):
    return lax.optimization_barrier((x, *others))[0]


def across(x, flips, devices=8):
    return lax.ppermute(x, "seq", [(i, i ^ flips) for i in range(devices)])


def place(reverse):
    index = lax.axis_index("seq")
    index = 7 - index if reverse else index
    return lax.rem(index, 2), lax.rem(lax.div(index, 2), 2), lax.div(index, 4)


def pair_kernel(reverse, state_ref, other_ref, pass_ref, beside_ref, x_ref, y_ref, chip_ref):
    core, _, _ = place(reverse)
    quarter = x_ref.shape[0]
    chip_ref[...] = pass_ref[...] * beside_ref[...]
    for i in range(quarter):
        for at, out_ref in ((i, x_ref), (quarter + i, y_ref)):
            h = core * 2 * quarter + at
            mine, other = state_ref[h], other_ref[h]

            @pl.when(core == 0)
            def _():
                out_ref[i] = beside_ref[pl.ds(h, 1), :] * mine + other

            @pl.when(core == 1)
            def _():
                out_ref[i] = pass_ref[pl.ds(h, 1), :] * other + mine


def row_kernel(
    reverse, to_x_ref, to_y_ref, from_x_ref, from_y_ref, chip_ref, side_ref, far_ref,
    row_ref, sent_ref,
):
    core, x, y = place(reverse)
    quarter = row_ref.shape[0]
    for i in range(quarter):
        h = core * 2 * quarter + i
        hy = h + quarter

        @pl.when(x == 0)
        def _():
            row_ref[i] = side_ref[pl.ds(h, 1), :] * to_x_ref[i] + from_x_ref[i]

        @pl.when(x == 1)
        def _():
            row_ref[i] = chip_ref[pl.ds(h, 1), :] * from_x_ref[i] + to_x_ref[i]

        @pl.when(y == 0)
        def _():
            sent_ref[i] = to_y_ref[i]

        @pl.when((y == 1) & (x == 0))
        def _():
            far = far_ref[pl.ds(hy, 1), :] * from_y_ref[i]
            sent_ref[i] = chip_ref[pl.ds(hy, 1), :] * far + to_y_ref[i]

        @pl.when((y == 1) & (x == 1))
        def _():
            sent_ref[i] = from_y_ref[i]


def ahead_kernel(
    reverse, from_x_ref, from_y_ref, row_ref, sent_ref, side_ref, far_ref, out_ref,
):
    core, x, y = place(reverse)
    quarter = row_ref.shape[0]
    for i in range(quarter):
        h = core * 2 * quarter + i
        hy = h + quarter

        @pl.when((y == 0) & (x == 0))
        def _():
            out_ref[i] = jnp.zeros_like(out_ref[i])
            out_ref[quarter + i] = jnp.zeros_like(out_ref[i])

        @pl.when((y == 0) & (x == 1))
        def _():
            out_ref[i] = from_x_ref[i]
            out_ref[quarter + i] = sent_ref[i]

        @pl.when((y == 1) & (x == 0))
        def _():
            out_ref[i] = row_ref[i]
            out_ref[quarter + i] = far_ref[pl.ds(hy, 1), :] * from_y_ref[i] + sent_ref[i]

        @pl.when((y == 1) & (x == 1))
        def _():
            out_ref[i] = side_ref[pl.ds(h, 1), :] * row_ref[i] + from_x_ref[i]
            out_ref[quarter + i] = side_ref[pl.ds(hy, 1), :] * from_y_ref[i] + sent_ref[i]


def cube_entering(reverse, refs, h):
    ahead_ref, beside_ref, other_ref, beside_pass_ref = refs
    core, _, _ = place(reverse)
    half = ahead_ref.shape[0]
    at = lax.rem(h, half)
    chip = jnp.where(lax.div(h, half) == core, ahead_ref[at], beside_ref[at])
    through = beside_pass_ref[pl.ds(h, 1), :] * chip + other_ref[h]
    return jnp.where(core == 0, chip, through)


def plain_entering(refs, h):
    return refs[0][h]


def cube_scan(state, own_pass, passes, fill, reverse):
    heads = state.shape[0]
    quarter = heads // 4
    part = keep((quarter, HD, HD), F32)

    other = across(state, 1)
    beside_pass = passes[0] if passes else across(own_pass, 1)
    other, beside_pass = lax.optimization_barrier((other, beside_pass, fill(0, state)))[:2]
    to_x, to_y, chip_pass = call(
        functools.partial(pair_kernel, reverse), (),
        kept(state, other, own_pass, beside_pass), [part, part, keep((heads, HD), F32)], room=2,
    )

    from_x, from_y = across(to_x, 2), across(to_y, 4)
    x_pass, far_pass = passes[1:] if passes else (across(chip_pass, 2), across(chip_pass, 6))
    from_x, from_y, x_pass, far_pass = lax.optimization_barrier(
        (from_x, from_y, x_pass, far_pass, fill(1, to_y))
    )[:4]
    row, sent = call(
        functools.partial(row_kernel, reverse), (),
        kept(to_x, to_y, from_x, from_y, chip_pass, x_pass, far_pass), [part, part], room=2,
    )

    row_in, sent_in = across(row, 4), across(sent, 2)
    row_in, sent_in = lax.optimization_barrier((row_in, sent_in, fill(2, sent)))[:2]
    (ahead,) = call(
        functools.partial(ahead_kernel, reverse), (),
        kept(from_x, from_y, row_in, sent_in, x_pass, far_pass),
        [keep((2 * quarter, HD, HD), F32)], room=2,
    )

    beside = across(ahead, 1)
    beside = after(beside, fill(3, ahead))
    entering = functools.partial(cube_entering, reverse)
    return entering, (ahead, beside, other, beside_pass), (beside_pass, x_pass, far_pass)


def doubling_scan(state, own_pass, fill, reverse):
    devices = lax.axis_size("seq")
    index = lax.axis_index("seq")
    passes = lax.all_gather(own_pass, "seq")
    if reverse:
        passes = passes[::-1]
        index = devices - 1 - index
    route = lambda hop: [
        (i, i - hop if reverse else i + hop)
        for i in range(devices)
        if 0 <= (i - hop if reverse else i + hop) < devices
    ]
    for window in range(WINDOWS):
        state = after(state, fill(window, state))
    hop = 1
    while hop < devices:
        factor = lax.dynamic_index_in_dim(passes, index, 0, False)
        state = factor[:, None, :] * lax.ppermute(state, "seq", route(hop)) + state
        before = jnp.concatenate([jnp.zeros_like(passes[:hop]), passes[:-hop]], axis=0)
        passes = passes * before
        hop *= 2
    return lax.ppermute(state, "seq", route(1))


def scan_devices(state, own_pass, passes, fill, reverse):
    if lax.axis_size("seq") == 8 and state.shape[0] % 4 == 0:
        return cube_scan(state, own_pass, passes, fill, reverse)
    return plain_entering, (doubling_scan(state, own_pass, fill, reverse),), None


def body(queries, key_rows, value_rows, log_decay, doc_start, gate_input, norm_gain, out_grad):
    rows, cols = queries.shape
    heads = cols // HD
    chunks = rows // CHUNK
    parts = lax.axis_size("head")
    grid = (heads // GROUP,)
    share = heads // WINDOWS
    big = rows * cols * 2
    tile = 2 * rows * CHUNK * cols
    small = 2 * rows * HD * cols

    whole = lambda *dims: pl.BlockSpec(dims, lambda i: (0,) * len(dims))
    anywhere = pl.BlockSpec(memory_space=pl.ANY)

    def wide(base=0, group=1):
        return pl.BlockSpec((rows, group * HD), lambda i: (0, i + base // group))

    def gain_spec(base=0):
        return pl.BlockSpec((1, HD), lambda i: (0, i + base))

    probs_spec = pl.BlockSpec((1, chunks, CHUNK, CHUNK), lambda i: (i, 0, 0, 0))
    by_head = (heads, HD, rows)
    local_dims = (heads, chunks, HD, HD)
    wide_shape = pltpu.HBM((rows, cols), BF16)
    queries, key_rows, value_rows, gate_input, out_grad = map(
        hbm, (queries, key_rows, value_rows, gate_input, out_grad)
    )
    doc_row = doc_start.reshape(1, rows)
    gain_row = norm_gain.reshape(1, cols)

    by_token = (rows, cols)
    steps = heads // GROUP
    crow, enter, leave, rrow, keys, values, local, state, own_pass = call(
        functools.partial(state_kernel, chunks, steps),
        grid,
        [
            (hbm(log_decay), whole(heads, rows)), (hbm(doc_row), whole(1, rows)),
            (key_rows, anywhere), (value_rows, anywhere),
        ],
        [keep((heads, rows), F32)] * 3
        + [
            keep((8, rows), F32), keep(by_token, BF16), keep(by_token, BF16),
            keep(local_dims, F32), keep((heads, HD, HD), F32), keep((heads, HD), F32),
        ],
        [pltpu.SemaphoreType.DMA((2, steps))],
        flops=small, moved=2 * big,
    )

    ready = []
    made = []
    probs = []

    def fill_forward(window, tie):
        base = window * share
        if not ready:
            ready[:] = call(
                prepare_kernel, (), kept(after(rrow, tie), crow, enter),
                [keep((chunks, CHUNK, CHUNK), F32), keep((rows, HD), F32)],
                flops=8 * rows * CHUNK,
            )
        mask, columns = ready
        ins = kept(after(crow, tie), columns, mask, keys, values) + [
            (hbm(gain_row), gain_spec(base)), (queries, anywhere), (gate_input, wide(base)),
            (out_grad, wide(base)),
        ]
        aliases = {len(ins) + i: i for i in range(len(made))}
        ins += kept(*made)
        *made[:], fresh = call(
            functools.partial(inside_kernel, chunks, base, share),
            (share,),
            ins,
            [
                keep(by_token, F32), keep(by_token, BF16), keep(by_token, BF16),
                keep(by_head, BF16),
                (pltpu.HBM((share, chunks, CHUNK, CHUNK), BF16), probs_spec),
            ],
            [pltpu.SemaphoreType.DMA((share,))],
            aliases=aliases, room=6,
            flops=2 * tile // WINDOWS, moved=5 * big // WINDOWS,
            exps=rows * (CHUNK + HD) * heads // WINDOWS,
        )
        probs.append(fresh)
        return fresh

    entering, incoming, passes = scan_devices(state, own_pass, None, fill_forward, False)
    mask, columns = ready
    inside, gnorm, kept_q, turned_q = made
    tall = pltpu.VMEM((rows, HD), F32)

    attn, held, sums = call(
        functools.partial(outside_kernel, chunks, entering, len(incoming)),
        grid,
        kept(columns, enter, kept_q, gnorm, local, *incoming, inside),
        [keep(by_token, F32), keep(local_dims, BF16), keep((2, rows), F32)],
        [tall, tall],
        {5 + len(incoming): 0},
        flops=small, moved=big,
    )

    apart = 1
    while apart < parts // 2:
        other_sums = lax.ppermute(sums, "head", [(i, i ^ apart) for i in range(parts)])
        (sums,) = call(add_kernel, (), kept(sums, other_sums), [keep((2, rows), F32)], room=2)
        apart *= 2
    other_sums = lax.ppermute(sums, "head", [(i, i ^ apart) for i in range(parts)])

    agrad, turned_agrad, bloc, back, alpha, _ = call(
        functools.partial(grad_kernel, chunks, 2),
        grid,
        kept(enter, sums, other_sums, turned_q, gnorm, attn),
        [
            keep(by_token, BF16), keep(by_head, BF16), keep(local_dims, F32),
            keep((heads, HD, HD), F32), keep((rows, HD), F32), keep((rows, HD), F32),
        ],
        flops=small, moved=big,
    )

    inner = [turned_q, turned_agrad]
    outs = []

    def fill_backward(window, tie):
        base = window * share
        ins = kept(
            after(crow, tie), alpha, columns, mask, keys, values, attn, held, agrad, *inner
        )
        aliases = {len(ins) - 2: 0, len(ins) - 1: 1}
        ins += [
            (hbm(gain_row), gain_spec(base)), (gate_input, wide(base)), (out_grad, wide(base)),
            (hbm(probs[window]), probs_spec),
        ]
        aliases.update({len(ins) + i: 2 + i for i in range(len(outs))})
        ins += [(hbm(x), anywhere) for x in outs]
        inner[0], inner[1], *outs[:] = call(
            functools.partial(inner_grad_kernel, chunks, base),
            (share,),
            ins,
            [keep(by_head, BF16)] * 2 + [(wide_shape, wide(base))] * 3,
            aliases=aliases, room=6,
            flops=(4 * tile + small) // WINDOWS, moved=7 * big // WINDOWS,
            exps=rows * (CHUNK + HD) * heads // WINDOWS,
        )
        return outs[0]

    entering, outgoing, _ = scan_devices(back, own_pass, passes, fill_backward, True)
    dq, gated, gate_grad = outs

    dk, dv = call(
        functools.partial(outer_grad_kernel, chunks, entering, len(outgoing)),
        grid,
        kept(enter, leave, keys, values, *outgoing, *inner, bloc),
        [(wide_shape, wide(0, GROUP))] * 2,
        flops=2 * small, moved=2 * big,
    )
    return (gated, gate_grad, dq, dk, dv)


def solution(mesh):
    in_specs = (
        P("seq", "head"),
        P("seq", "head"),
        P("seq", "head"),
        P("head", "seq"),
        P("seq"),
        P("seq", "head"),
        P("head"),
        P("seq", "head"),
    )
    out_specs = (P("seq", "head"),) * 5
    return jax.shard_map(body, mesh=mesh, in_specs=in_specs, out_specs=out_specs, check_vma=False)
```

```python
import functools

import jax
import jax.numpy as jnp
from jax import lax
from jax.experimental import pallas as pl
from jax.experimental.pallas import tpu as pltpu
from jax.sharding import PartitionSpec as P

HEAD_TOTAL = 64
HD = 128
CHUNK = 256
GROUP = 2
RING = 1
WINDOWS = 4
ROOM = 4
WIDTH = HEAD_TOTAL * HD

epsilon = 1e-06
LOG2E = 1.4426950408889634

F32 = jnp.float32
BF16 = jnp.bfloat16
MIB = 1024 * 1024
NT = ((1,), (1,))


def dot(a, b, dims=((1,), (0,))):
    return lax.dot_general(a, b, (dims, ((), ())), preferred_element_type=F32)


def chunk_cumsum(x):
    lane = lax.broadcasted_iota(jnp.int32, x.shape, 1) % CHUNK
    shift = 1
    while shift < CHUNK:
        x = x + jnp.where(lane >= shift, pltpu.roll(x, shift, 1), 0.0)
        shift *= 2
    return x


def spans(chunks):
    return [slice(n * CHUNK, (n + 1) * CHUNK) for n in range(chunks)]


def head_span(head, count=1):
    return pl.ds(pl.multiple_of(head * HD, HD), count * HD)


def save(stores):
    for ref, index, value in stores:
        ref[index] = value


def sigmoid(x):
    return 0.5 * jnp.tanh(0.5 * x) + 0.5


def spread(cols, lane):
    return jnp.broadcast_to(cols[:, lane : lane + 1], cols.shape)


def turned(cols_ref, lane):
    return pltpu.roll(cols_ref[...], (HD - lane) % HD, 1)


def column(row):
    return jnp.broadcast_to(row, (HD, row.shape[1])).T


def start(copies):
    for copy in copies:
        copy.start()


def wait(copies):
    for copy in copies:
        copy.wait()


def group_of(at):
    return head_span(at * RING, RING)


def fetch_gates(at, gate_hbm, grad_hbm, gate_ring, grad_ring, sems):
    slot = at % 2
    return [
        pltpu.make_async_copy(gate_hbm.at[:, group_of(at)], gate_ring.at[slot], sems.at[0]),
        pltpu.make_async_copy(grad_hbm.at[:, group_of(at)], grad_ring.at[slot], sems.at[1]),
    ]


def fetch_q(at, q_hbm, q_ref, sem):
    return [pltpu.make_async_copy(q_hbm.at[:, group_of(at)], q_ref.at[:, group_of(at)], sem)]


def fetch_probs(at, probs_hbm, probs_ring, sem):
    heads = pl.ds(at * RING, RING)
    return [pltpu.make_async_copy(probs_hbm.at[heads], probs_ring.at[at % 2], sem)]


def put_probs(at, probs_ring, probs_hbm, sem):
    heads = pl.ds(at * RING, RING)
    return [pltpu.make_async_copy(probs_ring.at[at % 2], probs_hbm.at[heads], sem)]


def put_outs(at, out_ring, outs_hbm, sems):
    return [
        pltpu.make_async_copy(out_ring.at[at % 2, i], out.at[:, group_of(at)], sems.at[i])
        for i, out in enumerate(outs_hbm)
    ]


def state_kernel(
    chunks, steps, lc_hbm, doc_hbm, gain_hbm, k_hbm, v_hbm, q_hbm, gate_hbm, grad_hbm,
    crow_ref, enter_ref, leave_ref, rrow_ref, k_ref, v_ref, loc_ref, state_ref, pass_ref,
    gain_ref, q_ref, gate_ring, grad_ring, lc_ref, doc_ref, sems, small_sems, next_sems,
):
    step = pl.program_id(0)
    small = [
        pltpu.make_async_copy(lc_hbm, lc_ref, small_sems.at[0]),
        pltpu.make_async_copy(doc_hbm, doc_ref, small_sems.at[1]),
        pltpu.make_async_copy(gain_hbm, gain_ref, small_sems.at[2]),
    ]
    following = fetch_gates(0, gate_hbm, grad_hbm, gate_ring, grad_ring, next_sems)
    following += fetch_q(0, q_hbm, q_ref, next_sems.at[2])

    def copies(at):
        here = head_span(at * GROUP, GROUP)
        return (
            pltpu.make_async_copy(k_hbm.at[:, here], k_ref.at[:, here], sems.at[0, at]),
            pltpu.make_async_copy(v_hbm.at[:, here], v_ref.at[:, here], sems.at[1, at]),
        )

    @pl.when(step == 0)
    def _():
        start(small)
        for at in range(steps):
            start(copies(at))
        start(following)
        wait(small)
        c = chunk_cumsum(lc_ref[...] * LOG2E)
        r = chunk_cumsum(jnp.broadcast_to(doc_ref[...].astype(F32), (8, doc_ref.shape[1])))
        crow_ref[...] = c
        rrow_ref[...] = r
        enter_ref[...] = jnp.where(r[0:1] == 0.0, jnp.exp2(c), 0.0)
        for span in spans(chunks):
            cn, rn = c[:, span], r[0:1, span]
            leave_ref[:, span] = jnp.where(rn == rn[:, -1:], jnp.exp2(cn[:, -1:] - cn), 0.0)

    wait(copies(step))
    late = []
    for g in range(GROUP):
        h = step * GROUP + g
        mine = head_span(h)
        state = None
        total = None
        for n, span in enumerate(spans(chunks)):
            keyed = (k_ref[span, mine].T.astype(F32) * leave_ref[pl.ds(h, 1), span]).astype(BF16)
            local = dot(keyed, v_ref[span, mine])
            passing = enter_ref[pl.ds(h, 1), span][:, CHUNK - 1 : CHUNK]
            state = local if state is None else passing * state + local
            total = passing if total is None else passing * total
            save(late)
            late = [(loc_ref, (h, n), local)]
        late.append((state_ref, h, state))
        late.append((pass_ref, (pl.ds(h, 1), slice(None)), jnp.broadcast_to(total, (1, HD))))
    save(late)

    @pl.when(step == steps - 1)
    def _():
        wait(following)


def prepare_kernel(rrow_ref, crow_ref, enter_ref, mask_ref, cols_ref):
    sub = lax.broadcasted_iota(jnp.int32, (CHUNK, CHUNK), 0)
    lane = lax.broadcasted_iota(jnp.int32, (CHUNK, CHUNK), 1)
    spare = jnp.zeros((HD - 2 * crow_ref.shape[0], CHUNK), F32)
    for n, span in enumerate(spans(mask_ref.shape[0])):
        r_row = rrow_ref[0:1, span]
        r_col = jnp.concatenate([column(r_row)] * (CHUNK // HD), axis=1)
        mask_ref[n] = jnp.where((r_col == r_row) & (lane <= sub), 0.0, -jnp.inf)
        cols_ref[span, :] = jnp.concatenate([crow_ref[:, span], enter_ref[:, span], spare], axis=0).T


def decayed(scores, c_col, c_row, mask):
    top, low = slice(0, HD), slice(HD, CHUNK)
    row_blocks = []
    for rows, width in ((top, HD), (low, CHUNK)):
        col = c_col[rows]
        col = col if width == HD else jnp.concatenate([col] * (width // HD), axis=1)
        weight = jnp.exp2(col - c_row[:, :width] + mask[rows, :width])
        row_blocks.append((scores[rows, :width] * weight).astype(BF16))
    row_blocks[0] = jnp.concatenate([row_blocks[0], jnp.zeros((HD, CHUNK - HD), BF16)], axis=1)
    return jnp.concatenate(row_blocks, axis=0)


def inside_kernel(
    chunks, first, steps, crow_ref, cols_ref, mask_ref, k_ref, v_ref, gain_ref, q_hbm, gate_hbm,
    grad_hbm, *refs,
):
    q_ref, gate_ring, grad_ring, attn_ref, gnorm_ref, turned_q_ref, probs_ring, probs_hbm, sems = (
        refs[-9:]
    )
    step = first + pl.program_id(0)
    slot = step % 2
    fetches = fetch_gates(step + 1, gate_hbm, grad_hbm, gate_ring, grad_ring, sems)
    fetches += fetch_q(step + 1, q_hbm, q_ref, sems.at[2])
    puts = put_probs(step - 1, probs_ring, probs_hbm, sems.at[3])
    pl.when(step + 1 < steps)(lambda: start(fetches))
    pl.when(step > 0)(lambda: start(puts))

    cols_now = turned(cols_ref, step * RING)
    late = []
    for g in range(RING):
        h = step * RING + g
        cols = slice(g * HD, (g + 1) * HD)
        mine = head_span(h)
        for n, span in enumerate(spans(chunks)):
            q = q_ref[span, mine]
            scores = dot(q, k_ref[span, mine], NT)
            c_row = crow_ref[pl.ds(h, 1), span]
            probs = decayed(scores, spread(cols_now[span], g), c_row, mask_ref.at[n])
            inside = dot(probs, v_ref[span, mine])
            sig = sigmoid(gate_ring[slot, span, cols].astype(F32))
            gnorm = grad_ring[slot, span, cols].astype(F32) * sig * gain_ref[0:1, mine]
            save(late)
            late = [
                (probs_ring, (slot, g, n), probs),
                (attn_ref, (span, mine), inside),
                (turned_q_ref, (h, slice(None), span), q.T),
                (gnorm_ref, (span, mine), gnorm.astype(BF16)),
            ]
    save(late)
    pl.when(step + 1 < steps)(lambda: wait(fetches))
    pl.when(step > 0)(lambda: wait(puts))


def outside_kernel(chunks, last, entering, inputs, cols_ref, enter_ref, q_ref, gnorm_ref, loc_ref, *refs):
    in_refs = refs[:inputs]
    probs_ring, inside_ref, _, attn_ref, probs_hbm, held_ref, sums_ref, sq_ref, inner_ref, sem = (
        refs[inputs:]
    )
    step = pl.program_id(0)
    steps = pl.num_programs(0)
    puts = put_probs(last, probs_ring, probs_hbm, sem.at[0])

    @pl.when(step == 0)
    def _():
        start(puts)
        sq_ref[...] = jnp.zeros_like(sq_ref)
        inner_ref[...] = jnp.zeros_like(inner_ref)

    heads = [step * GROUP + g for g in range(GROUP)]
    cols_now = turned(cols_ref, enter_ref.shape[0] + step * GROUP)
    carries = [entering(in_refs, h) for h in heads]
    late = []
    for n, span in enumerate(spans(chunks)):
        squares = sq_ref[span, :]
        inners = inner_ref[span, :]
        for g, h in enumerate(heads):
            mine = head_span(h)
            held = carries[g].astype(BF16)
            enter = spread(cols_now[span], g)
            attn = inside_ref[span, mine] + enter * dot(q_ref[span, mine], held)
            squares = squares + attn * attn
            inners = inners + gnorm_ref[span, mine].astype(F32) * attn
            if n + 1 < chunks:
                passing = enter_ref[pl.ds(h, 1), span][:, CHUNK - 1 : CHUNK]
                carries[g] = passing * carries[g] + loc_ref[h, n]
            save(late)
            late = [(held_ref, (h, n), held), (attn_ref, (span, mine), attn)]
        late += [(sq_ref, (span, slice(None)), squares), (inner_ref, (span, slice(None)), inners)]
    save(late)

    @pl.when(step == steps - 1)
    def _():
        wait(puts)
        sums_ref[0:1, :] = jnp.sum(sq_ref[...].T, axis=0, keepdims=True)
        sums_ref[1:2, :] = jnp.sum(inner_ref[...].T, axis=0, keepdims=True)


def grad_kernel(chunks, parts, enter_ref, *refs):
    turned_q_ref, gnorm_ref, attn_ref, gate_hbm, grad_hbm, probs_hbm = refs[parts : parts + 6]
    agrad_ref, turned_ref, bloc_ref, back_ref, alpha_ref = refs[parts + 6 : parts + 11]
    gate_ring, grad_ring, probs_ring, beta_ref, sems = refs[parts + 11 :]
    step = pl.program_id(0)
    following = fetch_gates(0, gate_hbm, grad_hbm, gate_ring, grad_ring, sems)
    following += fetch_probs(0, probs_hbm, probs_ring, sems.at[2])

    @pl.when(step == 0)
    def _():
        start(following)
        sums = refs[0][...]
        for ref in refs[1:parts]:
            sums = sums + ref[...]
        inverse = lax.rsqrt(sums[0:1] / WIDTH + epsilon)
        alpha_ref[...] = column(inverse)
        beta_ref[...] = column(inverse * inverse * inverse * sums[1:2] / WIDTH)

    late = []
    for g in range(GROUP):
        h = step * GROUP + g
        mine = head_span(h)
        back = None
        for n, span in reversed(list(enumerate(spans(chunks)))):
            enter = enter_ref[pl.ds(h, 1), span]
            gnorm = gnorm_ref[span, mine].astype(F32)
            agrad = alpha_ref[span, :] * gnorm - attn_ref[span, mine] * beta_ref[span, :]
            agrad = agrad.astype(BF16)
            qkeyed = (turned_q_ref[h, :, span].astype(F32) * enter).astype(BF16)
            local = dot(qkeyed, agrad)
            back = local if back is None else local + enter[:, CHUNK - 1 : CHUNK] * back
            save(late)
            late = [
                (agrad_ref, (span, mine), agrad),
                (turned_ref, (h, slice(None), span), agrad.T),
                (bloc_ref, (h, n), local),
            ]
        late.append((back_ref, h, back))
    save(late)

    @pl.when(step == pl.num_programs(0) - 1)
    def _():
        wait(following)


def inner_grad_kernel(
    chunks, first, steps, crow_ref, alpha_ref, cols_ref, mask_ref, k_ref, v_ref, attn_ref,
    held_ref, agrad_ref, turned_q_ref, turned_agrad_ref, gain_ref, gate_hbm, grad_hbm, probs_hbm,
    *refs,
):
    dk_ref, dv_ref, gate_ring, grad_ring, probs_ring, out_ring, *outs_hbm, sems = refs[-10:]
    step = first + pl.program_id(0)
    slot = step % 2
    fetches = fetch_gates(step + 1, gate_hbm, grad_hbm, gate_ring, grad_ring, sems)
    fetches += fetch_probs(step + 1, probs_hbm, probs_ring, sems.at[2])
    puts = put_outs(step - 1, out_ring, outs_hbm, sems.at[pl.ds(3, 3)])
    pl.when(step + 1 < steps)(lambda: start(fetches))
    pl.when(step > 0)(lambda: start(puts))

    cols_now = turned(cols_ref, step * RING)
    late = []
    for g in range(RING):
        h = step * RING + g
        cols = slice(g * HD, (g + 1) * HD)
        mine = head_span(h)
        for n, span in enumerate(spans(chunks)):
            k, v, agrad = k_ref[span, mine], v_ref[span, mine], agrad_ref[span, mine]
            both = dot(agrad, jnp.concatenate([v, held_ref[h, n]], axis=0), NT)
            c_row = crow_ref[pl.ds(h, 1), span]
            dscore = decayed(both[:, :CHUNK], spread(cols_now[span], g), c_row, mask_ref.at[n])
            enter = spread(cols_now[span], crow_ref.shape[0] + g)
            dq = dot(dscore, k) + enter * both[:, CHUNK:]
            dv = dot(turned_agrad_ref[h, :, span], probs_ring[slot, g, n])
            dk = dot(turned_q_ref[h, :, span], dscore)
            normed = attn_ref[span, mine] * alpha_ref[span, :] * gain_ref[0:1, mine]
            sig = sigmoid(gate_ring[slot, span, cols].astype(F32))
            gated = normed * sig
            ggate = grad_ring[slot, span, cols].astype(F32) * gated * (1.0 - sig)
            save(late)
            late = [
                (out_ring, (slot, 0, span, cols), dq.astype(BF16)),
                (dv_ref, (h, slice(None), span), dv.astype(BF16)),
                (dk_ref, (h, slice(None), span), dk.astype(BF16)),
                (out_ring, (slot, 1, span, cols), gated.astype(BF16)),
                (out_ring, (slot, 2, span, cols), ggate.astype(BF16)),
            ]
    save(late)
    pl.when(step + 1 < steps)(lambda: wait(fetches))
    pl.when(step > 0)(lambda: wait(puts))


def outer_grad_kernel(chunks, last, entering, inputs, enter_ref, leave_ref, k_ref, v_ref, *refs):
    in_refs = refs[:inputs]
    dkin_ref, dvin_ref, bloc_ref, out_ring = refs[inputs : inputs + 4]
    dk_ref, dv_ref, *outs_hbm, sems = refs[inputs + 7 :]
    step = pl.program_id(0)
    steps = pl.num_programs(0)
    puts = put_outs(last, out_ring, outs_hbm, sems)
    pl.when(step == 0)(lambda: start(puts))
    late = []
    for g in range(GROUP):
        h = step * GROUP + g
        cols = slice(g * HD, (g + 1) * HD)
        mine = head_span(h)
        carry = entering(in_refs, h)
        for n, span in reversed(list(enumerate(spans(chunks)))):
            leave = leave_ref[pl.ds(h, 1), span]
            back = carry.astype(BF16)
            dk = dkin_ref[h, :, span].astype(F32) + leave * dot(back, v_ref[span, mine], NT)
            dv = dvin_ref[h, :, span].astype(F32) + leave * dot(back.T, k_ref[span, mine], NT)
            if n > 0:
                passing = enter_ref[pl.ds(h, 1), span][:, CHUNK - 1 : CHUNK]
                carry = bloc_ref[h, n] + passing * carry
            save(late)
            late = [
                (dk_ref, (span, cols), dk.astype(BF16).T),
                (dv_ref, (span, cols), dv.astype(BF16).T),
            ]
    save(late)
    pl.when(step == steps - 1)(lambda: wait(puts))


def hbm(x):
    return pltpu.with_memory_space_constraint(x, pltpu.HBM)


def kept(*arrays):
    spec = pl.BlockSpec(memory_space=pltpu.VMEM)
    return [(pltpu.with_memory_space_constraint(x, pltpu.VMEM), spec) for x in arrays]


def keep(dims, dtype):
    return pltpu.VMEM(dims, dtype), pl.BlockSpec(memory_space=pltpu.VMEM)


def add_kernel(a_ref, b_ref, out_ref):
    out_ref[...] = a_ref[...] + b_ref[...]


def call(kernel, grid, ins, outs, scratch=(), aliases=None, room=4, flops=0, moved=0, exps=0):
    return pl.pallas_call(
        kernel,
        grid=grid,
        in_specs=[spec for _, spec in ins],
        out_specs=[spec for _, spec in outs],
        out_shape=[shape for shape, _ in outs],
        scratch_shapes=list(scratch),
        input_output_aliases=aliases or {},
        compiler_params=pltpu.CompilerParams(
            dimension_semantics=("arbitrary",) * len(grid), vmem_limit_bytes=room * MIB
        ),
        cost_estimate=pl.CostEstimate(flops=flops, bytes_accessed=moved, transcendentals=exps),
    )(*[x for x, _ in ins])


def after(x, *others):
    return lax.optimization_barrier((x, *others))[0]


def across(x, flips, devices=8):
    return lax.ppermute(x, "seq", [(i, i ^ flips) for i in range(devices)])


def place(reverse):
    index = lax.axis_index("seq")
    index = 7 - index if reverse else index
    return lax.rem(index, 2), lax.rem(lax.div(index, 2), 2), lax.div(index, 4)


def pair_kernel(reverse, state_ref, other_ref, pass_ref, beside_ref, x_ref, y_ref, chip_ref):
    core, _, _ = place(reverse)
    quarter = x_ref.shape[0]
    chip_ref[...] = pass_ref[...] * beside_ref[...]
    for i in range(quarter):
        for at, out_ref in ((i, x_ref), (quarter + i, y_ref)):
            h = core * 2 * quarter + at
            mine, other = state_ref[h], other_ref[h]

            @pl.when(core == 0)
            def _():
                out_ref[i] = beside_ref[pl.ds(h, 1), :] * mine + other

            @pl.when(core == 1)
            def _():
                out_ref[i] = pass_ref[pl.ds(h, 1), :] * other + mine


def row_kernel(
    reverse, to_x_ref, to_y_ref, from_x_ref, from_y_ref, chip_ref, side_ref, far_ref,
    row_ref, sent_ref,
):
    core, x, y = place(reverse)
    quarter = row_ref.shape[0]
    for i in range(quarter):
        h = core * 2 * quarter + i
        hy = h + quarter

        @pl.when(x == 0)
        def _():
            row_ref[i] = side_ref[pl.ds(h, 1), :] * to_x_ref[i] + from_x_ref[i]

        @pl.when(x == 1)
        def _():
            row_ref[i] = chip_ref[pl.ds(h, 1), :] * from_x_ref[i] + to_x_ref[i]

        @pl.when(y == 0)
        def _():
            sent_ref[i] = to_y_ref[i]

        @pl.when((y == 1) & (x == 0))
        def _():
            far = far_ref[pl.ds(hy, 1), :] * from_y_ref[i]
            sent_ref[i] = chip_ref[pl.ds(hy, 1), :] * far + to_y_ref[i]

        @pl.when((y == 1) & (x == 1))
        def _():
            sent_ref[i] = from_y_ref[i]


def ahead_kernel(
    reverse, from_x_ref, from_y_ref, row_ref, sent_ref, side_ref, far_ref, out_ref,
):
    core, x, y = place(reverse)
    quarter = row_ref.shape[0]
    for i in range(quarter):
        h = core * 2 * quarter + i
        hy = h + quarter

        @pl.when((y == 0) & (x == 0))
        def _():
            out_ref[i] = jnp.zeros_like(out_ref[i])
            out_ref[quarter + i] = jnp.zeros_like(out_ref[i])

        @pl.when((y == 0) & (x == 1))
        def _():
            out_ref[i] = from_x_ref[i]
            out_ref[quarter + i] = sent_ref[i]

        @pl.when((y == 1) & (x == 0))
        def _():
            out_ref[i] = row_ref[i]
            out_ref[quarter + i] = far_ref[pl.ds(hy, 1), :] * from_y_ref[i] + sent_ref[i]

        @pl.when((y == 1) & (x == 1))
        def _():
            out_ref[i] = side_ref[pl.ds(h, 1), :] * row_ref[i] + from_x_ref[i]
            out_ref[quarter + i] = side_ref[pl.ds(hy, 1), :] * from_y_ref[i] + sent_ref[i]


def cube_entering(reverse, refs, h):
    ahead_ref, beside_ref, other_ref, beside_pass_ref = refs
    core, _, _ = place(reverse)
    half = ahead_ref.shape[0]
    at = lax.rem(h, half)
    chip = jnp.where(lax.div(h, half) == core, ahead_ref[at], beside_ref[at])
    through = beside_pass_ref[pl.ds(h, 1), :] * chip + other_ref[h]
    return jnp.where(core == 0, chip, through)


def plain_entering(refs, h):
    return refs[0][h]


def cube_scan(state, own_pass, passes, fill, reverse):
    heads = state.shape[0]
    quarter = heads // 4
    part = keep((quarter, HD, HD), F32)

    other = across(state, 1)
    beside_pass = passes[0] if passes else across(own_pass, 1)
    other, beside_pass = lax.optimization_barrier((other, beside_pass, fill(0, state)))[:2]
    to_x, to_y, chip_pass = call(
        functools.partial(pair_kernel, reverse), (),
        kept(state, other, own_pass, beside_pass), [part, part, keep((heads, HD), F32)], room=ROOM,
    )

    from_x, from_y = across(to_x, 2), across(to_y, 4)
    x_pass, far_pass = passes[1:] if passes else (across(chip_pass, 2), across(chip_pass, 6))
    from_x, from_y, x_pass, far_pass = lax.optimization_barrier(
        (from_x, from_y, x_pass, far_pass, fill(1, to_y))
    )[:4]
    row, sent = call(
        functools.partial(row_kernel, reverse), (),
        kept(to_x, to_y, from_x, from_y, chip_pass, x_pass, far_pass), [part, part], room=ROOM,
    )

    row_in, sent_in = across(row, 4), across(sent, 2)
    row_in, sent_in = lax.optimization_barrier((row_in, sent_in, fill(2, sent)))[:2]
    (ahead,) = call(
        functools.partial(ahead_kernel, reverse), (),
        kept(from_x, from_y, row_in, sent_in, x_pass, far_pass),
        [keep((2 * quarter, HD, HD), F32)], room=ROOM,
    )

    beside = across(ahead, 1)
    beside = after(beside, fill(3, ahead))
    entering = functools.partial(cube_entering, reverse)
    return entering, (ahead, beside, other, beside_pass), (beside_pass, x_pass, far_pass)


def doubling_scan(state, own_pass, fill, reverse):
    devices = lax.axis_size("seq")
    index = lax.axis_index("seq")
    passes = lax.all_gather(own_pass, "seq")
    if reverse:
        passes = passes[::-1]
        index = devices - 1 - index
    route = lambda hop: [
        (i, i - hop if reverse else i + hop)
        for i in range(devices)
        if 0 <= (i - hop if reverse else i + hop) < devices
    ]
    for window in range(WINDOWS):
        state = after(state, fill(window, state))
    hop = 1
    while hop < devices:
        factor = lax.dynamic_index_in_dim(passes, index, 0, False)
        state = factor[:, None, :] * lax.ppermute(state, "seq", route(hop)) + state
        before = jnp.concatenate([jnp.zeros_like(passes[:hop]), passes[:-hop]], axis=0)
        passes = passes * before
        hop *= 2
    return lax.ppermute(state, "seq", route(1))


def scan_devices(state, own_pass, passes, fill, reverse):
    if lax.axis_size("seq") == 8 and state.shape[0] % 4 == 0:
        return cube_scan(state, own_pass, passes, fill, reverse)
    return plain_entering, (doubling_scan(state, own_pass, fill, reverse),), None


def body(queries, key_rows, value_rows, log_decay, doc_start, gate_input, norm_gain, out_grad):
    rows, cols = queries.shape
    heads = cols // HD
    chunks = rows // CHUNK
    parts = lax.axis_size("head")
    grid = (heads // GROUP,)
    share = heads // WINDOWS
    big = rows * cols * 2
    tile = 2 * rows * CHUNK * cols
    small = 2 * rows * HD * cols

    whole = lambda *dims: pl.BlockSpec(dims, lambda i: (0,) * len(dims))
    anywhere = pl.BlockSpec(memory_space=pl.ANY)

    by_head = (heads, HD, rows)
    local_dims = (heads, chunks, HD, HD)
    wide_out = (pltpu.HBM((rows, cols), BF16), anywhere)
    probs_out = (pltpu.HBM((heads, chunks, CHUNK, CHUNK), BF16), anywhere)
    ring = keep((2, rows, RING * HD), BF16)
    probs_ring = keep((2, RING, chunks, CHUNK, CHUNK), BF16)
    out_ring = keep((2, 3, rows, RING * HD), BF16)
    sems = pltpu.SemaphoreType.DMA
    queries, key_rows, value_rows, gate_input, out_grad = map(
        hbm, (queries, key_rows, value_rows, gate_input, out_grad)
    )
    doc_row = doc_start.reshape(1, rows)
    gain_row = norm_gain.reshape(1, cols)

    by_token = (rows, cols)
    steps = heads // GROUP
    (
        crow, enter, leave, rrow, keys, values, local, state, own_pass, gain, kept_q, *rings
    ) = call(
        functools.partial(state_kernel, chunks, steps),
        grid,
        [
            (hbm(x), anywhere)
            for x in (
                log_decay, doc_row, gain_row, key_rows, value_rows, queries, gate_input, out_grad
            )
        ],
        [keep((heads, rows), F32)] * 3
        + [
            keep((8, rows), F32), keep(by_token, BF16), keep(by_token, BF16),
            keep(local_dims, F32), keep((heads, HD, HD), F32), keep((heads, HD), F32),
            keep((1, cols), F32), keep(by_token, BF16), ring, ring,
        ],
        [
            pltpu.VMEM((heads, rows), F32), pltpu.VMEM((1, rows), jnp.int32),
            sems((2, steps)), sems((3,)), sems((3,)),
        ],
        room=ROOM, flops=small, moved=2 * big,
    )

    ready = []
    made = [kept_q, *rings]

    def fill_forward(window, tie):
        if not ready:
            ready[:] = call(
                prepare_kernel, (), kept(after(rrow, tie), crow, enter),
                [keep((chunks, CHUNK, CHUNK), F32), keep((rows, HD), F32)],
                room=ROOM, flops=8 * rows * CHUNK,
            )
        mask, columns = ready
        ins = kept(after(crow, tie), columns, mask, keys, values, gain)
        ins += [(x, anywhere) for x in (queries, gate_input, out_grad)]
        aliases = {len(ins) + i: i for i in range(len(made))}
        ins += kept(*made[:7]) + [(hbm(x), anywhere) for x in made[7:]]
        made[:] = call(
            functools.partial(inside_kernel, chunks, window * share // RING, heads // RING),
            (share // RING,),
            ins,
            [
                keep(by_token, BF16), ring, ring, keep(by_token, F32), keep(by_token, BF16),
                keep(by_head, BF16), probs_ring, probs_out,
            ],
            [sems((4,))],
            aliases=aliases, room=ROOM,
            flops=2 * tile // WINDOWS, moved=5 * big // WINDOWS,
            exps=rows * (CHUNK + HD) * heads // WINDOWS,
        )
        return made[7]

    entering, incoming, passes = scan_devices(state, own_pass, None, fill_forward, False)
    mask, columns = ready
    kept_q, _, _, inside, gnorm, turned_q, probs_ringed, probs = made
    tall = pltpu.VMEM((rows, HD), F32)

    attn, probs, held, sums = call(
        functools.partial(outside_kernel, chunks, heads // RING - 1, entering, len(incoming)),
        grid,
        kept(columns, enter, kept_q, gnorm, local, *incoming, probs_ringed, inside)
        + [(hbm(probs), anywhere)],
        [keep(by_token, F32), probs_out, keep(local_dims, BF16), keep((2, rows), F32)],
        [tall, tall, sems((1,))],
        {6 + len(incoming): 0, 7 + len(incoming): 1},
        room=ROOM, flops=small, moved=big,
    )

    apart = 1
    while apart < parts // 2:
        other_sums = lax.ppermute(sums, "head", [(i, i ^ apart) for i in range(parts)])
        (sums,) = call(add_kernel, (), kept(sums, other_sums), [keep((2, rows), F32)], room=ROOM)
        apart *= 2
    other_sums = lax.ppermute(sums, "head", [(i, i ^ apart) for i in range(parts)])

    agrad, turned_agrad, bloc, back, alpha, *rings = call(
        functools.partial(grad_kernel, chunks, 2),
        grid,
        kept(enter, sums, other_sums, turned_q, gnorm, attn)
        + [(hbm(x), anywhere) for x in (gate_input, out_grad, probs)],
        [
            keep(by_token, BF16), keep(by_head, BF16), keep(local_dims, F32),
            keep((heads, HD, HD), F32), keep((rows, HD), F32), ring, ring, probs_ring,
        ],
        [tall, sems((3,))],
        room=ROOM, flops=small, moved=big,
    )

    inner = [turned_q, turned_agrad, *rings]

    def fill_backward(window, tie):
        ins = kept(
            after(crow, tie), alpha, columns, mask, keys, values, attn, held, agrad, *inner[:2], gain
        )
        ins += [(hbm(x), anywhere) for x in (gate_input, out_grad, probs)]
        aliases = {9: 0, 10: 1}
        aliases.update({len(ins) - 2 + i: i for i in range(2, len(inner))})
        ins += kept(*inner[2:6]) + [(hbm(x), anywhere) for x in inner[6:]]
        inner[:] = call(
            functools.partial(inner_grad_kernel, chunks, window * share // RING, heads // RING),
            (share // RING,),
            ins,
            [keep(by_head, BF16)] * 2 + [ring, ring, probs_ring, out_ring] + [wide_out] * 3,
            [sems((6,))],
            aliases=aliases, room=ROOM,
            flops=(4 * tile + small) // WINDOWS, moved=7 * big // WINDOWS,
            exps=rows * (CHUNK + HD) * heads // WINDOWS,
        )
        return inner[6]

    entering, outgoing, _ = scan_devices(back, own_pass, passes, fill_backward, True)
    wide = pl.BlockSpec((rows, GROUP * HD), lambda i: (0, i))
    dk, dv, dq, gated, gate_grad = call(
        functools.partial(outer_grad_kernel, chunks, heads // RING - 1, entering, len(outgoing)),
        grid,
        kept(enter, leave, keys, values, *outgoing, *inner[:2], bloc, inner[5])
        + [(hbm(x), anywhere) for x in inner[6:]],
        [(pltpu.HBM((rows, cols), BF16), wide)] * 2 + [wide_out] * 3,
        [sems((3,))],
        {8 + len(outgoing) + i: 2 + i for i in range(3)},
        room=ROOM, flops=2 * small, moved=2 * big,
    )
    return (gated, gate_grad, dq, dk, dv)


def solution(mesh):
    in_specs = (
        P("seq", "head"),
        P("seq", "head"),
        P("seq", "head"),
        P("head", "seq"),
        P("seq"),
        P("seq", "head"),
        P("head"),
        P("seq", "head"),
    )
    out_specs = (P("seq", "head"),) * 5
    return jax.shard_map(body, mesh=mesh, in_specs=in_specs, out_specs=out_specs, check_vma=False)
```

```python
import functools

import jax
import jax.numpy as jnp
from jax import lax
from jax.experimental import pallas as pl
from jax.experimental.pallas import tpu as pltpu
from jax.sharding import PartitionSpec as P

HEAD_TOTAL = 64
HD = 128
CHUNK = 256
GROUP = 2
RING = 2
FIRST = 4
WINDOWS = 4
ROOM = 4
WIDTH = HEAD_TOTAL * HD

epsilon = 1e-06
LOG2E = 1.4426950408889634

F32 = jnp.float32
BF16 = jnp.bfloat16
MIB = 1024 * 1024
NT = ((1,), (1,))


def dot(a, b, dims=((1,), (0,))):
    return lax.dot_general(a, b, (dims, ((), ())), preferred_element_type=F32)


def chunk_cumsum(x):
    lane = lax.broadcasted_iota(jnp.int32, x.shape, 1) % CHUNK
    shift = 1
    while shift < CHUNK:
        x = x + jnp.where(lane >= shift, pltpu.roll(x, shift, 1), 0.0)
        shift *= 2
    return x


def spans(chunks):
    return [slice(n * CHUNK, (n + 1) * CHUNK) for n in range(chunks)]


def head_span(head, count=1):
    return pl.ds(pl.multiple_of(head * HD, HD), count * HD)


def save(stores):
    for ref, index, value in stores:
        ref[index] = value


def sigmoid(x):
    return 0.5 * jnp.tanh(0.5 * x) + 0.5


def spread(cols, lane):
    return jnp.broadcast_to(cols[:, lane : lane + 1], cols.shape)


def turned(cols_ref, lane):
    return pltpu.roll(cols_ref[...], (HD - lane) % HD, 1)


def column(row):
    return jnp.broadcast_to(row, (HD, row.shape[1])).T


def start(copies):
    for copy in copies:
        copy.start()


def wait(copies):
    for copy in copies:
        copy.wait()


def group_of(at):
    return head_span(at * RING, RING)


def fetch_gates(at, gate_hbm, grad_hbm, gate_ring, grad_ring, sems):
    slot = at % 2
    return [
        pltpu.make_async_copy(gate_hbm.at[:, group_of(at)], gate_ring.at[slot], sems.at[0]),
        pltpu.make_async_copy(grad_hbm.at[:, group_of(at)], grad_ring.at[slot], sems.at[1]),
    ]


def fetch_q(at, q_hbm, q_ref, sem):
    return [pltpu.make_async_copy(q_hbm.at[:, group_of(at)], q_ref.at[:, group_of(at)], sem)]


def fetch_probs(at, probs_hbm, probs_ring, sem):
    heads = pl.ds(at * RING, RING)
    return [pltpu.make_async_copy(probs_hbm.at[heads], probs_ring.at[at % 2], sem)]


def put_probs(at, probs_ring, probs_hbm, sem):
    heads = pl.ds(at * RING, RING)
    return [pltpu.make_async_copy(probs_ring.at[at % 2], probs_hbm.at[heads], sem)]


def put_outs(at, out_ring, outs_hbm, sems):
    return [
        pltpu.make_async_copy(out_ring.at[at % 2, i], out.at[:, group_of(at)], sems.at[i])
        for i, out in enumerate(outs_hbm)
    ]


def state_kernel(
    chunks, steps, lc_hbm, doc_hbm, gain_hbm, k_hbm, v_hbm, q_hbm, gate_hbm, grad_hbm,
    crow_ref, enter_ref, leave_ref, rrow_ref, k_ref, v_ref, loc_ref, state_ref, pass_ref,
    gain_ref, q_ref, gate_ring, grad_ring, lc_ref, doc_ref, sems, small_sems, next_sems,
):
    step = pl.program_id(0)
    small = [
        pltpu.make_async_copy(lc_hbm, lc_ref, small_sems.at[0]),
        pltpu.make_async_copy(doc_hbm, doc_ref, small_sems.at[1]),
        pltpu.make_async_copy(gain_hbm, gain_ref, small_sems.at[2]),
    ]
    following = fetch_gates(0, gate_hbm, grad_hbm, gate_ring, grad_ring, next_sems)
    following += fetch_q(0, q_hbm, q_ref, next_sems.at[2])

    def copies(at):
        here = head_span(at * FIRST, FIRST)
        return (
            pltpu.make_async_copy(k_hbm.at[:, here], k_ref.at[:, here], sems.at[0, at]),
            pltpu.make_async_copy(v_hbm.at[:, here], v_ref.at[:, here], sems.at[1, at]),
        )

    @pl.when(step == 0)
    def _():
        start(small)
        for at in range(steps * GROUP // FIRST):
            start(copies(at))
        start(following)
        wait(small)
        c = chunk_cumsum(lc_ref[...] * LOG2E)
        r = chunk_cumsum(jnp.broadcast_to(doc_ref[...].astype(F32), (8, doc_ref.shape[1])))
        crow_ref[...] = c
        rrow_ref[...] = r
        enter_ref[...] = jnp.where(r[0:1] == 0.0, jnp.exp2(c), 0.0)
        for span in spans(chunks):
            cn, rn = c[:, span], r[0:1, span]
            leave_ref[:, span] = jnp.where(rn == rn[:, -1:], jnp.exp2(cn[:, -1:] - cn), 0.0)

    fresh = step * GROUP % FIRST == 0
    pl.when(fresh)(lambda: wait(copies(step * GROUP // FIRST)))
    late = []
    for g in range(GROUP):
        h = step * GROUP + g
        mine = head_span(h)
        state = None
        total = None
        for n, span in enumerate(spans(chunks)):
            keyed = (k_ref[span, mine].T.astype(F32) * leave_ref[pl.ds(h, 1), span]).astype(BF16)
            local = dot(keyed, v_ref[span, mine])
            passing = enter_ref[pl.ds(h, 1), span][:, CHUNK - 1 : CHUNK]
            state = local if state is None else passing * state + local
            total = passing if total is None else passing * total
            save(late)
            late = [(loc_ref, (h, n), local)] if n + 1 < chunks else []
        late.append((state_ref, h, state))
        late.append((pass_ref, (pl.ds(h, 1), slice(None)), jnp.broadcast_to(total, (1, HD))))
    save(late)

    @pl.when(step == steps - 1)
    def _():
        wait(following)


def prepare_kernel(rrow_ref, crow_ref, enter_ref, mask_ref, cols_ref):
    sub = lax.broadcasted_iota(jnp.int32, (CHUNK, CHUNK), 0)
    lane = lax.broadcasted_iota(jnp.int32, (CHUNK, CHUNK), 1)
    spare = jnp.zeros((HD - 2 * crow_ref.shape[0], CHUNK), F32)
    for n, span in enumerate(spans(mask_ref.shape[0])):
        r_row = rrow_ref[0:1, span]
        r_col = jnp.concatenate([column(r_row)] * (CHUNK // HD), axis=1)
        mask_ref[n] = jnp.where((r_col == r_row) & (lane <= sub), 0.0, -jnp.inf)
        cols_ref[span, :] = jnp.concatenate([crow_ref[:, span], enter_ref[:, span], spare], axis=0).T


def decayed(scores, c_col, c_row, mask):
    top, low = slice(0, HD), slice(HD, CHUNK)
    row_blocks = []
    for rows, width in ((top, HD), (low, CHUNK)):
        col = c_col[rows]
        col = col if width == HD else jnp.concatenate([col] * (width // HD), axis=1)
        weight = jnp.exp2(col - c_row[:, :width] + mask[rows, :width])
        row_blocks.append((scores[rows, :width] * weight).astype(BF16))
    row_blocks[0] = jnp.concatenate([row_blocks[0], jnp.zeros((HD, CHUNK - HD), BF16)], axis=1)
    return jnp.concatenate(row_blocks, axis=0)


def inside_kernel(
    chunks, first, steps, crow_ref, cols_ref, mask_ref, k_ref, v_ref, gain_ref, q_hbm, gate_hbm,
    grad_hbm, *refs,
):
    q_ref, gate_ring, grad_ring, attn_ref, gnorm_ref, turned_q_ref, probs_ring, probs_hbm, sems = (
        refs[-9:]
    )
    step = first + pl.program_id(0)
    slot = step % 2
    fetches = fetch_gates(step + 1, gate_hbm, grad_hbm, gate_ring, grad_ring, sems)
    fetches += fetch_q(step + 1, q_hbm, q_ref, sems.at[2])
    puts = put_probs(step - 1, probs_ring, probs_hbm, sems.at[3])
    pl.when(step + 1 < steps)(lambda: start(fetches))
    pl.when(step > 0)(lambda: start(puts))

    cols_now = turned(cols_ref, step * RING)
    late = []
    for g in range(RING):
        h = step * RING + g
        cols = slice(g * HD, (g + 1) * HD)
        mine = head_span(h)
        for n, span in enumerate(spans(chunks)):
            q = q_ref[span, mine]
            scores = dot(q, k_ref[span, mine], NT)
            c_row = crow_ref[pl.ds(h, 1), span]
            probs = decayed(scores, spread(cols_now[span], g), c_row, mask_ref.at[n])
            inside = dot(probs, v_ref[span, mine])
            sig = sigmoid(gate_ring[slot, span, cols].astype(F32))
            gnorm = grad_ring[slot, span, cols].astype(F32) * sig * gain_ref[0:1, mine]
            save(late)
            late = [
                (probs_ring, (slot, g, n), probs),
                (attn_ref, (span, mine), inside),
                (turned_q_ref, (h, slice(None), span), q.T),
                (gnorm_ref, (span, mine), gnorm.astype(BF16)),
            ]
    save(late)
    pl.when(step + 1 < steps)(lambda: wait(fetches))
    pl.when(step > 0)(lambda: wait(puts))


def outside_kernel(chunks, last, entering, inputs, cols_ref, enter_ref, q_ref, gnorm_ref, loc_ref, *refs):
    in_refs = refs[:inputs]
    probs_ring, inside_ref, _, attn_ref, probs_hbm, held_ref, sums_ref, sq_ref, inner_ref, sem = (
        refs[inputs:]
    )
    step = pl.program_id(0)
    steps = pl.num_programs(0)
    puts = put_probs(last, probs_ring, probs_hbm, sem.at[0])

    @pl.when(step == 0)
    def _():
        start(puts)
        sq_ref[...] = jnp.zeros_like(sq_ref)
        inner_ref[...] = jnp.zeros_like(inner_ref)

    heads = [step * GROUP + g for g in range(GROUP)]
    cols_now = turned(cols_ref, enter_ref.shape[0] + step * GROUP)
    carries = [entering(in_refs, h) for h in heads]
    late = []
    for n, span in enumerate(spans(chunks)):
        squares = sq_ref[span, :]
        inners = inner_ref[span, :]
        for g, h in enumerate(heads):
            mine = head_span(h)
            held = carries[g].astype(BF16)
            enter = spread(cols_now[span], g)
            attn = inside_ref[span, mine] + enter * dot(q_ref[span, mine], held)
            squares = squares + attn * attn
            inners = inners + gnorm_ref[span, mine].astype(F32) * attn
            if n + 1 < chunks:
                passing = enter_ref[pl.ds(h, 1), span][:, CHUNK - 1 : CHUNK]
                carries[g] = passing * carries[g] + loc_ref[h, n]
            save(late)
            late = [(held_ref, (h, n), held), (attn_ref, (span, mine), attn)]
        late += [(sq_ref, (span, slice(None)), squares), (inner_ref, (span, slice(None)), inners)]
    save(late)

    @pl.when(step == steps - 1)
    def _():
        wait(puts)
        sums_ref[0:1, :] = jnp.sum(sq_ref[...].T, axis=0, keepdims=True)
        sums_ref[1:2, :] = jnp.sum(inner_ref[...].T, axis=0, keepdims=True)


def grad_kernel(chunks, parts, enter_ref, *refs):
    turned_q_ref, gnorm_ref, attn_ref, gate_hbm, grad_hbm, probs_hbm = refs[parts : parts + 6]
    agrad_ref, turned_ref, bloc_ref, back_ref, normed_ref = refs[parts + 6 : parts + 11]
    gate_ring, grad_ring, probs_ring, alpha_ref, beta_ref, sems = refs[parts + 11 :]
    step = pl.program_id(0)
    following = fetch_gates(0, gate_hbm, grad_hbm, gate_ring, grad_ring, sems)
    following += fetch_probs(0, probs_hbm, probs_ring, sems.at[2])

    @pl.when(step == 0)
    def _():
        start(following)
        sums = refs[0][...]
        for ref in refs[1:parts]:
            sums = sums + ref[...]
        inverse = lax.rsqrt(sums[0:1] / WIDTH + epsilon)
        alpha_ref[...] = column(inverse)
        beta_ref[...] = column(inverse * inverse * inverse * sums[1:2] / WIDTH)

    late = []
    for g in range(GROUP):
        h = step * GROUP + g
        mine = head_span(h)
        back = None
        for n, span in reversed(list(enumerate(spans(chunks)))):
            enter = enter_ref[pl.ds(h, 1), span]
            gnorm = gnorm_ref[span, mine].astype(F32)
            attn, alpha = attn_ref[span, mine], alpha_ref[span, :]
            agrad = alpha * gnorm - attn * beta_ref[span, :]
            agrad = agrad.astype(BF16)
            qkeyed = (turned_q_ref[h, :, span].astype(F32) * enter).astype(BF16)
            local = dot(qkeyed, agrad)
            back = local if back is None else local + enter[:, CHUNK - 1 : CHUNK] * back
            save(late)
            late = [
                (agrad_ref, (span, mine), agrad),
                (turned_ref, (h, slice(None), span), agrad.T),
                (normed_ref, (span, mine), (attn * alpha).astype(BF16)),
            ]
            if n > 0:
                late.append((bloc_ref, (h, n - 1), local))
        late.append((back_ref, h, back))
    save(late)

    @pl.when(step == pl.num_programs(0) - 1)
    def _():
        wait(following)


def inner_grad_kernel(
    chunks, first, steps, crow_ref, cols_ref, mask_ref, k_ref, v_ref, normed_ref, held_ref,
    agrad_ref, turned_q_ref, turned_agrad_ref, gain_ref, gate_hbm, grad_hbm, probs_hbm,
    *refs,
):
    dk_ref, dv_ref, gate_ring, grad_ring, probs_ring, out_ring, *outs_hbm, sems = refs[-10:]
    step = first + pl.program_id(0)
    slot = step % 2
    fetches = fetch_gates(step + 1, gate_hbm, grad_hbm, gate_ring, grad_ring, sems)
    fetches += fetch_probs(step + 1, probs_hbm, probs_ring, sems.at[2])
    puts = put_outs(step - 1, out_ring, outs_hbm, sems.at[pl.ds(3, 3)])
    pl.when(step + 1 < steps)(lambda: start(fetches))
    pl.when(step > 0)(lambda: start(puts))

    cols_now = turned(cols_ref, step * RING)
    late = []
    for g in range(RING):
        h = step * RING + g
        cols = slice(g * HD, (g + 1) * HD)
        mine = head_span(h)
        for n, span in enumerate(spans(chunks)):
            k, v, agrad = k_ref[span, mine], v_ref[span, mine], agrad_ref[span, mine]
            both = dot(agrad, jnp.concatenate([v, held_ref[h, n]], axis=0), NT)
            c_row = crow_ref[pl.ds(h, 1), span]
            dscore = decayed(both[:, :CHUNK], spread(cols_now[span], g), c_row, mask_ref.at[n])
            enter = spread(cols_now[span], crow_ref.shape[0] + g)
            dq = dot(dscore, k) + enter * both[:, CHUNK:]
            dv = dot(turned_agrad_ref[h, :, span], probs_ring[slot, g, n])
            dk = dot(turned_q_ref[h, :, span], dscore)
            normed = normed_ref[span, mine].astype(F32) * gain_ref[0:1, mine]
            sig = sigmoid(gate_ring[slot, span, cols].astype(F32))
            gated = normed * sig
            ggate = grad_ring[slot, span, cols].astype(F32) * gated * (1.0 - sig)
            save(late)
            late = [
                (out_ring, (slot, 0, span, cols), dq.astype(BF16)),
                (dv_ref, (h, slice(None), span), dv.astype(BF16)),
                (dk_ref, (h, slice(None), span), dk.astype(BF16)),
                (out_ring, (slot, 1, span, cols), gated.astype(BF16)),
                (out_ring, (slot, 2, span, cols), ggate.astype(BF16)),
            ]
    save(late)
    pl.when(step + 1 < steps)(lambda: wait(fetches))
    pl.when(step > 0)(lambda: wait(puts))


def outer_grad_kernel(chunks, last, entering, inputs, enter_ref, leave_ref, k_ref, v_ref, *refs):
    in_refs = refs[:inputs]
    dkin_ref, dvin_ref, bloc_ref, out_ring = refs[inputs : inputs + 4]
    dk_ref, dv_ref, *outs_hbm, sems = refs[inputs + 7 :]
    step = pl.program_id(0)
    steps = pl.num_programs(0)
    puts = put_outs(last, out_ring, outs_hbm, sems)
    pl.when(step == 0)(lambda: start(puts))
    late = []
    for g in range(GROUP):
        h = step * GROUP + g
        cols = slice(g * HD, (g + 1) * HD)
        mine = head_span(h)
        carry = entering(in_refs, h)
        for n, span in reversed(list(enumerate(spans(chunks)))):
            leave = leave_ref[pl.ds(h, 1), span]
            back = carry.astype(BF16)
            dk = dkin_ref[h, :, span].astype(F32) + leave * dot(back, v_ref[span, mine], NT)
            dv = dvin_ref[h, :, span].astype(F32) + leave * dot(back.T, k_ref[span, mine], NT)
            if n > 0:
                passing = enter_ref[pl.ds(h, 1), span][:, CHUNK - 1 : CHUNK]
                carry = bloc_ref[h, n - 1] + passing * carry
            save(late)
            late = [
                (dk_ref, (span, cols), dk.astype(BF16).T),
                (dv_ref, (span, cols), dv.astype(BF16).T),
            ]
    save(late)
    pl.when(step == steps - 1)(lambda: wait(puts))


def hbm(x):
    return pltpu.with_memory_space_constraint(x, pltpu.HBM)


def kept(*arrays):
    spec = pl.BlockSpec(memory_space=pltpu.VMEM)
    return [(pltpu.with_memory_space_constraint(x, pltpu.VMEM), spec) for x in arrays]


def keep(dims, dtype):
    return pltpu.VMEM(dims, dtype), pl.BlockSpec(memory_space=pltpu.VMEM)


def add_kernel(a_ref, b_ref, out_ref):
    out_ref[...] = a_ref[...] + b_ref[...]


def call(kernel, grid, ins, outs, scratch=(), aliases=None, room=4, flops=0, moved=0, exps=0):
    return pl.pallas_call(
        kernel,
        grid=grid,
        in_specs=[spec for _, spec in ins],
        out_specs=[spec for _, spec in outs],
        out_shape=[shape for shape, _ in outs],
        scratch_shapes=list(scratch),
        input_output_aliases=aliases or {},
        compiler_params=pltpu.CompilerParams(
            dimension_semantics=("arbitrary",) * len(grid), vmem_limit_bytes=room * MIB
        ),
        cost_estimate=pl.CostEstimate(flops=flops, bytes_accessed=moved, transcendentals=exps),
    )(*[x for x, _ in ins])


def after(x, *others):
    return lax.optimization_barrier((x, *others))[0]


def across(x, flips, devices=8):
    return lax.ppermute(x, "seq", [(i, i ^ flips) for i in range(devices)])


def place(reverse):
    index = lax.axis_index("seq")
    index = 7 - index if reverse else index
    return lax.rem(index, 2), lax.rem(lax.div(index, 2), 2), lax.div(index, 4)


def pair_kernel(reverse, state_ref, other_ref, pass_ref, beside_ref, x_ref, y_ref, chip_ref):
    core, _, _ = place(reverse)
    quarter = x_ref.shape[0]
    chip_ref[...] = pass_ref[...] * beside_ref[...]
    for i in range(quarter):
        for at, out_ref in ((i, x_ref), (quarter + i, y_ref)):
            h = core * 2 * quarter + at
            mine, other = state_ref[h], other_ref[h]

            @pl.when(core == 0)
            def _():
                out_ref[i] = beside_ref[pl.ds(h, 1), :] * mine + other

            @pl.when(core == 1)
            def _():
                out_ref[i] = pass_ref[pl.ds(h, 1), :] * other + mine


def row_kernel(
    reverse, to_x_ref, to_y_ref, from_x_ref, from_y_ref, chip_ref, side_ref, far_ref,
    row_ref, sent_ref,
):
    core, x, y = place(reverse)
    quarter = row_ref.shape[0]
    for i in range(quarter):
        h = core * 2 * quarter + i
        hy = h + quarter

        @pl.when(x == 0)
        def _():
            row_ref[i] = side_ref[pl.ds(h, 1), :] * to_x_ref[i] + from_x_ref[i]

        @pl.when(x == 1)
        def _():
            row_ref[i] = chip_ref[pl.ds(h, 1), :] * from_x_ref[i] + to_x_ref[i]

        @pl.when(y == 0)
        def _():
            sent_ref[i] = to_y_ref[i]

        @pl.when((y == 1) & (x == 0))
        def _():
            far = far_ref[pl.ds(hy, 1), :] * from_y_ref[i]
            sent_ref[i] = chip_ref[pl.ds(hy, 1), :] * far + to_y_ref[i]

        @pl.when((y == 1) & (x == 1))
        def _():
            sent_ref[i] = from_y_ref[i]


def ahead_kernel(
    reverse, from_x_ref, from_y_ref, row_ref, sent_ref, side_ref, far_ref, out_ref,
):
    core, x, y = place(reverse)
    quarter = row_ref.shape[0]
    for i in range(quarter):
        h = core * 2 * quarter + i
        hy = h + quarter

        @pl.when((y == 0) & (x == 0))
        def _():
            out_ref[i] = jnp.zeros_like(out_ref[i])
            out_ref[quarter + i] = jnp.zeros_like(out_ref[i])

        @pl.when((y == 0) & (x == 1))
        def _():
            out_ref[i] = from_x_ref[i]
            out_ref[quarter + i] = sent_ref[i]

        @pl.when((y == 1) & (x == 0))
        def _():
            out_ref[i] = row_ref[i]
            out_ref[quarter + i] = far_ref[pl.ds(hy, 1), :] * from_y_ref[i] + sent_ref[i]

        @pl.when((y == 1) & (x == 1))
        def _():
            out_ref[i] = side_ref[pl.ds(h, 1), :] * row_ref[i] + from_x_ref[i]
            out_ref[quarter + i] = side_ref[pl.ds(hy, 1), :] * from_y_ref[i] + sent_ref[i]


def cube_entering(reverse, refs, h):
    ahead_ref, beside_ref, other_ref, beside_pass_ref = refs
    core, _, _ = place(reverse)
    half = ahead_ref.shape[0]
    at = lax.rem(h, half)
    chip = jnp.where(lax.div(h, half) == core, ahead_ref[at], beside_ref[at])
    through = beside_pass_ref[pl.ds(h, 1), :] * chip + other_ref[h]
    return jnp.where(core == 0, chip, through)


def plain_entering(refs, h):
    return refs[0][h]


def cube_scan(state, own_pass, passes, fill, reverse):
    heads = state.shape[0]
    quarter = heads // 4
    part = keep((quarter, HD, HD), F32)

    other = across(state, 1)
    beside_pass = passes[0] if passes else across(own_pass, 1)
    other, beside_pass = lax.optimization_barrier((other, beside_pass, fill(0, state)))[:2]
    to_x, to_y, chip_pass = call(
        functools.partial(pair_kernel, reverse), (),
        kept(state, other, own_pass, beside_pass), [part, part, keep((heads, HD), F32)], room=ROOM,
    )

    from_x, from_y = across(to_x, 2), across(to_y, 4)
    x_pass, far_pass = passes[1:] if passes else (across(chip_pass, 2), across(chip_pass, 6))
    from_x, from_y, x_pass, far_pass = lax.optimization_barrier(
        (from_x, from_y, x_pass, far_pass, fill(1, to_y))
    )[:4]
    row, sent = call(
        functools.partial(row_kernel, reverse), (),
        kept(to_x, to_y, from_x, from_y, chip_pass, x_pass, far_pass), [part, part], room=ROOM,
    )

    row_in, sent_in = across(row, 4), across(sent, 2)
    row_in, sent_in = lax.optimization_barrier((row_in, sent_in, fill(2, sent)))[:2]
    (ahead,) = call(
        functools.partial(ahead_kernel, reverse), (),
        kept(from_x, from_y, row_in, sent_in, x_pass, far_pass),
        [keep((2 * quarter, HD, HD), F32)], room=ROOM,
    )

    beside = across(ahead, 1)
    beside = after(beside, fill(3, ahead))
    entering = functools.partial(cube_entering, reverse)
    return entering, (ahead, beside, other, beside_pass), (beside_pass, x_pass, far_pass)


def doubling_scan(state, own_pass, fill, reverse):
    devices = lax.axis_size("seq")
    index = lax.axis_index("seq")
    passes = lax.all_gather(own_pass, "seq")
    if reverse:
        passes = passes[::-1]
        index = devices - 1 - index
    route = lambda hop: [
        (i, i - hop if reverse else i + hop)
        for i in range(devices)
        if 0 <= (i - hop if reverse else i + hop) < devices
    ]
    for window in range(WINDOWS):
        state = after(state, fill(window, state))
    hop = 1
    while hop < devices:
        factor = lax.dynamic_index_in_dim(passes, index, 0, False)
        state = factor[:, None, :] * lax.ppermute(state, "seq", route(hop)) + state
        before = jnp.concatenate([jnp.zeros_like(passes[:hop]), passes[:-hop]], axis=0)
        passes = passes * before
        hop *= 2
    return lax.ppermute(state, "seq", route(1))


def scan_devices(state, own_pass, passes, fill, reverse):
    if lax.axis_size("seq") == 8 and state.shape[0] % 4 == 0:
        return cube_scan(state, own_pass, passes, fill, reverse)
    return plain_entering, (doubling_scan(state, own_pass, fill, reverse),), None


def body(queries, key_rows, value_rows, log_decay, doc_start, gate_input, norm_gain, out_grad):
    rows, cols = queries.shape
    heads = cols // HD
    chunks = rows // CHUNK
    parts = lax.axis_size("head")
    grid = (heads // GROUP,)
    share = heads // WINDOWS
    big = rows * cols * 2
    tile = 2 * rows * CHUNK * cols
    small = 2 * rows * HD * cols

    whole = lambda *dims: pl.BlockSpec(dims, lambda i: (0,) * len(dims))
    anywhere = pl.BlockSpec(memory_space=pl.ANY)

    by_head = (heads, HD, rows)
    local_dims = (heads, chunks, HD, HD)
    wide_out = (pltpu.HBM((rows, cols), BF16), anywhere)
    probs_out = (pltpu.HBM((heads, chunks, CHUNK, CHUNK), BF16), anywhere)
    ring = keep((2, rows, RING * HD), BF16)
    probs_ring = keep((2, RING, chunks, CHUNK, CHUNK), BF16)
    out_ring = keep((2, 3, rows, RING * HD), BF16)
    sems = pltpu.SemaphoreType.DMA
    queries, key_rows, value_rows, gate_input, out_grad = map(
        hbm, (queries, key_rows, value_rows, gate_input, out_grad)
    )
    doc_row = doc_start.reshape(1, rows)
    gain_row = norm_gain.reshape(1, cols)

    by_token = (rows, cols)
    steps = heads // GROUP
    (
        crow, enter, leave, rrow, keys, values, local, state, own_pass, gain, kept_q, *rings
    ) = call(
        functools.partial(state_kernel, chunks, steps),
        grid,
        [
            (hbm(x), anywhere)
            for x in (
                log_decay, doc_row, gain_row, key_rows, value_rows, queries, gate_input, out_grad
            )
        ],
        [keep((heads, rows), F32)] * 3
        + [
            keep((8, rows), F32), keep(by_token, BF16), keep(by_token, BF16),
            keep((heads, chunks - 1, HD, HD), F32), keep((heads, HD, HD), F32), keep((heads, HD), F32),
            keep((1, cols), F32), keep(by_token, BF16), ring, ring,
        ],
        [
            pltpu.VMEM((heads, rows), F32), pltpu.VMEM((1, rows), jnp.int32),
            sems((2, steps)), sems((3,)), sems((3,)),
        ],
        room=ROOM, flops=small, moved=2 * big,
    )

    ready = []
    made = [kept_q, *rings]

    def fill_forward(window, tie):
        if not ready:
            ready[:] = call(
                prepare_kernel, (), kept(after(rrow, tie), crow, enter),
                [keep((chunks, CHUNK, CHUNK), F32), keep((rows, HD), F32)],
                room=ROOM, flops=8 * rows * CHUNK,
            )
        mask, columns = ready
        ins = kept(after(crow, tie), columns, mask, keys, values, gain)
        ins += [(x, anywhere) for x in (queries, gate_input, out_grad)]
        aliases = {len(ins) + i: i for i in range(len(made))}
        ins += kept(*made[:7]) + [(hbm(x), anywhere) for x in made[7:]]
        made[:] = call(
            functools.partial(inside_kernel, chunks, window * share // RING, heads // RING),
            (share // RING,),
            ins,
            [
                keep(by_token, BF16), ring, ring, keep(by_token, F32), keep(by_token, BF16),
                keep(by_head, BF16), probs_ring, probs_out,
            ],
            [sems((4,))],
            aliases=aliases, room=ROOM,
            flops=2 * tile // WINDOWS, moved=5 * big // WINDOWS,
            exps=rows * (CHUNK + HD) * heads // WINDOWS,
        )
        return made[7]

    entering, incoming, passes = scan_devices(state, own_pass, None, fill_forward, False)
    mask, columns = ready
    kept_q, _, _, inside, gnorm, turned_q, probs_ringed, probs = made
    tall = pltpu.VMEM((rows, HD), F32)

    attn, probs, held, sums = call(
        functools.partial(outside_kernel, chunks, heads // RING - 1, entering, len(incoming)),
        grid,
        kept(columns, enter, kept_q, gnorm, local, *incoming, probs_ringed, inside)
        + [(hbm(probs), anywhere)],
        [keep(by_token, F32), probs_out, keep(local_dims, BF16), keep((2, rows), F32)],
        [tall, tall, sems((1,))],
        {6 + len(incoming): 0, 7 + len(incoming): 1},
        room=ROOM, flops=small, moved=big,
    )

    apart = 1
    while apart < parts // 2:
        other_sums = lax.ppermute(sums, "head", [(i, i ^ apart) for i in range(parts)])
        (sums,) = call(add_kernel, (), kept(sums, other_sums), [keep((2, rows), F32)], room=ROOM)
        apart *= 2
    other_sums = lax.ppermute(sums, "head", [(i, i ^ apart) for i in range(parts)])

    agrad, turned_agrad, bloc, back, normed, *rings = call(
        functools.partial(grad_kernel, chunks, 2),
        grid,
        kept(enter, sums, other_sums, turned_q, gnorm, attn)
        + [(hbm(x), anywhere) for x in (gate_input, out_grad, probs)],
        [
            keep(by_token, BF16), keep(by_head, BF16), keep((heads, chunks - 1, HD, HD), F32),
            keep((heads, HD, HD), F32), keep(by_token, BF16), ring, ring, probs_ring,
        ],
        [tall, tall, sems((3,))],
        {4: 0},
        room=ROOM, flops=small, moved=big,
    )

    inner = [turned_q, turned_agrad, *rings]

    def fill_backward(window, tie):
        ins = kept(
            after(crow, tie), columns, mask, keys, values, normed, held, agrad, *inner[:2], gain
        )
        ins += [(hbm(x), anywhere) for x in (gate_input, out_grad, probs)]
        aliases = {8: 0, 9: 1}
        aliases.update({len(ins) - 2 + i: i for i in range(2, len(inner))})
        ins += kept(*inner[2:6]) + [(hbm(x), anywhere) for x in inner[6:]]
        inner[:] = call(
            functools.partial(inner_grad_kernel, chunks, window * share // RING, heads // RING),
            (share // RING,),
            ins,
            [keep(by_head, BF16)] * 2 + [ring, ring, probs_ring, out_ring] + [wide_out] * 3,
            [sems((6,))],
            aliases=aliases, room=ROOM,
            flops=(4 * tile + small) // WINDOWS, moved=7 * big // WINDOWS,
            exps=rows * (CHUNK + HD) * heads // WINDOWS,
        )
        return inner[6]

    entering, outgoing, _ = scan_devices(back, own_pass, passes, fill_backward, True)
    wide = pl.BlockSpec((rows, GROUP * HD), lambda i: (0, i))
    dk, dv, dq, gated, gate_grad = call(
        functools.partial(outer_grad_kernel, chunks, heads // RING - 1, entering, len(outgoing)),
        grid,
        kept(enter, leave, keys, values, *outgoing, *inner[:2], bloc, inner[5])
        + [(hbm(x), anywhere) for x in inner[6:]],
        [(pltpu.HBM((rows, cols), BF16), wide)] * 2 + [wide_out] * 3,
        [sems((3,))],
        {8 + len(outgoing) + i: 2 + i for i in range(3)},
        room=ROOM, flops=2 * small, moved=2 * big,
    )
    return (gated, gate_grad, dq, dk, dv)


def solution(mesh):
    in_specs = (
        P("seq", "head"),
        P("seq", "head"),
        P("seq", "head"),
        P("head", "seq"),
        P("seq"),
        P("seq", "head"),
        P("head"),
        P("seq", "head"),
    )
    out_specs = (P("seq", "head"),) * 5
    return jax.shard_map(body, mesh=mesh, in_specs=in_specs, out_specs=out_specs, check_vma=False)
```

```python
import functools

import jax
import jax.numpy as jnp
from jax import lax
from jax.experimental import pallas as pl
from jax.experimental.pallas import tpu as pltpu
from jax.sharding import PartitionSpec as P

HEAD_TOTAL = 64
HD = 128
CHUNK = 256
GROUP = 2
RING = 2
AHEAD = 3
WINDOWS = 3
ROOM = 4
WIDTH = HEAD_TOTAL * HD

epsilon = 1e-06
LOG2E = 1.4426950408889634

F32 = jnp.float32
BF16 = jnp.bfloat16
MIB = 1024 * 1024
NT = ((1,), (1,))


def dot(a, b, dims=((1,), (0,))):
    return lax.dot_general(a, b, (dims, ((), ())), preferred_element_type=F32)


def chunk_cumsum(x):
    lane = lax.broadcasted_iota(jnp.int32, x.shape, 1) % CHUNK
    shift = 1
    while shift < CHUNK:
        x = x + jnp.where(lane >= shift, pltpu.roll(x, shift, 1), 0.0)
        shift *= 2
    return x


def spans(chunks):
    return [slice(n * CHUNK, (n + 1) * CHUNK) for n in range(chunks)]


def head_span(head, count=1):
    return pl.ds(pl.multiple_of(head * HD, HD), count * HD)


def save(stores):
    for ref, index, value in stores:
        ref[index] = value


def sigmoid(x):
    return 0.5 * jnp.tanh(0.5 * x) + 0.5


def spread(cols, lane):
    return jnp.broadcast_to(cols[:, lane : lane + 1], cols.shape)


def turned(cols_ref, lane):
    return pltpu.roll(cols_ref[...], (HD - lane) % HD, 1)


def column(row):
    return jnp.broadcast_to(row, (HD, row.shape[1])).T


def start(copies):
    for copy in copies:
        copy.start()


def wait(copies):
    for copy in copies:
        copy.wait()


def group_of(at):
    return head_span(at * RING, RING)


def fetch_gates(at, gate_hbm, grad_hbm, gate_ring, grad_ring, sems):
    slot = at % 2
    return [
        pltpu.make_async_copy(gate_hbm.at[:, group_of(at)], gate_ring.at[slot], sems.at[0]),
        pltpu.make_async_copy(grad_hbm.at[:, group_of(at)], grad_ring.at[slot], sems.at[1]),
    ]


def fetch_q(at, q_hbm, q_ref, sem):
    return [pltpu.make_async_copy(q_hbm.at[:, group_of(at)], q_ref.at[:, group_of(at)], sem)]


def fetch_probs(at, probs_hbm, probs_ring, sem):
    heads = pl.ds(at * RING, RING)
    return [pltpu.make_async_copy(probs_hbm.at[heads], probs_ring.at[at % 2], sem)]


def put_probs(at, probs_ring, probs_hbm, sem):
    heads = pl.ds(at * RING, RING)
    return [pltpu.make_async_copy(probs_ring.at[at % 2], probs_hbm.at[heads], sem)]


def put_outs(at, out_ring, outs_hbm, sems):
    return [
        pltpu.make_async_copy(out_ring.at[at % 2, i], out.at[:, group_of(at)], sems.at[i])
        for i, out in enumerate(outs_hbm)
    ]


def state_kernel(
    chunks, steps, lc_hbm, doc_hbm, gain_hbm, k_hbm, v_hbm, q_hbm, gate_hbm, grad_hbm,
    crow_ref, enter_ref, leave_ref, rrow_ref, k_ref, v_ref, loc_ref, state_ref, pass_ref,
    gain_ref, q_ref, gate_ring, grad_ring, lc_ref, doc_ref, sems, small_sems, next_sems,
):
    step = pl.program_id(0)
    small = [
        pltpu.make_async_copy(lc_hbm, lc_ref, small_sems.at[0]),
        pltpu.make_async_copy(doc_hbm, doc_ref, small_sems.at[1]),
        pltpu.make_async_copy(gain_hbm, gain_ref, small_sems.at[2]),
    ]
    following = fetch_gates(0, gate_hbm, grad_hbm, gate_ring, grad_ring, next_sems)
    following += fetch_q(0, q_hbm, q_ref, next_sems.at[2])

    def copies(at):
        here = head_span(at * GROUP, GROUP)
        return (
            pltpu.make_async_copy(k_hbm.at[:, here], k_ref.at[:, here], sems.at[0, at]),
            pltpu.make_async_copy(v_hbm.at[:, here], v_ref.at[:, here], sems.at[1, at]),
        )

    @pl.when(step == 0)
    def _():
        start(small)
        for at in range(min(AHEAD, steps)):
            start(copies(at))
        wait(small)
        c = chunk_cumsum(lc_ref[...] * LOG2E)
        r = chunk_cumsum(jnp.broadcast_to(doc_ref[...].astype(F32), (8, doc_ref.shape[1])))
        crow_ref[...] = c
        rrow_ref[...] = r
        enter_ref[...] = jnp.where(r[0:1] == 0.0, jnp.exp2(c), 0.0)
        for span in spans(chunks):
            cn, rn = c[:, span], r[0:1, span]
            leave_ref[:, span] = jnp.where(rn == rn[:, -1:], jnp.exp2(cn[:, -1:] - cn), 0.0)

    pl.when(step + AHEAD < steps)(lambda: start(copies(step + AHEAD)))
    pl.when(step + AHEAD == steps)(lambda: start(following))
    wait(copies(step))
    late = []
    for g in range(GROUP):
        h = step * GROUP + g
        mine = head_span(h)
        state = None
        total = None
        for n, span in enumerate(spans(chunks)):
            keyed = (k_ref[span, mine].T.astype(F32) * leave_ref[pl.ds(h, 1), span]).astype(BF16)
            local = dot(keyed, v_ref[span, mine])
            passing = enter_ref[pl.ds(h, 1), span][:, CHUNK - 1 : CHUNK]
            state = local if state is None else passing * state + local
            total = passing if total is None else passing * total
            save(late)
            late = [(loc_ref, (h, n), local)] if n + 1 < chunks else []
        late.append((state_ref, h, state))
        late.append((pass_ref, (pl.ds(h, 1), slice(None)), jnp.broadcast_to(total, (1, HD))))
    save(late)

    @pl.when(step == steps - 1)
    def _():
        wait(following)


def prepare_kernel(rrow_ref, crow_ref, enter_ref, mask_ref, cols_ref):
    sub = lax.broadcasted_iota(jnp.int32, (CHUNK, CHUNK), 0)
    lane = lax.broadcasted_iota(jnp.int32, (CHUNK, CHUNK), 1)
    spare = jnp.zeros((HD - 2 * crow_ref.shape[0], CHUNK), F32)
    for n, span in enumerate(spans(mask_ref.shape[0])):
        r_row = rrow_ref[0:1, span]
        r_col = jnp.concatenate([column(r_row)] * (CHUNK // HD), axis=1)
        mask_ref[n] = jnp.where((r_col == r_row) & (lane <= sub), 0.0, -jnp.inf)
        cols_ref[span, :] = jnp.concatenate([crow_ref[:, span], enter_ref[:, span], spare], axis=0).T


def decayed(scores, c_col, c_row, mask):
    top, low = slice(0, HD), slice(HD, CHUNK)
    row_blocks = []
    for rows, width in ((top, HD), (low, CHUNK)):
        col = c_col[rows]
        col = col if width == HD else jnp.concatenate([col] * (width // HD), axis=1)
        weight = jnp.exp2(col - c_row[:, :width] + mask[rows, :width])
        row_blocks.append((scores[rows, :width] * weight).astype(BF16))
    row_blocks[0] = jnp.concatenate([row_blocks[0], jnp.zeros((HD, CHUNK - HD), BF16)], axis=1)
    return jnp.concatenate(row_blocks, axis=0)


def inside_kernel(
    chunks, first, steps, crow_ref, cols_ref, mask_ref, k_ref, v_ref, gain_ref, q_hbm, gate_hbm,
    grad_hbm, *refs,
):
    q_ref, gate_ring, grad_ring, attn_ref, gnorm_ref, turned_q_ref, probs_ring, probs_hbm, sems = (
        refs[-9:]
    )
    step = first + pl.program_id(0)
    slot = step % 2
    fetches = fetch_gates(step + 1, gate_hbm, grad_hbm, gate_ring, grad_ring, sems)
    fetches += fetch_q(step + 1, q_hbm, q_ref, sems.at[2])
    puts = put_probs(step - 1, probs_ring, probs_hbm, sems.at[3])
    pl.when(step + 1 < steps)(lambda: start(fetches))
    pl.when(step > 0)(lambda: start(puts))

    cols_now = turned(cols_ref, step * RING)
    late = []
    for g in range(RING):
        h = step * RING + g
        cols = slice(g * HD, (g + 1) * HD)
        mine = head_span(h)
        for n, span in enumerate(spans(chunks)):
            q = q_ref[span, mine]
            scores = dot(q, k_ref[span, mine], NT)
            c_row = crow_ref[pl.ds(h, 1), span]
            probs = decayed(scores, spread(cols_now[span], g), c_row, mask_ref.at[n])
            inside = dot(probs, v_ref[span, mine])
            sig = sigmoid(gate_ring[slot, span, cols].astype(F32))
            gnorm = grad_ring[slot, span, cols].astype(F32) * sig * gain_ref[0:1, mine]
            save(late)
            late = [
                (probs_ring, (slot, g, n), probs),
                (attn_ref, (span, mine), inside),
                (turned_q_ref, (h, slice(None), span), q.T),
                (gnorm_ref, (span, mine), gnorm.astype(BF16)),
            ]
    save(late)
    pl.when(step + 1 < steps)(lambda: wait(fetches))
    pl.when(step > 0)(lambda: wait(puts))


def first_head(part, half, reverse):
    if part is None:
        return 0
    core, _, _ = place(reverse)
    return (core if part == 0 else 1 - core) * half


def outside_kernel(chunks, last, entering, inputs, part, cols_ref, enter_ref, q_ref, gnorm_ref, loc_ref, *refs):
    in_refs = refs[:inputs]
    if part == 1:
        before_ref, inside_ref, _, attn_ref, held_ref, sums_ref, sq_ref, inner_ref = refs[inputs:]
    else:
        probs_ring, inside_ref, _, attn_ref, held_ref, sums_ref, probs_hbm = refs[inputs:-3]
        sq_ref, inner_ref, sem = refs[-3:]
        puts = put_probs(last, probs_ring, probs_hbm, sem.at[0])
    step = pl.program_id(0)
    steps = pl.num_programs(0)

    @pl.when(step == 0)
    def _():
        if part != 1:
            start(puts)
        sq_ref[...] = jnp.zeros_like(sq_ref)
        inner_ref[...] = jnp.zeros_like(inner_ref)

    start_head = first_head(part, steps * GROUP, False) + step * GROUP
    heads = [start_head + g for g in range(GROUP)]
    cols_now = turned(cols_ref, enter_ref.shape[0] + start_head)
    carries = [entering(in_refs, h) for h in heads]
    late = []
    for n, span in enumerate(spans(chunks)):
        squares = sq_ref[span, :]
        inners = inner_ref[span, :]
        for g, h in enumerate(heads):
            mine = head_span(h)
            held = carries[g].astype(BF16)
            enter = spread(cols_now[span], g)
            attn = inside_ref[span, mine] + enter * dot(q_ref[span, mine], held)
            squares = squares + attn * attn
            inners = inners + gnorm_ref[span, mine].astype(F32) * attn
            if n + 1 < chunks:
                passing = enter_ref[pl.ds(h, 1), span][:, CHUNK - 1 : CHUNK]
                carries[g] = passing * carries[g] + loc_ref[h, n]
            save(late)
            late = [(held_ref, (h, n), held), (attn_ref, (span, mine), attn)]
        late += [(sq_ref, (span, slice(None)), squares), (inner_ref, (span, slice(None)), inners)]
    save(late)

    @pl.when(step == steps - 1)
    def _():
        if part != 1:
            wait(puts)
        for i, ref in enumerate((sq_ref, inner_ref)):
            total = jnp.sum(ref[...].T, axis=0, keepdims=True)
            sums_ref[i : i + 1, :] = total + before_ref[i : i + 1, :] if part == 1 else total


def grad_kernel(chunks, parts, enter_ref, *refs):
    turned_q_ref, gnorm_ref, attn_ref, gate_hbm, grad_hbm, probs_hbm = refs[parts : parts + 6]
    agrad_ref, turned_ref, bloc_ref, back_ref, normed_ref = refs[parts + 6 : parts + 11]
    gate_ring, grad_ring, probs_ring, alpha_ref, beta_ref, sems = refs[parts + 11 :]
    step = pl.program_id(0)
    following = fetch_gates(0, gate_hbm, grad_hbm, gate_ring, grad_ring, sems)
    following += fetch_probs(0, probs_hbm, probs_ring, sems.at[2])

    @pl.when(step == 0)
    def _():
        start(following)
        sums = refs[0][...]
        for ref in refs[1:parts]:
            sums = sums + ref[...]
        inverse = lax.rsqrt(sums[0:1] / WIDTH + epsilon)
        alpha_ref[...] = column(inverse)
        beta_ref[...] = column(inverse * inverse * inverse * sums[1:2] / WIDTH)

    late = []
    for g in range(GROUP):
        h = step * GROUP + g
        mine = head_span(h)
        back = None
        for n, span in reversed(list(enumerate(spans(chunks)))):
            enter = enter_ref[pl.ds(h, 1), span]
            gnorm = gnorm_ref[span, mine].astype(F32)
            attn, alpha = attn_ref[span, mine], alpha_ref[span, :]
            agrad = alpha * gnorm - attn * beta_ref[span, :]
            agrad = agrad.astype(BF16)
            qkeyed = (turned_q_ref[h, :, span].astype(F32) * enter).astype(BF16)
            local = dot(qkeyed, agrad)
            back = local if back is None else local + enter[:, CHUNK - 1 : CHUNK] * back
            save(late)
            late = [
                (agrad_ref, (span, mine), agrad),
                (turned_ref, (h, slice(None), span), agrad.T),
                (normed_ref, (span, mine), (attn * alpha).astype(BF16)),
            ]
            if n > 0:
                late.append((bloc_ref, (h, n - 1), local))
        late.append((back_ref, h, back))
    save(late)

    @pl.when(step == pl.num_programs(0) - 1)
    def _():
        wait(following)


def inner_grad_kernel(
    chunks, first, steps, crow_ref, cols_ref, mask_ref, k_ref, v_ref, normed_ref, held_ref,
    agrad_ref, turned_q_ref, turned_agrad_ref, gain_ref, gate_hbm, grad_hbm, probs_hbm,
    *refs,
):
    dk_ref, dv_ref, gate_ring, grad_ring, probs_ring, out_ring, *outs_hbm, sems = refs[-10:]
    step = first + pl.program_id(0)
    slot = step % 2
    fetches = fetch_gates(step + 1, gate_hbm, grad_hbm, gate_ring, grad_ring, sems)
    fetches += fetch_probs(step + 1, probs_hbm, probs_ring, sems.at[2])
    puts = put_outs(step - 1, out_ring, outs_hbm, sems.at[pl.ds(3, 3)])
    pl.when(step + 1 < steps)(lambda: start(fetches))
    pl.when(step > 0)(lambda: start(puts))

    cols_now = turned(cols_ref, step * RING)
    late = []
    for g in range(RING):
        h = step * RING + g
        cols = slice(g * HD, (g + 1) * HD)
        mine = head_span(h)
        for n, span in enumerate(spans(chunks)):
            k, v, agrad = k_ref[span, mine], v_ref[span, mine], agrad_ref[span, mine]
            both = dot(agrad, jnp.concatenate([v, held_ref[h, n]], axis=0), NT)
            c_row = crow_ref[pl.ds(h, 1), span]
            dscore = decayed(both[:, :CHUNK], spread(cols_now[span], g), c_row, mask_ref.at[n])
            enter = spread(cols_now[span], crow_ref.shape[0] + g)
            dq = dot(dscore, k) + enter * both[:, CHUNK:]
            dv = dot(turned_agrad_ref[h, :, span], probs_ring[slot, g, n])
            dk = dot(turned_q_ref[h, :, span], dscore)
            normed = normed_ref[span, mine].astype(F32) * gain_ref[0:1, mine]
            sig = sigmoid(gate_ring[slot, span, cols].astype(F32))
            gated = normed * sig
            ggate = grad_ring[slot, span, cols].astype(F32) * gated * (1.0 - sig)
            save(late)
            late = [
                (out_ring, (slot, 0, span, cols), dq.astype(BF16)),
                (dv_ref, (h, slice(None), span), dv.astype(BF16)),
                (dk_ref, (h, slice(None), span), dk.astype(BF16)),
                (out_ring, (slot, 1, span, cols), gated.astype(BF16)),
                (out_ring, (slot, 2, span, cols), ggate.astype(BF16)),
            ]
    save(late)
    pl.when(step + 1 < steps)(lambda: wait(fetches))
    pl.when(step > 0)(lambda: wait(puts))


def outer_grad_kernel(chunks, last, entering, inputs, part, enter_ref, leave_ref, k_ref, v_ref, *refs):
    in_refs = refs[:inputs]
    dkin_ref, dvin_ref, bloc_ref = refs[inputs : inputs + 3]
    step = pl.program_id(0)
    steps = pl.num_programs(0)
    start_head = first_head(part, steps * GROUP, True) + step * GROUP
    if part == 1:
        *grads_hbm, parts_ref, sems = refs[-4:]
    else:
        out_ring = refs[inputs + 3]
        *outs_hbm, dk_hbm, dv_hbm, parts_ref, sems, last_sems = refs[-8:]
        grads_hbm = [dk_hbm, dv_hbm]
        puts = put_outs(last, out_ring, outs_hbm, last_sems)
        pl.when(step == 0)(lambda: start(puts))

    def put(back):
        slot = (step - back) % 2
        here = head_span(start_head - back * GROUP, GROUP)
        return [
            pltpu.make_async_copy(parts_ref.at[slot, i], out.at[:, here], sems.at[slot, i])
            for i, out in enumerate(grads_hbm)
        ]

    slot = step % 2
    pl.when(step > 1)(lambda: wait(put(2)))
    late = []
    for g in range(GROUP):
        h = start_head + g
        cols = slice(g * HD, (g + 1) * HD)
        mine = head_span(h)
        carry = entering(in_refs, h)
        for n, span in reversed(list(enumerate(spans(chunks)))):
            leave = leave_ref[pl.ds(h, 1), span]
            back = carry.astype(BF16)
            dk = dkin_ref[h, :, span].astype(F32) + leave * dot(back, v_ref[span, mine], NT)
            dv = dvin_ref[h, :, span].astype(F32) + leave * dot(back.T, k_ref[span, mine], NT)
            if n > 0:
                passing = enter_ref[pl.ds(h, 1), span][:, CHUNK - 1 : CHUNK]
                carry = bloc_ref[h, n - 1] + passing * carry
            save(late)
            late = [
                (parts_ref, (slot, 0, span, cols), dk.astype(BF16).T),
                (parts_ref, (slot, 1, span, cols), dv.astype(BF16).T),
            ]
    save(late)
    start(put(0))

    @pl.when(step == steps - 1)
    def _():
        pl.when(step > 0)(lambda: wait(put(1)))
        wait(put(0))
        if part != 1:
            wait(puts)


def hbm(x):
    return pltpu.with_memory_space_constraint(x, pltpu.HBM)


def kept(*arrays):
    spec = pl.BlockSpec(memory_space=pltpu.VMEM)
    return [(pltpu.with_memory_space_constraint(x, pltpu.VMEM), spec) for x in arrays]


def keep(dims, dtype):
    return pltpu.VMEM(dims, dtype), pl.BlockSpec(memory_space=pltpu.VMEM)


def add_kernel(a_ref, b_ref, out_ref):
    out_ref[...] = a_ref[...] + b_ref[...]


def call(kernel, grid, ins, outs, scratch=(), aliases=None, room=4, flops=0, moved=0, exps=0):
    return pl.pallas_call(
        kernel,
        grid=grid,
        in_specs=[spec for _, spec in ins],
        out_specs=[spec for _, spec in outs],
        out_shape=[shape for shape, _ in outs],
        scratch_shapes=list(scratch),
        input_output_aliases=aliases or {},
        compiler_params=pltpu.CompilerParams(
            dimension_semantics=("arbitrary",) * len(grid), vmem_limit_bytes=room * MIB
        ),
        cost_estimate=pl.CostEstimate(flops=flops, bytes_accessed=moved, transcendentals=exps),
    )(*[x for x, _ in ins])


def after(x, *others):
    return lax.optimization_barrier((x, *others))[0]


def across(x, flips, devices=8):
    return lax.ppermute(x, "seq", [(i, i ^ flips) for i in range(devices)])


def place(reverse):
    index = lax.axis_index("seq")
    index = 7 - index if reverse else index
    return lax.rem(index, 2), lax.rem(lax.div(index, 2), 2), lax.div(index, 4)


def pair_kernel(reverse, state_ref, other_ref, pass_ref, beside_ref, x_ref, y_ref, chip_ref):
    core, _, _ = place(reverse)
    quarter = x_ref.shape[0]
    chip_ref[...] = pass_ref[...] * beside_ref[...]
    for i in range(quarter):
        for at, out_ref in ((i, x_ref), (quarter + i, y_ref)):
            h = core * 2 * quarter + at
            mine, other = state_ref[h], other_ref[h]

            @pl.when(core == 0)
            def _():
                out_ref[i] = beside_ref[pl.ds(h, 1), :] * mine + other

            @pl.when(core == 1)
            def _():
                out_ref[i] = pass_ref[pl.ds(h, 1), :] * other + mine


def row_kernel(
    reverse, to_x_ref, to_y_ref, from_x_ref, from_y_ref, chip_ref, side_ref, far_ref,
    row_ref, sent_ref,
):
    core, x, y = place(reverse)
    quarter = row_ref.shape[0]
    for i in range(quarter):
        h = core * 2 * quarter + i
        hy = h + quarter

        @pl.when(x == 0)
        def _():
            row_ref[i] = side_ref[pl.ds(h, 1), :] * to_x_ref[i] + from_x_ref[i]

        @pl.when(x == 1)
        def _():
            row_ref[i] = chip_ref[pl.ds(h, 1), :] * from_x_ref[i] + to_x_ref[i]

        @pl.when(y == 0)
        def _():
            sent_ref[i] = to_y_ref[i]

        @pl.when((y == 1) & (x == 0))
        def _():
            far = far_ref[pl.ds(hy, 1), :] * from_y_ref[i]
            sent_ref[i] = chip_ref[pl.ds(hy, 1), :] * far + to_y_ref[i]

        @pl.when((y == 1) & (x == 1))
        def _():
            sent_ref[i] = from_y_ref[i]


def ahead_kernel(
    reverse, from_x_ref, from_y_ref, row_ref, sent_ref, side_ref, far_ref, out_ref,
):
    core, x, y = place(reverse)
    quarter = row_ref.shape[0]
    for i in range(quarter):
        h = core * 2 * quarter + i
        hy = h + quarter

        @pl.when((y == 0) & (x == 0))
        def _():
            out_ref[i] = jnp.zeros_like(out_ref[i])
            out_ref[quarter + i] = jnp.zeros_like(out_ref[i])

        @pl.when((y == 0) & (x == 1))
        def _():
            out_ref[i] = from_x_ref[i]
            out_ref[quarter + i] = sent_ref[i]

        @pl.when((y == 1) & (x == 0))
        def _():
            out_ref[i] = row_ref[i]
            out_ref[quarter + i] = far_ref[pl.ds(hy, 1), :] * from_y_ref[i] + sent_ref[i]

        @pl.when((y == 1) & (x == 1))
        def _():
            out_ref[i] = side_ref[pl.ds(h, 1), :] * row_ref[i] + from_x_ref[i]
            out_ref[quarter + i] = side_ref[pl.ds(hy, 1), :] * from_y_ref[i] + sent_ref[i]


def cube_entering(reverse, refs, h):
    chip_ref, other_ref, beside_pass_ref = refs
    core, _, _ = place(reverse)
    chip = chip_ref[lax.rem(h, chip_ref.shape[0])]
    through = beside_pass_ref[pl.ds(h, 1), :] * chip + other_ref[h]
    return jnp.where(core == 0, chip, through)


def plain_entering(refs, h):
    return refs[0][h]


def cube_scan(state, own_pass, passes, fill, finish, reverse):
    heads = state.shape[0]
    quarter = heads // 4
    part = keep((quarter, HD, HD), F32)

    other = across(state, 1)
    beside_pass = passes[0] if passes else across(own_pass, 1)
    other, beside_pass = lax.optimization_barrier((other, beside_pass, fill(0, state)))[:2]
    to_x, to_y, chip_pass = call(
        functools.partial(pair_kernel, reverse), (),
        kept(state, other, own_pass, beside_pass), [part, part, keep((heads, HD), F32)], room=ROOM,
    )

    from_x, from_y = across(to_x, 2), across(to_y, 4)
    x_pass, far_pass = passes[1:] if passes else (across(chip_pass, 2), across(chip_pass, 6))
    from_x, from_y, x_pass, far_pass = lax.optimization_barrier(
        (from_x, from_y, x_pass, far_pass, fill(1, to_y))
    )[:4]
    row, sent = call(
        functools.partial(row_kernel, reverse), (),
        kept(to_x, to_y, from_x, from_y, chip_pass, x_pass, far_pass), [part, part], room=ROOM,
    )

    row_in, sent_in = across(row, 4), across(sent, 2)
    row_in, sent_in = lax.optimization_barrier((row_in, sent_in, fill(2, sent)))[:2]
    (ahead,) = call(
        functools.partial(ahead_kernel, reverse), (),
        kept(from_x, from_y, row_in, sent_in, x_pass, far_pass),
        [keep((2 * quarter, HD, HD), F32)], room=ROOM,
    )

    beside = across(ahead, 1)
    entering = functools.partial(cube_entering, reverse)
    beside = after(beside, finish(0, entering, (ahead, other, beside_pass)))
    finish(1, entering, (beside, other, beside_pass))
    return beside_pass, x_pass, far_pass


def doubling_scan(state, own_pass, fill, reverse):
    devices = lax.axis_size("seq")
    index = lax.axis_index("seq")
    passes = lax.all_gather(own_pass, "seq")
    if reverse:
        passes = passes[::-1]
        index = devices - 1 - index
    route = lambda hop: [
        (i, i - hop if reverse else i + hop)
        for i in range(devices)
        if 0 <= (i - hop if reverse else i + hop) < devices
    ]
    for window in range(WINDOWS):
        state = after(state, fill(window, state))
    hop = 1
    while hop < devices:
        factor = lax.dynamic_index_in_dim(passes, index, 0, False)
        state = factor[:, None, :] * lax.ppermute(state, "seq", route(hop)) + state
        before = jnp.concatenate([jnp.zeros_like(passes[:hop]), passes[:-hop]], axis=0)
        passes = passes * before
        hop *= 2
    return lax.ppermute(state, "seq", route(1))


def scan_devices(state, own_pass, passes, fill, finish, reverse):
    if lax.axis_size("seq") == 8 and state.shape[0] % 4 == 0:
        return cube_scan(state, own_pass, passes, fill, finish, reverse)
    finish(None, plain_entering, (doubling_scan(state, own_pass, fill, reverse),))
    return None


def body(queries, key_rows, value_rows, log_decay, doc_start, gate_input, norm_gain, out_grad):
    rows, cols = queries.shape
    heads = cols // HD
    chunks = rows // CHUNK
    parts = lax.axis_size("head")
    grid = (heads // GROUP,)
    shares = [heads // 4]
    shares.append((heads - shares[0] + RING) // 2 // RING * RING)
    shares.append(heads - sum(shares))
    bases = [0, shares[0], heads - shares[2]]
    big = rows * cols * 2
    tile = 2 * rows * CHUNK * cols
    small = 2 * rows * HD * cols

    whole = lambda *dims: pl.BlockSpec(dims, lambda i: (0,) * len(dims))
    anywhere = pl.BlockSpec(memory_space=pl.ANY)

    by_head = (heads, HD, rows)
    local_dims = (heads, chunks, HD, HD)
    wide_out = (pltpu.HBM((rows, cols), BF16), anywhere)
    probs_out = (pltpu.HBM((heads, chunks, CHUNK, CHUNK), BF16), anywhere)
    ring = keep((2, rows, RING * HD), BF16)
    probs_ring = keep((2, RING, chunks, CHUNK, CHUNK), BF16)
    out_ring = keep((2, 3, rows, RING * HD), BF16)
    sems = pltpu.SemaphoreType.DMA
    queries, key_rows, value_rows, gate_input, out_grad = map(
        hbm, (queries, key_rows, value_rows, gate_input, out_grad)
    )
    doc_row = doc_start.reshape(1, rows)
    gain_row = norm_gain.reshape(1, cols)

    by_token = (rows, cols)
    steps = heads // GROUP
    (
        crow, enter, leave, rrow, keys, values, local, state, own_pass, gain, kept_q, *rings
    ) = call(
        functools.partial(state_kernel, chunks, steps),
        grid,
        [
            (hbm(x), anywhere)
            for x in (
                log_decay, doc_row, gain_row, key_rows, value_rows, queries, gate_input, out_grad
            )
        ],
        [keep((heads, rows), F32)] * 3
        + [
            keep((8, rows), F32), keep(by_token, BF16), keep(by_token, BF16),
            keep((heads, chunks - 1, HD, HD), F32), keep((heads, HD, HD), F32), keep((heads, HD), F32),
            keep((1, cols), F32), keep(by_token, BF16), ring, ring,
        ],
        [
            pltpu.VMEM((heads, rows), F32), pltpu.VMEM((1, rows), jnp.int32),
            sems((2, steps)), sems((3,)), sems((3,)),
        ],
        room=ROOM, flops=small, moved=2 * big,
    )

    ready = []
    made = [kept_q, *rings]

    def fill_forward(window, tie):
        if not ready:
            ready[:] = call(
                prepare_kernel, (), kept(after(rrow, tie), crow, enter),
                [keep((chunks, CHUNK, CHUNK), F32), keep((rows, HD), F32)],
                room=ROOM, flops=8 * rows * CHUNK,
            )
        mask, columns = ready
        ins = kept(after(crow, tie), columns, mask, keys, values, gain)
        ins += [(x, anywhere) for x in (queries, gate_input, out_grad)]
        aliases = {len(ins) + i: i for i in range(len(made))}
        ins += kept(*made[:7]) + [(hbm(x), anywhere) for x in made[7:]]
        made[:] = call(
            functools.partial(inside_kernel, chunks, bases[window] // RING, heads // RING),
            (shares[window] // RING,),
            ins,
            [
                keep(by_token, BF16), ring, ring, keep(by_token, F32), keep(by_token, BF16),
                keep(by_head, BF16), probs_ring, probs_out,
            ],
            [sems((4,))],
            aliases=aliases, room=ROOM,
            flops=2 * tile // WINDOWS, moved=5 * big // WINDOWS,
            exps=rows * (CHUNK + HD) * heads // WINDOWS,
        )
        return made[7]

    tall = pltpu.VMEM((rows, HD), F32)
    reduced = []

    def finish_forward(part, entering, refs):
        mask, columns = ready
        kept_q, _, _, inside, gnorm, _, probs_ringed, probs = made[:8]
        ins = kept(columns, enter, kept_q, gnorm, local, *refs)
        outs = [keep(by_token, F32), keep(local_dims, BF16), keep((2, rows), F32)]
        scratch = [tall, tall]
        if part == 1:
            aliases = {len(ins) + 1: 0, len(ins) + 2: 1}
            ins += kept(reduced[1], inside, reduced[0])
        else:
            aliases = {len(ins) + 1: 0, len(ins) + 2: 3}
            ins += kept(probs_ringed, inside) + [(hbm(probs), anywhere)]
            outs.append(probs_out)
            scratch.append(sems((1,)))
        results = call(
            functools.partial(
                outside_kernel, chunks, heads // RING - 1, entering, len(refs), part
            ),
            (steps if part is None else steps // 2,),
            ins, outs, scratch, aliases,
            room=ROOM, flops=small, moved=big,
        )
        made[3], reduced[:] = results[0], results[1:3]
        if part != 1:
            made[7] = results[3]
        return reduced[1]

    passes = scan_devices(state, own_pass, None, fill_forward, finish_forward, False)
    mask, columns = ready
    _, _, _, attn, gnorm, turned_q, _, probs = made
    held, sums = reduced

    apart = 1
    while apart < parts // 2:
        other_sums = lax.ppermute(sums, "head", [(i, i ^ apart) for i in range(parts)])
        (sums,) = call(add_kernel, (), kept(sums, other_sums), [keep((2, rows), F32)], room=ROOM)
        apart *= 2
    other_sums = lax.ppermute(sums, "head", [(i, i ^ apart) for i in range(parts)])

    agrad, turned_agrad, bloc, back, normed, *rings = call(
        functools.partial(grad_kernel, chunks, 2),
        grid,
        kept(enter, sums, other_sums, turned_q, gnorm, attn)
        + [(hbm(x), anywhere) for x in (gate_input, out_grad, probs)],
        [
            keep(by_token, BF16), keep(by_head, BF16), keep((heads, chunks - 1, HD, HD), F32),
            keep((heads, HD, HD), F32), keep(by_token, BF16), ring, ring, probs_ring,
        ],
        [tall, tall, sems((3,))],
        {4: 0},
        room=ROOM, flops=small, moved=big,
    )

    inner = [turned_q, turned_agrad, *rings]

    def fill_backward(window, tie):
        ins = kept(
            after(crow, tie), columns, mask, keys, values, normed, held, agrad, *inner[:2], gain
        )
        ins += [(hbm(x), anywhere) for x in (gate_input, out_grad, probs)]
        aliases = {8: 0, 9: 1}
        aliases.update({len(ins) - 2 + i: i for i in range(2, len(inner))})
        ins += kept(*inner[2:6]) + [(hbm(x), anywhere) for x in inner[6:]]
        inner[:] = call(
            functools.partial(inner_grad_kernel, chunks, bases[window] // RING, heads // RING),
            (shares[window] // RING,),
            ins,
            [keep(by_head, BF16)] * 2 + [ring, ring, probs_ring, out_ring] + [wide_out] * 3,
            [sems((6,))],
            aliases=aliases, room=ROOM,
            flops=(4 * tile + small) // WINDOWS, moved=7 * big // WINDOWS,
            exps=rows * (CHUNK + HD) * heads // WINDOWS,
        )
        return inner[6]

    grads = []

    def finish_backward(part, entering, refs):
        ins = kept(enter, leave, keys, values, *refs, *inner[:2], bloc)
        scratch = [pltpu.VMEM((2, 2, rows, GROUP * HD), BF16), sems((2, 2))]
        if part == 1:
            aliases = {len(ins): 0, len(ins) + 1: 1}
            ins += [(hbm(x), anywhere) for x in grads]
            outs = [wide_out] * 2
        else:
            aliases = {len(ins) + 1 + i: i for i in range(3)}
            ins += kept(inner[5]) + [(hbm(x), anywhere) for x in inner[6:]]
            outs = [wide_out] * 5
            scratch.append(sems((3,)))
        results = call(
            functools.partial(
                outer_grad_kernel, chunks, heads // RING - 1, entering, len(refs), part
            ),
            (steps if part is None else steps // 2,),
            ins, outs, scratch, aliases,
            room=ROOM, flops=2 * small, moved=2 * big,
        )
        grads[:] = results[-2:]
        if part != 1:
            inner[6:] = results[:3]
        return grads[0]

    scan_devices(back, own_pass, passes, fill_backward, finish_backward, True)
    dq, gated, gate_grad = inner[6:]
    return (gated, gate_grad, dq, *grads)


def solution(mesh):
    in_specs = (
        P("seq", "head"),
        P("seq", "head"),
        P("seq", "head"),
        P("head", "seq"),
        P("seq"),
        P("seq", "head"),
        P("head"),
        P("seq", "head"),
    )
    out_specs = (P("seq", "head"),) * 5
    return jax.shard_map(body, mesh=mesh, in_specs=in_specs, out_specs=out_specs, check_vma=False)
```

```python
import functools

import jax
import jax.numpy as jnp
from jax import lax
from jax.experimental import pallas as pl
from jax.experimental.pallas import tpu as pltpu
from jax.sharding import PartitionSpec as P

HEAD_TOTAL = 64
HD = 128
CHUNK = 256
GROUP = 2
RING = 2
AHEAD = 3
WINDOWS = 3
ROOM = 4
WIDTH = HEAD_TOTAL * HD

epsilon = 1e-06
LOG2E = 1.4426950408889634

F32 = jnp.float32
BF16 = jnp.bfloat16
MIB = 1024 * 1024
NT = ((1,), (1,))


def dot(a, b, dims=((1,), (0,))):
    return lax.dot_general(a, b, (dims, ((), ())), preferred_element_type=F32)


def chunk_cumsum(x):
    lane = lax.broadcasted_iota(jnp.int32, x.shape, 1) % CHUNK
    shift = 1
    while shift < CHUNK:
        x = x + jnp.where(lane >= shift, pltpu.roll(x, shift, 1), 0.0)
        shift *= 2
    return x


def spans(chunks):
    return [slice(n * CHUNK, (n + 1) * CHUNK) for n in range(chunks)]


def head_span(head, count=1):
    return pl.ds(pl.multiple_of(head * HD, HD), count * HD)


def save(stores):
    for ref, index, value in stores:
        ref[index] = value


def sigmoid(x):
    return 0.5 * jnp.tanh(0.5 * x) + 0.5


def spread(cols, lane):
    return jnp.broadcast_to(cols[:, lane : lane + 1], cols.shape)


def turned(cols_ref, lane):
    return pltpu.roll(cols_ref[...], (HD - lane) % HD, 1)


def column(row):
    return jnp.broadcast_to(row, (HD, row.shape[1])).T


def start(copies):
    for copy in copies:
        copy.start()


def wait(copies):
    for copy in copies:
        copy.wait()


def group_of(at):
    return head_span(at * RING, RING)


def fetch_gates(at, gate_hbm, grad_hbm, gate_ring, grad_ring, sems):
    slot = at % 2
    return [
        pltpu.make_async_copy(gate_hbm.at[:, group_of(at)], gate_ring.at[slot], sems.at[0]),
        pltpu.make_async_copy(grad_hbm.at[:, group_of(at)], grad_ring.at[slot], sems.at[1]),
    ]


def fetch_q(at, q_hbm, q_ref, sem):
    return [pltpu.make_async_copy(q_hbm.at[:, group_of(at)], q_ref.at[:, group_of(at)], sem)]


def fetch_probs(at, probs_hbm, probs_ring, sem):
    heads = pl.ds(at * RING, RING)
    return [pltpu.make_async_copy(probs_hbm.at[heads], probs_ring.at[at % 2], sem)]


def put_probs(at, probs_ring, probs_hbm, sem):
    heads = pl.ds(at * RING, RING)
    return [pltpu.make_async_copy(probs_ring.at[at % 2], probs_hbm.at[heads], sem)]


def put_outs(at, out_ring, outs_hbm, sems):
    return [
        pltpu.make_async_copy(out_ring.at[at % 2, i], out.at[:, group_of(at)], sems.at[i])
        for i, out in enumerate(outs_hbm)
    ]


def state_kernel(
    chunks, steps, lc_hbm, doc_hbm, gain_hbm, k_hbm, v_hbm, q_hbm, gate_hbm, grad_hbm,
    crow_ref, enter_ref, leave_ref, rrow_ref, k_ref, v_ref, loc_ref, state_ref, pass_ref,
    gain_ref, q_ref, gate_ring, grad_ring, lc_ref, doc_ref, sems, small_sems, next_sems,
):
    step = pl.program_id(0)
    small = [
        pltpu.make_async_copy(lc_hbm, lc_ref, small_sems.at[0]),
        pltpu.make_async_copy(doc_hbm, doc_ref, small_sems.at[1]),
        pltpu.make_async_copy(gain_hbm, gain_ref, small_sems.at[2]),
    ]
    following = fetch_gates(0, gate_hbm, grad_hbm, gate_ring, grad_ring, next_sems)
    following += fetch_q(0, q_hbm, q_ref, next_sems.at[2])

    def copies(at):
        here = head_span(at * GROUP, GROUP)
        return (
            pltpu.make_async_copy(k_hbm.at[:, here], k_ref.at[:, here], sems.at[0, at]),
            pltpu.make_async_copy(v_hbm.at[:, here], v_ref.at[:, here], sems.at[1, at]),
        )

    @pl.when(step == 0)
    def _():
        start(small)
        for at in range(min(AHEAD, steps)):
            start(copies(at))
        wait(small)
        c = chunk_cumsum(lc_ref[...] * LOG2E)
        r = chunk_cumsum(jnp.broadcast_to(doc_ref[...].astype(F32), (8, doc_ref.shape[1])))
        crow_ref[...] = c
        rrow_ref[...] = r
        enter_ref[...] = jnp.where(r[0:1] == 0.0, jnp.exp2(c), 0.0)
        for span in spans(chunks):
            cn, rn = c[:, span], r[0:1, span]
            leave_ref[:, span] = jnp.where(rn == rn[:, -1:], jnp.exp2(cn[:, -1:] - cn), 0.0)

    pl.when(step + AHEAD < steps)(lambda: start(copies(step + AHEAD)))
    pl.when(step + AHEAD == steps)(lambda: start(following))
    wait(copies(step))
    late = []
    for g in range(GROUP):
        h = step * GROUP + g
        mine = head_span(h)
        state = None
        total = None
        for n, span in enumerate(spans(chunks)):
            keyed = (k_ref[span, mine].T.astype(F32) * leave_ref[pl.ds(h, 1), span]).astype(BF16)
            local = dot(keyed, v_ref[span, mine])
            passing = enter_ref[pl.ds(h, 1), span][:, CHUNK - 1 : CHUNK]
            state = local if state is None else passing * state + local
            total = passing if total is None else passing * total
            save(late)
            late = [(loc_ref, (h, n), local)] if n + 1 < chunks else []
        late.append((state_ref, h, state))
        late.append((pass_ref, (pl.ds(h, 1), slice(None)), jnp.broadcast_to(total, (1, HD))))
    save(late)

    @pl.when(step == steps - 1)
    def _():
        wait(following)


def prepare_kernel(rrow_ref, crow_ref, enter_ref, mask_ref, cols_ref):
    sub = lax.broadcasted_iota(jnp.int32, (CHUNK, CHUNK), 0)
    lane = lax.broadcasted_iota(jnp.int32, (CHUNK, CHUNK), 1)
    spare = jnp.zeros((HD - 2 * crow_ref.shape[0], CHUNK), F32)
    for n, span in enumerate(spans(mask_ref.shape[0])):
        r_row = rrow_ref[0:1, span]
        r_col = jnp.concatenate([column(r_row)] * (CHUNK // HD), axis=1)
        mask_ref[n] = jnp.where((r_col == r_row) & (lane <= sub), 0.0, -jnp.inf)
        cols_ref[span, :] = jnp.concatenate([crow_ref[:, span], enter_ref[:, span], spare], axis=0).T


def decayed(scores, c_col, c_row, mask):
    top, low = slice(0, HD), slice(HD, CHUNK)
    row_blocks = []
    for rows, width in ((top, HD), (low, CHUNK)):
        col = c_col[rows]
        col = col if width == HD else jnp.concatenate([col] * (width // HD), axis=1)
        weight = jnp.exp2(col - c_row[:, :width] + mask[rows, :width])
        row_blocks.append((scores[rows, :width] * weight).astype(BF16))
    row_blocks[0] = jnp.concatenate([row_blocks[0], jnp.zeros((HD, CHUNK - HD), BF16)], axis=1)
    return jnp.concatenate(row_blocks, axis=0)


def inside_kernel(
    chunks, first, steps, crow_ref, cols_ref, mask_ref, k_ref, v_ref, gain_ref, q_hbm, gate_hbm,
    grad_hbm, *refs,
):
    q_ref, gate_ring, grad_ring, attn_ref, gnorm_ref, probs_ring, probs_hbm, sems = refs[-8:]
    step = first + pl.program_id(0)
    slot = step % 2
    fetches = fetch_gates(step + 1, gate_hbm, grad_hbm, gate_ring, grad_ring, sems)
    fetches += fetch_q(step + 1, q_hbm, q_ref, sems.at[2])
    puts = put_probs(step - 1, probs_ring, probs_hbm, sems.at[3])
    pl.when(step + 1 < steps)(lambda: start(fetches))
    pl.when(step > 0)(lambda: start(puts))

    cols_now = turned(cols_ref, step * RING)
    late = []
    for g in range(RING):
        h = step * RING + g
        cols = slice(g * HD, (g + 1) * HD)
        mine = head_span(h)
        for n, span in enumerate(spans(chunks)):
            q = q_ref[span, mine]
            scores = dot(q, k_ref[span, mine], NT)
            c_row = crow_ref[pl.ds(h, 1), span]
            probs = decayed(scores, spread(cols_now[span], g), c_row, mask_ref.at[n])
            inside = dot(probs, v_ref[span, mine])
            sig = sigmoid(gate_ring[slot, span, cols].astype(F32))
            gnorm = grad_ring[slot, span, cols].astype(F32) * sig * gain_ref[0:1, mine]
            save(late)
            late = [
                (probs_ring, (slot, g, n), probs),
                (attn_ref, (span, mine), inside),
                (gnorm_ref, (span, mine), gnorm.astype(BF16)),
            ]
    save(late)
    pl.when(step + 1 < steps)(lambda: wait(fetches))
    pl.when(step > 0)(lambda: wait(puts))


def first_head(part, half, reverse):
    if part is None:
        return 0
    core, _, _ = place(reverse)
    return (core if part == 0 else 1 - core) * half


def outside_kernel(chunks, last, entering, inputs, part, cols_ref, enter_ref, q_ref, gnorm_ref, loc_ref, *refs):
    in_refs = refs[:inputs]
    if part == 1:
        before_ref, inside_ref, _, attn_ref, held_ref, sums_ref, sq_ref, inner_ref = refs[inputs:]
    else:
        probs_ring, inside_ref, _, attn_ref, held_ref, sums_ref, probs_hbm = refs[inputs:-3]
        sq_ref, inner_ref, sem = refs[-3:]
        puts = put_probs(last, probs_ring, probs_hbm, sem.at[0])
    step = pl.program_id(0)
    steps = pl.num_programs(0)

    @pl.when(step == 0)
    def _():
        if part != 1:
            start(puts)
        sq_ref[...] = jnp.zeros_like(sq_ref)
        inner_ref[...] = jnp.zeros_like(inner_ref)

    start_head = first_head(part, steps * GROUP, False) + step * GROUP
    heads = [start_head + g for g in range(GROUP)]
    cols_now = turned(cols_ref, enter_ref.shape[0] + start_head)
    carries = [entering(in_refs, h) for h in heads]
    late = []
    for n, span in enumerate(spans(chunks)):
        squares = sq_ref[span, :]
        inners = inner_ref[span, :]
        for g, h in enumerate(heads):
            mine = head_span(h)
            held = carries[g].astype(BF16)
            enter = spread(cols_now[span], g)
            attn = inside_ref[span, mine] + enter * dot(q_ref[span, mine], held)
            squares = squares + attn * attn
            inners = inners + gnorm_ref[span, mine].astype(F32) * attn
            if n + 1 < chunks:
                passing = enter_ref[pl.ds(h, 1), span][:, CHUNK - 1 : CHUNK]
                carries[g] = passing * carries[g] + loc_ref[h, n]
            save(late)
            late = [(held_ref, (h, n), held), (attn_ref, (span, mine), attn)]
        late += [(sq_ref, (span, slice(None)), squares), (inner_ref, (span, slice(None)), inners)]
    save(late)

    @pl.when(step == steps - 1)
    def _():
        if part != 1:
            wait(puts)
        for i, ref in enumerate((sq_ref, inner_ref)):
            total = jnp.sum(ref[...].T, axis=0, keepdims=True)
            sums_ref[i : i + 1, :] = total + before_ref[i : i + 1, :] if part == 1 else total


def turn_kernel(chunks, first, q_ref, attn_ref, *refs):
    turned_ref, flat_ref, done_ref = refs[-3:]
    step = pl.program_id(0)
    done_ref[...] = jnp.zeros_like(done_ref)
    late = []
    for g in range(GROUP):
        h = first + step * GROUP + g
        mine = head_span(h)
        for span in spans(chunks):
            turned_q = q_ref[span, mine].T
            flat = attn_ref[span, mine].astype(BF16)
            save(late)
            late = [(turned_ref, (h, slice(None), span), turned_q), (flat_ref, (span, mine), flat)]
    save(late)


def grad_kernel(chunks, enter_ref, sums_ref, others_ref, _, *refs):
    turned_q_ref, gnorm_ref, attn_ref, gate_hbm, grad_hbm, probs_hbm = refs[:6]
    agrad_ref, bloc_ref, back_ref, alpha_ref = refs[6:10]
    gate_ring, grad_ring, probs_ring, beta_ref, sems = refs[10:]
    step = pl.program_id(0)
    following = fetch_gates(0, gate_hbm, grad_hbm, gate_ring, grad_ring, sems)
    following += fetch_probs(0, probs_hbm, probs_ring, sems.at[2])

    @pl.when(step == 0)
    def _():
        start(following)
        sums = sums_ref[...] + others_ref[...]
        inverse = lax.rsqrt(sums[0:1] / WIDTH + epsilon)
        alpha_ref[...] = column(inverse)
        beta_ref[...] = column(inverse * inverse * inverse * sums[1:2] / WIDTH)

    late = []
    for g in range(GROUP):
        h = step * GROUP + g
        mine = head_span(h)
        back = None
        for n, span in reversed(list(enumerate(spans(chunks)))):
            enter = enter_ref[pl.ds(h, 1), span]
            gnorm = gnorm_ref[span, mine].astype(F32)
            attn, alpha = attn_ref[span, mine], alpha_ref[span, :]
            agrad = alpha * gnorm - attn * beta_ref[span, :]
            agrad = agrad.astype(BF16)
            qkeyed = (turned_q_ref[h, :, span].astype(F32) * enter).astype(BF16)
            local = dot(qkeyed, agrad)
            back = local if back is None else local + enter[:, CHUNK - 1 : CHUNK] * back
            save(late)
            late = [
                (agrad_ref, (span, mine), agrad),
            ]
            if n > 0:
                late.append((bloc_ref, (h, n - 1), local))
        late.append((back_ref, h, back))
    save(late)

    @pl.when(step == pl.num_programs(0) - 1)
    def _():
        wait(following)


def inner_grad_kernel(
    chunks, first, steps, crow_ref, alpha_ref, cols_ref, mask_ref, k_ref, v_ref, flat_ref,
    held_ref, agrad_ref, turned_q_ref, gain_ref, gate_hbm, grad_hbm, probs_hbm,
    *refs,
):
    dk_ref, gate_ring, grad_ring, probs_ring, dv_ref, out_ring, *outs_hbm, sems = refs[-10:]
    step = first + pl.program_id(0)
    slot = step % 2
    fetches = fetch_gates(step + 1, gate_hbm, grad_hbm, gate_ring, grad_ring, sems)
    fetches += fetch_probs(step + 1, probs_hbm, probs_ring, sems.at[2])
    puts = put_outs(step - 1, out_ring, outs_hbm, sems.at[pl.ds(3, 3)])
    pl.when(step + 1 < steps)(lambda: start(fetches))
    pl.when(step > 0)(lambda: start(puts))

    cols_now = turned(cols_ref, step * RING)
    late = []
    for g in range(RING):
        h = step * RING + g
        cols = slice(g * HD, (g + 1) * HD)
        mine = head_span(h)
        for n, span in enumerate(spans(chunks)):
            k, v, agrad = k_ref[span, mine], v_ref[span, mine], agrad_ref[span, mine]
            both = dot(agrad, jnp.concatenate([v, held_ref[h, n]], axis=0), NT)
            c_row = crow_ref[pl.ds(h, 1), span]
            dscore = decayed(both[:, :CHUNK], spread(cols_now[span], g), c_row, mask_ref.at[n])
            enter = spread(cols_now[span], crow_ref.shape[0] + g)
            dq = dot(dscore, k) + enter * both[:, CHUNK:]
            dv = dot(agrad.T, probs_ring[slot, g, n])
            dk = dot(turned_q_ref[h, :, span], dscore)
            normed = flat_ref[span, mine].astype(F32) * alpha_ref[span, :] * gain_ref[0:1, mine]
            sig = sigmoid(gate_ring[slot, span, cols].astype(F32))
            gated = normed * sig
            ggate = grad_ring[slot, span, cols].astype(F32) * gated * (1.0 - sig)
            save(late)
            late = [
                (out_ring, (slot, 0, span, cols), dq.astype(BF16)),
                (dv_ref, (h, slice(None), span), dv.astype(BF16)),
                (dk_ref, (h, slice(None), span), dk.astype(BF16)),
                (out_ring, (slot, 1, span, cols), gated.astype(BF16)),
                (out_ring, (slot, 2, span, cols), ggate.astype(BF16)),
            ]
    save(late)
    pl.when(step + 1 < steps)(lambda: wait(fetches))
    pl.when(step > 0)(lambda: wait(puts))


def outer_grad_kernel(chunks, last, entering, inputs, part, enter_ref, leave_ref, k_ref, v_ref, *refs):
    in_refs = refs[:inputs]
    dkin_ref, dvin_ref, bloc_ref = refs[inputs : inputs + 3]
    step = pl.program_id(0)
    steps = pl.num_programs(0)
    start_head = first_head(part, steps * GROUP, True) + step * GROUP
    if part == 1:
        *grads_hbm, parts_ref, sems = refs[-4:]
    else:
        out_ring = refs[inputs + 3]
        *outs_hbm, dk_hbm, dv_hbm, parts_ref, sems, last_sems = refs[-8:]
        grads_hbm = [dk_hbm, dv_hbm]
        puts = put_outs(last, out_ring, outs_hbm, last_sems)
        pl.when(step == 0)(lambda: start(puts))

    def put(back):
        slot = (step - back) % 2
        here = head_span(start_head - back * GROUP, GROUP)
        return [
            pltpu.make_async_copy(parts_ref.at[slot, i], out.at[:, here], sems.at[slot, i])
            for i, out in enumerate(grads_hbm)
        ]

    slot = step % 2
    pl.when(step > 1)(lambda: wait(put(2)))
    late = []
    for g in range(GROUP):
        h = start_head + g
        cols = slice(g * HD, (g + 1) * HD)
        mine = head_span(h)
        carry = entering(in_refs, h)
        for n, span in reversed(list(enumerate(spans(chunks)))):
            leave = leave_ref[pl.ds(h, 1), span]
            back = carry.astype(BF16)
            dk = dkin_ref[h, :, span].astype(F32) + leave * dot(back, v_ref[span, mine], NT)
            dv = dvin_ref[h, :, span].astype(F32) + leave * dot(back.T, k_ref[span, mine], NT)
            if n > 0:
                passing = enter_ref[pl.ds(h, 1), span][:, CHUNK - 1 : CHUNK]
                carry = bloc_ref[h, n - 1] + passing * carry
            save(late)
            late = [
                (parts_ref, (slot, 0, span, cols), dk.astype(BF16).T),
                (parts_ref, (slot, 1, span, cols), dv.astype(BF16).T),
            ]
    save(late)
    start(put(0))

    @pl.when(step == steps - 1)
    def _():
        pl.when(step > 0)(lambda: wait(put(1)))
        wait(put(0))
        if part != 1:
            wait(puts)


def hbm(x):
    return pltpu.with_memory_space_constraint(x, pltpu.HBM)


def kept(*arrays):
    spec = pl.BlockSpec(memory_space=pltpu.VMEM)
    return [(pltpu.with_memory_space_constraint(x, pltpu.VMEM), spec) for x in arrays]


def keep(dims, dtype):
    return pltpu.VMEM(dims, dtype), pl.BlockSpec(memory_space=pltpu.VMEM)


def add_kernel(a_ref, b_ref, _, out_ref):
    out_ref[...] = a_ref[...] + b_ref[...]


def call(kernel, grid, ins, outs, scratch=(), aliases=None, flops=0, moved=0, exps=0):
    return pl.pallas_call(
        kernel,
        grid=grid,
        in_specs=[spec for _, spec in ins],
        out_specs=[spec for _, spec in outs],
        out_shape=[shape for shape, _ in outs],
        scratch_shapes=list(scratch),
        input_output_aliases=aliases or {},
        compiler_params=pltpu.CompilerParams(
            dimension_semantics=("arbitrary",) * len(grid), vmem_limit_bytes=ROOM * MIB
        ),
        cost_estimate=pl.CostEstimate(flops=flops, bytes_accessed=moved, transcendentals=exps),
    )(*[x for x, _ in ins])


def after(x, *others):
    return lax.optimization_barrier((x, *others))[0]


def across(x, flips, devices=8):
    return lax.ppermute(x, "seq", [(i, i ^ flips) for i in range(devices)])


def place(reverse):
    index = lax.axis_index("seq")
    index = 7 - index if reverse else index
    return lax.rem(index, 2), lax.rem(lax.div(index, 2), 2), lax.div(index, 4)


def pair_kernel(reverse, state_ref, other_ref, pass_ref, beside_ref, x_ref, y_ref, chip_ref):
    core, _, _ = place(reverse)
    quarter = x_ref.shape[0]
    chip_ref[...] = pass_ref[...] * beside_ref[...]
    for i in range(quarter):
        for at, out_ref in ((i, x_ref), (quarter + i, y_ref)):
            h = core * 2 * quarter + at
            mine, other = state_ref[h], other_ref[h]

            @pl.when(core == 0)
            def _():
                out_ref[i] = beside_ref[pl.ds(h, 1), :] * mine + other

            @pl.when(core == 1)
            def _():
                out_ref[i] = pass_ref[pl.ds(h, 1), :] * other + mine


def row_kernel(
    reverse, to_x_ref, to_y_ref, from_x_ref, from_y_ref, chip_ref, side_ref, far_ref,
    row_ref, sent_ref,
):
    core, x, y = place(reverse)
    quarter = row_ref.shape[0]
    for i in range(quarter):
        h = core * 2 * quarter + i
        hy = h + quarter

        @pl.when(x == 0)
        def _():
            row_ref[i] = side_ref[pl.ds(h, 1), :] * to_x_ref[i] + from_x_ref[i]

        @pl.when(x == 1)
        def _():
            row_ref[i] = chip_ref[pl.ds(h, 1), :] * from_x_ref[i] + to_x_ref[i]

        @pl.when(y == 0)
        def _():
            sent_ref[i] = to_y_ref[i]

        @pl.when((y == 1) & (x == 0))
        def _():
            far = far_ref[pl.ds(hy, 1), :] * from_y_ref[i]
            sent_ref[i] = chip_ref[pl.ds(hy, 1), :] * far + to_y_ref[i]

        @pl.when((y == 1) & (x == 1))
        def _():
            sent_ref[i] = from_y_ref[i]


def ahead_kernel(
    reverse, from_x_ref, from_y_ref, row_ref, sent_ref, side_ref, far_ref, out_ref,
):
    core, x, y = place(reverse)
    quarter = row_ref.shape[0]
    for i in range(quarter):
        h = core * 2 * quarter + i
        hy = h + quarter

        @pl.when((y == 0) & (x == 0))
        def _():
            out_ref[i] = jnp.zeros_like(out_ref[i])
            out_ref[quarter + i] = jnp.zeros_like(out_ref[i])

        @pl.when((y == 0) & (x == 1))
        def _():
            out_ref[i] = from_x_ref[i]
            out_ref[quarter + i] = sent_ref[i]

        @pl.when((y == 1) & (x == 0))
        def _():
            out_ref[i] = row_ref[i]
            out_ref[quarter + i] = far_ref[pl.ds(hy, 1), :] * from_y_ref[i] + sent_ref[i]

        @pl.when((y == 1) & (x == 1))
        def _():
            out_ref[i] = side_ref[pl.ds(h, 1), :] * row_ref[i] + from_x_ref[i]
            out_ref[quarter + i] = side_ref[pl.ds(hy, 1), :] * from_y_ref[i] + sent_ref[i]


def cube_entering(reverse, refs, h):
    chip_ref, other_ref, beside_pass_ref = refs
    core, _, _ = place(reverse)
    chip = chip_ref[lax.rem(h, chip_ref.shape[0])]
    through = beside_pass_ref[pl.ds(h, 1), :] * chip + other_ref[h]
    return jnp.where(core == 0, chip, through)


def plain_entering(refs, h):
    return refs[0][h]


def cube_scan(state, own_pass, passes, fill, finish, reverse):
    heads = state.shape[0]
    quarter = heads // 4
    part = keep((quarter, HD, HD), F32)

    other = across(state, 1)
    beside_pass = passes[0] if passes else across(own_pass, 1)
    other, beside_pass = lax.optimization_barrier((other, beside_pass, fill(0, state)))[:2]
    to_x, to_y, chip_pass = call(
        functools.partial(pair_kernel, reverse), (),
        kept(state, other, own_pass, beside_pass), [part, part, keep((heads, HD), F32)],
    )

    from_x, from_y = across(to_x, 2), across(to_y, 4)
    x_pass, far_pass = passes[1:] if passes else (across(chip_pass, 2), across(chip_pass, 6))
    from_x, from_y, x_pass, far_pass = lax.optimization_barrier(
        (from_x, from_y, x_pass, far_pass, fill(1, to_y))
    )[:4]
    row, sent = call(
        functools.partial(row_kernel, reverse), (),
        kept(to_x, to_y, from_x, from_y, chip_pass, x_pass, far_pass), [part, part],
    )

    row_in, sent_in = across(row, 4), across(sent, 2)
    row_in, sent_in = lax.optimization_barrier((row_in, sent_in, fill(2, sent)))[:2]
    (ahead,) = call(
        functools.partial(ahead_kernel, reverse), (),
        kept(from_x, from_y, row_in, sent_in, x_pass, far_pass),
        [keep((2 * quarter, HD, HD), F32)],
    )

    beside = across(ahead, 1)
    entering = functools.partial(cube_entering, reverse)
    beside = after(beside, finish(0, entering, (ahead, other, beside_pass)))
    finish(1, entering, (beside, other, beside_pass))
    return beside_pass, x_pass, far_pass


def doubling_scan(state, own_pass, fill, reverse):
    devices = lax.axis_size("seq")
    index = lax.axis_index("seq")
    passes = lax.all_gather(own_pass, "seq")
    if reverse:
        passes = passes[::-1]
        index = devices - 1 - index
    route = lambda hop: [
        (i, i - hop if reverse else i + hop)
        for i in range(devices)
        if 0 <= (i - hop if reverse else i + hop) < devices
    ]
    for window in range(WINDOWS):
        state = after(state, fill(window, state))
    hop = 1
    while hop < devices:
        factor = lax.dynamic_index_in_dim(passes, index, 0, False)
        state = factor[:, None, :] * lax.ppermute(state, "seq", route(hop)) + state
        before = jnp.concatenate([jnp.zeros_like(passes[:hop]), passes[:-hop]], axis=0)
        passes = passes * before
        hop *= 2
    return lax.ppermute(state, "seq", route(1))


def scan_devices(state, own_pass, passes, fill, finish, reverse):
    if lax.axis_size("seq") == 8 and state.shape[0] % 4 == 0:
        return cube_scan(state, own_pass, passes, fill, finish, reverse)
    finish(None, plain_entering, (doubling_scan(state, own_pass, fill, reverse),))
    return None


def body(queries, key_rows, value_rows, log_decay, doc_start, gate_input, norm_gain, out_grad):
    rows, cols = queries.shape
    heads = cols // HD
    chunks = rows // CHUNK
    parts = lax.axis_size("head")
    grid = (heads // GROUP,)
    shares = [heads // 4]
    shares.append((heads - shares[0] + RING) // 2 // RING * RING)
    shares.append(heads - sum(shares))
    bases = [0, shares[0], heads - shares[2]]
    big = rows * cols * 2
    tile = 2 * rows * CHUNK * cols
    small = 2 * rows * HD * cols

    whole = lambda *dims: pl.BlockSpec(dims, lambda i: (0,) * len(dims))
    anywhere = pl.BlockSpec(memory_space=pl.ANY)

    by_head = (heads, HD, rows)
    local_dims = (heads, chunks, HD, HD)
    wide_out = (pltpu.HBM((rows, cols), BF16), anywhere)
    probs_out = (pltpu.HBM((heads, chunks, CHUNK, CHUNK), BF16), anywhere)
    ring = keep((2, rows, RING * HD), BF16)
    probs_ring = keep((2, RING, chunks, CHUNK, CHUNK), BF16)
    out_ring = keep((2, 3, rows, RING * HD), BF16)
    sems = pltpu.SemaphoreType.DMA
    queries, key_rows, value_rows, gate_input, out_grad = map(
        hbm, (queries, key_rows, value_rows, gate_input, out_grad)
    )
    doc_row = doc_start.reshape(1, rows)
    gain_row = norm_gain.reshape(1, cols)

    by_token = (rows, cols)
    steps = heads // GROUP
    (
        crow, enter, leave, rrow, keys, values, local, state, own_pass, gain, kept_q, *rings
    ) = call(
        functools.partial(state_kernel, chunks, steps),
        grid,
        [
            (hbm(x), anywhere)
            for x in (
                log_decay, doc_row, gain_row, key_rows, value_rows, queries, gate_input, out_grad
            )
        ],
        [keep((heads, rows), F32)] * 3
        + [
            keep((8, rows), F32), keep(by_token, BF16), keep(by_token, BF16),
            keep((heads, chunks - 1, HD, HD), F32), keep((heads, HD, HD), F32), keep((heads, HD), F32),
            keep((1, cols), F32), keep(by_token, BF16), ring, ring,
        ],
        [
            pltpu.VMEM((heads, rows), F32), pltpu.VMEM((1, rows), jnp.int32),
            sems((2, steps)), sems((3,)), sems((3,)),
        ],
        flops=small, moved=2 * big,
    )

    ready = []
    made = [kept_q, *rings]

    def fill_forward(window, tie):
        if not ready:
            ready[:] = call(
                prepare_kernel, (), kept(after(rrow, tie), crow, enter),
                [keep((chunks, CHUNK, CHUNK), F32), keep((rows, HD), F32)],
                flops=8 * rows * CHUNK,
            )
        mask, columns = ready
        ins = kept(after(crow, tie), columns, mask, keys, values, gain)
        ins += [(x, anywhere) for x in (queries, gate_input, out_grad)]
        aliases = {len(ins) + i: i for i in range(len(made))}
        ins += kept(*made[:6]) + [(hbm(x), anywhere) for x in made[6:]]
        made[:] = call(
            functools.partial(inside_kernel, chunks, bases[window] // RING, heads // RING),
            (shares[window] // RING,),
            ins,
            [
                keep(by_token, BF16), ring, ring, keep(by_token, F32), keep(by_token, BF16),
                probs_ring, probs_out,
            ],
            [sems((4,))],
            aliases=aliases,
            flops=2 * tile // WINDOWS, moved=5 * big // WINDOWS,
            exps=rows * (CHUNK + HD) * heads // WINDOWS,
        )
        return made[6]

    tall = pltpu.VMEM((rows, HD), F32)
    reduced = []

    def finish_forward(part, entering, refs):
        mask, columns = ready
        kept_q, _, _, inside, gnorm, probs_ringed, probs = made
        ins = kept(columns, enter, kept_q, gnorm, local, *refs)
        outs = [keep(by_token, F32), keep(local_dims, BF16), keep((2, rows), F32)]
        scratch = [tall, tall]
        if part == 1:
            aliases = {len(ins) + 1: 0, len(ins) + 2: 1}
            ins += kept(reduced[1], inside, reduced[0])
        else:
            aliases = {len(ins) + 1: 0, len(ins) + 2: 3}
            ins += kept(probs_ringed, inside) + [(hbm(probs), anywhere)]
            outs.append(probs_out)
            scratch.append(sems((1,)))
        results = call(
            functools.partial(
                outside_kernel, chunks, heads // RING - 1, entering, len(refs), part
            ),
            (steps if part is None else steps // 2,),
            ins, outs, scratch, aliases,
            flops=small, moved=big,
        )
        made[3], reduced[:] = results[0], results[1:3]
        if part != 1:
            made[6] = results[3]
        return reduced[1]

    passes = scan_devices(state, own_pass, None, fill_forward, finish_forward, False)
    mask, columns = ready
    kept_q, _, _, attn, gnorm, _, probs = made
    held, sums = reduced

    flat = []
    halves = [0, heads // 2]
    token = keep((8, HD), F32)

    def turn(sums):
        first = halves.pop(0)
        results = call(
            functools.partial(turn_kernel, chunks, first),
            (steps // 2,),
            kept(kept_q, attn, sums, *flat),
            [keep(by_head, BF16), keep(by_token, BF16), token],
            aliases={3 + i: i for i in range(len(flat))},
            flops=rows * cols, moved=2 * big,
        )
        flat[:] = results[:2]
        return results[2]

    apart = 1
    while True:
        other_sums = lax.ppermute(sums, "head", [(i, i ^ apart) for i in range(parts)])
        done = turn(sums) if halves else done
        apart *= 2
        if apart >= parts:
            break
        (sums,) = call(add_kernel, (), kept(sums, other_sums, done), [keep((2, rows), F32)])
    while halves:
        done = turn(sums)
    turned_q, attn_flat = flat

    agrad, bloc, back, alpha, *rings = call(
        functools.partial(grad_kernel, chunks),
        grid,
        kept(enter, sums, other_sums, done, turned_q, gnorm, attn)
        + [(hbm(x), anywhere) for x in (gate_input, out_grad, probs)],
        [
            keep(by_token, BF16), keep((heads, chunks - 1, HD, HD), F32),
            keep((heads, HD, HD), F32), keep((rows, HD), F32), ring, ring, probs_ring,
        ],
        [tall, sems((3,))],
        {5: 0},
        flops=small, moved=big,
    )

    inner = [turned_q, *rings]

    def fill_backward(window, tie):
        ins = kept(
            after(crow, tie), alpha, columns, mask, keys, values, attn_flat, held, agrad, inner[0],
            gain,
        )
        ins += [(hbm(x), anywhere) for x in (gate_input, out_grad, probs)]
        aliases = {9: 0}
        aliases.update({len(ins) - 1 + i: i for i in range(1, len(inner))})
        ins += kept(*inner[1:6]) + [(hbm(x), anywhere) for x in inner[6:]]
        inner[:] = call(
            functools.partial(inner_grad_kernel, chunks, bases[window] // RING, heads // RING),
            (shares[window] // RING,),
            ins,
            [keep(by_head, BF16), ring, ring, probs_ring, keep(by_head, BF16), out_ring]
            + [wide_out] * 3,
            [sems((6,))],
            aliases=aliases,
            flops=(4 * tile + small) // WINDOWS, moved=7 * big // WINDOWS,
            exps=rows * (CHUNK + HD) * heads // WINDOWS,
        )
        return inner[6]

    grads = []

    def finish_backward(part, entering, refs):
        ins = kept(enter, leave, keys, values, *refs, inner[0], inner[4], bloc)
        scratch = [pltpu.VMEM((2, 2, rows, GROUP * HD), BF16), sems((2, 2))]
        if part == 1:
            aliases = {len(ins): 0, len(ins) + 1: 1}
            ins += [(hbm(x), anywhere) for x in grads]
            outs = [wide_out] * 2
        else:
            aliases = {len(ins) + 1 + i: i for i in range(3)}
            ins += kept(inner[5]) + [(hbm(x), anywhere) for x in inner[6:]]
            outs = [wide_out] * 5
            scratch.append(sems((3,)))
        results = call(
            functools.partial(
                outer_grad_kernel, chunks, heads // RING - 1, entering, len(refs), part
            ),
            (steps if part is None else steps // 2,),
            ins, outs, scratch, aliases,
            flops=2 * small, moved=2 * big,
        )
        grads[:] = results[-2:]
        if part != 1:
            inner[6:] = results[:3]
        return grads[0]

    scan_devices(back, own_pass, passes, fill_backward, finish_backward, True)
    dq, gated, gate_grad = inner[6:]
    return (gated, gate_grad, dq, *grads)


def solution(mesh):
    in_specs = (
        P("seq", "head"),
        P("seq", "head"),
        P("seq", "head"),
        P("head", "seq"),
        P("seq"),
        P("seq", "head"),
        P("head"),
        P("seq", "head"),
    )
    out_specs = (P("seq", "head"),) * 5
    return jax.shard_map(body, mesh=mesh, in_specs=in_specs, out_specs=out_specs, check_vma=False)
```

```python
import functools

import jax
import jax.numpy as jnp
from jax import lax
from jax.experimental import pallas as pl
from jax.experimental.pallas import tpu as pltpu
from jax.sharding import PartitionSpec as P

HEAD_TOTAL = 64
HD = 128
CHUNK = 256
GROUP = 2
RING = 2
AHEAD = 3
WINDOWS = 3
ROOM = 4
WIDTH = HEAD_TOTAL * HD

epsilon = 1e-06
LOG2E = 1.4426950408889634

F32 = jnp.float32
BF16 = jnp.bfloat16
MIB = 1024 * 1024
NT = ((1,), (1,))


def dot(a, b, dims=((1,), (0,))):
    return lax.dot_general(a, b, (dims, ((), ())), preferred_element_type=F32)


def chunk_cumsum(x):
    lane = lax.broadcasted_iota(jnp.int32, x.shape, 1) % CHUNK
    shift = 1
    while shift < CHUNK:
        x = x + jnp.where(lane >= shift, pltpu.roll(x, shift, 1), 0.0)
        shift *= 2
    return x


def spans(chunks):
    return [slice(n * CHUNK, (n + 1) * CHUNK) for n in range(chunks)]


def head_span(head, count=1):
    return pl.ds(pl.multiple_of(head * HD, HD), count * HD)


def save(stores):
    for ref, index, value in stores:
        ref[index] = value


def save_probs(probs_ref, h, n, probs):
    left, right = slice(0, CHUNK), slice(CHUNK, CHUNK + HD)
    return [
        (probs_ref, (h, n, left), probs[:, :HD]),
        (probs_ref, (h, n, right), probs[HD:, HD:]),
    ]


def load_probs(probs_ref, h, n):
    right = jnp.concatenate([jnp.zeros((HD, HD), BF16), probs_ref[h, n, CHUNK:, :]], axis=0)
    return jnp.concatenate([probs_ref[h, n, :CHUNK, :], right], axis=1)


def sigmoid(x):
    return 0.5 * jnp.tanh(0.5 * x) + 0.5


def spread(cols, lane):
    return jnp.broadcast_to(cols[:, lane : lane + 1], cols.shape)


def turned(cols_ref, lane):
    return pltpu.roll(cols_ref[...], (HD - lane) % HD, 1)


def column(row):
    return jnp.broadcast_to(row, (HD, row.shape[1])).T


def start(copies):
    for copy in copies:
        copy.start()


def wait(copies):
    for copy in copies:
        copy.wait()


def group_of(at):
    return head_span(at * RING, RING)


def fetch_gates(at, gate_hbm, grad_hbm, gate_ring, grad_ring, sems):
    slot = at % 2
    return [
        pltpu.make_async_copy(gate_hbm.at[:, group_of(at)], gate_ring.at[slot], sems.at[0]),
        pltpu.make_async_copy(grad_hbm.at[:, group_of(at)], grad_ring.at[slot], sems.at[1]),
    ]


def fetch_q(at, q_hbm, q_ref, sem):
    return [pltpu.make_async_copy(q_hbm.at[:, group_of(at)], q_ref.at[:, group_of(at)], sem)]


def put_outs(at, out_ring, outs_hbm, sems):
    return [
        pltpu.make_async_copy(out_ring.at[at % 2, i], out.at[:, group_of(at)], sems.at[i])
        for i, out in enumerate(outs_hbm)
    ]


def state_kernel(
    chunks, steps, lc_hbm, doc_hbm, gain_hbm, k_hbm, v_hbm, q_hbm, gate_hbm, grad_hbm,
    crow_ref, enter_ref, leave_ref, rrow_ref, k_ref, v_ref, loc_ref, state_ref, pass_ref,
    gain_ref, q_ref, gate_ring, grad_ring, lc_ref, doc_ref, sems, small_sems, next_sems,
):
    step = pl.program_id(0)
    small = [
        pltpu.make_async_copy(lc_hbm, lc_ref, small_sems.at[0]),
        pltpu.make_async_copy(doc_hbm, doc_ref, small_sems.at[1]),
        pltpu.make_async_copy(gain_hbm, gain_ref, small_sems.at[2]),
    ]
    following = fetch_gates(0, gate_hbm, grad_hbm, gate_ring, grad_ring, next_sems)
    following += fetch_q(0, q_hbm, q_ref, next_sems.at[2])

    def copies(at):
        here = head_span(at * GROUP, GROUP)
        return (
            pltpu.make_async_copy(k_hbm.at[:, here], k_ref.at[:, here], sems.at[0, at]),
            pltpu.make_async_copy(v_hbm.at[:, here], v_ref.at[:, here], sems.at[1, at]),
        )

    @pl.when(step == 0)
    def _():
        start(small)
        for at in range(min(AHEAD, steps)):
            start(copies(at))
        wait(small)
        c = chunk_cumsum(lc_ref[...] * LOG2E)
        r = chunk_cumsum(jnp.broadcast_to(doc_ref[...].astype(F32), (8, doc_ref.shape[1])))
        crow_ref[...] = c
        rrow_ref[...] = r
        enter_ref[...] = jnp.where(r[0:1] == 0.0, jnp.exp2(c), 0.0)
        for span in spans(chunks):
            cn, rn = c[:, span], r[0:1, span]
            leave_ref[:, span] = jnp.where(rn == rn[:, -1:], jnp.exp2(cn[:, -1:] - cn), 0.0)

    pl.when(step + AHEAD < steps)(lambda: start(copies(step + AHEAD)))
    pl.when(step + AHEAD == steps)(lambda: start(following))
    wait(copies(step))
    late = []
    for g in range(GROUP):
        h = step * GROUP + g
        mine = head_span(h)
        state = None
        total = None
        for n, span in enumerate(spans(chunks)):
            keyed = (k_ref[span, mine].T.astype(F32) * leave_ref[pl.ds(h, 1), span]).astype(BF16)
            local = dot(keyed, v_ref[span, mine])
            passing = enter_ref[pl.ds(h, 1), span][:, CHUNK - 1 : CHUNK]
            state = local if state is None else passing * state + local
            total = passing if total is None else passing * total
            save(late)
            late = [(loc_ref, (h, n), local)] if n + 1 < chunks else []
        late.append((state_ref, h, state))
        late.append((pass_ref, (pl.ds(h, 1), slice(None)), jnp.broadcast_to(total, (1, HD))))
    save(late)

    @pl.when(step == steps - 1)
    def _():
        wait(following)


def prepare_kernel(rrow_ref, crow_ref, enter_ref, mask_ref, cols_ref):
    sub = lax.broadcasted_iota(jnp.int32, (CHUNK, CHUNK), 0)
    lane = lax.broadcasted_iota(jnp.int32, (CHUNK, CHUNK), 1)
    spare = jnp.zeros((HD - 2 * crow_ref.shape[0], CHUNK), F32)
    for n, span in enumerate(spans(mask_ref.shape[0])):
        r_row = rrow_ref[0:1, span]
        r_col = jnp.concatenate([column(r_row)] * (CHUNK // HD), axis=1)
        mask_ref[n] = jnp.where((r_col == r_row) & (lane <= sub), 0.0, -jnp.inf)
        cols_ref[span, :] = jnp.concatenate([crow_ref[:, span], enter_ref[:, span], spare], axis=0).T


def decayed(scores, c_col, c_row, mask):
    top, low = slice(0, HD), slice(HD, CHUNK)
    row_blocks = []
    for rows, width in ((top, HD), (low, CHUNK)):
        col = c_col[rows]
        col = col if width == HD else jnp.concatenate([col] * (width // HD), axis=1)
        weight = jnp.exp2(col - c_row[:, :width] + mask[rows, :width])
        row_blocks.append((scores[rows, :width] * weight).astype(BF16))
    row_blocks[0] = jnp.concatenate([row_blocks[0], jnp.zeros((HD, CHUNK - HD), BF16)], axis=1)
    return jnp.concatenate(row_blocks, axis=0)


def inside_kernel(
    chunks, first, steps, crow_ref, cols_ref, mask_ref, k_ref, v_ref, gain_ref, q_hbm, gate_hbm,
    grad_hbm, *refs,
):
    q_ref, gate_ring, grad_ring, attn_ref, gnorm_ref, probs_ref, sems = refs[-7:]
    step = first + pl.program_id(0)
    slot = step % 2
    fetches = fetch_gates(step + 1, gate_hbm, grad_hbm, gate_ring, grad_ring, sems)
    fetches += fetch_q(step + 1, q_hbm, q_ref, sems.at[2])
    pl.when(step + 1 < steps)(lambda: start(fetches))

    cols_now = turned(cols_ref, step * RING)
    late = []
    for g in range(RING):
        h = step * RING + g
        cols = slice(g * HD, (g + 1) * HD)
        mine = head_span(h)
        for n, span in enumerate(spans(chunks)):
            q = q_ref[span, mine]
            scores = dot(q, k_ref[span, mine], NT)
            c_row = crow_ref[pl.ds(h, 1), span]
            probs = decayed(scores, spread(cols_now[span], g), c_row, mask_ref.at[n])
            inside = dot(probs, v_ref[span, mine])
            sig = sigmoid(gate_ring[slot, span, cols].astype(F32))
            gnorm = grad_ring[slot, span, cols].astype(F32) * sig * gain_ref[0:1, mine]
            save(late)
            late = save_probs(probs_ref, h, n, probs)
            late += [
                (attn_ref, (span, mine), inside),
                (gnorm_ref, (span, mine), gnorm.astype(BF16)),
            ]
    save(late)
    pl.when(step + 1 < steps)(lambda: wait(fetches))


def first_head(part, half, reverse):
    if part is None:
        return 0
    core, _, _ = place(reverse)
    return (core if part == 0 else 1 - core) * half


def outside_kernel(chunks, entering, inputs, part, cols_ref, enter_ref, q_ref, gnorm_ref, loc_ref, *refs):
    in_refs = refs[:inputs]
    if part == 1:
        before_ref, inside_ref, _, attn_ref, held_ref, sums_ref, sq_ref, inner_ref = refs[inputs:]
    else:
        inside_ref, attn_ref, held_ref, sums_ref, sq_ref, inner_ref = refs[inputs:]
    step = pl.program_id(0)
    steps = pl.num_programs(0)

    @pl.when(step == 0)
    def _():
        sq_ref[...] = jnp.zeros_like(sq_ref)
        inner_ref[...] = jnp.zeros_like(inner_ref)

    start_head = first_head(part, steps * GROUP, False) + step * GROUP
    heads = [start_head + g for g in range(GROUP)]
    cols_now = turned(cols_ref, enter_ref.shape[0] + start_head)
    carries = [entering(in_refs, h) for h in heads]
    late = []
    for n, span in enumerate(spans(chunks)):
        squares = sq_ref[span, :]
        inners = inner_ref[span, :]
        for g, h in enumerate(heads):
            mine = head_span(h)
            held = carries[g].astype(BF16)
            enter = spread(cols_now[span], g)
            attn = inside_ref[span, mine] + enter * dot(q_ref[span, mine], held)
            squares = squares + attn * attn
            inners = inners + gnorm_ref[span, mine].astype(F32) * attn
            if n + 1 < chunks:
                passing = enter_ref[pl.ds(h, 1), span][:, CHUNK - 1 : CHUNK]
                carries[g] = passing * carries[g] + loc_ref[h, n]
            save(late)
            late = [(held_ref, (h, n), held), (attn_ref, (span, mine), attn)]
        late += [(sq_ref, (span, slice(None)), squares), (inner_ref, (span, slice(None)), inners)]
    save(late)

    @pl.when(step == steps - 1)
    def _():
        for i, ref in enumerate((sq_ref, inner_ref)):
            total = jnp.sum(ref[...].T, axis=0, keepdims=True)
            sums_ref[i : i + 1, :] = total + before_ref[i : i + 1, :] if part == 1 else total


def turn_kernel(chunks, first, q_ref, attn_ref, *refs):
    turned_ref, flat_ref, done_ref = refs[-3:]
    step = pl.program_id(0)
    done_ref[...] = jnp.zeros_like(done_ref)
    late = []
    for g in range(GROUP):
        h = first + step * GROUP + g
        mine = head_span(h)
        for span in spans(chunks):
            turned_q = q_ref[span, mine].T
            flat = attn_ref[span, mine].astype(BF16)
            save(late)
            late = [(turned_ref, (h, slice(None), span), turned_q), (flat_ref, (span, mine), flat)]
    save(late)


def grad_kernel(chunks, enter_ref, sums_ref, others_ref, _, *refs):
    turned_q_ref, gnorm_ref, attn_ref, gate_hbm, grad_hbm = refs[:5]
    agrad_ref, bloc_ref, back_ref, alpha_ref = refs[5:9]
    gate_ring, grad_ring, beta_ref, sems = refs[9:]
    step = pl.program_id(0)
    following = fetch_gates(0, gate_hbm, grad_hbm, gate_ring, grad_ring, sems)

    @pl.when(step == 0)
    def _():
        start(following)
        sums = sums_ref[...] + others_ref[...]
        inverse = lax.rsqrt(sums[0:1] / WIDTH + epsilon)
        alpha_ref[...] = column(inverse)
        beta_ref[...] = column(inverse * inverse * inverse * sums[1:2] / WIDTH)

    late = []
    for g in range(GROUP):
        h = step * GROUP + g
        mine = head_span(h)
        back = None
        for n, span in reversed(list(enumerate(spans(chunks)))):
            enter = enter_ref[pl.ds(h, 1), span]
            gnorm = gnorm_ref[span, mine].astype(F32)
            attn, alpha = attn_ref[span, mine], alpha_ref[span, :]
            agrad = alpha * gnorm - attn * beta_ref[span, :]
            agrad = agrad.astype(BF16)
            qkeyed = (turned_q_ref[h, :, span].astype(F32) * enter).astype(BF16)
            local = dot(qkeyed, agrad)
            back = local if back is None else local + enter[:, CHUNK - 1 : CHUNK] * back
            save(late)
            late = [
                (agrad_ref, (span, mine), agrad),
            ]
            if n > 0:
                late.append((bloc_ref, (h, n - 1), local))
        late.append((back_ref, h, back))
    save(late)

    @pl.when(step == pl.num_programs(0) - 1)
    def _():
        wait(following)


def inner_grad_kernel(
    chunks, first, steps, crow_ref, alpha_ref, cols_ref, mask_ref, k_ref, v_ref, flat_ref,
    held_ref, agrad_ref, probs_ref, turned_q_ref, gain_ref, gate_hbm, grad_hbm,
    *refs,
):
    dk_ref, gate_ring, grad_ring, dv_ref, out_ring, *outs_hbm, sems = refs[-9:]
    step = first + pl.program_id(0)
    slot = step % 2
    fetches = fetch_gates(step + 1, gate_hbm, grad_hbm, gate_ring, grad_ring, sems)
    puts = put_outs(step - 1, out_ring, outs_hbm, sems.at[pl.ds(2, 3)])
    pl.when(step + 1 < steps)(lambda: start(fetches))
    pl.when(step > 0)(lambda: start(puts))

    cols_now = turned(cols_ref, step * RING)
    late = []
    for g in range(RING):
        h = step * RING + g
        cols = slice(g * HD, (g + 1) * HD)
        mine = head_span(h)
        for n, span in enumerate(spans(chunks)):
            k, v, agrad = k_ref[span, mine], v_ref[span, mine], agrad_ref[span, mine]
            both = dot(agrad, jnp.concatenate([v, held_ref[h, n]], axis=0), NT)
            c_row = crow_ref[pl.ds(h, 1), span]
            dscore = decayed(both[:, :CHUNK], spread(cols_now[span], g), c_row, mask_ref.at[n])
            enter = spread(cols_now[span], crow_ref.shape[0] + g)
            dq = dot(dscore, k) + enter * both[:, CHUNK:]
            dv = dot(agrad.T, load_probs(probs_ref, h, n))
            dk = dot(turned_q_ref[h, :, span], dscore)
            normed = flat_ref[span, mine].astype(F32) * alpha_ref[span, :] * gain_ref[0:1, mine]
            sig = sigmoid(gate_ring[slot, span, cols].astype(F32))
            gated = normed * sig
            ggate = grad_ring[slot, span, cols].astype(F32) * gated * (1.0 - sig)
            save(late)
            late = [
                (out_ring, (slot, 0, span, cols), dq.astype(BF16)),
                (dv_ref, (h, slice(None), span), dv.astype(BF16)),
                (dk_ref, (h, slice(None), span), dk.astype(BF16)),
                (out_ring, (slot, 1, span, cols), gated.astype(BF16)),
                (out_ring, (slot, 2, span, cols), ggate.astype(BF16)),
            ]
    save(late)
    pl.when(step + 1 < steps)(lambda: wait(fetches))
    pl.when(step > 0)(lambda: wait(puts))


def outer_grad_kernel(chunks, last, entering, inputs, part, enter_ref, leave_ref, k_ref, v_ref, *refs):
    in_refs = refs[:inputs]
    dkin_ref, dvin_ref, bloc_ref = refs[inputs : inputs + 3]
    step = pl.program_id(0)
    steps = pl.num_programs(0)
    start_head = first_head(part, steps * GROUP, True) + step * GROUP
    if part == 1:
        *grads_hbm, parts_ref, sems = refs[-4:]
    else:
        out_ring = refs[inputs + 3]
        *outs_hbm, dk_hbm, dv_hbm, parts_ref, sems, last_sems = refs[-8:]
        grads_hbm = [dk_hbm, dv_hbm]
        puts = put_outs(last, out_ring, outs_hbm, last_sems)
        pl.when(step == 0)(lambda: start(puts))

    def put(back):
        slot = (step - back) % 2
        here = head_span(start_head - back * GROUP, GROUP)
        return [
            pltpu.make_async_copy(parts_ref.at[slot, i], out.at[:, here], sems.at[slot, i])
            for i, out in enumerate(grads_hbm)
        ]

    slot = step % 2
    pl.when(step > 1)(lambda: wait(put(2)))
    late = []
    for g in range(GROUP):
        h = start_head + g
        cols = slice(g * HD, (g + 1) * HD)
        mine = head_span(h)
        carry = entering(in_refs, h)
        for n, span in reversed(list(enumerate(spans(chunks)))):
            leave = leave_ref[pl.ds(h, 1), span]
            back = carry.astype(BF16)
            dk = dkin_ref[h, :, span].astype(F32) + leave * dot(back, v_ref[span, mine], NT)
            dv = dvin_ref[h, :, span].astype(F32) + leave * dot(back.T, k_ref[span, mine], NT)
            if n > 0:
                passing = enter_ref[pl.ds(h, 1), span][:, CHUNK - 1 : CHUNK]
                carry = bloc_ref[h, n - 1] + passing * carry
            save(late)
            late = [
                (parts_ref, (slot, 0, span, cols), dk.astype(BF16).T),
                (parts_ref, (slot, 1, span, cols), dv.astype(BF16).T),
            ]
    save(late)
    start(put(0))

    @pl.when(step == steps - 1)
    def _():
        pl.when(step > 0)(lambda: wait(put(1)))
        wait(put(0))
        if part != 1:
            wait(puts)


def hbm(x):
    return pltpu.with_memory_space_constraint(x, pltpu.HBM)


def kept(*arrays):
    spec = pl.BlockSpec(memory_space=pltpu.VMEM)
    return [(pltpu.with_memory_space_constraint(x, pltpu.VMEM), spec) for x in arrays]


def keep(dims, dtype):
    return pltpu.VMEM(dims, dtype), pl.BlockSpec(memory_space=pltpu.VMEM)


def add_kernel(a_ref, b_ref, _, out_ref):
    out_ref[...] = a_ref[...] + b_ref[...]


def call(kernel, grid, ins, outs, scratch=(), aliases=None, flops=0, moved=0, exps=0):
    return pl.pallas_call(
        kernel,
        grid=grid,
        in_specs=[spec for _, spec in ins],
        out_specs=[spec for _, spec in outs],
        out_shape=[shape for shape, _ in outs],
        scratch_shapes=list(scratch),
        input_output_aliases=aliases or {},
        compiler_params=pltpu.CompilerParams(
            dimension_semantics=("arbitrary",) * len(grid), vmem_limit_bytes=ROOM * MIB
        ),
        cost_estimate=pl.CostEstimate(flops=flops, bytes_accessed=moved, transcendentals=exps),
    )(*[x for x, _ in ins])


def after(x, *others):
    return lax.optimization_barrier((x, *others))[0]


def across(x, flips, devices=8):
    return lax.ppermute(x, "seq", [(i, i ^ flips) for i in range(devices)])


def place(reverse):
    index = lax.axis_index("seq")
    index = 7 - index if reverse else index
    return lax.rem(index, 2), lax.rem(lax.div(index, 2), 2), lax.div(index, 4)


def pair_kernel(reverse, state_ref, other_ref, pass_ref, beside_ref, x_ref, y_ref, chip_ref):
    core, _, _ = place(reverse)
    quarter = x_ref.shape[0]
    chip_ref[...] = pass_ref[...] * beside_ref[...]
    for i in range(quarter):
        for at, out_ref in ((i, x_ref), (quarter + i, y_ref)):
            h = core * 2 * quarter + at
            mine, other = state_ref[h], other_ref[h]

            @pl.when(core == 0)
            def _():
                out_ref[i] = beside_ref[pl.ds(h, 1), :] * mine + other

            @pl.when(core == 1)
            def _():
                out_ref[i] = pass_ref[pl.ds(h, 1), :] * other + mine


def row_kernel(
    reverse, to_x_ref, to_y_ref, from_x_ref, from_y_ref, chip_ref, side_ref, far_ref,
    row_ref, sent_ref,
):
    core, x, y = place(reverse)
    quarter = row_ref.shape[0]
    for i in range(quarter):
        h = core * 2 * quarter + i
        hy = h + quarter

        @pl.when(x == 0)
        def _():
            row_ref[i] = side_ref[pl.ds(h, 1), :] * to_x_ref[i] + from_x_ref[i]

        @pl.when(x == 1)
        def _():
            row_ref[i] = chip_ref[pl.ds(h, 1), :] * from_x_ref[i] + to_x_ref[i]

        @pl.when(y == 0)
        def _():
            sent_ref[i] = to_y_ref[i]

        @pl.when((y == 1) & (x == 0))
        def _():
            far = far_ref[pl.ds(hy, 1), :] * from_y_ref[i]
            sent_ref[i] = chip_ref[pl.ds(hy, 1), :] * far + to_y_ref[i]

        @pl.when((y == 1) & (x == 1))
        def _():
            sent_ref[i] = from_y_ref[i]


def ahead_kernel(
    reverse, from_x_ref, from_y_ref, row_ref, sent_ref, side_ref, far_ref, out_ref,
):
    core, x, y = place(reverse)
    quarter = row_ref.shape[0]
    for i in range(quarter):
        h = core * 2 * quarter + i
        hy = h + quarter

        @pl.when((y == 0) & (x == 0))
        def _():
            out_ref[i] = jnp.zeros_like(out_ref[i])
            out_ref[quarter + i] = jnp.zeros_like(out_ref[i])

        @pl.when((y == 0) & (x == 1))
        def _():
            out_ref[i] = from_x_ref[i]
            out_ref[quarter + i] = sent_ref[i]

        @pl.when((y == 1) & (x == 0))
        def _():
            out_ref[i] = row_ref[i]
            out_ref[quarter + i] = far_ref[pl.ds(hy, 1), :] * from_y_ref[i] + sent_ref[i]

        @pl.when((y == 1) & (x == 1))
        def _():
            out_ref[i] = side_ref[pl.ds(h, 1), :] * row_ref[i] + from_x_ref[i]
            out_ref[quarter + i] = side_ref[pl.ds(hy, 1), :] * from_y_ref[i] + sent_ref[i]


def cube_entering(reverse, refs, h):
    chip_ref, other_ref, beside_pass_ref = refs
    core, _, _ = place(reverse)
    chip = chip_ref[lax.rem(h, chip_ref.shape[0])]
    through = beside_pass_ref[pl.ds(h, 1), :] * chip + other_ref[h]
    return jnp.where(core == 0, chip, through)


def plain_entering(refs, h):
    return refs[0][h]


def cube_scan(state, own_pass, passes, fill, finish, reverse):
    heads = state.shape[0]
    quarter = heads // 4
    part = keep((quarter, HD, HD), F32)

    other = across(state, 1)
    beside_pass = passes[0] if passes else across(own_pass, 1)
    other, beside_pass = lax.optimization_barrier((other, beside_pass, fill(0, state)))[:2]
    to_x, to_y, chip_pass = call(
        functools.partial(pair_kernel, reverse), (),
        kept(state, other, own_pass, beside_pass), [part, part, keep((heads, HD), F32)],
    )

    from_x, from_y = across(to_x, 2), across(to_y, 4)
    x_pass, far_pass = passes[1:] if passes else (across(chip_pass, 2), across(chip_pass, 6))
    from_x, from_y, x_pass, far_pass = lax.optimization_barrier(
        (from_x, from_y, x_pass, far_pass, fill(1, to_y))
    )[:4]
    row, sent = call(
        functools.partial(row_kernel, reverse), (),
        kept(to_x, to_y, from_x, from_y, chip_pass, x_pass, far_pass), [part, part],
    )

    row_in, sent_in = across(row, 4), across(sent, 2)
    row_in, sent_in = lax.optimization_barrier((row_in, sent_in, fill(2, sent)))[:2]
    (ahead,) = call(
        functools.partial(ahead_kernel, reverse), (),
        kept(from_x, from_y, row_in, sent_in, x_pass, far_pass),
        [keep((2 * quarter, HD, HD), F32)],
    )

    beside = across(ahead, 1)
    entering = functools.partial(cube_entering, reverse)
    beside = after(beside, finish(0, entering, (ahead, other, beside_pass)))
    finish(1, entering, (beside, other, beside_pass))
    return beside_pass, x_pass, far_pass


def doubling_scan(state, own_pass, fill, reverse):
    devices = lax.axis_size("seq")
    index = lax.axis_index("seq")
    passes = lax.all_gather(own_pass, "seq")
    if reverse:
        passes = passes[::-1]
        index = devices - 1 - index
    route = lambda hop: [
        (i, i - hop if reverse else i + hop)
        for i in range(devices)
        if 0 <= (i - hop if reverse else i + hop) < devices
    ]
    for window in range(WINDOWS):
        state = after(state, fill(window, state))
    hop = 1
    while hop < devices:
        factor = lax.dynamic_index_in_dim(passes, index, 0, False)
        state = factor[:, None, :] * lax.ppermute(state, "seq", route(hop)) + state
        before = jnp.concatenate([jnp.zeros_like(passes[:hop]), passes[:-hop]], axis=0)
        passes = passes * before
        hop *= 2
    return lax.ppermute(state, "seq", route(1))


def scan_devices(state, own_pass, passes, fill, finish, reverse):
    if lax.axis_size("seq") == 8 and state.shape[0] % 4 == 0:
        return cube_scan(state, own_pass, passes, fill, finish, reverse)
    finish(None, plain_entering, (doubling_scan(state, own_pass, fill, reverse),))
    return None


def body(queries, key_rows, value_rows, log_decay, doc_start, gate_input, norm_gain, out_grad):
    rows, cols = queries.shape
    heads = cols // HD
    chunks = rows // CHUNK
    parts = lax.axis_size("head")
    grid = (heads // GROUP,)
    shares = [heads // 4]
    shares.append((heads - shares[0] + RING) // 2 // RING * RING)
    shares.append(heads - sum(shares))
    bases = [0, shares[0], heads - shares[2]]
    big = rows * cols * 2
    tile = 2 * rows * CHUNK * cols
    small = 2 * rows * HD * cols

    whole = lambda *dims: pl.BlockSpec(dims, lambda i: (0,) * len(dims))
    anywhere = pl.BlockSpec(memory_space=pl.ANY)

    by_head = (heads, HD, rows)
    local_dims = (heads, chunks, HD, HD)
    wide_out = (pltpu.HBM((rows, cols), BF16), anywhere)
    ring = keep((2, rows, RING * HD), BF16)
    probs_kept = keep((heads, chunks, CHUNK + HD, HD), BF16)
    out_ring = keep((2, 3, rows, RING * HD), BF16)
    sems = pltpu.SemaphoreType.DMA
    queries, key_rows, value_rows, gate_input, out_grad = map(
        hbm, (queries, key_rows, value_rows, gate_input, out_grad)
    )
    doc_row = doc_start.reshape(1, rows)
    gain_row = norm_gain.reshape(1, cols)

    by_token = (rows, cols)
    steps = heads // GROUP
    (
        crow, enter, leave, rrow, keys, values, local, state, own_pass, gain, kept_q, *rings
    ) = call(
        functools.partial(state_kernel, chunks, steps),
        grid,
        [
            (hbm(x), anywhere)
            for x in (
                log_decay, doc_row, gain_row, key_rows, value_rows, queries, gate_input, out_grad
            )
        ],
        [keep((heads, rows), F32)] * 3
        + [
            keep((8, rows), F32), keep(by_token, BF16), keep(by_token, BF16),
            keep((heads, chunks - 1, HD, HD), F32), keep((heads, HD, HD), F32), keep((heads, HD), F32),
            keep((1, cols), F32), keep(by_token, BF16), ring, ring,
        ],
        [
            pltpu.VMEM((heads, rows), F32), pltpu.VMEM((1, rows), jnp.int32),
            sems((2, steps)), sems((3,)), sems((3,)),
        ],
        flops=small, moved=2 * big,
    )

    ready = []
    made = [kept_q, *rings]

    def fill_forward(window, tie):
        if not ready:
            ready[:] = call(
                prepare_kernel, (), kept(after(rrow, tie), crow, enter),
                [keep((chunks, CHUNK, CHUNK), F32), keep((rows, HD), F32)],
                flops=8 * rows * CHUNK,
            )
        mask, columns = ready
        ins = kept(after(crow, tie), columns, mask, keys, values, gain)
        ins += [(x, anywhere) for x in (queries, gate_input, out_grad)]
        aliases = {len(ins) + i: i for i in range(len(made))}
        ins += kept(*made)
        made[:] = call(
            functools.partial(inside_kernel, chunks, bases[window] // RING, heads // RING),
            (shares[window] // RING,),
            ins,
            [
                keep(by_token, BF16), ring, ring, keep(by_token, F32), keep(by_token, BF16),
                probs_kept,
            ],
            [sems((3,))],
            aliases=aliases,
            flops=2 * tile // WINDOWS, moved=5 * big // WINDOWS,
            exps=rows * (CHUNK + HD) * heads // WINDOWS,
        )
        return made[1]

    tall = pltpu.VMEM((rows, HD), F32)
    reduced = []

    def finish_forward(part, entering, refs):
        mask, columns = ready
        kept_q, _, _, inside, gnorm, _ = made
        ins = kept(columns, enter, kept_q, gnorm, local, *refs)
        outs = [keep(by_token, F32), keep(local_dims, BF16), keep((2, rows), F32)]
        scratch = [tall, tall]
        if part == 1:
            aliases = {len(ins) + 1: 0, len(ins) + 2: 1}
            ins += kept(reduced[1], inside, reduced[0])
        else:
            aliases = {len(ins): 0}
            ins += kept(inside)
        results = call(
            functools.partial(
                outside_kernel, chunks, entering, len(refs), part
            ),
            (steps if part is None else steps // 2,),
            ins, outs, scratch, aliases,
            flops=small, moved=big,
        )
        made[3], *reduced[:] = results
        return reduced[1]

    passes = scan_devices(state, own_pass, None, fill_forward, finish_forward, False)
    mask, columns = ready
    kept_q, _, _, attn, gnorm, probs = made
    held, sums = reduced

    flat = []
    halves = [0, heads // 2]
    token = keep((8, HD), F32)

    def turn(sums):
        first = halves.pop(0)
        results = call(
            functools.partial(turn_kernel, chunks, first),
            (steps // 2,),
            kept(kept_q, attn, sums, *flat),
            [keep(by_head, BF16), keep(by_token, BF16), token],
            aliases={3 + i: i for i in range(len(flat))},
            flops=rows * cols, moved=2 * big,
        )
        flat[:] = results[:2]
        return results[2]

    apart = 1
    while True:
        other_sums = lax.ppermute(sums, "head", [(i, i ^ apart) for i in range(parts)])
        done = turn(sums) if halves else done
        apart *= 2
        if apart >= parts:
            break
        (sums,) = call(add_kernel, (), kept(sums, other_sums, done), [keep((2, rows), F32)])
    while halves:
        done = turn(sums)
    turned_q, attn_flat = flat

    agrad, bloc, back, alpha, *rings = call(
        functools.partial(grad_kernel, chunks),
        grid,
        kept(enter, sums, other_sums, done, turned_q, gnorm, attn)
        + [(hbm(x), anywhere) for x in (gate_input, out_grad)],
        [
            keep(by_token, BF16), keep((heads, chunks - 1, HD, HD), F32),
            keep((heads, HD, HD), F32), keep((rows, HD), F32), ring, ring,
        ],
        [tall, sems((2,))],
        {5: 0},
        flops=small, moved=big,
    )

    inner = [turned_q, *rings]

    def fill_backward(window, tie):
        ins = kept(
            after(crow, tie), alpha, columns, mask, keys, values, attn_flat, held, agrad, probs,
            inner[0], gain,
        )
        ins += [(hbm(x), anywhere) for x in (gate_input, out_grad)]
        aliases = {10: 0}
        aliases.update({len(ins) - 1 + i: i for i in range(1, len(inner))})
        ins += kept(*inner[1:5]) + [(hbm(x), anywhere) for x in inner[5:]]
        inner[:] = call(
            functools.partial(inner_grad_kernel, chunks, bases[window] // RING, heads // RING),
            (shares[window] // RING,),
            ins,
            [keep(by_head, BF16), ring, ring, keep(by_head, BF16), out_ring] + [wide_out] * 3,
            [sems((5,))],
            aliases=aliases,
            flops=(4 * tile + small) // WINDOWS, moved=7 * big // WINDOWS,
            exps=rows * (CHUNK + HD) * heads // WINDOWS,
        )
        return inner[5]

    grads = []

    def finish_backward(part, entering, refs):
        ins = kept(enter, leave, keys, values, *refs, inner[0], inner[3], bloc)
        scratch = [pltpu.VMEM((2, 2, rows, GROUP * HD), BF16), sems((2, 2))]
        if part == 1:
            aliases = {len(ins): 0, len(ins) + 1: 1}
            ins += [(hbm(x), anywhere) for x in grads]
            outs = [wide_out] * 2
        else:
            aliases = {len(ins) + 1 + i: i for i in range(3)}
            ins += kept(inner[4]) + [(hbm(x), anywhere) for x in inner[5:]]
            outs = [wide_out] * 5
            scratch.append(sems((3,)))
        results = call(
            functools.partial(
                outer_grad_kernel, chunks, heads // RING - 1, entering, len(refs), part
            ),
            (steps if part is None else steps // 2,),
            ins, outs, scratch, aliases,
            flops=2 * small, moved=2 * big,
        )
        grads[:] = results[-2:]
        if part != 1:
            inner[5:] = results[:3]
        return grads[0]

    scan_devices(back, own_pass, passes, fill_backward, finish_backward, True)
    dq, gated, gate_grad = inner[5:]
    return (gated, gate_grad, dq, *grads)


def solution(mesh):
    in_specs = (
        P("seq", "head"),
        P("seq", "head"),
        P("seq", "head"),
        P("head", "seq"),
        P("seq"),
        P("seq", "head"),
        P("head"),
        P("seq", "head"),
    )
    out_specs = (P("seq", "head"),) * 5
    return jax.shard_map(body, mesh=mesh, in_specs=in_specs, out_specs=out_specs, check_vma=False)
```

```python
import functools

import jax
import jax.numpy as jnp
from jax import lax
from jax.experimental import pallas as pl
from jax.experimental.pallas import tpu as pltpu
from jax.sharding import PartitionSpec as P

HEAD_TOTAL = 64
HD = 128
CHUNK = 256
GROUP = 2
WIDE = 4
RING = 2
AHEAD = 3
WINDOWS = 3
ROOM = 4
WIDTH = HEAD_TOTAL * HD

epsilon = 1e-06
LOG2E = 1.4426950408889634

F32 = jnp.float32
BF16 = jnp.bfloat16
MIB = 1024 * 1024
NT = ((1,), (1,))


def dot(a, b, dims=((1,), (0,))):
    return lax.dot_general(a, b, (dims, ((), ())), preferred_element_type=F32)


def chunk_cumsum(x):
    lane = lax.broadcasted_iota(jnp.int32, x.shape, 1) % CHUNK
    shift = 1
    while shift < CHUNK:
        x = x + jnp.where(lane >= shift, pltpu.roll(x, shift, 1), 0.0)
        shift *= 2
    return x


def spans(chunks):
    return [slice(n * CHUNK, (n + 1) * CHUNK) for n in range(chunks)]


def head_span(head, count=1):
    return pl.ds(pl.multiple_of(head * HD, HD), count * HD)


def save(stores):
    for ref, index, value in stores:
        ref[index] = value


def save_probs(probs_ref, h, n, probs):
    left, right = slice(0, CHUNK), slice(CHUNK, CHUNK + HD)
    return [
        (probs_ref, (h, n, left), probs[:, :HD]),
        (probs_ref, (h, n, right), probs[HD:, HD:]),
    ]


def load_probs(probs_ref, h, n):
    right = jnp.concatenate([jnp.zeros((HD, HD), BF16), probs_ref[h, n, CHUNK:, :]], axis=0)
    return jnp.concatenate([probs_ref[h, n, :CHUNK, :], right], axis=1)


def sigmoid(x):
    return 0.5 * jnp.tanh(0.5 * x) + 0.5


def spread(cols, lane):
    return jnp.broadcast_to(cols[:, lane : lane + 1], cols.shape)


def turned(cols_ref, lane):
    return pltpu.roll(cols_ref[...], (HD - lane) % HD, 1)


def column(row):
    return jnp.broadcast_to(row, (HD, row.shape[1])).T


def start(copies):
    for copy in copies:
        copy.start()


def wait(copies):
    for copy in copies:
        copy.wait()


def group_of(at):
    return head_span(at * RING, RING)


def fetch_gates(at, gate_hbm, grad_hbm, gate_ring, grad_ring, sems):
    slot = at % 2
    return [
        pltpu.make_async_copy(gate_hbm.at[:, group_of(at)], gate_ring.at[slot], sems.at[0]),
        pltpu.make_async_copy(grad_hbm.at[:, group_of(at)], grad_ring.at[slot], sems.at[1]),
    ]


def fetch_q(at, q_hbm, q_ref, sem):
    return [pltpu.make_async_copy(q_hbm.at[:, group_of(at)], q_ref.at[:, group_of(at)], sem)]


def put_outs(at, out_ring, outs_hbm, sems):
    return [
        pltpu.make_async_copy(out_ring.at[at % 2, i], out.at[:, group_of(at)], sems.at[i])
        for i, out in enumerate(outs_hbm)
    ]


def state_kernel(
    chunks, steps, lc_hbm, doc_hbm, gain_hbm, k_hbm, v_hbm, q_hbm, gate_hbm, grad_hbm,
    crow_ref, enter_ref, leave_ref, rrow_ref, k_ref, v_ref, loc_ref, state_ref, pass_ref,
    gain_ref, q_ref, gate_ring, grad_ring, lc_ref, doc_ref, sems, small_sems, next_sems,
):
    step = pl.program_id(0)
    small = [
        pltpu.make_async_copy(lc_hbm, lc_ref, small_sems.at[0]),
        pltpu.make_async_copy(doc_hbm, doc_ref, small_sems.at[1]),
        pltpu.make_async_copy(gain_hbm, gain_ref, small_sems.at[2]),
    ]
    following = fetch_gates(0, gate_hbm, grad_hbm, gate_ring, grad_ring, next_sems)
    following += fetch_q(0, q_hbm, q_ref, next_sems.at[2])

    def copies(at):
        here = head_span(at * GROUP, GROUP)
        return (
            pltpu.make_async_copy(k_hbm.at[:, here], k_ref.at[:, here], sems.at[0, at]),
            pltpu.make_async_copy(v_hbm.at[:, here], v_ref.at[:, here], sems.at[1, at]),
        )

    @pl.when(step == 0)
    def _():
        start(small)
        for at in range(min(AHEAD, steps)):
            start(copies(at))
        wait(small)
        c = chunk_cumsum(lc_ref[...] * LOG2E)
        r = chunk_cumsum(jnp.broadcast_to(doc_ref[...].astype(F32), (8, doc_ref.shape[1])))
        crow_ref[...] = c
        rrow_ref[...] = r
        enter_ref[...] = jnp.where(r[0:1] == 0.0, jnp.exp2(c), 0.0)
        for span in spans(chunks):
            cn, rn = c[:, span], r[0:1, span]
            leave_ref[:, span] = jnp.where(rn == rn[:, -1:], jnp.exp2(cn[:, -1:] - cn), 0.0)

    pl.when(step + AHEAD < steps)(lambda: start(copies(step + AHEAD)))
    pl.when(step + AHEAD == steps)(lambda: start(following))
    wait(copies(step))
    late = []
    for g in range(GROUP):
        h = step * GROUP + g
        mine = head_span(h)
        state = None
        total = None
        for n, span in enumerate(spans(chunks)):
            keyed = (k_ref[span, mine].T.astype(F32) * leave_ref[pl.ds(h, 1), span]).astype(BF16)
            local = dot(keyed, v_ref[span, mine])
            passing = enter_ref[pl.ds(h, 1), span][:, CHUNK - 1 : CHUNK]
            state = local if state is None else passing * state + local
            total = passing if total is None else passing * total
            save(late)
            late = [(loc_ref, (h, n), local)] if n + 1 < chunks else []
        late.append((state_ref, h, state))
        late.append((pass_ref, (pl.ds(h, 1), slice(None)), jnp.broadcast_to(total, (1, HD))))
    save(late)

    @pl.when(step == steps - 1)
    def _():
        wait(following)


def prepare_kernel(rrow_ref, crow_ref, enter_ref, mask_ref, cols_ref):
    sub = lax.broadcasted_iota(jnp.int32, (CHUNK, CHUNK), 0)
    lane = lax.broadcasted_iota(jnp.int32, (CHUNK, CHUNK), 1)
    spare = jnp.zeros((HD - 2 * crow_ref.shape[0], CHUNK), F32)
    for n, span in enumerate(spans(mask_ref.shape[0])):
        r_row = rrow_ref[0:1, span]
        r_col = jnp.concatenate([column(r_row)] * (CHUNK // HD), axis=1)
        mask_ref[n] = jnp.where((r_col == r_row) & (lane <= sub), 0.0, -jnp.inf)
        cols_ref[span, :] = jnp.concatenate([crow_ref[:, span], enter_ref[:, span], spare], axis=0).T


def decayed(scores, c_col, c_row, mask):
    top, low = slice(0, HD), slice(HD, CHUNK)
    row_blocks = []
    for rows, width in ((top, HD), (low, CHUNK)):
        col = c_col[rows]
        col = col if width == HD else jnp.concatenate([col] * (width // HD), axis=1)
        weight = jnp.exp2(col - c_row[:, :width] + mask[rows, :width])
        row_blocks.append((scores[rows, :width] * weight).astype(BF16))
    row_blocks[0] = jnp.concatenate([row_blocks[0], jnp.zeros((HD, CHUNK - HD), BF16)], axis=1)
    return jnp.concatenate(row_blocks, axis=0)


def inside_kernel(
    chunks, first, steps, crow_ref, cols_ref, mask_ref, k_ref, v_ref, gain_ref, q_hbm, gate_hbm,
    grad_hbm, *refs,
):
    q_ref, gate_ring, grad_ring, attn_ref, gnorm_ref, probs_ref, sems = refs[-7:]
    step = first + pl.program_id(0)
    slot = step % 2
    fetches = fetch_gates(step + 1, gate_hbm, grad_hbm, gate_ring, grad_ring, sems)
    fetches += fetch_q(step + 1, q_hbm, q_ref, sems.at[2])
    pl.when(step + 1 < steps)(lambda: start(fetches))

    cols_now = turned(cols_ref, step * RING)
    late = []
    for g in range(RING):
        h = step * RING + g
        cols = slice(g * HD, (g + 1) * HD)
        mine = head_span(h)
        for n, span in enumerate(spans(chunks)):
            q = q_ref[span, mine]
            scores = dot(q, k_ref[span, mine], NT)
            c_row = crow_ref[pl.ds(h, 1), span]
            probs = decayed(scores, spread(cols_now[span], g), c_row, mask_ref.at[n])
            inside = dot(probs, v_ref[span, mine])
            sig = sigmoid(gate_ring[slot, span, cols].astype(F32))
            gnorm = grad_ring[slot, span, cols].astype(F32) * sig * gain_ref[0:1, mine]
            save(late)
            late = save_probs(probs_ref, h, n, probs)
            late += [
                (attn_ref, (span, mine), inside),
                (gnorm_ref, (span, mine), gnorm.astype(BF16)),
            ]
    save(late)
    pl.when(step + 1 < steps)(lambda: wait(fetches))


def first_head(part, half, reverse):
    if part is None:
        return 0
    core, _, _ = place(reverse)
    return (core if part == 0 else 1 - core) * half


def outside_kernel(chunks, entering, inputs, part, cols_ref, enter_ref, q_ref, gnorm_ref, loc_ref, *refs):
    in_refs = refs[:inputs]
    if part == 1:
        before_ref, inside_ref, _, attn_ref, held_ref, sums_ref, sq_ref, inner_ref = refs[inputs:]
    else:
        inside_ref, attn_ref, held_ref, sums_ref, sq_ref, inner_ref = refs[inputs:]
    step = pl.program_id(0)
    steps = pl.num_programs(0)

    @pl.when(step == 0)
    def _():
        sq_ref[...] = jnp.zeros_like(sq_ref)
        inner_ref[...] = jnp.zeros_like(inner_ref)

    start_head = first_head(part, steps * WIDE, False) + step * WIDE
    heads = [start_head + g for g in range(WIDE)]
    cols_now = turned(cols_ref, enter_ref.shape[0] + start_head)
    carries = [entering(in_refs, h) for h in heads]
    late = []
    for n, span in enumerate(spans(chunks)):
        squares = sq_ref[span, :]
        inners = inner_ref[span, :]
        for g, h in enumerate(heads):
            mine = head_span(h)
            held = carries[g].astype(BF16)
            enter = spread(cols_now[span], g)
            attn = inside_ref[span, mine] + enter * dot(q_ref[span, mine], held)
            squares = squares + attn * attn
            inners = inners + gnorm_ref[span, mine].astype(F32) * attn
            if n + 1 < chunks:
                passing = enter_ref[pl.ds(h, 1), span][:, CHUNK - 1 : CHUNK]
                carries[g] = passing * carries[g] + loc_ref[h, n]
            save(late)
            late = [(held_ref, (h, n), held), (attn_ref, (span, mine), attn)]
        late += [(sq_ref, (span, slice(None)), squares), (inner_ref, (span, slice(None)), inners)]
    save(late)

    @pl.when(step == steps - 1)
    def _():
        for i, ref in enumerate((sq_ref, inner_ref)):
            total = jnp.sum(ref[...].T, axis=0, keepdims=True)
            sums_ref[i : i + 1, :] = total + before_ref[i : i + 1, :] if part == 1 else total


def turn_kernel(chunks, first, q_ref, attn_ref, *refs):
    turned_ref, flat_ref, done_ref = refs[-3:]
    step = pl.program_id(0)
    done_ref[...] = jnp.zeros_like(done_ref)
    late = []
    for g in range(WIDE):
        h = first + step * WIDE + g
        mine = head_span(h)
        for span in spans(chunks):
            turned_q = q_ref[span, mine].T
            flat = attn_ref[span, mine].astype(BF16)
            save(late)
            late = [(turned_ref, (h, slice(None), span), turned_q), (flat_ref, (span, mine), flat)]
    save(late)


def grad_kernel(chunks, enter_ref, sums_ref, others_ref, _, *refs):
    turned_q_ref, gnorm_ref, attn_ref, gate_hbm, grad_hbm = refs[:5]
    agrad_ref, bloc_ref, back_ref, alpha_ref = refs[5:9]
    gate_ring, grad_ring, beta_ref, sems = refs[9:]
    step = pl.program_id(0)
    following = fetch_gates(0, gate_hbm, grad_hbm, gate_ring, grad_ring, sems)

    @pl.when(step == 0)
    def _():
        start(following)
        sums = sums_ref[...] + others_ref[...]
        inverse = lax.rsqrt(sums[0:1] / WIDTH + epsilon)
        alpha_ref[...] = column(inverse)
        beta_ref[...] = column(inverse * inverse * inverse * sums[1:2] / WIDTH)

    late = []
    for g in range(WIDE):
        h = step * WIDE + g
        mine = head_span(h)
        back = None
        for n, span in reversed(list(enumerate(spans(chunks)))):
            enter = enter_ref[pl.ds(h, 1), span]
            gnorm = gnorm_ref[span, mine].astype(F32)
            attn, alpha = attn_ref[span, mine], alpha_ref[span, :]
            agrad = alpha * gnorm - attn * beta_ref[span, :]
            agrad = agrad.astype(BF16)
            qkeyed = (turned_q_ref[h, :, span].astype(F32) * enter).astype(BF16)
            local = dot(qkeyed, agrad)
            back = local if back is None else local + enter[:, CHUNK - 1 : CHUNK] * back
            save(late)
            late = [
                (agrad_ref, (span, mine), agrad),
            ]
            if n > 0:
                late.append((bloc_ref, (h, n - 1), local))
        late.append((back_ref, h, back))
    save(late)

    @pl.when(step == pl.num_programs(0) - 1)
    def _():
        wait(following)


def inner_grad_kernel(
    chunks, first, steps, crow_ref, alpha_ref, cols_ref, mask_ref, k_ref, v_ref, flat_ref,
    held_ref, agrad_ref, probs_ref, turned_q_ref, gain_ref, gate_hbm, grad_hbm,
    *refs,
):
    dk_ref, gate_ring, grad_ring, dv_ref, out_ring, *outs_hbm, sems = refs[-9:]
    step = first + pl.program_id(0)
    slot = step % 2
    fetches = fetch_gates(step + 1, gate_hbm, grad_hbm, gate_ring, grad_ring, sems)
    puts = put_outs(step - 1, out_ring, outs_hbm, sems.at[pl.ds(2, 3)])
    pl.when(step + 1 < steps)(lambda: start(fetches))
    pl.when(step > 0)(lambda: start(puts))

    cols_now = turned(cols_ref, step * RING)
    late = []
    for g in range(RING):
        h = step * RING + g
        cols = slice(g * HD, (g + 1) * HD)
        mine = head_span(h)
        for n, span in enumerate(spans(chunks)):
            k, v, agrad = k_ref[span, mine], v_ref[span, mine], agrad_ref[span, mine]
            both = dot(agrad, jnp.concatenate([v, held_ref[h, n]], axis=0), NT)
            c_row = crow_ref[pl.ds(h, 1), span]
            dscore = decayed(both[:, :CHUNK], spread(cols_now[span], g), c_row, mask_ref.at[n])
            enter = spread(cols_now[span], crow_ref.shape[0] + g)
            dq = dot(dscore, k) + enter * both[:, CHUNK:]
            dv = dot(agrad.T, load_probs(probs_ref, h, n))
            dk = dot(turned_q_ref[h, :, span], dscore)
            normed = flat_ref[span, mine].astype(F32) * alpha_ref[span, :] * gain_ref[0:1, mine]
            sig = sigmoid(gate_ring[slot, span, cols].astype(F32))
            gated = normed * sig
            ggate = grad_ring[slot, span, cols].astype(F32) * gated * (1.0 - sig)
            save(late)
            late = [
                (out_ring, (slot, 0, span, cols), dq.astype(BF16)),
                (dv_ref, (h, slice(None), span), dv.astype(BF16)),
                (dk_ref, (h, slice(None), span), dk.astype(BF16)),
                (out_ring, (slot, 1, span, cols), gated.astype(BF16)),
                (out_ring, (slot, 2, span, cols), ggate.astype(BF16)),
            ]
    save(late)
    pl.when(step + 1 < steps)(lambda: wait(fetches))
    pl.when(step > 0)(lambda: wait(puts))


def outer_grad_kernel(chunks, last, entering, inputs, part, enter_ref, leave_ref, k_ref, v_ref, *refs):
    in_refs = refs[:inputs]
    dkin_ref, dvin_ref, bloc_ref = refs[inputs : inputs + 3]
    step = pl.program_id(0)
    steps = pl.num_programs(0)
    start_head = first_head(part, steps * GROUP, True) + step * GROUP
    if part == 1:
        *grads_hbm, parts_ref, sems = refs[-4:]
    else:
        out_ring = refs[inputs + 3]
        *outs_hbm, dk_hbm, dv_hbm, parts_ref, sems, last_sems = refs[-8:]
        grads_hbm = [dk_hbm, dv_hbm]
        puts = put_outs(last, out_ring, outs_hbm, last_sems)
        pl.when(step == 0)(lambda: start(puts))

    def put(back):
        slot = (step - back) % 2
        here = head_span(start_head - back * GROUP, GROUP)
        return [
            pltpu.make_async_copy(parts_ref.at[slot, i], out.at[:, here], sems.at[slot, i])
            for i, out in enumerate(grads_hbm)
        ]

    slot = step % 2
    pl.when(step > 1)(lambda: wait(put(2)))
    late = []
    for g in range(GROUP):
        h = start_head + g
        cols = slice(g * HD, (g + 1) * HD)
        mine = head_span(h)
        carry = entering(in_refs, h)
        for n, span in reversed(list(enumerate(spans(chunks)))):
            leave = leave_ref[pl.ds(h, 1), span]
            back = carry.astype(BF16)
            dk = dkin_ref[h, :, span].astype(F32) + leave * dot(back, v_ref[span, mine], NT)
            dv = dvin_ref[h, :, span].astype(F32) + leave * dot(back.T, k_ref[span, mine], NT)
            if n > 0:
                passing = enter_ref[pl.ds(h, 1), span][:, CHUNK - 1 : CHUNK]
                carry = bloc_ref[h, n - 1] + passing * carry
            save(late)
            late = [
                (parts_ref, (slot, 0, span, cols), dk.astype(BF16).T),
                (parts_ref, (slot, 1, span, cols), dv.astype(BF16).T),
            ]
    save(late)
    start(put(0))

    @pl.when(step == steps - 1)
    def _():
        pl.when(step > 0)(lambda: wait(put(1)))
        wait(put(0))
        if part != 1:
            wait(puts)


def hbm(x):
    return pltpu.with_memory_space_constraint(x, pltpu.HBM)


def kept(*arrays):
    spec = pl.BlockSpec(memory_space=pltpu.VMEM)
    return [(pltpu.with_memory_space_constraint(x, pltpu.VMEM), spec) for x in arrays]


def keep(dims, dtype):
    return pltpu.VMEM(dims, dtype), pl.BlockSpec(memory_space=pltpu.VMEM)


def add_kernel(a_ref, b_ref, _, out_ref):
    out_ref[...] = a_ref[...] + b_ref[...]


def call(kernel, grid, ins, outs, scratch=(), aliases=None, flops=0, moved=0, exps=0):
    return pl.pallas_call(
        kernel,
        grid=grid,
        in_specs=[spec for _, spec in ins],
        out_specs=[spec for _, spec in outs],
        out_shape=[shape for shape, _ in outs],
        scratch_shapes=list(scratch),
        input_output_aliases=aliases or {},
        compiler_params=pltpu.CompilerParams(
            dimension_semantics=("arbitrary",) * len(grid), vmem_limit_bytes=ROOM * MIB
        ),
        cost_estimate=pl.CostEstimate(flops=flops, bytes_accessed=moved, transcendentals=exps),
    )(*[x for x, _ in ins])


def after(x, *others):
    return lax.optimization_barrier((x, *others))[0]


def across(x, flips, devices=8):
    return lax.ppermute(x, "seq", [(i, i ^ flips) for i in range(devices)])


def place(reverse):
    index = lax.axis_index("seq")
    index = 7 - index if reverse else index
    return lax.rem(index, 2), lax.rem(lax.div(index, 2), 2), lax.div(index, 4)


def pair_kernel(reverse, state_ref, other_ref, pass_ref, beside_ref, x_ref, y_ref, chip_ref):
    core, _, _ = place(reverse)
    quarter = x_ref.shape[0]
    chip_ref[...] = pass_ref[...] * beside_ref[...]
    for i in range(quarter):
        for at, out_ref in ((i, x_ref), (quarter + i, y_ref)):
            h = core * 2 * quarter + at
            mine, other = state_ref[h], other_ref[h]

            @pl.when(core == 0)
            def _():
                out_ref[i] = beside_ref[pl.ds(h, 1), :] * mine + other

            @pl.when(core == 1)
            def _():
                out_ref[i] = pass_ref[pl.ds(h, 1), :] * other + mine


def row_kernel(
    reverse, to_x_ref, to_y_ref, from_x_ref, from_y_ref, chip_ref, side_ref, far_ref,
    row_ref, sent_ref,
):
    core, x, y = place(reverse)
    quarter = row_ref.shape[0]
    for i in range(quarter):
        h = core * 2 * quarter + i
        hy = h + quarter

        @pl.when(x == 0)
        def _():
            row_ref[i] = side_ref[pl.ds(h, 1), :] * to_x_ref[i] + from_x_ref[i]

        @pl.when(x == 1)
        def _():
            row_ref[i] = chip_ref[pl.ds(h, 1), :] * from_x_ref[i] + to_x_ref[i]

        @pl.when(y == 0)
        def _():
            sent_ref[i] = to_y_ref[i]

        @pl.when((y == 1) & (x == 0))
        def _():
            far = far_ref[pl.ds(hy, 1), :] * from_y_ref[i]
            sent_ref[i] = chip_ref[pl.ds(hy, 1), :] * far + to_y_ref[i]

        @pl.when((y == 1) & (x == 1))
        def _():
            sent_ref[i] = from_y_ref[i]


def ahead_kernel(
    reverse, from_x_ref, from_y_ref, row_ref, sent_ref, side_ref, far_ref, out_ref,
):
    core, x, y = place(reverse)
    quarter = row_ref.shape[0]
    for i in range(quarter):
        h = core * 2 * quarter + i
        hy = h + quarter

        @pl.when((y == 0) & (x == 0))
        def _():
            out_ref[i] = jnp.zeros_like(out_ref[i])
            out_ref[quarter + i] = jnp.zeros_like(out_ref[i])

        @pl.when((y == 0) & (x == 1))
        def _():
            out_ref[i] = from_x_ref[i]
            out_ref[quarter + i] = sent_ref[i]

        @pl.when((y == 1) & (x == 0))
        def _():
            out_ref[i] = row_ref[i]
            out_ref[quarter + i] = far_ref[pl.ds(hy, 1), :] * from_y_ref[i] + sent_ref[i]

        @pl.when((y == 1) & (x == 1))
        def _():
            out_ref[i] = side_ref[pl.ds(h, 1), :] * row_ref[i] + from_x_ref[i]
            out_ref[quarter + i] = side_ref[pl.ds(hy, 1), :] * from_y_ref[i] + sent_ref[i]


def cube_entering(reverse, refs, h):
    chip_ref, other_ref, beside_pass_ref = refs
    core, _, _ = place(reverse)
    chip = chip_ref[lax.rem(h, chip_ref.shape[0])]
    through = beside_pass_ref[pl.ds(h, 1), :] * chip + other_ref[h]
    return jnp.where(core == 0, chip, through)


def plain_entering(refs, h):
    return refs[0][h]


def cube_scan(state, own_pass, passes, fill, finish, reverse):
    heads = state.shape[0]
    quarter = heads // 4
    part = keep((quarter, HD, HD), F32)

    other = across(state, 1)
    beside_pass = passes[0] if passes else across(own_pass, 1)
    other, beside_pass = lax.optimization_barrier((other, beside_pass, fill(0, state)))[:2]
    to_x, to_y, chip_pass = call(
        functools.partial(pair_kernel, reverse), (),
        kept(state, other, own_pass, beside_pass), [part, part, keep((heads, HD), F32)],
    )

    from_x, from_y = across(to_x, 2), across(to_y, 4)
    x_pass, far_pass = passes[1:] if passes else (across(chip_pass, 2), across(chip_pass, 6))
    from_x, from_y, x_pass, far_pass = lax.optimization_barrier(
        (from_x, from_y, x_pass, far_pass, fill(1, to_y))
    )[:4]
    row, sent = call(
        functools.partial(row_kernel, reverse), (),
        kept(to_x, to_y, from_x, from_y, chip_pass, x_pass, far_pass), [part, part],
    )

    row_in, sent_in = across(row, 4), across(sent, 2)
    row_in, sent_in = lax.optimization_barrier((row_in, sent_in, fill(2, sent)))[:2]
    (ahead,) = call(
        functools.partial(ahead_kernel, reverse), (),
        kept(from_x, from_y, row_in, sent_in, x_pass, far_pass),
        [keep((2 * quarter, HD, HD), F32)],
    )

    beside = across(ahead, 1)
    entering = functools.partial(cube_entering, reverse)
    beside = after(beside, finish(0, entering, (ahead, other, beside_pass)))
    finish(1, entering, (beside, other, beside_pass))
    return beside_pass, x_pass, far_pass


def doubling_scan(state, own_pass, fill, reverse):
    devices = lax.axis_size("seq")
    index = lax.axis_index("seq")
    passes = lax.all_gather(own_pass, "seq")
    if reverse:
        passes = passes[::-1]
        index = devices - 1 - index
    route = lambda hop: [
        (i, i - hop if reverse else i + hop)
        for i in range(devices)
        if 0 <= (i - hop if reverse else i + hop) < devices
    ]
    for window in range(WINDOWS):
        state = after(state, fill(window, state))
    hop = 1
    while hop < devices:
        factor = lax.dynamic_index_in_dim(passes, index, 0, False)
        state = factor[:, None, :] * lax.ppermute(state, "seq", route(hop)) + state
        before = jnp.concatenate([jnp.zeros_like(passes[:hop]), passes[:-hop]], axis=0)
        passes = passes * before
        hop *= 2
    return lax.ppermute(state, "seq", route(1))


def scan_devices(state, own_pass, passes, fill, finish, reverse):
    if lax.axis_size("seq") == 8 and state.shape[0] % 4 == 0:
        return cube_scan(state, own_pass, passes, fill, finish, reverse)
    finish(None, plain_entering, (doubling_scan(state, own_pass, fill, reverse),))
    return None


def body(queries, key_rows, value_rows, log_decay, doc_start, gate_input, norm_gain, out_grad):
    rows, cols = queries.shape
    heads = cols // HD
    chunks = rows // CHUNK
    parts = lax.axis_size("head")
    grid = (heads // GROUP,)
    shares = [heads // 4]
    shares.append((heads - shares[0] + RING) // 2 // RING * RING)
    shares.append(heads - sum(shares))
    bases = [0, shares[0], heads - shares[2]]
    big = rows * cols * 2
    tile = 2 * rows * CHUNK * cols
    small = 2 * rows * HD * cols

    whole = lambda *dims: pl.BlockSpec(dims, lambda i: (0,) * len(dims))
    anywhere = pl.BlockSpec(memory_space=pl.ANY)

    by_head = (heads, HD, rows)
    local_dims = (heads, chunks, HD, HD)
    wide_out = (pltpu.HBM((rows, cols), BF16), anywhere)
    ring = keep((2, rows, RING * HD), BF16)
    probs_kept = keep((heads, chunks, CHUNK + HD, HD), BF16)
    out_ring = keep((2, 3, rows, RING * HD), BF16)
    sems = pltpu.SemaphoreType.DMA
    queries, key_rows, value_rows, gate_input, out_grad = map(
        hbm, (queries, key_rows, value_rows, gate_input, out_grad)
    )
    doc_row = doc_start.reshape(1, rows)
    gain_row = norm_gain.reshape(1, cols)

    by_token = (rows, cols)
    steps = heads // GROUP
    (
        crow, enter, leave, rrow, keys, values, local, state, own_pass, gain, kept_q, *rings
    ) = call(
        functools.partial(state_kernel, chunks, steps),
        grid,
        [
            (hbm(x), anywhere)
            for x in (
                log_decay, doc_row, gain_row, key_rows, value_rows, queries, gate_input, out_grad
            )
        ],
        [keep((heads, rows), F32)] * 3
        + [
            keep((8, rows), F32), keep(by_token, BF16), keep(by_token, BF16),
            keep((heads, chunks - 1, HD, HD), F32), keep((heads, HD, HD), F32), keep((heads, HD), F32),
            keep((1, cols), F32), keep(by_token, BF16), ring, ring,
        ],
        [
            pltpu.VMEM((heads, rows), F32), pltpu.VMEM((1, rows), jnp.int32),
            sems((2, steps)), sems((3,)), sems((3,)),
        ],
        flops=small, moved=2 * big,
    )

    ready = []
    made = [kept_q, *rings]

    def fill_forward(window, tie):
        if not ready:
            ready[:] = call(
                prepare_kernel, (), kept(after(rrow, tie), crow, enter),
                [keep((chunks, CHUNK, CHUNK), F32), keep((rows, HD), F32)],
                flops=8 * rows * CHUNK,
            )
        mask, columns = ready
        ins = kept(after(crow, tie), columns, mask, keys, values, gain)
        ins += [(x, anywhere) for x in (queries, gate_input, out_grad)]
        aliases = {len(ins) + i: i for i in range(len(made))}
        ins += kept(*made)
        made[:] = call(
            functools.partial(inside_kernel, chunks, bases[window] // RING, heads // RING),
            (shares[window] // RING,),
            ins,
            [
                keep(by_token, BF16), ring, ring, keep(by_token, F32), keep(by_token, BF16),
                probs_kept,
            ],
            [sems((3,))],
            aliases=aliases,
            flops=2 * tile // WINDOWS, moved=5 * big // WINDOWS,
            exps=rows * (CHUNK + HD) * heads // WINDOWS,
        )
        return made[4]

    tall = pltpu.VMEM((rows, HD), F32)
    reduced = []

    def finish_forward(part, entering, refs):
        mask, columns = ready
        kept_q, _, _, inside, gnorm, _ = made
        ins = kept(columns, enter, kept_q, gnorm, local, *refs)
        outs = [keep(by_token, F32), keep(local_dims, BF16), keep((2, rows), F32)]
        scratch = [tall, tall]
        if part == 1:
            aliases = {len(ins) + 1: 0, len(ins) + 2: 1}
            ins += kept(reduced[1], inside, reduced[0])
        else:
            aliases = {len(ins): 0}
            ins += kept(inside)
        results = call(
            functools.partial(
                outside_kernel, chunks, entering, len(refs), part
            ),
            (heads // WIDE if part is None else heads // 2 // WIDE,),
            ins, outs, scratch, aliases,
            flops=small, moved=big,
        )
        made[3], *reduced[:] = results
        return reduced[1]

    passes = scan_devices(state, own_pass, None, fill_forward, finish_forward, False)
    mask, columns = ready
    kept_q, _, _, attn, gnorm, probs = made
    held, sums = reduced

    flat = []
    halves = [0, heads // 2]
    token = keep((8, HD), F32)

    def turn(sums):
        first = halves.pop(0)
        results = call(
            functools.partial(turn_kernel, chunks, first),
            (heads // 2 // WIDE,),
            kept(kept_q, attn, sums, *flat),
            [keep(by_head, BF16), keep(by_token, BF16), token],
            aliases={3 + i: i for i in range(len(flat))},
            flops=rows * cols, moved=2 * big,
        )
        flat[:] = results[:2]
        return results[2]

    apart = 1
    while True:
        other_sums = lax.ppermute(sums, "head", [(i, i ^ apart) for i in range(parts)])
        done = turn(sums) if halves else done
        apart *= 2
        if apart >= parts:
            break
        (sums,) = call(add_kernel, (), kept(sums, other_sums, done), [keep((2, rows), F32)])
    while halves:
        done = turn(sums)
    turned_q, attn_flat = flat

    agrad, bloc, back, alpha, *rings = call(
        functools.partial(grad_kernel, chunks),
        (heads // WIDE,),
        kept(enter, sums, other_sums, done, turned_q, gnorm, attn)
        + [(hbm(x), anywhere) for x in (gate_input, out_grad)],
        [
            keep(by_token, BF16), keep((heads, chunks - 1, HD, HD), F32),
            keep((heads, HD, HD), F32), keep((rows, HD), F32), ring, ring,
        ],
        [tall, sems((2,))],
        {5: 0},
        flops=small, moved=big,
    )

    inner = [turned_q, *rings]

    def fill_backward(window, tie):
        ins = kept(
            after(crow, tie), alpha, columns, mask, keys, values, attn_flat, held, agrad, probs,
            inner[0], gain,
        )
        ins += [(hbm(x), anywhere) for x in (gate_input, out_grad)]
        aliases = {10: 0}
        aliases.update({len(ins) - 1 + i: i for i in range(1, len(inner))})
        ins += kept(*inner[1:5]) + [(hbm(x), anywhere) for x in inner[5:]]
        inner[:] = call(
            functools.partial(inner_grad_kernel, chunks, bases[window] // RING, heads // RING),
            (shares[window] // RING,),
            ins,
            [keep(by_head, BF16), ring, ring, keep(by_head, BF16), out_ring] + [wide_out] * 3,
            [sems((5,))],
            aliases=aliases,
            flops=(4 * tile + small) // WINDOWS, moved=7 * big // WINDOWS,
            exps=rows * (CHUNK + HD) * heads // WINDOWS,
        )
        return inner[5]

    grads = []

    def finish_backward(part, entering, refs):
        ins = kept(enter, leave, keys, values, *refs, inner[0], inner[3], bloc)
        scratch = [pltpu.VMEM((2, 2, rows, GROUP * HD), BF16), sems((2, 2))]
        if part == 1:
            aliases = {len(ins): 0, len(ins) + 1: 1}
            ins += [(hbm(x), anywhere) for x in grads]
            outs = [wide_out] * 2
        else:
            aliases = {len(ins) + 1 + i: i for i in range(3)}
            ins += kept(inner[4]) + [(hbm(x), anywhere) for x in inner[5:]]
            outs = [wide_out] * 5
            scratch.append(sems((3,)))
        results = call(
            functools.partial(
                outer_grad_kernel, chunks, heads // RING - 1, entering, len(refs), part
            ),
            (steps if part is None else steps // 2,),
            ins, outs, scratch, aliases,
            flops=2 * small, moved=2 * big,
        )
        grads[:] = results[-2:]
        if part != 1:
            inner[5:] = results[:3]
        return grads[0]

    scan_devices(back, own_pass, passes, fill_backward, finish_backward, True)
    dq, gated, gate_grad = inner[5:]
    return (gated, gate_grad, dq, *grads)


def solution(mesh):
    in_specs = (
        P("seq", "head"),
        P("seq", "head"),
        P("seq", "head"),
        P("head", "seq"),
        P("seq"),
        P("seq", "head"),
        P("head"),
        P("seq", "head"),
    )
    out_specs = (P("seq", "head"),) * 5
    return jax.shard_map(body, mesh=mesh, in_specs=in_specs, out_specs=out_specs, check_vma=False)
```

```python
import functools

import jax
import jax.numpy as jnp
from jax import lax
from jax.experimental import pallas as pl
from jax.experimental.pallas import tpu as pltpu
from jax.sharding import PartitionSpec as P

HEAD_TOTAL = 64
HD = 128
CHUNK = 256
GROUP = 2
WIDE = 4
RING = 2
AHEAD = 3
WINDOWS = 3
ROOM = 4
WIDTH = HEAD_TOTAL * HD

epsilon = 1e-06
LOG2E = 1.4426950408889634

F32 = jnp.float32
BF16 = jnp.bfloat16
MIB = 1024 * 1024
NT = ((1,), (1,))


def dot(a, b, dims=((1,), (0,))):
    return lax.dot_general(a, b, (dims, ((), ())), preferred_element_type=F32)


def chunk_cumsum(x):
    lane = lax.broadcasted_iota(jnp.int32, x.shape, 1) % CHUNK
    shift = 1
    while shift < CHUNK:
        x = x + jnp.where(lane >= shift, pltpu.roll(x, shift, 1), 0.0)
        shift *= 2
    return x


def spans(chunks):
    return [slice(n * CHUNK, (n + 1) * CHUNK) for n in range(chunks)]


def head_span(head, count=1):
    return pl.ds(pl.multiple_of(head * HD, HD), count * HD)


def save(stores):
    for ref, index, value in stores:
        ref[index] = value


def save_probs(probs_ref, h, n, probs):
    left, right = slice(0, CHUNK), slice(CHUNK, CHUNK + HD)
    return [
        (probs_ref, (h, n, left), probs[:, :HD]),
        (probs_ref, (h, n, right), probs[HD:, HD:]),
    ]


def load_probs(probs_ref, h, n):
    right = jnp.concatenate([jnp.zeros((HD, HD), BF16), probs_ref[h, n, CHUNK:, :]], axis=0)
    return jnp.concatenate([probs_ref[h, n, :CHUNK, :], right], axis=1)


def sigmoid(x):
    return 0.5 * jnp.tanh(0.5 * x) + 0.5


def spread(cols, lane):
    return jnp.broadcast_to(cols[:, lane : lane + 1], cols.shape)


def turned(cols_ref, lane):
    return pltpu.roll(cols_ref[...], (HD - lane) % HD, 1)


def column(row):
    return jnp.broadcast_to(row, (HD, row.shape[1])).T


def start(copies):
    for copy in copies:
        copy.start()


def wait(copies):
    for copy in copies:
        copy.wait()


def group_of(at):
    return head_span(at * RING, RING)


def fetch_gates(at, gate_hbm, grad_hbm, gate_ring, grad_ring, sems):
    slot = at % 2
    return [
        pltpu.make_async_copy(gate_hbm.at[:, group_of(at)], gate_ring.at[slot], sems.at[0]),
        pltpu.make_async_copy(grad_hbm.at[:, group_of(at)], grad_ring.at[slot], sems.at[1]),
    ]


def fetch_q(at, q_hbm, q_ref, sem):
    return [pltpu.make_async_copy(q_hbm.at[:, group_of(at)], q_ref.at[:, group_of(at)], sem)]


def put_outs(at, out_ring, outs_hbm, sems):
    return [
        pltpu.make_async_copy(out_ring.at[at % 2, i], out.at[:, group_of(at)], sems.at[i])
        for i, out in enumerate(outs_hbm)
    ]


def state_kernel(
    chunks, steps, lc_hbm, doc_hbm, gain_hbm, k_hbm, v_hbm, q_hbm, gate_hbm, grad_hbm,
    crow_ref, enter_ref, leave_ref, rrow_ref, k_ref, v_ref, loc_ref, state_ref, pass_ref,
    gain_ref, q_ref, gate_ring, grad_ring, lc_ref, doc_ref, sems, small_sems, next_sems,
):
    step = pl.program_id(0)
    small = [
        pltpu.make_async_copy(lc_hbm, lc_ref, small_sems.at[0]),
        pltpu.make_async_copy(doc_hbm, doc_ref, small_sems.at[1]),
        pltpu.make_async_copy(gain_hbm, gain_ref, small_sems.at[2]),
    ]
    following = fetch_gates(0, gate_hbm, grad_hbm, gate_ring, grad_ring, next_sems)
    following += fetch_q(0, q_hbm, q_ref, next_sems.at[2])

    def copies(at):
        here = head_span(at * GROUP, GROUP)
        return (
            pltpu.make_async_copy(k_hbm.at[:, here], k_ref.at[:, here], sems.at[0, at]),
            pltpu.make_async_copy(v_hbm.at[:, here], v_ref.at[:, here], sems.at[1, at]),
        )

    @pl.when(step == 0)
    def _():
        start(small)
        for at in range(min(AHEAD, steps)):
            start(copies(at))
        wait(small)
        c = chunk_cumsum(lc_ref[...] * LOG2E)
        r = chunk_cumsum(jnp.broadcast_to(doc_ref[...].astype(F32), (8, doc_ref.shape[1])))
        crow_ref[...] = c
        rrow_ref[...] = r
        enter_ref[...] = jnp.where(r[0:1] == 0.0, jnp.exp2(c), 0.0)
        for span in spans(chunks):
            cn, rn = c[:, span], r[0:1, span]
            leave_ref[:, span] = jnp.where(rn == rn[:, -1:], jnp.exp2(cn[:, -1:] - cn), 0.0)

    pl.when(step + AHEAD < steps)(lambda: start(copies(step + AHEAD)))
    pl.when(step + AHEAD == steps)(lambda: start(following))
    wait(copies(step))
    late = []
    for g in range(GROUP):
        h = step * GROUP + g
        mine = head_span(h)
        state = None
        total = None
        for n, span in enumerate(spans(chunks)):
            keyed = (k_ref[span, mine].T.astype(F32) * leave_ref[pl.ds(h, 1), span]).astype(BF16)
            local = dot(keyed, v_ref[span, mine])
            passing = enter_ref[pl.ds(h, 1), span][:, CHUNK - 1 : CHUNK]
            state = local if state is None else passing * state + local
            total = passing if total is None else passing * total
            save(late)
            late = [(loc_ref, (h, n), local)] if n + 1 < chunks else []
        late.append((state_ref, h, state))
        late.append((pass_ref, (pl.ds(h, 1), slice(None)), jnp.broadcast_to(total, (1, HD))))
    save(late)

    @pl.when(step == steps - 1)
    def _():
        wait(following)


def prepare_kernel(rrow_ref, crow_ref, enter_ref, mask_ref, cols_ref):
    sub = lax.broadcasted_iota(jnp.int32, (CHUNK, CHUNK), 0)
    lane = lax.broadcasted_iota(jnp.int32, (CHUNK, CHUNK), 1)
    spare = jnp.zeros((HD - 2 * crow_ref.shape[0], CHUNK), F32)
    for n, span in enumerate(spans(mask_ref.shape[0])):
        r_row = rrow_ref[0:1, span]
        r_col = jnp.concatenate([column(r_row)] * (CHUNK // HD), axis=1)
        mask_ref[n] = jnp.where((r_col == r_row) & (lane <= sub), 0.0, -jnp.inf)
        cols_ref[span, :] = jnp.concatenate([crow_ref[:, span], enter_ref[:, span], spare], axis=0).T


def decayed(scores, c_col, c_row, mask):
    top, low = slice(0, HD), slice(HD, CHUNK)
    row_blocks = []
    for rows, width in ((top, HD), (low, CHUNK)):
        col = c_col[rows]
        col = col if width == HD else jnp.concatenate([col] * (width // HD), axis=1)
        weight = jnp.exp2(col - c_row[:, :width] + mask[rows, :width])
        row_blocks.append((scores[rows, :width] * weight).astype(BF16))
    row_blocks[0] = jnp.concatenate([row_blocks[0], jnp.zeros((HD, CHUNK - HD), BF16)], axis=1)
    return jnp.concatenate(row_blocks, axis=0)


def inside_kernel(
    chunks, first, steps, crow_ref, cols_ref, mask_ref, k_ref, v_ref, gain_ref, q_hbm, gate_hbm,
    grad_hbm, *refs,
):
    q_ref, gate_ring, grad_ring, attn_ref, gnorm_ref, probs_ref, sems = refs[-7:]
    step = first + pl.program_id(0)
    slot = step % 2
    fetches = fetch_gates(step + 1, gate_hbm, grad_hbm, gate_ring, grad_ring, sems)
    fetches += fetch_q(step + 1, q_hbm, q_ref, sems.at[2])
    pl.when(step + 1 < steps)(lambda: start(fetches))

    cols_now = turned(cols_ref, step * RING)
    late = []
    for g in range(RING):
        h = step * RING + g
        cols = slice(g * HD, (g + 1) * HD)
        mine = head_span(h)
        for n, span in enumerate(spans(chunks)):
            q = q_ref[span, mine]
            scores = dot(q, k_ref[span, mine], NT)
            c_row = crow_ref[pl.ds(h, 1), span]
            probs = decayed(scores, spread(cols_now[span], g), c_row, mask_ref.at[n])
            inside = dot(probs, v_ref[span, mine])
            sig = sigmoid(gate_ring[slot, span, cols].astype(F32))
            gnorm = grad_ring[slot, span, cols].astype(F32) * sig * gain_ref[0:1, mine]
            save(late)
            late = save_probs(probs_ref, h, n, probs)
            late += [
                (attn_ref, (span, mine), inside),
                (gnorm_ref, (span, mine), gnorm.astype(BF16)),
            ]
    save(late)
    pl.when(step + 1 < steps)(lambda: wait(fetches))


def first_head(part, half, reverse):
    if part is None:
        return 0
    core, _, _ = place(reverse)
    return (core if part == 0 else 1 - core) * half


def outside_kernel(chunks, entering, inputs, part, cols_ref, enter_ref, q_ref, gnorm_ref, loc_ref, *refs):
    in_refs = refs[:inputs]
    if part == 1:
        before_ref, inside_ref, _, attn_ref, held_ref, sums_ref, sq_ref, inner_ref = refs[inputs:]
    else:
        inside_ref, attn_ref, held_ref, sums_ref, sq_ref, inner_ref = refs[inputs:]
    step = pl.program_id(0)
    steps = pl.num_programs(0)

    @pl.when(step == 0)
    def _():
        sq_ref[...] = jnp.zeros_like(sq_ref)
        inner_ref[...] = jnp.zeros_like(inner_ref)

    start_head = first_head(part, steps * WIDE, False) + step * WIDE
    heads = [start_head + g for g in range(WIDE)]
    cols_now = turned(cols_ref, enter_ref.shape[0] + start_head)
    carries = [entering(in_refs, h) for h in heads]
    late = []
    for n, span in enumerate(spans(chunks)):
        squares = sq_ref[span, :]
        inners = inner_ref[span, :]
        for g, h in enumerate(heads):
            mine = head_span(h)
            held = carries[g].astype(BF16)
            enter = spread(cols_now[span], g)
            attn = inside_ref[span, mine] + enter * dot(q_ref[span, mine], held)
            squares = squares + attn * attn
            inners = inners + gnorm_ref[span, mine].astype(F32) * attn
            if n + 1 < chunks:
                passing = enter_ref[pl.ds(h, 1), span][:, CHUNK - 1 : CHUNK]
                carries[g] = passing * carries[g] + loc_ref[h, n]
            save(late)
            late = [(held_ref, (h, n), held), (attn_ref, (span, mine), attn)]
        late += [(sq_ref, (span, slice(None)), squares), (inner_ref, (span, slice(None)), inners)]
    save(late)

    @pl.when(step == steps - 1)
    def _():
        for i, ref in enumerate((sq_ref, inner_ref)):
            total = jnp.sum(ref[...].T, axis=0, keepdims=True)
            sums_ref[i : i + 1, :] = total + before_ref[i : i + 1, :] if part == 1 else total


def turn_kernel(chunks, first, q_ref, attn_ref, *refs):
    turned_ref, flat_ref, done_ref = refs[-3:]
    step = pl.program_id(0)
    done_ref[...] = jnp.zeros_like(done_ref)
    late = []
    for g in range(WIDE):
        h = first + step * WIDE + g
        mine = head_span(h)
        for span in spans(chunks):
            turned_q = q_ref[span, mine].T
            flat = attn_ref[span, mine].astype(BF16)
            save(late)
            late = [(turned_ref, (h, slice(None), span), turned_q), (flat_ref, (span, mine), flat)]
    save(late)


def grad_kernel(chunks, enter_ref, sums_ref, others_ref, _, *refs):
    turned_q_ref, gnorm_ref, attn_ref, gate_hbm, grad_hbm = refs[:5]
    agrad_ref, turned_ref, bloc_ref, back_ref, alpha_ref = refs[5:10]
    gate_ring, grad_ring, beta_ref, sems = refs[10:]
    step = pl.program_id(0)
    following = fetch_gates(0, gate_hbm, grad_hbm, gate_ring, grad_ring, sems)

    @pl.when(step == 0)
    def _():
        start(following)
        sums = sums_ref[...] + others_ref[...]
        inverse = lax.rsqrt(sums[0:1] / WIDTH + epsilon)
        alpha_ref[...] = column(inverse)
        beta_ref[...] = column(inverse * inverse * inverse * sums[1:2] / WIDTH)

    late = []
    for g in range(WIDE):
        h = step * WIDE + g
        mine = head_span(h)
        back = None
        for n, span in reversed(list(enumerate(spans(chunks)))):
            enter = enter_ref[pl.ds(h, 1), span]
            gnorm = gnorm_ref[span, mine].astype(F32)
            attn, alpha = attn_ref[span, mine], alpha_ref[span, :]
            agrad = alpha * gnorm - attn * beta_ref[span, :]
            agrad = agrad.astype(BF16)
            qkeyed = (turned_q_ref[h, :, span].astype(F32) * enter).astype(BF16)
            local = dot(qkeyed, agrad)
            back = local if back is None else local + enter[:, CHUNK - 1 : CHUNK] * back
            save(late)
            late = [
                (agrad_ref, (span, mine), agrad),
                (turned_ref, (h, slice(None), span), agrad.T),
            ]
            if n > 0:
                late.append((bloc_ref, (h, n - 1), local))
        late.append((back_ref, h, back))
    save(late)

    @pl.when(step == pl.num_programs(0) - 1)
    def _():
        wait(following)


def inner_grad_kernel(
    chunks, first, steps, crow_ref, alpha_ref, cols_ref, mask_ref, k_ref, v_ref, flat_ref,
    held_ref, agrad_ref, probs_ref, turned_q_ref, turned_agrad_ref, gain_ref,
    gate_hbm, grad_hbm, *refs,
):
    dk_ref, dv_ref, gate_ring, grad_ring, out_ring, *outs_hbm, sems = refs[-9:]
    step = first + pl.program_id(0)
    slot = step % 2
    fetches = fetch_gates(step + 1, gate_hbm, grad_hbm, gate_ring, grad_ring, sems)
    puts = put_outs(step - 1, out_ring, outs_hbm, sems.at[pl.ds(2, 3)])
    pl.when(step + 1 < steps)(lambda: start(fetches))
    pl.when(step > 0)(lambda: start(puts))

    cols_now = turned(cols_ref, step * RING)
    late = []
    for g in range(RING):
        h = step * RING + g
        cols = slice(g * HD, (g + 1) * HD)
        mine = head_span(h)
        for n, span in enumerate(spans(chunks)):
            k, v, agrad = k_ref[span, mine], v_ref[span, mine], agrad_ref[span, mine]
            both = dot(agrad, jnp.concatenate([v, held_ref[h, n]], axis=0), NT)
            c_row = crow_ref[pl.ds(h, 1), span]
            dscore = decayed(both[:, :CHUNK], spread(cols_now[span], g), c_row, mask_ref.at[n])
            enter = spread(cols_now[span], crow_ref.shape[0] + g)
            dq = dot(dscore, k) + enter * both[:, CHUNK:]
            dv = dot(turned_agrad_ref[h, :, span], load_probs(probs_ref, h, n))
            dk = dot(turned_q_ref[h, :, span], dscore)
            normed = flat_ref[span, mine].astype(F32) * alpha_ref[span, :] * gain_ref[0:1, mine]
            sig = sigmoid(gate_ring[slot, span, cols].astype(F32))
            gated = normed * sig
            ggate = grad_ring[slot, span, cols].astype(F32) * gated * (1.0 - sig)
            save(late)
            late = [
                (out_ring, (slot, 0, span, cols), dq.astype(BF16)),
                (dv_ref, (h, slice(None), span), dv.astype(BF16)),
                (dk_ref, (h, slice(None), span), dk.astype(BF16)),
                (out_ring, (slot, 1, span, cols), gated.astype(BF16)),
                (out_ring, (slot, 2, span, cols), ggate.astype(BF16)),
            ]
    save(late)
    pl.when(step + 1 < steps)(lambda: wait(fetches))
    pl.when(step > 0)(lambda: wait(puts))


def outer_grad_kernel(chunks, last, entering, inputs, part, enter_ref, leave_ref, k_ref, v_ref, *refs):
    in_refs = refs[:inputs]
    dkin_ref, dvin_ref, bloc_ref = refs[inputs : inputs + 3]
    step = pl.program_id(0)
    steps = pl.num_programs(0)
    start_head = first_head(part, steps * GROUP, True) + step * GROUP
    if part == 1:
        *grads_hbm, parts_ref, sems = refs[-4:]
    else:
        out_ring = refs[inputs + 3]
        *outs_hbm, dk_hbm, dv_hbm, parts_ref, sems, last_sems = refs[-8:]
        grads_hbm = [dk_hbm, dv_hbm]
        puts = put_outs(last, out_ring, outs_hbm, last_sems)
        pl.when(step == 0)(lambda: start(puts))

    def put(back):
        slot = (step - back) % 2
        here = head_span(start_head - back * GROUP, GROUP)
        return [
            pltpu.make_async_copy(parts_ref.at[slot, i], out.at[:, here], sems.at[slot, i])
            for i, out in enumerate(grads_hbm)
        ]

    slot = step % 2
    pl.when(step > 1)(lambda: wait(put(2)))
    late = []
    for g in range(GROUP):
        h = start_head + g
        cols = slice(g * HD, (g + 1) * HD)
        mine = head_span(h)
        carry = entering(in_refs, h)
        for n, span in reversed(list(enumerate(spans(chunks)))):
            leave = leave_ref[pl.ds(h, 1), span]
            back = carry.astype(BF16)
            dk = dkin_ref[h, :, span].astype(F32) + leave * dot(back, v_ref[span, mine], NT)
            dv = dvin_ref[h, :, span].astype(F32) + leave * dot(back.T, k_ref[span, mine], NT)
            if n > 0:
                passing = enter_ref[pl.ds(h, 1), span][:, CHUNK - 1 : CHUNK]
                carry = bloc_ref[h, n - 1] + passing * carry
            save(late)
            late = [
                (parts_ref, (slot, 0, span, cols), dk.astype(BF16).T),
                (parts_ref, (slot, 1, span, cols), dv.astype(BF16).T),
            ]
    save(late)
    start(put(0))

    @pl.when(step == steps - 1)
    def _():
        pl.when(step > 0)(lambda: wait(put(1)))
        wait(put(0))
        if part != 1:
            wait(puts)


def hbm(x):
    return pltpu.with_memory_space_constraint(x, pltpu.HBM)


def kept(*arrays):
    spec = pl.BlockSpec(memory_space=pltpu.VMEM)
    return [(pltpu.with_memory_space_constraint(x, pltpu.VMEM), spec) for x in arrays]


def keep(dims, dtype):
    return pltpu.VMEM(dims, dtype), pl.BlockSpec(memory_space=pltpu.VMEM)


def add_kernel(a_ref, b_ref, _, out_ref):
    out_ref[...] = a_ref[...] + b_ref[...]


def call(kernel, grid, ins, outs, scratch=(), aliases=None, flops=0, moved=0, exps=0):
    return pl.pallas_call(
        kernel,
        grid=grid,
        in_specs=[spec for _, spec in ins],
        out_specs=[spec for _, spec in outs],
        out_shape=[shape for shape, _ in outs],
        scratch_shapes=list(scratch),
        input_output_aliases=aliases or {},
        compiler_params=pltpu.CompilerParams(
            dimension_semantics=("arbitrary",) * len(grid), vmem_limit_bytes=ROOM * MIB
        ),
        cost_estimate=pl.CostEstimate(flops=flops, bytes_accessed=moved, transcendentals=exps),
    )(*[x for x, _ in ins])


def after(x, *others):
    return lax.optimization_barrier((x, *others))[0]


def across(x, flips, devices=8):
    return lax.ppermute(x, "seq", [(i, i ^ flips) for i in range(devices)])


def place(reverse):
    index = lax.axis_index("seq")
    index = 7 - index if reverse else index
    return lax.rem(index, 2), lax.rem(lax.div(index, 2), 2), lax.div(index, 4)


def pair_kernel(reverse, state_ref, other_ref, pass_ref, beside_ref, x_ref, y_ref, chip_ref):
    core, _, _ = place(reverse)
    quarter = x_ref.shape[0]
    chip_pass = pass_ref[...] * beside_ref[...]
    chip_ref[...] = chip_pass
    for i in range(quarter):
        rows = [chip_ref[pl.ds(core * 2 * quarter + at, 1), :] for at in (i, quarter + i)]
        x_ref[i, HD:, :] = jnp.concatenate(rows + [jnp.zeros((6, HD), F32)], axis=0)
        for at, out_ref in ((i, x_ref), (quarter + i, y_ref)):
            h = core * 2 * quarter + at
            mine, other = state_ref[h], other_ref[h]

            @pl.when(core == 0)
            def _():
                out_ref[i, :HD, :] = beside_ref[pl.ds(h, 1), :] * mine + other

            @pl.when(core == 1)
            def _():
                out_ref[i, :HD, :] = pass_ref[pl.ds(h, 1), :] * other + mine


def row_kernel(
    reverse, to_x_ref, to_y_ref, from_x_ref, from_y_ref, chip_ref, far_ref, row_ref, sent_ref,
):
    core, x, y = place(reverse)
    quarter = row_ref.shape[0]
    for i in range(quarter):
        h = core * 2 * quarter + i
        hy = h + quarter

        @pl.when(x == 0)
        def _():
            side = from_x_ref[i, HD : HD + 1, :]
            row_ref[i] = side * to_x_ref[i, :HD, :] + from_x_ref[i, :HD, :]

        @pl.when(x == 1)
        def _():
            through = chip_ref[pl.ds(h, 1), :] * from_x_ref[i, :HD, :]
            row_ref[i] = through + to_x_ref[i, :HD, :]

        @pl.when(y == 0)
        def _():
            sent_ref[i] = to_y_ref[i]

        @pl.when((y == 1) & (x == 0))
        def _():
            far = far_ref[pl.ds(hy, 1), :] * from_y_ref[i]
            sent_ref[i] = chip_ref[pl.ds(hy, 1), :] * far + to_y_ref[i]

        @pl.when((y == 1) & (x == 1))
        def _():
            sent_ref[i] = from_y_ref[i]


def ahead_kernel(
    reverse, from_x_ref, from_y_ref, row_ref, sent_ref, far_ref, out_ref,
):
    core, x, y = place(reverse)
    quarter = row_ref.shape[0]
    for i in range(quarter):
        h = core * 2 * quarter + i
        hy = h + quarter

        @pl.when((y == 0) & (x == 0))
        def _():
            out_ref[i] = jnp.zeros_like(out_ref[i])
            out_ref[quarter + i] = jnp.zeros_like(out_ref[i])

        @pl.when((y == 0) & (x == 1))
        def _():
            out_ref[i] = from_x_ref[i, :HD, :]
            out_ref[quarter + i] = sent_ref[i]

        @pl.when((y == 1) & (x == 0))
        def _():
            out_ref[i] = row_ref[i]
            out_ref[quarter + i] = far_ref[pl.ds(hy, 1), :] * from_y_ref[i] + sent_ref[i]

        @pl.when((y == 1) & (x == 1))
        def _():
            side_x, side_y = (from_x_ref[i, HD + j : HD + j + 1, :] for j in range(2))
            out_ref[i] = side_x * row_ref[i] + from_x_ref[i, :HD, :]
            out_ref[quarter + i] = side_y * from_y_ref[i] + sent_ref[i]


def cube_entering(reverse, refs, h):
    chip_ref, other_ref, beside_pass_ref = refs
    core, _, _ = place(reverse)
    chip = chip_ref[lax.rem(h, chip_ref.shape[0])]
    through = beside_pass_ref[pl.ds(h, 1), :] * chip + other_ref[h]
    return jnp.where(core == 0, chip, through)


def plain_entering(refs, h):
    return refs[0][h]


def cube_scan(state, own_pass, passes, fill, finish, reverse):
    heads = state.shape[0]
    quarter = heads // 4
    part = keep((quarter, HD, HD), F32)

    other = across(state, 1)
    beside_pass = passes[0] if passes else across(own_pass, 1)
    other, beside_pass = lax.optimization_barrier((other, beside_pass, fill(0, state)))[:2]
    to_x, to_y, chip_pass = call(
        functools.partial(pair_kernel, reverse), (),
        kept(state, other, own_pass, beside_pass),
        [keep((quarter, HD + 8, HD), F32), part, keep((heads, HD), F32)],
    )

    from_x, from_y = across(to_x, 2), across(to_y, 4)
    far_pass = passes[1] if passes else across(chip_pass, 6)
    from_x, from_y, far_pass = lax.optimization_barrier(
        (from_x, from_y, far_pass, fill(1, to_y))
    )[:3]
    row, sent = call(
        functools.partial(row_kernel, reverse), (),
        kept(to_x, to_y, from_x, from_y, chip_pass, far_pass), [part, part],
    )

    row_in, sent_in = across(row, 4), across(sent, 2)
    row_in, sent_in = lax.optimization_barrier((row_in, sent_in, fill(2, sent)))[:2]
    (ahead,) = call(
        functools.partial(ahead_kernel, reverse), (),
        kept(from_x, from_y, row_in, sent_in, far_pass),
        [keep((2 * quarter, HD, HD), F32)],
    )

    beside = across(ahead, 1)
    entering = functools.partial(cube_entering, reverse)
    beside = after(beside, finish(0, entering, (ahead, other, beside_pass)))
    finish(1, entering, (beside, other, beside_pass))
    return beside_pass, far_pass


def doubling_scan(state, own_pass, fill, reverse):
    devices = lax.axis_size("seq")
    index = lax.axis_index("seq")
    passes = lax.all_gather(own_pass, "seq")
    if reverse:
        passes = passes[::-1]
        index = devices - 1 - index
    route = lambda hop: [
        (i, i - hop if reverse else i + hop)
        for i in range(devices)
        if 0 <= (i - hop if reverse else i + hop) < devices
    ]
    for window in range(WINDOWS):
        state = after(state, fill(window, state))
    hop = 1
    while hop < devices:
        factor = lax.dynamic_index_in_dim(passes, index, 0, False)
        state = factor[:, None, :] * lax.ppermute(state, "seq", route(hop)) + state
        before = jnp.concatenate([jnp.zeros_like(passes[:hop]), passes[:-hop]], axis=0)
        passes = passes * before
        hop *= 2
    return lax.ppermute(state, "seq", route(1))


def scan_devices(state, own_pass, passes, fill, finish, reverse):
    if lax.axis_size("seq") == 8 and state.shape[0] % 4 == 0:
        return cube_scan(state, own_pass, passes, fill, finish, reverse)
    finish(None, plain_entering, (doubling_scan(state, own_pass, fill, reverse),))
    return None


def body(queries, key_rows, value_rows, log_decay, doc_start, gate_input, norm_gain, out_grad):
    rows, cols = queries.shape
    heads = cols // HD
    chunks = rows // CHUNK
    parts = lax.axis_size("head")
    grid = (heads // GROUP,)
    shares = [heads // 4]
    shares.append((heads - shares[0] + RING) // 2 // RING * RING)
    shares.append(heads - sum(shares))
    bases = [0, shares[0], heads - shares[2]]
    big = rows * cols * 2
    tile = 2 * rows * CHUNK * cols
    small = 2 * rows * HD * cols

    whole = lambda *dims: pl.BlockSpec(dims, lambda i: (0,) * len(dims))
    anywhere = pl.BlockSpec(memory_space=pl.ANY)

    by_head = (heads, HD, rows)
    local_dims = (heads, chunks, HD, HD)
    wide_out = (pltpu.HBM((rows, cols), BF16), anywhere)
    ring = keep((2, rows, RING * HD), BF16)
    probs_kept = keep((heads, chunks, CHUNK + HD, HD), BF16)
    out_ring = keep((2, 3, rows, RING * HD), BF16)
    sems = pltpu.SemaphoreType.DMA
    queries, key_rows, value_rows, gate_input, out_grad = map(
        hbm, (queries, key_rows, value_rows, gate_input, out_grad)
    )
    doc_row = doc_start.reshape(1, rows)
    gain_row = norm_gain.reshape(1, cols)

    by_token = (rows, cols)
    steps = heads // GROUP
    (
        crow, enter, leave, rrow, keys, values, local, state, own_pass, gain, kept_q, *rings
    ) = call(
        functools.partial(state_kernel, chunks, steps),
        grid,
        [
            (hbm(x), anywhere)
            for x in (
                log_decay, doc_row, gain_row, key_rows, value_rows, queries, gate_input, out_grad
            )
        ],
        [keep((heads, rows), F32)] * 3
        + [
            keep((8, rows), F32), keep(by_token, BF16), keep(by_token, BF16),
            keep((heads, chunks - 1, HD, HD), F32), keep((heads, HD, HD), F32), keep((heads, HD), F32),
            keep((1, cols), F32), keep(by_token, BF16), ring, ring,
        ],
        [
            pltpu.VMEM((heads, rows), F32), pltpu.VMEM((1, rows), jnp.int32),
            sems((2, steps)), sems((3,)), sems((3,)),
        ],
        flops=small, moved=2 * big,
    )

    ready = []
    made = [kept_q, *rings]

    def fill_forward(window, tie):
        if not ready:
            ready[:] = call(
                prepare_kernel, (), kept(after(rrow, tie), crow, enter),
                [keep((chunks, CHUNK, CHUNK), F32), keep((rows, HD), F32)],
                flops=8 * rows * CHUNK,
            )
        mask, columns = ready
        ins = kept(after(crow, tie), columns, mask, keys, values, gain)
        ins += [(x, anywhere) for x in (queries, gate_input, out_grad)]
        aliases = {len(ins) + i: i for i in range(len(made))}
        ins += kept(*made)
        made[:] = call(
            functools.partial(inside_kernel, chunks, bases[window] // RING, heads // RING),
            (shares[window] // RING,),
            ins,
            [
                keep(by_token, BF16), ring, ring, keep(by_token, F32), keep(by_token, BF16),
                probs_kept,
            ],
            [sems((3,))],
            aliases=aliases,
            flops=2 * tile // WINDOWS, moved=5 * big // WINDOWS,
            exps=rows * (CHUNK + HD) * heads // WINDOWS,
        )
        return made[4]

    tall = pltpu.VMEM((rows, HD), F32)
    reduced = []

    def finish_forward(part, entering, refs):
        mask, columns = ready
        kept_q, _, _, inside, gnorm, _ = made
        ins = kept(columns, enter, kept_q, gnorm, local, *refs)
        outs = [keep(by_token, F32), keep(local_dims, BF16), keep((2, rows), F32)]
        scratch = [tall, tall]
        if part == 1:
            aliases = {len(ins) + 1: 0, len(ins) + 2: 1}
            ins += kept(reduced[1], inside, reduced[0])
        else:
            aliases = {len(ins): 0}
            ins += kept(inside)
        results = call(
            functools.partial(
                outside_kernel, chunks, entering, len(refs), part
            ),
            (heads // WIDE if part is None else heads // 2 // WIDE,),
            ins, outs, scratch, aliases,
            flops=small, moved=big,
        )
        made[3], *reduced[:] = results
        return reduced[1]

    passes = scan_devices(state, own_pass, None, fill_forward, finish_forward, False)
    mask, columns = ready
    kept_q, _, _, attn, gnorm, probs = made
    held, sums = reduced

    flat = []
    halves = [0, heads // 2]
    token = keep((8, HD), F32)

    def turn(sums):
        first = halves.pop(0)
        results = call(
            functools.partial(turn_kernel, chunks, first),
            (heads // 2 // WIDE,),
            kept(kept_q, attn, sums, *flat),
            [keep(by_head, BF16), keep(by_token, BF16), token],
            aliases={3 + i: i for i in range(len(flat))},
            flops=rows * cols, moved=2 * big,
        )
        flat[:] = results[:2]
        return results[2]

    apart = 1
    while True:
        other_sums = lax.ppermute(sums, "head", [(i, i ^ apart) for i in range(parts)])
        done = turn(sums) if halves else done
        apart *= 2
        if apart >= parts:
            break
        (sums,) = call(add_kernel, (), kept(sums, other_sums, done), [keep((2, rows), F32)])
    while halves:
        done = turn(sums)
    turned_q, attn_flat = flat

    agrad, turned_agrad, bloc, back, alpha, *rings = call(
        functools.partial(grad_kernel, chunks),
        (heads // WIDE,),
        kept(enter, sums, other_sums, done, turned_q, gnorm, attn)
        + [(hbm(x), anywhere) for x in (gate_input, out_grad)],
        [
            keep(by_token, BF16), keep(by_head, BF16), keep((heads, chunks - 1, HD, HD), F32),
            keep((heads, HD, HD), F32), keep((rows, HD), F32), ring, ring,
        ],
        [tall, sems((2,))],
        {5: 0},
        flops=small, moved=big,
    )

    inner = [turned_q, turned_agrad, *rings]

    def fill_backward(window, tie):
        ins = kept(
            after(crow, tie), alpha, columns, mask, keys, values, attn_flat, held, agrad, probs,
            inner[0], inner[1], gain,
        )
        ins += [(hbm(x), anywhere) for x in (gate_input, out_grad)]
        aliases = {10: 0, 11: 1}
        aliases.update({len(ins) - 2 + i: i for i in range(2, len(inner))})
        ins += kept(*inner[2:5]) + [(hbm(x), anywhere) for x in inner[5:]]
        inner[:] = call(
            functools.partial(inner_grad_kernel, chunks, bases[window] // RING, heads // RING),
            (shares[window] // RING,),
            ins,
            [keep(by_head, BF16)] * 2 + [ring, ring, out_ring] + [wide_out] * 3,
            [sems((5,))],
            aliases=aliases,
            flops=(4 * tile + small) // WINDOWS, moved=7 * big // WINDOWS,
            exps=rows * (CHUNK + HD) * heads // WINDOWS,
        )
        return inner[5]

    grads = []

    def finish_backward(part, entering, refs):
        ins = kept(enter, leave, keys, values, *refs, inner[0], inner[1], bloc)
        scratch = [pltpu.VMEM((2, 2, rows, GROUP * HD), BF16), sems((2, 2))]
        if part == 1:
            aliases = {len(ins): 0, len(ins) + 1: 1}
            ins += [(hbm(x), anywhere) for x in grads]
            outs = [wide_out] * 2
        else:
            aliases = {len(ins) + 1 + i: i for i in range(3)}
            ins += kept(inner[4]) + [(hbm(x), anywhere) for x in inner[5:]]
            outs = [wide_out] * 5
            scratch.append(sems((3,)))
        results = call(
            functools.partial(
                outer_grad_kernel, chunks, heads // RING - 1, entering, len(refs), part
            ),
            (steps if part is None else steps // 2,),
            ins, outs, scratch, aliases,
            flops=2 * small, moved=2 * big,
        )
        grads[:] = results[-2:]
        if part != 1:
            inner[5:] = results[:3]
        return grads[0]

    scan_devices(back, own_pass, passes, fill_backward, finish_backward, True)
    dq, gated, gate_grad = inner[5:]
    return (gated, gate_grad, dq, *grads)


def solution(mesh):
    in_specs = (
        P("seq", "head"),
        P("seq", "head"),
        P("seq", "head"),
        P("head", "seq"),
        P("seq"),
        P("seq", "head"),
        P("head"),
        P("seq", "head"),
    )
    out_specs = (P("seq", "head"),) * 5
    return jax.shard_map(body, mesh=mesh, in_specs=in_specs, out_specs=out_specs, check_vma=False)
```

```python
import functools

import jax
import jax.numpy as jnp
from jax import lax
from jax.experimental import pallas as pl
from jax.experimental.pallas import tpu as pltpu
from jax.sharding import PartitionSpec as P

HEAD_TOTAL = 64
HD = 128
CHUNK = 256
GROUP = 2
WIDE = 4
RING = 2
AHEAD = 3
WINDOWS = 3
ROOM = 4
WIDTH = HEAD_TOTAL * HD

epsilon = 1e-06
LOG2E = 1.4426950408889634

F32 = jnp.float32
BF16 = jnp.bfloat16
MIB = 1024 * 1024
NT = ((1,), (1,))


def dot(a, b, dims=((1,), (0,))):
    return lax.dot_general(a, b, (dims, ((), ())), preferred_element_type=F32)


def chunk_cumsum(x):
    lane = lax.broadcasted_iota(jnp.int32, x.shape, 1) % CHUNK
    shift = 1
    while shift < CHUNK:
        x = x + jnp.where(lane >= shift, pltpu.roll(x, shift, 1), 0.0)
        shift *= 2
    return x


def spans(chunks):
    return [slice(n * CHUNK, (n + 1) * CHUNK) for n in range(chunks)]


def head_span(head, count=1):
    return pl.ds(pl.multiple_of(head * HD, HD), count * HD)


def save(stores):
    for ref, index, value in stores:
        ref[index] = value


def save_probs(probs_ref, h, n, probs):
    left, right = slice(0, CHUNK), slice(CHUNK, CHUNK + HD)
    return [
        (probs_ref, (h, n, left), probs[:, :HD]),
        (probs_ref, (h, n, right), probs[HD:, HD:]),
    ]


def load_probs(probs_ref, h, n):
    right = jnp.concatenate([jnp.zeros((HD, HD), BF16), probs_ref[h, n, CHUNK:, :]], axis=0)
    return jnp.concatenate([probs_ref[h, n, :CHUNK, :], right], axis=1)


def sigmoid(x):
    return 0.5 * jnp.tanh(0.5 * x) + 0.5


def spread(cols, lane):
    return jnp.broadcast_to(cols[:, lane : lane + 1], cols.shape)


def turned(cols_ref, lane):
    return pltpu.roll(cols_ref[...], (HD - lane) % HD, 1)


def column(row):
    return jnp.broadcast_to(row, (HD, row.shape[1])).T


def start(copies):
    for copy in copies:
        copy.start()


def wait(copies):
    for copy in copies:
        copy.wait()


def group_of(at):
    return head_span(at * RING, RING)


def fetch_gates(at, gate_hbm, grad_hbm, gate_ring, grad_ring, sems):
    slot = at % 2
    return [
        pltpu.make_async_copy(gate_hbm.at[:, group_of(at)], gate_ring.at[slot], sems.at[0]),
        pltpu.make_async_copy(grad_hbm.at[:, group_of(at)], grad_ring.at[slot], sems.at[1]),
    ]


def fetch_q(at, q_hbm, q_ref, sem):
    return [pltpu.make_async_copy(q_hbm.at[:, group_of(at)], q_ref.at[:, group_of(at)], sem)]


def put_outs(at, out_ring, outs_hbm, sems):
    return [
        pltpu.make_async_copy(out_ring.at[at % 2, i], out.at[:, group_of(at)], sems.at[i])
        for i, out in enumerate(outs_hbm)
    ]


def state_kernel(
    chunks, steps, lc_hbm, doc_hbm, gain_hbm, k_hbm, v_hbm, q_hbm, gate_hbm, grad_hbm,
    crow_ref, enter_ref, leave_ref, rrow_ref, k_ref, v_ref, loc_ref, state_ref, pass_ref,
    gain_ref, q_ref, gate_ring, grad_ring, lc_ref, doc_ref, sems, small_sems, next_sems,
):
    step = pl.program_id(0)
    small = [
        pltpu.make_async_copy(lc_hbm, lc_ref, small_sems.at[0]),
        pltpu.make_async_copy(doc_hbm, doc_ref, small_sems.at[1]),
        pltpu.make_async_copy(gain_hbm, gain_ref, small_sems.at[2]),
    ]
    following = fetch_gates(0, gate_hbm, grad_hbm, gate_ring, grad_ring, next_sems)
    following += fetch_q(0, q_hbm, q_ref, next_sems.at[2])

    def copies(at):
        here = head_span(at * GROUP, GROUP)
        return (
            pltpu.make_async_copy(k_hbm.at[:, here], k_ref.at[:, here], sems.at[0, at]),
            pltpu.make_async_copy(v_hbm.at[:, here], v_ref.at[:, here], sems.at[1, at]),
        )

    @pl.when(step == 0)
    def _():
        start(small)
        for at in range(min(AHEAD, steps)):
            start(copies(at))
        wait(small)
        c = chunk_cumsum(lc_ref[...] * LOG2E)
        r = chunk_cumsum(jnp.broadcast_to(doc_ref[...].astype(F32), (8, doc_ref.shape[1])))
        crow_ref[...] = c
        rrow_ref[...] = r
        enter_ref[...] = jnp.where(r[0:1] == 0.0, jnp.exp2(c), 0.0)
        for span in spans(chunks):
            cn, rn = c[:, span], r[0:1, span]
            leave_ref[:, span] = jnp.where(rn == rn[:, -1:], jnp.exp2(cn[:, -1:] - cn), 0.0)

    pl.when(step + AHEAD < steps)(lambda: start(copies(step + AHEAD)))
    pl.when(step + AHEAD == steps)(lambda: start(following))
    wait(copies(step))
    late = []
    for g in range(GROUP):
        h = step * GROUP + g
        mine = head_span(h)
        state = None
        total = None
        for n, span in enumerate(spans(chunks)):
            keyed = (k_ref[span, mine].T.astype(F32) * leave_ref[pl.ds(h, 1), span]).astype(BF16)
            local = dot(keyed, v_ref[span, mine])
            passing = enter_ref[pl.ds(h, 1), span][:, CHUNK - 1 : CHUNK]
            state = local if state is None else passing * state + local
            total = passing if total is None else passing * total
            save(late)
            late = [(loc_ref, (h, n), local)] if n + 1 < chunks else []
        late.append((state_ref, h, state))
        late.append((pass_ref, (pl.ds(h, 1), slice(None)), jnp.broadcast_to(total, (1, HD))))
    save(late)

    @pl.when(step == steps - 1)
    def _():
        wait(following)


def prepare_kernel(rrow_ref, crow_ref, enter_ref, mask_ref, cols_ref):
    sub = lax.broadcasted_iota(jnp.int32, (CHUNK, CHUNK), 0)
    lane = lax.broadcasted_iota(jnp.int32, (CHUNK, CHUNK), 1)
    spare = jnp.zeros((HD - 2 * crow_ref.shape[0], CHUNK), F32)
    for n, span in enumerate(spans(mask_ref.shape[0])):
        r_row = rrow_ref[0:1, span]
        r_col = jnp.concatenate([column(r_row)] * (CHUNK // HD), axis=1)
        mask_ref[n] = jnp.where((r_col == r_row) & (lane <= sub), 0.0, -jnp.inf)
        cols_ref[span, :] = jnp.concatenate([crow_ref[:, span], enter_ref[:, span], spare], axis=0).T


def decayed(scores, c_col, c_row, mask):
    top, low = slice(0, HD), slice(HD, CHUNK)
    row_blocks = []
    for rows, width in ((top, HD), (low, CHUNK)):
        col = c_col[rows]
        col = col if width == HD else jnp.concatenate([col] * (width // HD), axis=1)
        weight = jnp.exp2(col - c_row[:, :width] + mask[rows, :width])
        row_blocks.append((scores[rows, :width] * weight).astype(BF16))
    row_blocks[0] = jnp.concatenate([row_blocks[0], jnp.zeros((HD, CHUNK - HD), BF16)], axis=1)
    return jnp.concatenate(row_blocks, axis=0)


def inside_kernel(
    chunks, first, steps, crow_ref, cols_ref, mask_ref, k_ref, v_ref, gain_ref, q_hbm, gate_hbm,
    grad_hbm, *refs,
):
    q_ref, gate_ring, grad_ring, attn_ref, gnorm_ref, probs_ref, sems = refs[-7:]
    step = first + pl.program_id(0)
    slot = step % 2
    fetches = fetch_gates(step + 1, gate_hbm, grad_hbm, gate_ring, grad_ring, sems)
    fetches += fetch_q(step + 1, q_hbm, q_ref, sems.at[2])
    pl.when(step + 1 < steps)(lambda: start(fetches))

    cols_now = turned(cols_ref, step * RING)
    late = []
    for g in range(RING):
        h = step * RING + g
        cols = slice(g * HD, (g + 1) * HD)
        mine = head_span(h)
        for n, span in enumerate(spans(chunks)):
            q = q_ref[span, mine]
            scores = dot(q, k_ref[span, mine], NT)
            c_row = crow_ref[pl.ds(h, 1), span]
            probs = decayed(scores, spread(cols_now[span], g), c_row, mask_ref.at[n])
            inside = dot(probs, v_ref[span, mine])
            sig = sigmoid(gate_ring[slot, span, cols].astype(F32))
            gnorm = grad_ring[slot, span, cols].astype(F32) * sig * gain_ref[0:1, mine]
            save(late)
            late = save_probs(probs_ref, h, n, probs)
            late += [
                (attn_ref, (span, mine), inside),
                (gnorm_ref, (span, mine), gnorm.astype(BF16)),
            ]
    save(late)
    pl.when(step + 1 < steps)(lambda: wait(fetches))


def first_head(part, half, reverse):
    if part is None:
        return 0
    core, _, _ = place(reverse)
    return (core if part == 0 else 1 - core) * half


def outside_kernel(chunks, entering, inputs, part, cols_ref, enter_ref, q_ref, gnorm_ref, loc_ref, *refs):
    in_refs = refs[:inputs]
    if part == 1:
        before_ref, inside_ref, _, attn_ref, held_ref, sums_ref, sq_ref, inner_ref = refs[inputs:]
    else:
        inside_ref, attn_ref, held_ref, sums_ref, sq_ref, inner_ref = refs[inputs:]
    step = pl.program_id(0)
    steps = pl.num_programs(0)

    @pl.when(step == 0)
    def _():
        sq_ref[...] = jnp.zeros_like(sq_ref)
        inner_ref[...] = jnp.zeros_like(inner_ref)

    start_head = first_head(part, steps * WIDE, False) + step * WIDE
    heads = [start_head + g for g in range(WIDE)]
    cols_now = turned(cols_ref, enter_ref.shape[0] + start_head)
    carries = [entering(in_refs, h) for h in heads]
    late = []
    for n, span in enumerate(spans(chunks)):
        squares = sq_ref[span, :]
        inners = inner_ref[span, :]
        for g, h in enumerate(heads):
            mine = head_span(h)
            held = carries[g].astype(BF16)
            enter = spread(cols_now[span], g)
            attn = inside_ref[span, mine] + enter * dot(q_ref[span, mine], held)
            squares = squares + attn * attn
            inners = inners + gnorm_ref[span, mine].astype(F32) * attn
            if n + 1 < chunks:
                passing = enter_ref[pl.ds(h, 1), span][:, CHUNK - 1 : CHUNK]
                carries[g] = passing * carries[g] + loc_ref[h, n]
            save(late)
            late = [(held_ref, (h, n), held), (attn_ref, (span, mine), attn)]
        late += [(sq_ref, (span, slice(None)), squares), (inner_ref, (span, slice(None)), inners)]
    save(late)

    @pl.when(step == steps - 1)
    def _():
        for i, ref in enumerate((sq_ref, inner_ref)):
            total = jnp.sum(ref[...].T, axis=0, keepdims=True)
            sums_ref[i : i + 1, :] = total + before_ref[i : i + 1, :] if part == 1 else total


def turn_kernel(chunks, first, q_ref, attn_ref, gain_ref, *refs):
    turned_ref, flat_ref, done_ref = refs[-3:]
    step = pl.program_id(0)
    done_ref[...] = jnp.zeros_like(done_ref)
    late = []
    for g in range(WIDE):
        h = first + step * WIDE + g
        mine = head_span(h)
        for span in spans(chunks):
            turned_q = q_ref[span, mine].T
            flat = (attn_ref[span, mine] * gain_ref[0:1, mine]).astype(BF16)
            save(late)
            late = [(turned_ref, (h, slice(None), span), turned_q), (flat_ref, (span, mine), flat)]
    save(late)


def grad_kernel(chunks, enter_ref, sums_ref, others_ref, _, *refs):
    turned_q_ref, gnorm_ref, attn_ref, gate_hbm, grad_hbm = refs[:5]
    agrad_ref, turned_ref, bloc_ref, back_ref, alpha_ref = refs[5:10]
    gate_ring, grad_ring, beta_ref, sems = refs[10:]
    step = pl.program_id(0)
    following = fetch_gates(0, gate_hbm, grad_hbm, gate_ring, grad_ring, sems)

    @pl.when(step == 0)
    def _():
        start(following)
        sums = sums_ref[...] + others_ref[...]
        inverse = lax.rsqrt(sums[0:1] / WIDTH + epsilon)
        alpha_ref[...] = column(inverse)
        beta_ref[...] = column(inverse * inverse * inverse * sums[1:2] / WIDTH)

    late = []
    for g in range(WIDE):
        h = step * WIDE + g
        mine = head_span(h)
        back = None
        for n, span in reversed(list(enumerate(spans(chunks)))):
            enter = enter_ref[pl.ds(h, 1), span]
            gnorm = gnorm_ref[span, mine].astype(F32)
            attn, alpha = attn_ref[span, mine], alpha_ref[span, :]
            agrad = alpha * gnorm - attn * beta_ref[span, :]
            agrad = agrad.astype(BF16)
            qkeyed = (turned_q_ref[h, :, span].astype(F32) * enter).astype(BF16)
            local = dot(qkeyed, agrad)
            back = local if back is None else local + enter[:, CHUNK - 1 : CHUNK] * back
            save(late)
            late = [
                (agrad_ref, (span, mine), agrad),
                (turned_ref, (h, slice(None), span), agrad.T),
            ]
            if n > 0:
                late.append((bloc_ref, (h, n - 1), local))
        late.append((back_ref, h, back))
    save(late)

    @pl.when(step == pl.num_programs(0) - 1)
    def _():
        wait(following)


def inner_grad_kernel(
    chunks, first, steps, crow_ref, alpha_ref, cols_ref, mask_ref, k_ref, v_ref, flat_ref,
    held_ref, agrad_ref, probs_ref, turned_q_ref, turned_agrad_ref, gate_hbm,
    grad_hbm, *refs,
):
    dk_ref, dv_ref, gate_ring, grad_ring, out_ring, *outs_hbm, sems = refs[-9:]
    step = first + pl.program_id(0)
    slot = step % 2
    fetches = fetch_gates(step + 1, gate_hbm, grad_hbm, gate_ring, grad_ring, sems)
    puts = put_outs(step - 1, out_ring, outs_hbm, sems.at[pl.ds(2, 3)])
    pl.when(step + 1 < steps)(lambda: start(fetches))
    pl.when(step > 0)(lambda: start(puts))

    cols_now = turned(cols_ref, step * RING)
    late = []
    for g in range(RING):
        h = step * RING + g
        cols = slice(g * HD, (g + 1) * HD)
        mine = head_span(h)
        for n, span in enumerate(spans(chunks)):
            k, v, agrad = k_ref[span, mine], v_ref[span, mine], agrad_ref[span, mine]
            both = dot(agrad, jnp.concatenate([v, held_ref[h, n]], axis=0), NT)
            c_row = crow_ref[pl.ds(h, 1), span]
            dscore = decayed(both[:, :CHUNK], spread(cols_now[span], g), c_row, mask_ref.at[n])
            enter = spread(cols_now[span], crow_ref.shape[0] + g)
            dq = dot(dscore, k) + enter * both[:, CHUNK:]
            dv = dot(turned_agrad_ref[h, :, span], load_probs(probs_ref, h, n))
            dk = dot(turned_q_ref[h, :, span], dscore)
            normed = flat_ref[span, mine].astype(F32) * alpha_ref[span, :]
            sig = sigmoid(gate_ring[slot, span, cols].astype(F32))
            gated = normed * sig
            ggate = grad_ring[slot, span, cols].astype(F32) * gated * (1.0 - sig)
            save(late)
            late = [
                (out_ring, (slot, 0, span, cols), dq.astype(BF16)),
                (dv_ref, (h, slice(None), span), dv.astype(BF16)),
                (dk_ref, (h, slice(None), span), dk.astype(BF16)),
                (out_ring, (slot, 1, span, cols), gated.astype(BF16)),
                (out_ring, (slot, 2, span, cols), ggate.astype(BF16)),
            ]
    save(late)
    pl.when(step + 1 < steps)(lambda: wait(fetches))
    pl.when(step > 0)(lambda: wait(puts))


def outer_grad_kernel(chunks, last, entering, inputs, part, enter_ref, leave_ref, k_ref, v_ref, *refs):
    in_refs = refs[:inputs]
    dkin_ref, dvin_ref, bloc_ref = refs[inputs : inputs + 3]
    step = pl.program_id(0)
    steps = pl.num_programs(0)
    start_head = first_head(part, steps * GROUP, True) + step * GROUP
    if part == 1:
        *grads_hbm, parts_ref, sems = refs[-4:]
    else:
        out_ring = refs[inputs + 3]
        *outs_hbm, dk_hbm, dv_hbm, parts_ref, sems, last_sems = refs[-8:]
        grads_hbm = [dk_hbm, dv_hbm]
        puts = put_outs(last, out_ring, outs_hbm, last_sems)
        pl.when(step == 0)(lambda: start(puts))

    def put(back):
        slot = (step - back) % 2
        here = head_span(start_head - back * GROUP, GROUP)
        return [
            pltpu.make_async_copy(parts_ref.at[slot, i], out.at[:, here], sems.at[slot, i])
            for i, out in enumerate(grads_hbm)
        ]

    slot = step % 2
    pl.when(step > 1)(lambda: wait(put(2)))
    late = []
    for g in range(GROUP):
        h = start_head + g
        cols = slice(g * HD, (g + 1) * HD)
        mine = head_span(h)
        carry = entering(in_refs, h)
        for n, span in reversed(list(enumerate(spans(chunks)))):
            leave = leave_ref[pl.ds(h, 1), span]
            back = carry.astype(BF16)
            dk = dkin_ref[h, :, span].astype(F32) + leave * dot(back, v_ref[span, mine], NT)
            dv = dvin_ref[h, :, span].astype(F32) + leave * dot(back.T, k_ref[span, mine], NT)
            if n > 0:
                passing = enter_ref[pl.ds(h, 1), span][:, CHUNK - 1 : CHUNK]
                carry = bloc_ref[h, n - 1] + passing * carry
            save(late)
            late = [
                (parts_ref, (slot, 0, span, cols), dk.astype(BF16).T),
                (parts_ref, (slot, 1, span, cols), dv.astype(BF16).T),
            ]
    save(late)
    start(put(0))

    @pl.when(step == steps - 1)
    def _():
        pl.when(step > 0)(lambda: wait(put(1)))
        wait(put(0))
        if part != 1:
            wait(puts)


def hbm(x):
    return pltpu.with_memory_space_constraint(x, pltpu.HBM)


def kept(*arrays):
    spec = pl.BlockSpec(memory_space=pltpu.VMEM)
    return [(pltpu.with_memory_space_constraint(x, pltpu.VMEM), spec) for x in arrays]


def keep(dims, dtype):
    return pltpu.VMEM(dims, dtype), pl.BlockSpec(memory_space=pltpu.VMEM)


def add_kernel(a_ref, b_ref, _, out_ref):
    out_ref[...] = a_ref[...] + b_ref[...]


def call(kernel, grid, ins, outs, scratch=(), aliases=None, flops=0, moved=0, exps=0):
    return pl.pallas_call(
        kernel,
        grid=grid,
        in_specs=[spec for _, spec in ins],
        out_specs=[spec for _, spec in outs],
        out_shape=[shape for shape, _ in outs],
        scratch_shapes=list(scratch),
        input_output_aliases=aliases or {},
        compiler_params=pltpu.CompilerParams(
            dimension_semantics=("arbitrary",) * len(grid), vmem_limit_bytes=ROOM * MIB
        ),
        cost_estimate=pl.CostEstimate(flops=flops, bytes_accessed=moved, transcendentals=exps),
    )(*[x for x, _ in ins])


def after(x, *others):
    return lax.optimization_barrier((x, *others))[0]


def across(x, flips, devices=8):
    return lax.ppermute(x, "seq", [(i, i ^ flips) for i in range(devices)])


def place(reverse):
    index = lax.axis_index("seq")
    index = 7 - index if reverse else index
    return lax.rem(index, 2), lax.rem(lax.div(index, 2), 2), lax.div(index, 4)


def pair_kernel(reverse, state_ref, other_ref, pass_ref, beside_ref, x_ref, y_ref, chip_ref):
    core, _, _ = place(reverse)
    quarter = x_ref.shape[0]
    chip_pass = pass_ref[...] * beside_ref[...]
    chip_ref[...] = chip_pass
    for i in range(quarter):
        rows = [chip_ref[pl.ds(core * 2 * quarter + at, 1), :] for at in (i, quarter + i)]
        x_ref[i, HD:, :] = jnp.concatenate(rows + [jnp.zeros((6, HD), F32)], axis=0)
        for at, out_ref in ((i, x_ref), (quarter + i, y_ref)):
            h = core * 2 * quarter + at
            mine, other = state_ref[h], other_ref[h]

            @pl.when(core == 0)
            def _():
                out_ref[i, :HD, :] = beside_ref[pl.ds(h, 1), :] * mine + other

            @pl.when(core == 1)
            def _():
                out_ref[i, :HD, :] = pass_ref[pl.ds(h, 1), :] * other + mine


def row_kernel(
    reverse, to_x_ref, to_y_ref, from_x_ref, from_y_ref, chip_ref, far_ref, row_ref, sent_ref,
):
    core, x, y = place(reverse)
    quarter = row_ref.shape[0]
    for i in range(quarter):
        h = core * 2 * quarter + i
        hy = h + quarter

        @pl.when(x == 0)
        def _():
            side = from_x_ref[i, HD : HD + 1, :]
            row_ref[i] = side * to_x_ref[i, :HD, :] + from_x_ref[i, :HD, :]

        @pl.when(x == 1)
        def _():
            through = chip_ref[pl.ds(h, 1), :] * from_x_ref[i, :HD, :]
            row_ref[i] = through + to_x_ref[i, :HD, :]

        @pl.when(y == 0)
        def _():
            sent_ref[i] = to_y_ref[i]

        @pl.when((y == 1) & (x == 0))
        def _():
            far = far_ref[pl.ds(hy, 1), :] * from_y_ref[i]
            sent_ref[i] = chip_ref[pl.ds(hy, 1), :] * far + to_y_ref[i]

        @pl.when((y == 1) & (x == 1))
        def _():
            sent_ref[i] = from_y_ref[i]


def ahead_kernel(
    reverse, from_x_ref, from_y_ref, row_ref, sent_ref, far_ref, out_ref,
):
    core, x, y = place(reverse)
    quarter = row_ref.shape[0]
    for i in range(quarter):
        h = core * 2 * quarter + i
        hy = h + quarter

        @pl.when((y == 0) & (x == 0))
        def _():
            out_ref[i] = jnp.zeros_like(out_ref[i])
            out_ref[quarter + i] = jnp.zeros_like(out_ref[i])

        @pl.when((y == 0) & (x == 1))
        def _():
            out_ref[i] = from_x_ref[i, :HD, :]
            out_ref[quarter + i] = sent_ref[i]

        @pl.when((y == 1) & (x == 0))
        def _():
            out_ref[i] = row_ref[i]
            out_ref[quarter + i] = far_ref[pl.ds(hy, 1), :] * from_y_ref[i] + sent_ref[i]

        @pl.when((y == 1) & (x == 1))
        def _():
            side_x, side_y = (from_x_ref[i, HD + j : HD + j + 1, :] for j in range(2))
            out_ref[i] = side_x * row_ref[i] + from_x_ref[i, :HD, :]
            out_ref[quarter + i] = side_y * from_y_ref[i] + sent_ref[i]


def cube_entering(reverse, refs, h):
    chip_ref, other_ref, beside_pass_ref = refs
    core, _, _ = place(reverse)
    chip = chip_ref[lax.rem(h, chip_ref.shape[0])]
    through = beside_pass_ref[pl.ds(h, 1), :] * chip + other_ref[h]
    return jnp.where(core == 0, chip, through)


def plain_entering(refs, h):
    return refs[0][h]


def cube_scan(state, own_pass, passes, fill, finish, reverse):
    heads = state.shape[0]
    quarter = heads // 4
    part = keep((quarter, HD, HD), F32)

    other = across(state, 1)
    beside_pass = passes[0] if passes else across(own_pass, 1)
    other, beside_pass = lax.optimization_barrier((other, beside_pass, fill(0, state)))[:2]
    to_x, to_y, chip_pass = call(
        functools.partial(pair_kernel, reverse), (),
        kept(state, other, own_pass, beside_pass),
        [keep((quarter, HD + 8, HD), F32), part, keep((heads, HD), F32)],
    )

    from_x, from_y = across(to_x, 2), across(to_y, 4)
    far_pass = passes[1] if passes else across(chip_pass, 6)
    from_x, from_y, far_pass = lax.optimization_barrier(
        (from_x, from_y, far_pass, fill(1, to_y))
    )[:3]
    row, sent = call(
        functools.partial(row_kernel, reverse), (),
        kept(to_x, to_y, from_x, from_y, chip_pass, far_pass), [part, part],
    )

    row_in, sent_in = across(row, 4), across(sent, 2)
    row_in, sent_in = lax.optimization_barrier((row_in, sent_in, fill(2, sent)))[:2]
    (ahead,) = call(
        functools.partial(ahead_kernel, reverse), (),
        kept(from_x, from_y, row_in, sent_in, far_pass),
        [keep((2 * quarter, HD, HD), F32)],
    )

    beside = across(ahead, 1)
    entering = functools.partial(cube_entering, reverse)
    beside = after(beside, finish(0, entering, (ahead, other, beside_pass)))
    finish(1, entering, (beside, other, beside_pass))
    return beside_pass, far_pass


def doubling_scan(state, own_pass, fill, reverse):
    devices = lax.axis_size("seq")
    index = lax.axis_index("seq")
    passes = lax.all_gather(own_pass, "seq")
    if reverse:
        passes = passes[::-1]
        index = devices - 1 - index
    route = lambda hop: [
        (i, i - hop if reverse else i + hop)
        for i in range(devices)
        if 0 <= (i - hop if reverse else i + hop) < devices
    ]
    for window in range(WINDOWS):
        state = after(state, fill(window, state))
    hop = 1
    while hop < devices:
        factor = lax.dynamic_index_in_dim(passes, index, 0, False)
        state = factor[:, None, :] * lax.ppermute(state, "seq", route(hop)) + state
        before = jnp.concatenate([jnp.zeros_like(passes[:hop]), passes[:-hop]], axis=0)
        passes = passes * before
        hop *= 2
    return lax.ppermute(state, "seq", route(1))


def scan_devices(state, own_pass, passes, fill, finish, reverse):
    if lax.axis_size("seq") == 8 and state.shape[0] % 4 == 0:
        return cube_scan(state, own_pass, passes, fill, finish, reverse)
    finish(None, plain_entering, (doubling_scan(state, own_pass, fill, reverse),))
    return None


def body(queries, key_rows, value_rows, log_decay, doc_start, gate_input, norm_gain, out_grad):
    rows, cols = queries.shape
    heads = cols // HD
    chunks = rows // CHUNK
    parts = lax.axis_size("head")
    grid = (heads // GROUP,)

    def windows(first):
        second = (heads - first + RING) // 2 // RING * RING
        return [(0, first), (first, second), (first + second, heads - first - second)]

    forward, backward = windows(max(RING, heads // 8)), windows(heads // 4)
    big = rows * cols * 2
    tile = 2 * rows * CHUNK * cols
    small = 2 * rows * HD * cols

    whole = lambda *dims: pl.BlockSpec(dims, lambda i: (0,) * len(dims))
    anywhere = pl.BlockSpec(memory_space=pl.ANY)

    by_head = (heads, HD, rows)
    local_dims = (heads, chunks, HD, HD)
    wide_out = (pltpu.HBM((rows, cols), BF16), anywhere)
    ring = keep((2, rows, RING * HD), BF16)
    probs_kept = keep((heads, chunks, CHUNK + HD, HD), BF16)
    out_ring = keep((2, 3, rows, RING * HD), BF16)
    sems = pltpu.SemaphoreType.DMA
    queries, key_rows, value_rows, gate_input, out_grad = map(
        hbm, (queries, key_rows, value_rows, gate_input, out_grad)
    )
    doc_row = doc_start.reshape(1, rows)
    gain_row = norm_gain.reshape(1, cols)

    by_token = (rows, cols)
    steps = heads // GROUP
    (
        crow, enter, leave, rrow, keys, values, local, state, own_pass, gain, kept_q, *rings
    ) = call(
        functools.partial(state_kernel, chunks, steps),
        grid,
        [
            (hbm(x), anywhere)
            for x in (
                log_decay, doc_row, gain_row, key_rows, value_rows, queries, gate_input, out_grad
            )
        ],
        [keep((heads, rows), F32)] * 3
        + [
            keep((8, rows), F32), keep(by_token, BF16), keep(by_token, BF16),
            keep((heads, chunks - 1, HD, HD), F32), keep((heads, HD, HD), F32), keep((heads, HD), F32),
            keep((1, cols), F32), keep(by_token, BF16), ring, ring,
        ],
        [
            pltpu.VMEM((heads, rows), F32), pltpu.VMEM((1, rows), jnp.int32),
            sems((2, steps)), sems((3,)), sems((3,)),
        ],
        flops=small, moved=2 * big,
    )

    ready = []
    made = [kept_q, *rings]

    def fill_forward(window, tie):
        if not ready:
            ready[:] = call(
                prepare_kernel, (), kept(after(rrow, tie), crow, enter),
                [keep((chunks, CHUNK, CHUNK), F32), keep((rows, HD), F32)],
                flops=8 * rows * CHUNK,
            )
        mask, columns = ready
        ins = kept(after(crow, tie), columns, mask, keys, values, gain)
        ins += [(x, anywhere) for x in (queries, gate_input, out_grad)]
        aliases = {len(ins) + i: i for i in range(len(made))}
        ins += kept(*made)
        made[:] = call(
            functools.partial(inside_kernel, chunks, forward[window][0] // RING, heads // RING),
            (forward[window][1] // RING,),
            ins,
            [
                keep(by_token, BF16), ring, ring, keep(by_token, F32), keep(by_token, BF16),
                probs_kept,
            ],
            [sems((3,))],
            aliases=aliases,
            flops=2 * tile // WINDOWS, moved=5 * big // WINDOWS,
            exps=rows * (CHUNK + HD) * heads // WINDOWS,
        )
        return made[4]

    tall = pltpu.VMEM((rows, HD), F32)
    reduced = []

    def finish_forward(part, entering, refs):
        mask, columns = ready
        kept_q, _, _, inside, gnorm, _ = made
        ins = kept(columns, enter, kept_q, gnorm, local, *refs)
        outs = [keep(by_token, F32), keep(local_dims, BF16), keep((2, rows), F32)]
        scratch = [tall, tall]
        if part == 1:
            aliases = {len(ins) + 1: 0, len(ins) + 2: 1}
            ins += kept(reduced[1], inside, reduced[0])
        else:
            aliases = {len(ins): 0}
            ins += kept(inside)
        results = call(
            functools.partial(
                outside_kernel, chunks, entering, len(refs), part
            ),
            (heads // WIDE if part is None else heads // 2 // WIDE,),
            ins, outs, scratch, aliases,
            flops=small, moved=big,
        )
        made[3], *reduced[:] = results
        return reduced[1]

    passes = scan_devices(state, own_pass, None, fill_forward, finish_forward, False)
    mask, columns = ready
    kept_q, _, _, attn, gnorm, probs = made
    held, sums = reduced

    flat = []
    halves = [0, heads // 2]
    token = keep((8, HD), F32)

    def turn(sums):
        first = halves.pop(0)
        results = call(
            functools.partial(turn_kernel, chunks, first),
            (heads // 2 // WIDE,),
            kept(kept_q, attn, gain, sums, *flat),
            [keep(by_head, BF16), keep(by_token, BF16), token],
            aliases={4 + i: i for i in range(len(flat))},
            flops=rows * cols, moved=2 * big,
        )
        flat[:] = results[:2]
        return results[2]

    apart = 1
    while True:
        other_sums = lax.ppermute(sums, "head", [(i, i ^ apart) for i in range(parts)])
        done = turn(sums) if halves else done
        apart *= 2
        if apart >= parts:
            break
        (sums,) = call(add_kernel, (), kept(sums, other_sums, done), [keep((2, rows), F32)])
    while halves:
        done = turn(sums)
    turned_q, attn_flat = flat

    agrad, turned_agrad, bloc, back, alpha, *rings = call(
        functools.partial(grad_kernel, chunks),
        (heads // WIDE,),
        kept(enter, sums, other_sums, done, turned_q, gnorm, attn)
        + [(hbm(x), anywhere) for x in (gate_input, out_grad)],
        [
            keep(by_token, BF16), keep(by_head, BF16), keep((heads, chunks - 1, HD, HD), F32),
            keep((heads, HD, HD), F32), keep((rows, HD), F32), ring, ring,
        ],
        [tall, sems((2,))],
        {5: 0},
        flops=small, moved=big,
    )

    inner = [turned_q, turned_agrad, *rings]

    def fill_backward(window, tie):
        ins = kept(
            after(crow, tie), alpha, columns, mask, keys, values, attn_flat, held, agrad, probs,
            inner[0], inner[1],
        )
        ins += [(hbm(x), anywhere) for x in (gate_input, out_grad)]
        aliases = {10: 0, 11: 1}
        aliases.update({len(ins) - 2 + i: i for i in range(2, len(inner))})
        ins += kept(*inner[2:5]) + [(hbm(x), anywhere) for x in inner[5:]]
        inner[:] = call(
            functools.partial(
                inner_grad_kernel, chunks, backward[window][0] // RING, heads // RING
            ),
            (backward[window][1] // RING,),
            ins,
            [keep(by_head, BF16)] * 2 + [ring, ring, out_ring] + [wide_out] * 3,
            [sems((5,))],
            aliases=aliases,
            flops=(4 * tile + small) // WINDOWS, moved=7 * big // WINDOWS,
            exps=rows * (CHUNK + HD) * heads // WINDOWS,
        )
        return inner[5]

    grads = []

    def finish_backward(part, entering, refs):
        ins = kept(enter, leave, keys, values, *refs, inner[0], inner[1], bloc)
        scratch = [pltpu.VMEM((2, 2, rows, GROUP * HD), BF16), sems((2, 2))]
        if part == 1:
            aliases = {len(ins): 0, len(ins) + 1: 1}
            ins += [(hbm(x), anywhere) for x in grads]
            outs = [wide_out] * 2
        else:
            aliases = {len(ins) + 1 + i: i for i in range(3)}
            ins += kept(inner[4]) + [(hbm(x), anywhere) for x in inner[5:]]
            outs = [wide_out] * 5
            scratch.append(sems((3,)))
        results = call(
            functools.partial(
                outer_grad_kernel, chunks, heads // RING - 1, entering, len(refs), part
            ),
            (steps if part is None else steps // 2,),
            ins, outs, scratch, aliases,
            flops=2 * small, moved=2 * big,
        )
        grads[:] = results[-2:]
        if part != 1:
            inner[5:] = results[:3]
        return grads[0]

    scan_devices(back, own_pass, passes, fill_backward, finish_backward, True)
    dq, gated, gate_grad = inner[5:]
    return (gated, gate_grad, dq, *grads)


def solution(mesh):
    in_specs = (
        P("seq", "head"),
        P("seq", "head"),
        P("seq", "head"),
        P("head", "seq"),
        P("seq"),
        P("seq", "head"),
        P("head"),
        P("seq", "head"),
    )
    out_specs = (P("seq", "head"),) * 5
    return jax.shard_map(body, mesh=mesh, in_specs=in_specs, out_specs=out_specs, check_vma=False)
```

```python
import functools

import jax
import jax.numpy as jnp
from jax import lax
from jax.experimental import pallas as pl
from jax.experimental.pallas import tpu as pltpu
from jax.sharding import PartitionSpec as P

HEAD_TOTAL = 64
HD = 128
CHUNK = 256
GROUP = 2
WIDE = 4
RING = 2
AHEAD = 2
WINDOWS = 3
ROOM = 4
WIDTH = HEAD_TOTAL * HD

epsilon = 1e-06
LOG2E = 1.4426950408889634

F32 = jnp.float32
BF16 = jnp.bfloat16
MIB = 1024 * 1024
NT = ((1,), (1,))


def dot(a, b, dims=((1,), (0,))):
    return lax.dot_general(a, b, (dims, ((), ())), preferred_element_type=F32)


def chunk_cumsum(x):
    lane = lax.broadcasted_iota(jnp.int32, x.shape, 1) % CHUNK
    shift = 1
    while shift < CHUNK:
        x = x + jnp.where(lane >= shift, pltpu.roll(x, shift, 1), 0.0)
        shift *= 2
    return x


def spans(chunks):
    return [slice(n * CHUNK, (n + 1) * CHUNK) for n in range(chunks)]


def head_span(head, count=1):
    return pl.ds(pl.multiple_of(head * HD, HD), count * HD)


def save(stores):
    for ref, index, value in stores:
        ref[index] = value


def save_probs(probs_ref, h, n, probs):
    left, right = slice(0, CHUNK), slice(CHUNK, CHUNK + HD)
    return [
        (probs_ref, (h, n, left), probs[:, :HD]),
        (probs_ref, (h, n, right), probs[HD:, HD:]),
    ]


def load_probs(probs_ref, h, n):
    right = jnp.concatenate([jnp.zeros((HD, HD), BF16), probs_ref[h, n, CHUNK:, :]], axis=0)
    return jnp.concatenate([probs_ref[h, n, :CHUNK, :], right], axis=1)


def sigmoid(x):
    return 0.5 * jnp.tanh(0.5 * x) + 0.5


def spread(cols, lane):
    return jnp.broadcast_to(cols[:, lane : lane + 1], cols.shape)


def turned(cols_ref, lane):
    return pltpu.roll(cols_ref[...], (HD - lane) % HD, 1)


def column(row):
    return jnp.broadcast_to(row, (HD, row.shape[1])).T


def start(copies):
    for copy in copies:
        copy.start()


def wait(copies):
    for copy in copies:
        copy.wait()


def group_of(at):
    return head_span(at * RING, RING)


def fetch_gates(at, gate_hbm, grad_hbm, gate_ring, grad_ring, sems):
    slot = at % 2
    return [
        pltpu.make_async_copy(gate_hbm.at[:, group_of(at)], gate_ring.at[slot], sems.at[0]),
        pltpu.make_async_copy(grad_hbm.at[:, group_of(at)], grad_ring.at[slot], sems.at[1]),
    ]


def fetch_q(at, q_hbm, q_ref, sem):
    return [pltpu.make_async_copy(q_hbm.at[:, group_of(at)], q_ref.at[:, group_of(at)], sem)]


def put_outs(at, out_ring, outs_hbm, sems):
    return [
        pltpu.make_async_copy(out_ring.at[at % 2, i], out.at[:, group_of(at)], sems.at[i])
        for i, out in enumerate(outs_hbm)
    ]


def state_kernel(
    chunks, steps, lc_hbm, doc_hbm, gain_hbm, k_hbm, v_hbm, q_hbm, gate_hbm, grad_hbm,
    crow_ref, enter_ref, leave_ref, rrow_ref, k_ref, v_ref, loc_ref, state_ref, pass_ref,
    gain_ref, q_ref, gate_ring, grad_ring, lc_ref, doc_ref, sems, small_sems, next_sems,
):
    step = pl.program_id(0)
    small = [
        pltpu.make_async_copy(lc_hbm, lc_ref, small_sems.at[0]),
        pltpu.make_async_copy(doc_hbm, doc_ref, small_sems.at[1]),
        pltpu.make_async_copy(gain_hbm, gain_ref, small_sems.at[2]),
    ]
    following = fetch_gates(0, gate_hbm, grad_hbm, gate_ring, grad_ring, next_sems)
    following += fetch_q(0, q_hbm, q_ref, next_sems.at[2])

    def copies(at):
        here = head_span(at * GROUP, GROUP)
        return (
            pltpu.make_async_copy(k_hbm.at[:, here], k_ref.at[:, here], sems.at[0, at]),
            pltpu.make_async_copy(v_hbm.at[:, here], v_ref.at[:, here], sems.at[1, at]),
        )

    @pl.when(step == 0)
    def _():
        start(small)
        for at in range(min(AHEAD, steps)):
            start(copies(at))
        wait(small)
        c = chunk_cumsum(lc_ref[...] * LOG2E)
        r = chunk_cumsum(jnp.broadcast_to(doc_ref[...].astype(F32), (8, doc_ref.shape[1])))
        crow_ref[...] = c
        rrow_ref[...] = r
        enter_ref[...] = jnp.where(r[0:1] == 0.0, jnp.exp2(c), 0.0)
        for span in spans(chunks):
            cn, rn = c[:, span], r[0:1, span]
            leave_ref[:, span] = jnp.where(rn == rn[:, -1:], jnp.exp2(cn[:, -1:] - cn), 0.0)

    pl.when(step + AHEAD < steps)(lambda: start(copies(step + AHEAD)))
    pl.when(step + AHEAD == steps)(lambda: start(following))
    wait(copies(step))
    late = []
    for g in range(GROUP):
        h = step * GROUP + g
        mine = head_span(h)
        state = None
        total = None
        for n, span in enumerate(spans(chunks)):
            keyed = (k_ref[span, mine].T.astype(F32) * leave_ref[pl.ds(h, 1), span]).astype(BF16)
            local = dot(keyed, v_ref[span, mine])
            passing = enter_ref[pl.ds(h, 1), span][:, CHUNK - 1 : CHUNK]
            state = local if state is None else passing * state + local
            total = passing if total is None else passing * total
            save(late)
            late = [(loc_ref, (h, n), local)] if n + 1 < chunks else []
        late.append((state_ref, h, state))
        late.append((pass_ref, (pl.ds(h, 1), slice(None)), jnp.broadcast_to(total, (1, HD))))
    save(late)

    @pl.when(step == steps - 1)
    def _():
        wait(following)


def prepare_kernel(rrow_ref, crow_ref, enter_ref, mask_ref, cols_ref):
    sub = lax.broadcasted_iota(jnp.int32, (CHUNK, CHUNK), 0)
    lane = lax.broadcasted_iota(jnp.int32, (CHUNK, CHUNK), 1)
    spare = jnp.zeros((HD - 2 * crow_ref.shape[0], CHUNK), F32)
    for n, span in enumerate(spans(mask_ref.shape[0])):
        r_row = rrow_ref[0:1, span]
        r_col = jnp.concatenate([column(r_row)] * (CHUNK // HD), axis=1)
        mask_ref[n] = jnp.where((r_col == r_row) & (lane <= sub), 0.0, -jnp.inf)
        cols_ref[span, :] = jnp.concatenate([crow_ref[:, span], enter_ref[:, span], spare], axis=0).T


def decayed(scores, c_col, c_row, mask):
    top, low = slice(0, HD), slice(HD, CHUNK)
    row_blocks = []
    for rows, width in ((top, HD), (low, CHUNK)):
        col = c_col[rows]
        col = col if width == HD else jnp.concatenate([col] * (width // HD), axis=1)
        weight = jnp.exp2(col - c_row[:, :width] + mask[rows, :width])
        row_blocks.append((scores[rows, :width] * weight).astype(BF16))
    row_blocks[0] = jnp.concatenate([row_blocks[0], jnp.zeros((HD, CHUNK - HD), BF16)], axis=1)
    return jnp.concatenate(row_blocks, axis=0)


def inside_kernel(
    chunks, first, steps, crow_ref, cols_ref, mask_ref, k_ref, v_ref, gain_ref, q_hbm, gate_hbm,
    grad_hbm, *refs,
):
    q_ref, gate_ring, grad_ring, attn_ref, gnorm_ref, probs_ref, sems = refs[-7:]
    step = first + pl.program_id(0)
    slot = step % 2
    fetches = fetch_gates(step + 1, gate_hbm, grad_hbm, gate_ring, grad_ring, sems)
    fetches += fetch_q(step + 1, q_hbm, q_ref, sems.at[2])
    pl.when(step + 1 < steps)(lambda: start(fetches))

    cols_now = turned(cols_ref, step * RING)
    late = []
    for g in range(RING):
        h = step * RING + g
        cols = slice(g * HD, (g + 1) * HD)
        mine = head_span(h)
        for n, span in enumerate(spans(chunks)):
            q = q_ref[span, mine]
            scores = dot(q, k_ref[span, mine], NT)
            c_row = crow_ref[pl.ds(h, 1), span]
            probs = decayed(scores, spread(cols_now[span], g), c_row, mask_ref.at[n])
            inside = dot(probs, v_ref[span, mine])
            sig = sigmoid(gate_ring[slot, span, cols].astype(F32))
            gnorm = grad_ring[slot, span, cols].astype(F32) * sig * gain_ref[0:1, mine]
            save(late)
            late = save_probs(probs_ref, h, n, probs)
            late += [
                (attn_ref, (span, mine), inside),
                (gnorm_ref, (span, mine), gnorm.astype(BF16)),
            ]
    save(late)
    pl.when(step + 1 < steps)(lambda: wait(fetches))


def first_head(part, half, reverse):
    if part is None:
        return 0
    core, _, _ = place(reverse)
    return (core if part == 0 else 1 - core) * half


def outside_kernel(chunks, entering, inputs, part, cols_ref, enter_ref, q_ref, gnorm_ref, loc_ref, *refs):
    in_refs = refs[:inputs]
    if part == 1:
        before_ref, inside_ref, _, attn_ref, held_ref, sums_ref, sq_ref, inner_ref = refs[inputs:]
    else:
        inside_ref, attn_ref, held_ref, sums_ref, sq_ref, inner_ref = refs[inputs:]
    step = pl.program_id(0)
    steps = pl.num_programs(0)

    @pl.when(step == 0)
    def _():
        sq_ref[...] = jnp.zeros_like(sq_ref)
        inner_ref[...] = jnp.zeros_like(inner_ref)

    start_head = first_head(part, steps * WIDE, False) + step * WIDE
    heads = [start_head + g for g in range(WIDE)]
    cols_now = turned(cols_ref, enter_ref.shape[0] + start_head)
    carries = [entering(in_refs, h) for h in heads]
    late = []
    for n, span in enumerate(spans(chunks)):
        squares = sq_ref[span, :]
        inners = inner_ref[span, :]
        for g, h in enumerate(heads):
            mine = head_span(h)
            held = carries[g].astype(BF16)
            enter = spread(cols_now[span], g)
            attn = inside_ref[span, mine] + enter * dot(q_ref[span, mine], held)
            squares = squares + attn * attn
            inners = inners + gnorm_ref[span, mine].astype(F32) * attn
            if n + 1 < chunks:
                passing = enter_ref[pl.ds(h, 1), span][:, CHUNK - 1 : CHUNK]
                carries[g] = passing * carries[g] + loc_ref[h, n]
            save(late)
            late = [(held_ref, (h, n), held), (attn_ref, (span, mine), attn)]
        late += [(sq_ref, (span, slice(None)), squares), (inner_ref, (span, slice(None)), inners)]
    save(late)

    @pl.when(step == steps - 1)
    def _():
        for i, ref in enumerate((sq_ref, inner_ref)):
            total = jnp.sum(ref[...].T, axis=0, keepdims=True)
            sums_ref[i : i + 1, :] = total + before_ref[i : i + 1, :] if part == 1 else total


def turn_kernel(chunks, first, q_ref, attn_ref, gain_ref, *refs):
    turned_ref, flat_ref, done_ref = refs[-3:]
    step = pl.program_id(0)
    done_ref[...] = jnp.zeros_like(done_ref)
    late = []
    for g in range(WIDE):
        h = first + step * WIDE + g
        mine = head_span(h)
        for span in spans(chunks):
            turned_q = q_ref[span, mine].T
            flat = (attn_ref[span, mine] * gain_ref[0:1, mine]).astype(BF16)
            save(late)
            late = [(turned_ref, (h, slice(None), span), turned_q), (flat_ref, (span, mine), flat)]
    save(late)


def grad_kernel(chunks, enter_ref, sums_ref, others_ref, _, *refs):
    turned_q_ref, gnorm_ref, attn_ref, gate_hbm, grad_hbm = refs[:5]
    agrad_ref, turned_ref, bloc_ref, back_ref, alpha_ref = refs[5:10]
    gate_ring, grad_ring, beta_ref, sems = refs[10:]
    step = pl.program_id(0)
    following = fetch_gates(0, gate_hbm, grad_hbm, gate_ring, grad_ring, sems)

    @pl.when(step == 0)
    def _():
        start(following)
        sums = sums_ref[...] + others_ref[...]
        inverse = lax.rsqrt(sums[0:1] / WIDTH + epsilon)
        alpha_ref[...] = column(inverse)
        beta_ref[...] = column(inverse * inverse * inverse * sums[1:2] / WIDTH)

    late = []
    for g in range(WIDE):
        h = step * WIDE + g
        mine = head_span(h)
        back = None
        for n, span in reversed(list(enumerate(spans(chunks)))):
            enter = enter_ref[pl.ds(h, 1), span]
            gnorm = gnorm_ref[span, mine].astype(F32)
            attn, alpha = attn_ref[span, mine], alpha_ref[span, :]
            agrad = alpha * gnorm - attn * beta_ref[span, :]
            agrad = agrad.astype(BF16)
            qkeyed = (turned_q_ref[h, :, span].astype(F32) * enter).astype(BF16)
            local = dot(qkeyed, agrad)
            back = local if back is None else local + enter[:, CHUNK - 1 : CHUNK] * back
            save(late)
            late = [
                (agrad_ref, (span, mine), agrad),
                (turned_ref, (h, slice(None), span), agrad.T),
            ]
            if n > 0:
                late.append((bloc_ref, (h, n - 1), local))
        late.append((back_ref, h, back))
    save(late)

    @pl.when(step == pl.num_programs(0) - 1)
    def _():
        wait(following)


def inner_grad_kernel(
    chunks, first, steps, crow_ref, alpha_ref, cols_ref, mask_ref, k_ref, v_ref, flat_ref,
    held_ref, agrad_ref, probs_ref, turned_q_ref, turned_agrad_ref, gate_hbm,
    grad_hbm, *refs,
):
    dk_ref, dv_ref, gate_ring, grad_ring, out_ring, *outs_hbm, sems = refs[-9:]
    step = first + pl.program_id(0)
    slot = step % 2
    fetches = fetch_gates(step + 1, gate_hbm, grad_hbm, gate_ring, grad_ring, sems)
    puts = put_outs(step - 1, out_ring, outs_hbm, sems.at[pl.ds(2, 3)])
    pl.when(step + 1 < steps)(lambda: start(fetches))
    pl.when(step > 0)(lambda: start(puts))

    cols_now = turned(cols_ref, step * RING)
    late = []
    for g in range(RING):
        h = step * RING + g
        cols = slice(g * HD, (g + 1) * HD)
        mine = head_span(h)
        for n, span in enumerate(spans(chunks)):
            k, v, agrad = k_ref[span, mine], v_ref[span, mine], agrad_ref[span, mine]
            both = dot(agrad, jnp.concatenate([v, held_ref[h, n]], axis=0), NT)
            c_row = crow_ref[pl.ds(h, 1), span]
            dscore = decayed(both[:, :CHUNK], spread(cols_now[span], g), c_row, mask_ref.at[n])
            enter = spread(cols_now[span], crow_ref.shape[0] + g)
            dq = dot(dscore, k) + enter * both[:, CHUNK:]
            dv = dot(turned_agrad_ref[h, :, span], load_probs(probs_ref, h, n))
            dk = dot(turned_q_ref[h, :, span], dscore)
            normed = flat_ref[span, mine].astype(F32) * alpha_ref[span, :]
            sig = sigmoid(gate_ring[slot, span, cols].astype(F32))
            gated = normed * sig
            ggate = grad_ring[slot, span, cols].astype(F32) * gated * (1.0 - sig)
            save(late)
            late = [
                (out_ring, (slot, 0, span, cols), dq.astype(BF16)),
                (dv_ref, (h, slice(None), span), dv.astype(BF16)),
                (dk_ref, (h, slice(None), span), dk.astype(BF16)),
                (out_ring, (slot, 1, span, cols), gated.astype(BF16)),
                (out_ring, (slot, 2, span, cols), ggate.astype(BF16)),
            ]
    save(late)
    pl.when(step + 1 < steps)(lambda: wait(fetches))
    pl.when(step > 0)(lambda: wait(puts))


def outer_grad_kernel(chunks, last, entering, inputs, part, enter_ref, leave_ref, k_ref, v_ref, *refs):
    in_refs = refs[:inputs]
    dkin_ref, dvin_ref, bloc_ref = refs[inputs : inputs + 3]
    step = pl.program_id(0)
    steps = pl.num_programs(0)
    start_head = first_head(part, steps * GROUP, True) + step * GROUP
    if part == 1:
        *grads_hbm, parts_ref, sems = refs[-4:]
    else:
        out_ring = refs[inputs + 3]
        *outs_hbm, dk_hbm, dv_hbm, parts_ref, sems, last_sems = refs[-8:]
        grads_hbm = [dk_hbm, dv_hbm]
        puts = put_outs(last, out_ring, outs_hbm, last_sems)
        pl.when(step == 0)(lambda: start(puts))

    def put(back):
        slot = (step - back) % 2
        here = head_span(start_head - back * GROUP, GROUP)
        return [
            pltpu.make_async_copy(parts_ref.at[slot, i], out.at[:, here], sems.at[slot, i])
            for i, out in enumerate(grads_hbm)
        ]

    slot = step % 2
    pl.when(step > 1)(lambda: wait(put(2)))
    late = []
    for g in range(GROUP):
        h = start_head + g
        cols = slice(g * HD, (g + 1) * HD)
        mine = head_span(h)
        carry = entering(in_refs, h)
        for n, span in reversed(list(enumerate(spans(chunks)))):
            leave = leave_ref[pl.ds(h, 1), span]
            back = carry.astype(BF16)
            dk = dkin_ref[h, :, span].astype(F32) + leave * dot(back, v_ref[span, mine], NT)
            dv = dvin_ref[h, :, span].astype(F32) + leave * dot(back.T, k_ref[span, mine], NT)
            if n > 0:
                passing = enter_ref[pl.ds(h, 1), span][:, CHUNK - 1 : CHUNK]
                carry = bloc_ref[h, n - 1] + passing * carry
            save(late)
            late = [
                (parts_ref, (slot, 0, span, cols), dk.astype(BF16).T),
                (parts_ref, (slot, 1, span, cols), dv.astype(BF16).T),
            ]
    save(late)
    start(put(0))

    @pl.when(step == steps - 1)
    def _():
        pl.when(step > 0)(lambda: wait(put(1)))
        wait(put(0))
        if part != 1:
            wait(puts)


def hbm(x):
    return pltpu.with_memory_space_constraint(x, pltpu.HBM)


def kept(*arrays):
    spec = pl.BlockSpec(memory_space=pltpu.VMEM)
    return [(pltpu.with_memory_space_constraint(x, pltpu.VMEM), spec) for x in arrays]


def keep(dims, dtype):
    return pltpu.VMEM(dims, dtype), pl.BlockSpec(memory_space=pltpu.VMEM)


def add_kernel(a_ref, b_ref, _, out_ref):
    out_ref[...] = a_ref[...] + b_ref[...]


def call(kernel, grid, ins, outs, scratch=(), aliases=None, flops=0, moved=0, exps=0):
    return pl.pallas_call(
        kernel,
        grid=grid,
        in_specs=[spec for _, spec in ins],
        out_specs=[spec for _, spec in outs],
        out_shape=[shape for shape, _ in outs],
        scratch_shapes=list(scratch),
        input_output_aliases=aliases or {},
        compiler_params=pltpu.CompilerParams(
            dimension_semantics=("arbitrary",) * len(grid), vmem_limit_bytes=ROOM * MIB
        ),
        cost_estimate=pl.CostEstimate(flops=flops, bytes_accessed=moved, transcendentals=exps),
    )(*[x for x, _ in ins])


def after(x, *others):
    return lax.optimization_barrier((x, *others))[0]


def across(x, flips, devices=8):
    return lax.ppermute(x, "seq", [(i, i ^ flips) for i in range(devices)])


def place(reverse):
    index = lax.axis_index("seq")
    index = 7 - index if reverse else index
    return lax.rem(index, 2), lax.rem(lax.div(index, 2), 2), lax.div(index, 4)


def pair_kernel(reverse, state_ref, other_ref, pass_ref, beside_ref, x_ref, y_ref, chip_ref):
    core, _, _ = place(reverse)
    quarter = x_ref.shape[0]
    chip_pass = pass_ref[...] * beside_ref[...]
    chip_ref[...] = chip_pass
    for i in range(quarter):
        rows = [chip_ref[pl.ds(core * 2 * quarter + at, 1), :] for at in (i, quarter + i)]
        x_ref[i, HD:, :] = jnp.concatenate(rows + [jnp.zeros((6, HD), F32)], axis=0)
        for at, out_ref in ((i, x_ref), (quarter + i, y_ref)):
            h = core * 2 * quarter + at
            mine, other = state_ref[h], other_ref[h]

            @pl.when(core == 0)
            def _():
                out_ref[i, :HD, :] = beside_ref[pl.ds(h, 1), :] * mine + other

            @pl.when(core == 1)
            def _():
                out_ref[i, :HD, :] = pass_ref[pl.ds(h, 1), :] * other + mine


def row_kernel(
    reverse, to_x_ref, to_y_ref, from_x_ref, from_y_ref, chip_ref, far_ref, row_ref, sent_ref,
):
    core, x, y = place(reverse)
    quarter = row_ref.shape[0]
    for i in range(quarter):
        h = core * 2 * quarter + i
        hy = h + quarter

        @pl.when(x == 0)
        def _():
            side = from_x_ref[i, HD : HD + 1, :]
            row_ref[i] = side * to_x_ref[i, :HD, :] + from_x_ref[i, :HD, :]

        @pl.when(x == 1)
        def _():
            through = chip_ref[pl.ds(h, 1), :] * from_x_ref[i, :HD, :]
            row_ref[i] = through + to_x_ref[i, :HD, :]

        @pl.when(y == 0)
        def _():
            sent_ref[i] = to_y_ref[i]

        @pl.when((y == 1) & (x == 0))
        def _():
            far = far_ref[pl.ds(hy, 1), :] * from_y_ref[i]
            sent_ref[i] = chip_ref[pl.ds(hy, 1), :] * far + to_y_ref[i]

        @pl.when((y == 1) & (x == 1))
        def _():
            sent_ref[i] = from_y_ref[i]


def ahead_kernel(
    reverse, from_x_ref, from_y_ref, row_ref, sent_ref, far_ref, out_ref,
):
    core, x, y = place(reverse)
    quarter = row_ref.shape[0]
    for i in range(quarter):
        h = core * 2 * quarter + i
        hy = h + quarter

        @pl.when((y == 0) & (x == 0))
        def _():
            out_ref[i] = jnp.zeros_like(out_ref[i])
            out_ref[quarter + i] = jnp.zeros_like(out_ref[i])

        @pl.when((y == 0) & (x == 1))
        def _():
            out_ref[i] = from_x_ref[i, :HD, :]
            out_ref[quarter + i] = sent_ref[i]

        @pl.when((y == 1) & (x == 0))
        def _():
            out_ref[i] = row_ref[i]
            out_ref[quarter + i] = far_ref[pl.ds(hy, 1), :] * from_y_ref[i] + sent_ref[i]

        @pl.when((y == 1) & (x == 1))
        def _():
            side_x, side_y = (from_x_ref[i, HD + j : HD + j + 1, :] for j in range(2))
            out_ref[i] = side_x * row_ref[i] + from_x_ref[i, :HD, :]
            out_ref[quarter + i] = side_y * from_y_ref[i] + sent_ref[i]


def cube_entering(reverse, refs, h):
    chip_ref, other_ref, beside_pass_ref = refs
    core, _, _ = place(reverse)
    chip = chip_ref[lax.rem(h, chip_ref.shape[0])]
    through = beside_pass_ref[pl.ds(h, 1), :] * chip + other_ref[h]
    return jnp.where(core == 0, chip, through)


def plain_entering(refs, h):
    return refs[0][h]


def cube_scan(state, own_pass, passes, fill, finish, reverse):
    heads = state.shape[0]
    quarter = heads // 4
    part = keep((quarter, HD, HD), F32)

    other = across(state, 1)
    beside_pass = passes[0] if passes else across(own_pass, 1)
    other, beside_pass = lax.optimization_barrier((other, beside_pass, fill(0, state)))[:2]
    to_x, to_y, chip_pass = call(
        functools.partial(pair_kernel, reverse), (),
        kept(state, other, own_pass, beside_pass),
        [keep((quarter, HD + 8, HD), F32), part, keep((heads, HD), F32)],
    )

    from_x, from_y = across(to_x, 2), across(to_y, 4)
    far_pass = passes[1] if passes else across(chip_pass, 6)
    from_x, from_y, far_pass = lax.optimization_barrier(
        (from_x, from_y, far_pass, fill(1, to_y))
    )[:3]
    row, sent = call(
        functools.partial(row_kernel, reverse), (),
        kept(to_x, to_y, from_x, from_y, chip_pass, far_pass), [part, part],
    )

    row_in, sent_in = across(row, 4), across(sent, 2)
    row_in, sent_in = lax.optimization_barrier((row_in, sent_in, fill(2, sent)))[:2]
    (ahead,) = call(
        functools.partial(ahead_kernel, reverse), (),
        kept(from_x, from_y, row_in, sent_in, far_pass),
        [keep((2 * quarter, HD, HD), F32)],
    )

    beside = across(ahead, 1)
    entering = functools.partial(cube_entering, reverse)
    beside = after(beside, finish(0, entering, (ahead, other, beside_pass)))
    finish(1, entering, (beside, other, beside_pass))
    return beside_pass, far_pass


def doubling_scan(state, own_pass, fill, reverse):
    devices = lax.axis_size("seq")
    index = lax.axis_index("seq")
    passes = lax.all_gather(own_pass, "seq")
    if reverse:
        passes = passes[::-1]
        index = devices - 1 - index
    route = lambda hop: [
        (i, i - hop if reverse else i + hop)
        for i in range(devices)
        if 0 <= (i - hop if reverse else i + hop) < devices
    ]
    for window in range(WINDOWS):
        state = after(state, fill(window, state))
    hop = 1
    while hop < devices:
        factor = lax.dynamic_index_in_dim(passes, index, 0, False)
        state = factor[:, None, :] * lax.ppermute(state, "seq", route(hop)) + state
        before = jnp.concatenate([jnp.zeros_like(passes[:hop]), passes[:-hop]], axis=0)
        passes = passes * before
        hop *= 2
    return lax.ppermute(state, "seq", route(1))


def scan_devices(state, own_pass, passes, fill, finish, reverse):
    if lax.axis_size("seq") == 8 and state.shape[0] % 4 == 0:
        return cube_scan(state, own_pass, passes, fill, finish, reverse)
    finish(None, plain_entering, (doubling_scan(state, own_pass, fill, reverse),))
    return None


def body(queries, key_rows, value_rows, log_decay, doc_start, gate_input, norm_gain, out_grad):
    rows, cols = queries.shape
    heads = cols // HD
    chunks = rows // CHUNK
    parts = lax.axis_size("head")
    grid = (heads // GROUP,)

    def windows(first):
        second = (heads - first + RING) // 2 // RING * RING
        return [(0, first), (first, second), (first + second, heads - first - second)]

    forward, backward = windows(max(RING, heads // 8)), windows(heads // 4)
    big = rows * cols * 2
    tile = 2 * rows * CHUNK * cols
    small = 2 * rows * HD * cols

    whole = lambda *dims: pl.BlockSpec(dims, lambda i: (0,) * len(dims))
    anywhere = pl.BlockSpec(memory_space=pl.ANY)

    by_head = (heads, HD, rows)
    local_dims = (heads, chunks, HD, HD)
    wide_out = (pltpu.HBM((rows, cols), BF16), anywhere)
    ring = keep((2, rows, RING * HD), BF16)
    probs_kept = keep((heads, chunks, CHUNK + HD, HD), BF16)
    out_ring = keep((2, 3, rows, RING * HD), BF16)
    sems = pltpu.SemaphoreType.DMA
    queries, key_rows, value_rows, gate_input, out_grad = map(
        hbm, (queries, key_rows, value_rows, gate_input, out_grad)
    )
    doc_row = doc_start.reshape(1, rows)
    gain_row = norm_gain.reshape(1, cols)

    by_token = (rows, cols)
    steps = heads // GROUP
    (
        crow, enter, leave, rrow, keys, values, local, state, own_pass, gain, kept_q, *rings
    ) = call(
        functools.partial(state_kernel, chunks, steps),
        grid,
        [
            (hbm(x), anywhere)
            for x in (
                log_decay, doc_row, gain_row, key_rows, value_rows, queries, gate_input, out_grad
            )
        ],
        [keep((heads, rows), F32)] * 3
        + [
            keep((8, rows), F32), keep(by_token, BF16), keep(by_token, BF16),
            keep((heads, chunks - 1, HD, HD), F32), keep((heads, HD, HD), F32), keep((heads, HD), F32),
            keep((1, cols), F32), keep(by_token, BF16), ring, ring,
        ],
        [
            pltpu.VMEM((heads, rows), F32), pltpu.VMEM((1, rows), jnp.int32),
            sems((2, steps)), sems((3,)), sems((3,)),
        ],
        flops=small, moved=2 * big,
    )

    ready = []
    made = [kept_q, *rings]

    def fill_forward(window, tie):
        if not ready:
            ready[:] = call(
                prepare_kernel, (), kept(after(rrow, tie), crow, enter),
                [keep((chunks, CHUNK, CHUNK), F32), keep((rows, HD), F32)],
                flops=8 * rows * CHUNK,
            )
        mask, columns = ready
        ins = kept(after(crow, tie), columns, mask, keys, values, gain)
        ins += [(x, anywhere) for x in (queries, gate_input, out_grad)]
        aliases = {len(ins) + i: i for i in range(len(made))}
        ins += kept(*made)
        made[:] = call(
            functools.partial(inside_kernel, chunks, forward[window][0] // RING, heads // RING),
            (forward[window][1] // RING,),
            ins,
            [
                keep(by_token, BF16), ring, ring, keep(by_token, F32), keep(by_token, BF16),
                probs_kept,
            ],
            [sems((3,))],
            aliases=aliases,
            flops=2 * tile // WINDOWS, moved=5 * big // WINDOWS,
            exps=rows * (CHUNK + HD) * heads // WINDOWS,
        )
        return made[4]

    tall = pltpu.VMEM((rows, HD), F32)
    reduced = []

    def finish_forward(part, entering, refs):
        mask, columns = ready
        kept_q, _, _, inside, gnorm, _ = made
        ins = kept(columns, enter, kept_q, gnorm, local, *refs)
        outs = [keep(by_token, F32), keep(local_dims, BF16), keep((2, rows), F32)]
        scratch = [tall, tall]
        if part == 1:
            aliases = {len(ins) + 1: 0, len(ins) + 2: 1}
            ins += kept(reduced[1], inside, reduced[0])
        else:
            aliases = {len(ins): 0}
            ins += kept(inside)
        results = call(
            functools.partial(
                outside_kernel, chunks, entering, len(refs), part
            ),
            (heads // WIDE if part is None else heads // 2 // WIDE,),
            ins, outs, scratch, aliases,
            flops=small, moved=big,
        )
        made[3], *reduced[:] = results
        return reduced[1]

    passes = scan_devices(state, own_pass, None, fill_forward, finish_forward, False)
    mask, columns = ready
    kept_q, _, _, attn, gnorm, probs = made
    held, sums = reduced

    flat = []
    halves = [0, heads // 2]
    token = keep((8, HD), F32)

    def turn(sums):
        first = halves.pop(0)
        results = call(
            functools.partial(turn_kernel, chunks, first),
            (heads // 2 // WIDE,),
            kept(kept_q, attn, gain, sums, *flat),
            [keep(by_head, BF16), keep(by_token, BF16), token],
            aliases={4 + i: i for i in range(len(flat))},
            flops=rows * cols, moved=2 * big,
        )
        flat[:] = results[:2]
        return results[2]

    apart = 1
    while True:
        other_sums = lax.ppermute(sums, "head", [(i, i ^ apart) for i in range(parts)])
        done = turn(sums) if halves else done
        apart *= 2
        if apart >= parts:
            break
        (sums,) = call(add_kernel, (), kept(sums, other_sums, done), [keep((2, rows), F32)])
    while halves:
        done = turn(sums)
    turned_q, attn_flat = flat

    agrad, turned_agrad, bloc, back, alpha, *rings = call(
        functools.partial(grad_kernel, chunks),
        (heads // WIDE,),
        kept(enter, sums, other_sums, done, turned_q, gnorm, attn)
        + [(hbm(x), anywhere) for x in (gate_input, out_grad)],
        [
            keep(by_token, BF16), keep(by_head, BF16), keep((heads, chunks - 1, HD, HD), F32),
            keep((heads, HD, HD), F32), keep((rows, HD), F32), ring, ring,
        ],
        [tall, sems((2,))],
        {5: 0},
        flops=small, moved=big,
    )

    inner = [turned_q, turned_agrad, *rings]

    def fill_backward(window, tie):
        ins = kept(
            after(crow, tie), alpha, columns, mask, keys, values, attn_flat, held, agrad, probs,
            inner[0], inner[1],
        )
        ins += [(hbm(x), anywhere) for x in (gate_input, out_grad)]
        aliases = {10: 0, 11: 1}
        aliases.update({len(ins) - 2 + i: i for i in range(2, len(inner))})
        ins += kept(*inner[2:5]) + [(hbm(x), anywhere) for x in inner[5:]]
        inner[:] = call(
            functools.partial(
                inner_grad_kernel, chunks, backward[window][0] // RING, heads // RING
            ),
            (backward[window][1] // RING,),
            ins,
            [keep(by_head, BF16)] * 2 + [ring, ring, out_ring] + [wide_out] * 3,
            [sems((5,))],
            aliases=aliases,
            flops=(4 * tile + small) // WINDOWS, moved=7 * big // WINDOWS,
            exps=rows * (CHUNK + HD) * heads // WINDOWS,
        )
        return inner[5]

    grads = []

    def finish_backward(part, entering, refs):
        ins = kept(enter, leave, keys, values, *refs, inner[0], inner[1], bloc)
        scratch = [pltpu.VMEM((2, 2, rows, GROUP * HD), BF16), sems((2, 2))]
        if part == 1:
            aliases = {len(ins): 0, len(ins) + 1: 1}
            ins += [(hbm(x), anywhere) for x in grads]
            outs = [wide_out] * 2
        else:
            aliases = {len(ins) + 1 + i: i for i in range(3)}
            ins += kept(inner[4]) + [(hbm(x), anywhere) for x in inner[5:]]
            outs = [wide_out] * 5
            scratch.append(sems((3,)))
        results = call(
            functools.partial(
                outer_grad_kernel, chunks, heads // RING - 1, entering, len(refs), part
            ),
            (steps if part is None else steps // 2,),
            ins, outs, scratch, aliases,
            flops=2 * small, moved=2 * big,
        )
        grads[:] = results[-2:]
        if part != 1:
            inner[5:] = results[:3]
        return grads[0]

    scan_devices(back, own_pass, passes, fill_backward, finish_backward, True)
    dq, gated, gate_grad = inner[5:]
    return (gated, gate_grad, dq, *grads)


def solution(mesh):
    in_specs = (
        P("seq", "head"),
        P("seq", "head"),
        P("seq", "head"),
        P("head", "seq"),
        P("seq"),
        P("seq", "head"),
        P("head"),
        P("seq", "head"),
    )
    out_specs = (P("seq", "head"),) * 5
    return jax.shard_map(body, mesh=mesh, in_specs=in_specs, out_specs=out_specs, check_vma=False)
```
